32 devices in a mesh: dp: 8 (over z, y), head: 4 (over x, core).
Axes of the slice: x: 2, y: 2, z: 4, core: 2. Of those that a mesh axis runs over, the one named last changes fastest.
Arguments:
- ids: int32 [16, 512], P('dp'), may hold values from 0 to 31999
- targets: int32 [16, 512], P('dp'), may hold values from 0 to 31999
- target_mask: int32 [16, 512], P('dp'), may hold values from 0 to 1, as said below
- memory: bfloat16 [16, 512, 1024], P('dp'), may hold values from -6 to 6
- old_states: bfloat16 [16, 1536, 1024], P('dp'), may hold values from -6 to 6
- mem_fill: int32 [16], P('dp'), may hold values from 0 to 512, as said below
- comp_fill: int32 [16], P('dp'), may hold values from 0 to 512, as said below
- table: float32 [32000, 1024], P('head', 'dp'), may hold values from -0.5625 to 0.5625
- qkv: float32 [3, 1024, 1024], P(None, 'dp', 'head'), may hold values from -0.1875 to 0.1875
- wout: float32 [1024, 1024], P('head', 'dp'), may hold values from -1.5 to 1.5
- wconv: float32 [8, 384, 128], P('head', None, 'dp'), may hold values from -0.3125 to 0.3125
- wup: float32 [1024, 4096], P('dp', 'head'), may hold values from -0.1875 to 0.1875
- wdown: float32 [4096, 1024], P('head', 'dp'), may hold values from -0.09375 to 0.09375
- gains: float32 [3, 1024], P(None, 'dp'), may hold values from 0.5 to 1.5
- table_rows: float32 [32000], P('head'), may hold values from 3.0517577e-09 to 1.1444092e-08
- table_cols: float32 [1024], P('dp'), may hold values from 3.0517577e-09 to 1.1444092e-08
- qkv_rows: float32 [3, 1024], P(None, 'dp'), may hold values from 9.536743e-08 to 3.5762787e-07
- qkv_cols: float32 [1024], P('head'), may hold values from 9.536743e-08 to 3.5762787e-07
- out_rows: float32 [1024], P('head'), may hold values from 9.536743e-08 to 3.5762787e-07
- out_cols: float32 [1024], P('dp'), may hold values from 9.536743e-08 to 3.5762787e-07
- conv_rows: float32 [8, 384], P('head'), may hold values from 9.536743e-08 to 3.5762787e-07
- conv_cols: float32 [128], P('dp'), may hold values from 9.536743e-08 to 3.5762787e-07
- up_rows: float32 [1024], P('dp'), may hold values from 9.536743e-08 to 3.5762787e-07
- up_cols: float32 [4096], P('head'), may hold values from 9.536743e-08 to 3.5762787e-07
- down_rows: float32 [4096], P('head'), may hold values from 9.536743e-08 to 3.5762787e-07
- down_cols: float32 [1024], P('dp'), may hold values from 9.536743e-08 to 3.5762787e-07
- gains_second: float32 [3, 1024], P(None, 'dp'), may hold values from 3.8146973e-07 to 1.4305115e-06
Outputs:
- loss_sum: float32 [], replicated
- token_count: float32 [], replicated
- new_table: float32 [32000, 1024], P('head', 'dp')
- table_grad: float32 [32000, 1024], P('head', 'dp')
- new_table_rows: float32 [32000], P('head')
- new_table_cols: float32 [1024], P('dp')
- new_qkv: float32 [3, 1024, 1024], P(None, 'dp', 'head')
- qkv_grad: float32 [3, 1024, 1024], P(None, 'dp', 'head')
- new_qkv_rows: float32 [3, 1024], P(None, 'dp')
- new_qkv_cols: float32 [1024], P('head')
- new_wout: float32 [1024, 1024], P('head', 'dp')
- wout_grad: float32 [1024, 1024], P('head', 'dp')
- new_out_rows: float32 [1024], P('head')
- new_out_cols: float32 [1024], P('dp')
- new_wconv: float32 [8, 384, 128], P('head', None, 'dp')
- wconv_grad: float32 [8, 384, 128], P('head', None, 'dp')
- new_conv_rows: float32 [8, 384], P('head')
- new_conv_cols: float32 [128], P('dp')
- new_wup: float32 [1024, 4096], P('dp', 'head')
- wup_grad: float32 [1024, 4096], P('dp', 'head')
- new_up_rows: float32 [1024], P('dp')
- new_up_cols: float32 [4096], P('head')
- new_wdown: float32 [4096, 1024], P('head', 'dp')
- wdown_grad: float32 [4096, 1024], P('head', 'dp')
- new_down_rows: float32 [4096], P('head')
- new_down_cols: float32 [1024], P('dp')
- new_gains: float32 [3, 1024], P(None, 'dp')
- gains_grad: float32 [3, 1024], P(None, 'dp')
- new_gains_second: float32 [3, 1024], P(None, 'dp')
The draws below stay inside these ranges and needn't reach their ends.
Inputs may be any that keep to these rules, and one draw needn't show every extreme that they name: `target_mask`: position 0 of every stream counts. `mem_fill`: some stream has a full memory and some an empty one. `comp_fill`: some stream has a full compressed memory and some an empty one.
All inputs are finite; a program needn't handle non-finite values.
Results may differ from the reference program's by a relative error of at most 0.013.
The reference program's roundings to bfloat16 on the way count: a program that leaves them out, or rounds other values in their place, can miss the bound.
Values may be sent and summed in bfloat16 or wider, within the bound.
No kernel may reach another device: no remote copies, remote signals or barrier semaphores. Data moves between devices by JAX's collectives and lax.ppermute only.
A program may use at most 320 MiB of HBM per device.

```python
import math
import jax
import jax.numpy as jnp
import numpy as np
from jax import lax

D = 1024
H = 8
DH = 128
FF = 4096
V = 32000
SEG = 512
MEM = 512
CMEM = 512
RATE = 3
STEP = 10
STREAMS = 16


def draw_target_mask(key, part):
    key = jax.random.fold_in(key, 5)
    level = 250 + 500 * jnp.arange(STREAMS, dtype=jnp.int32) // STREAMS
    rolled = jax.random.randint(key, (STREAMS, SEG), 0, 1000)
    picked = (rolled < level[:, None]).astype(jnp.int32)
    return picked.at[:, 0].set(1)


def fill_counts(key, most):
    first, second = jax.random.split(key)
    counts = jax.random.randint(first, (STREAMS,), 0, most + 1)
    chosen = jax.random.randint(second, (), 0, STREAMS)
    counts = counts.at[chosen].set(most)
    return counts.at[(chosen + 1) % STREAMS].set(0)


def draw_mem_fill(key, part):
    key = jax.random.fold_in(key, 7)
    return fill_counts(key, MEM)


def draw_comp_fill(key, part):
    key = jax.random.fold_in(key, 9)
    return fill_counts(key, CMEM)


def draw_table(key, part):
    key = jax.random.fold_in(key, 11)
    ramp = jnp.arange(V, dtype=jnp.float32)[:, None] / V
    base = jnp.clip(jax.random.normal(key, (V, D), jnp.float32), -6.0, 6.0)
    rise = 1.0 + 2.0 * ramp
    return base * rise / math.sqrt(D)


def place_ends(values, key, least, high):
    longest = values.shape.index(max(values.shape))
    spots = []
    for shift in (0, 1):
        where = [jax.random.randint(jax.random.fold_in(key, axis), (), 0, length) for axis, length in enumerate(values.shape)]
        where[longest] = (where[longest] + shift) % values.shape[longest]
        spots.append(tuple(where))
    return values.at[spots[0]].set(least).at[spots[1]].set(high)


def steps_of(rng, dims, cuts, low, high):
    level = 1.0
    for dim, parts in cuts:
        draws = jax.random.uniform(jax.random.fold_in(jax.random.fold_in(rng, 6), dim), (parts,), jnp.float32, low / len(cuts), high / len(cuts))
        level = level * jnp.repeat(jnp.exp(draws), dims[dim] // parts).reshape((-1,) + (1,) * (len(dims) - 1 - dim))
    return level


def cumulative_ranks(count, skew):
    loads = [(1 << 20) // math.isqrt(standing ** skew) + 1 for standing in range(1, count + 1)]
    scale = 1 + sum(loads) // (1 << 30)
    return np.cumsum(np.array([max(1, weight // scale) for weight in loads]))


def ranked(key, shape, number_of, slope):
    listing = cumulative_ranks(number_of, slope)
    ticket = jax.random.randint(jax.random.fold_in(key, 1), shape, 0, int(listing[number_of - 1]))
    grade = jnp.searchsorted(jnp.asarray(listing, jnp.int32), ticket, side="right")
    return jax.random.permutation(jax.random.fold_in(key, 2), number_of)[grade].astype(jnp.int32)


def normal_values(stream_key, dims, spread, most, shards=(), held_as=jnp.bfloat16):
    values = jax.random.normal(stream_key, dims, jnp.float32) * spread
    if len(shards) > 0:
        values = steps_of(stream_key, dims, shards, -0.22, 0.18) * values
    return jnp.clip(values, min=-most, max=most).astype(held_as)


def setup_inputs(seed: int = 0) -> dict:
    arg_keys = jax.random.split(jax.random.key(seed), 28)
    return {
        "ids": place_ends(ranked(arg_keys[0], (STREAMS, SEG), V, 2), jax.random.fold_in(arg_keys[0], 3), 0, V - 1).astype(jnp.int32),
        "targets": place_ends(ranked(arg_keys[1], (STREAMS, SEG), V, 2), jax.random.fold_in(arg_keys[1], 3), 0, V - 1).astype(jnp.int32),
        "target_mask": draw_target_mask(jax.random.fold_in(arg_keys[27], 71), 0),
        "memory": normal_values(arg_keys[3], (STREAMS, MEM, D), 1.0, 6.0, ((0, 8),)),
        "old_states": normal_values(arg_keys[4], (STREAMS, RATE * CMEM, D), 1.0, 6.0, ((0, 8),)),
        "mem_fill": draw_mem_fill(jax.random.fold_in(arg_keys[27], 71), 0),
        "comp_fill": draw_comp_fill(jax.random.fold_in(arg_keys[27], 71), 0),
        "table": draw_table(jax.random.fold_in(arg_keys[27], 71), 0),
        "qkv": normal_values(arg_keys[8], (3, D, H * DH), D ** -0.5, 0.1875, ((1, 8), (2, 4)), jnp.float32),
        "wout": normal_values(arg_keys[9], (H * DH, D), (H * DH // 64) ** -0.5, 1.5, ((0, 4), (1, 8)), jnp.float32),
        "wconv": normal_values(arg_keys[10], (H, RATE * DH, DH), (RATE * DH) ** -0.5, 0.3125, ((0, 4), (2, 8)), jnp.float32),
        "wup": normal_values(arg_keys[11], (D, FF), D ** -0.5, 0.1875, ((0, 8), (1, 4)), jnp.float32),
        "wdown": normal_values(arg_keys[12], (FF, D), FF ** -0.5, 0.09375, ((0, 4), (1, 8)), jnp.float32),
        "gains": jnp.clip(1.0 + 0.1 * jax.random.normal(arg_keys[13], (3, D), jnp.float32), 0.5, 1.5),
        "table_rows": jnp.clip(jnp.exp(math.log(1.1444091896350983e-08) - 1.3217559 * jax.random.uniform(arg_keys[14], (V,), jnp.float32) ** steps_of(arg_keys[14], (V,), ((0, 4),), -0.2, 0.2)), 3.051757735406113e-09, 1.1444091896350983e-08),
        "table_cols": jnp.clip(jnp.exp(math.log(1.1444091896350983e-08) - 1.3217559 * jax.random.uniform(arg_keys[15], (D,), jnp.float32) ** steps_of(arg_keys[15], (D,), ((0, 8),), -0.2, 0.2)), 3.051757735406113e-09, 1.1444091896350983e-08),
        "qkv_rows": jnp.clip(jnp.exp(math.log(3.5762786865234375e-07) - 1.3217558 * jax.random.uniform(arg_keys[16], (3, D), jnp.float32) ** steps_of(arg_keys[16], (3, D), ((1, 8),), -0.2, 0.2)), 9.536743306171047e-08, 3.5762786865234375e-07),
        "qkv_cols": jnp.clip(jnp.exp(math.log(3.5762786865234375e-07) - 1.3217558 * jax.random.uniform(arg_keys[17], (H * DH,), jnp.float32) ** steps_of(arg_keys[17], (H * DH,), ((0, 4),), -0.2, 0.2)), 9.536743306171047e-08, 3.5762786865234375e-07),
        "out_rows": jnp.clip(jnp.exp(math.log(3.5762786865234375e-07) - 1.3217558 * jax.random.uniform(arg_keys[18], (H * DH,), jnp.float32) ** steps_of(arg_keys[18], (H * DH,), ((0, 4),), -0.2, 0.2)), 9.536743306171047e-08, 3.5762786865234375e-07),
        "out_cols": jnp.clip(jnp.exp(math.log(3.5762786865234375e-07) - 1.3217558 * jax.random.uniform(arg_keys[19], (D,), jnp.float32) ** steps_of(arg_keys[19], (D,), ((0, 8),), -0.2, 0.2)), 9.536743306171047e-08, 3.5762786865234375e-07),
        "conv_rows": jnp.clip(jnp.exp(math.log(3.5762786865234375e-07) - 1.3217558 * jax.random.uniform(arg_keys[20], (H, RATE * DH), jnp.float32) ** steps_of(arg_keys[20], (H, RATE * DH), ((0, 4),), -0.2, 0.2)), 9.536743306171047e-08, 3.5762786865234375e-07),
        "conv_cols": jnp.clip(jnp.exp(math.log(3.5762786865234375e-07) - 1.3217558 * jax.random.uniform(arg_keys[21], (DH,), jnp.float32) ** steps_of(arg_keys[21], (DH,), ((0, 8),), -0.2, 0.2)), 9.536743306171047e-08, 3.5762786865234375e-07),
        "up_rows": jnp.clip(jnp.exp(math.log(3.5762786865234375e-07) - 1.3217558 * jax.random.uniform(arg_keys[22], (D,), jnp.float32) ** steps_of(arg_keys[22], (D,), ((0, 8),), -0.2, 0.2)), 9.536743306171047e-08, 3.5762786865234375e-07),
        "up_cols": jnp.clip(jnp.exp(math.log(3.5762786865234375e-07) - 1.3217558 * jax.random.uniform(arg_keys[23], (FF,), jnp.float32) ** steps_of(arg_keys[23], (FF,), ((0, 4),), -0.2, 0.2)), 9.536743306171047e-08, 3.5762786865234375e-07),
        "down_rows": jnp.clip(jnp.exp(math.log(3.5762786865234375e-07) - 1.3217558 * jax.random.uniform(arg_keys[24], (FF,), jnp.float32) ** steps_of(arg_keys[24], (FF,), ((0, 4),), -0.2, 0.2)), 9.536743306171047e-08, 3.5762786865234375e-07),
        "down_cols": jnp.clip(jnp.exp(math.log(3.5762786865234375e-07) - 1.3217558 * jax.random.uniform(arg_keys[25], (D,), jnp.float32) ** steps_of(arg_keys[25], (D,), ((0, 8),), -0.2, 0.2)), 9.536743306171047e-08, 3.5762786865234375e-07),
        "gains_second": jnp.clip(jnp.exp(math.log(1.430511474609375e-06) - 1.3217558 * jax.random.uniform(arg_keys[26], (3, D), jnp.float32) ** steps_of(arg_keys[26], (3, D), ((1, 8),), -0.2, 0.2)), 3.814697322468419e-07, 1.430511474609375e-06),
    }


@jax.custom_vjp
def low(v):
    return lax.optimization_barrier(v.astype(jnp.bfloat16)).astype(jnp.float32)

@jax.custom_vjp
def low_back(v):
    return v

def low_keep(v):
    return (low(v), None)

def low_pass(kept, grad):
    return (grad,)

def back_keep(v):
    return (v, None)

def back_low(kept, grad):
    return (low(grad),)
low.defvjp(low_keep, low_pass)
low_back.defvjp(back_keep, back_low)
TINY_NORM = 1e-06
TINY_SQUARE = 1e-30
LEARN_RATE = 0.5
CLIP_LEVEL = 1.0
precise = lax.Precision.HIGHEST

def rms_norm(values, gain):
    return values * lax.rsqrt(lax.optimization_barrier(jnp.mean(values * values, axis=-1, keepdims=True)) + TINY_NORM) * gain

def round_both(values):
    return low(low_back(values))

def project(inputs, weight):
    return jnp.einsum('...d,de->...e', inputs, weight, precision=precise)

def visible_keys(mem_fill, comp_fill, seg_len):
    slots = jnp.arange(CMEM + MEM + seg_len, dtype=jnp.int32)[None, None, :]
    position = jnp.arange(seg_len, dtype=jnp.int32)[None, :, None]
    mem_count = mem_fill.astype(jnp.int32)[:, None, None]
    comp_count = comp_fill.astype(jnp.int32)[:, None, None]
    comp_ok = (slots < CMEM) & (slots >= CMEM - comp_count)
    mem_ok = (slots >= CMEM) & (slots < CMEM + MEM) & (slots >= CMEM + MEM - mem_count)
    own_ok = (slots >= CMEM + MEM) & (slots - CMEM - MEM <= position)
    return comp_ok | mem_ok | own_ok

def group_loss(weights, batch):
    table, qkv, wout, wconv, wup, wdown, gains = weights
    ids, targets, target_mask, memory, old_states, mem_fill, comp_fill = batch
    streams = ids.shape[0]
    width = H * DH
    embedded = table[ids].reshape(streams * SEG, D)
    normed = low(rms_norm(embedded, gains[0]))
    mem_normed = low(rms_norm(memory.astype(jnp.float32), gains[0]))
    old_normed = low(rms_norm(old_states.astype(jnp.float32), gains[0]))
    queries = round_both(project(normed, qkv[0]))
    conv_blocks = wconv.reshape(H, RATE, DH, DH)

    def squeeze(weight):
        raw = round_both(project(old_normed, weight)).reshape(streams, CMEM, RATE, H, DH)
        folded = jnp.einsum('scjhd,hjde->sche', raw, conv_blocks, precision=precise)
        return round_both(folded.reshape(streams, CMEM, width))

    def stacked(which):
        seg_part = round_both(project(normed, qkv[which])).reshape(streams, SEG, width)
        mem_part = round_both(project(mem_normed, qkv[which]))
        joined = jnp.concatenate([squeeze(qkv[which]), mem_part, seg_part], axis=1)
        return joined.reshape(streams, CMEM + MEM + SEG, H, DH)
    all_keys = stacked(1)
    all_values = stacked(2)
    scores = low_back(jnp.einsum('sqhd,skhd->shqk', queries.reshape(streams, SEG, H, DH), all_keys, precision=precise) * DH ** (-0.5))
    allowed = visible_keys(mem_fill, comp_fill, SEG)[:, None]
    probs = jax.nn.softmax(jnp.where(allowed, scores, -1e+30), axis=-1)
    mixed = round_both(jnp.einsum('shqk,skhd->sqhd', low(probs), all_values, precision=precise).reshape(streams * SEG, width))
    after_attn = embedded + low_back(jnp.dot(mixed, wout, precision=precise))
    ffn_in = low(rms_norm(after_attn, gains[1]))
    hidden_pre = low_back(jnp.dot(ffn_in, wup, precision=precise))
    hidden_act = low(jax.nn.gelu(hidden_pre))
    after_ffn = after_attn + low_back(jnp.dot(hidden_act, wdown, precision=precise))
    final_in = low(rms_norm(after_ffn, gains[2]))
    logits = low_back(jnp.einsum('rd,vd->rv', final_in, table, precision=precise))
    log_total = jax.nn.logsumexp(logits, axis=-1)
    picked = jnp.take_along_axis(logits, targets.reshape(-1, 1).astype(jnp.int32), axis=1)[:, 0]
    return jnp.sum(target_mask.reshape(-1).astype(jnp.float32) * (log_total - picked))

def reference(ids, targets, target_mask, memory, old_states, mem_fill, comp_fill, table, qkv, wout, wconv, wup, wdown, gains, table_rows, table_cols, qkv_rows, qkv_cols, out_rows, out_cols, conv_rows, conv_cols, up_rows, up_cols, down_rows, down_cols, gains_second):
    group = math.gcd(STREAMS, max(1, 4096 // SEG))
    batch = tuple((item.reshape((STREAMS // group, group) + item.shape[1:]) for item in (ids, targets, target_mask, memory, old_states, mem_fill, comp_fill)))
    mats = (table, qkv, wout, wconv, wup, wdown, gains)

    def total(weights):
        rounded = tuple((low(weight) for weight in weights))
        pieces = lax.map(jax.checkpoint(lambda packed: group_loss(rounded, packed)), batch)
        return jnp.sum(pieces)
    loss_sum, pull = jax.vjp(total, mats)
    raw = pull(jnp.ones_like(loss_sum))[0]
    token_count = jnp.sum(target_mask).astype(jnp.float32)
    grads = tuple((piece / token_count for piece in raw))
    decay = 1.0 - STEP ** (-0.8)
    shapes = ((V, D), (3 * D, H * DH), (H * DH, D), (H * RATE * DH, DH), (D, FF), (FF, D))
    stats = ((table_rows, table_cols), (qkv_rows, qkv_cols), (out_rows, out_cols), (conv_rows, conv_cols), (up_rows, up_cols), (down_rows, down_cols))
    results = [loss_sum, token_count]
    for index in range(6):
        weight = mats[index]
        matrix = grads[index].reshape(shapes[index])
        square = matrix * matrix + TINY_SQUARE
        rows_old, cols_old = stats[index]
        rows_new = decay * rows_old.reshape(-1) + (1.0 - decay) * lax.optimization_barrier(jnp.mean(square, axis=1))
        cols_new = decay * cols_old + (1.0 - decay) * lax.optimization_barrier(jnp.mean(square, axis=0))
        second = rows_new[:, None] * cols_new[None, :] / jnp.mean(rows_new)
        update = matrix * lax.rsqrt(second)
        scale = jnp.maximum(0.001, jnp.sqrt(jnp.mean(weight * weight)))
        denom = jnp.maximum(1.0, jnp.sqrt(jnp.mean(update * update)) / CLIP_LEVEL)
        new_weight = weight - LEARN_RATE * scale * update.reshape(weight.shape) / denom
        results += [new_weight, grads[index], rows_new.reshape(rows_old.shape), cols_new]
    gain_grad = grads[6]
    second_new = decay * gains_second + (1.0 - decay) * (gain_grad * gain_grad + TINY_SQUARE)
    update = gain_grad * lax.rsqrt(second_new)
    scale = jnp.maximum(0.001, jnp.sqrt(lax.optimization_barrier(jnp.mean(gains * gains, axis=1, keepdims=True))))
    denom = jnp.maximum(1.0, jnp.sqrt(lax.optimization_barrier(jnp.mean(update * update, axis=1, keepdims=True))) / CLIP_LEVEL)
    results += [gains - LEARN_RATE * scale * update / denom, gain_grad, second_new]
    return tuple(results)
```

```python
import math

import jax
import jax.numpy as jnp
from jax import lax
from jax.sharding import PartitionSpec as P

D = 1024
H = 8
DH = 128
MEM = 512
CMEM = 512
RATE = 3
STEP = 10


TINY_NORM = 1e-06
TINY_SQUARE = 1e-30
LEARN_RATE = 0.5
CLIP_LEVEL = 1.0


def merged(value, axis, combine):
    everything = jax.tree.map(lambda part: lax.all_gather(part, axis), value)
    first = jax.tree.map(lambda part: part[0], everything)

    def turn(k, so_far):
        return combine(so_far, jax.tree.map(lambda part: part[k], everything))

    return lax.fori_loop(1, lax.axis_size(axis), turn, first)


def swap(value, axis, mask):
    size = lax.axis_size(axis)
    return lax.ppermute(value, axis, [(i, i ^ mask) for i in range(size)])


def head_sum(part):
    rows, cols = part.shape
    low_bit = lax.axis_index("head") % 2
    high_bit = lax.axis_index("head") // 2
    cut = part.astype(jnp.bfloat16).reshape(2, 2, rows // 4, cols)
    kept = lax.dynamic_index_in_dim(cut, low_bit, 1, keepdims=False)
    gone = lax.dynamic_index_in_dim(cut, 1 - low_bit, 1, keepdims=False)
    half = kept.astype(jnp.float32) + swap(gone, "head", 1).astype(jnp.float32)
    half = half.astype(jnp.bfloat16)
    mine = lax.dynamic_index_in_dim(half, high_bit, 0, keepdims=False)
    other = lax.dynamic_index_in_dim(half, 1 - high_bit, 0, keepdims=False)
    own = mine.astype(jnp.float32) + swap(other, "head", 2).astype(jnp.float32)
    own = own.astype(jnp.bfloat16)
    far = swap(own, "head", 2)
    pair = jnp.where(high_bit == 0, jnp.stack([own, far]), jnp.stack([far, own]))
    near = swap(pair, "head", 1)
    both = jnp.where(low_bit == 0, jnp.stack([pair, near], 1), jnp.stack([near, pair], 1))
    return both.reshape(rows, cols).astype(jnp.float32)


def rms_norm(values, gain):
    return values * lax.rsqrt(jnp.mean(values * values, axis=-1, keepdims=True) + TINY_NORM) * gain


def norm_back(values, gain, upstream):
    return jax.vjp(rms_norm, values, gain)[1](upstream)


def gain_only(values, gain, upstream):
    return jax.vjp(lambda scaled: rms_norm(values, scaled), gain)[1](upstream)[0]


def visible_keys(mem_fill, comp_fill, seg_len):
    slots = jnp.arange(CMEM + MEM + seg_len, dtype=jnp.int32)[None, None, :]
    position = jnp.arange(seg_len, dtype=jnp.int32)[None, :, None]
    mem_count = mem_fill[:, None, None]
    comp_count = comp_fill[:, None, None]
    comp_ok = (slots < CMEM) & (slots >= CMEM - comp_count)
    mem_ok = (slots >= CMEM) & (slots < CMEM + MEM) & (slots >= CMEM + MEM - mem_count)
    own_ok = (slots >= CMEM + MEM) & (slots - CMEM - MEM <= position)
    return comp_ok | mem_ok | own_ok


def project(inputs, weight):
    return jnp.einsum("...d,de->...e", inputs, weight, preferred_element_type=jnp.float32)


def local(
    ids,
    targets,
    target_mask,
    memory,
    old_states,
    mem_fill,
    comp_fill,
    table,
    qkv,
    wout,
    wconv,
    wup,
    wdown,
    gains,
    table_rows,
    table_cols,
    qkv_rows,
    qkv_cols,
    out_rows,
    out_cols,
    conv_rows,
    conv_cols,
    up_rows,
    up_cols,
    down_rows,
    down_cols,
    gains_second,
):
    lowp = jnp.bfloat16
    single = jnp.float32
    axis_info = {
        "dp": (lax.axis_size("dp"), lax.axis_index("dp")),
        "head": (lax.axis_size("head"), lax.axis_index("head")),
    }
    heads_here, head_index = axis_info["head"]
    streams = ids.shape[0]
    seg_len = ids.shape[1]
    rows_here = streams * seg_len
    local_heads = H // heads_here
    width = local_heads * DH
    keys_total = CMEM + MEM + seg_len
    scale = DH ** (-0.5)
    full_table, full_qkv, full_out, full_conv, full_up, full_down, full_gains = (
        lax.all_gather(table.astype(lowp), "dp", axis=1, tiled=True),
        lax.all_gather(qkv.astype(lowp), "dp", axis=1, tiled=True),
        lax.all_gather(wout.astype(lowp), "dp", axis=1, tiled=True),
        lax.all_gather(wconv.astype(lowp), "dp", axis=2, tiled=True),
        lax.all_gather(wup.astype(lowp), "dp", axis=0, tiled=True),
        lax.all_gather(wdown.astype(lowp), "dp", axis=1, tiled=True),
        lax.all_gather(gains.astype(lowp), "dp", axis=1, tiled=True),
    )
    gain_vals = full_gains.astype(single)
    gain_one = gain_vals[0]
    vocab_here = full_table.shape[0]
    first_word = head_index * vocab_here
    local_ids = ids.reshape(-1) - first_word
    inside = (local_ids >= 0) & (local_ids < vocab_here)
    safe_ids = jnp.clip(local_ids, 0, vocab_here - 1)
    looked = jnp.where(inside[:, None], jnp.take(full_table, safe_ids, axis=0), jnp.zeros((), lowp))
    embedded = head_sum(looked)
    mem_float = memory.astype(single)
    old_float = old_states.astype(single)
    normed = rms_norm(embedded, gain_one).astype(lowp)
    mem_normed = rms_norm(mem_float, gain_one).astype(lowp)
    old_normed = rms_norm(old_float, gain_one).astype(lowp)
    queries = project(normed, full_qkv[0]).astype(lowp)
    conv_blocks = full_conv.reshape(local_heads, RATE, DH, DH)

    def old_blocks(raw):
        return raw.reshape(streams, CMEM, RATE, local_heads, DH)

    def squeeze(raw):
        folded = jnp.einsum(
            "scjhd,hjde->sche", old_blocks(raw), conv_blocks, preferred_element_type=single
        )
        return folded.reshape(streams, CMEM, width).astype(lowp)

    def stacked(which):
        seg_part = project(normed, full_qkv[which]).astype(lowp)
        mem_part = project(mem_normed, full_qkv[which]).astype(lowp)
        old_part = project(old_normed, full_qkv[which]).astype(lowp)
        joined = jnp.concatenate(
            [squeeze(old_part), mem_part, seg_part.reshape(streams, seg_len, width)], axis=1
        )
        return (joined.reshape(streams, keys_total, local_heads, DH), old_part)

    all_keys, old_keys = stacked(1)
    all_values, old_values = stacked(2)
    query_heads = queries.reshape(streams, seg_len, local_heads, DH)
    allowed = visible_keys(mem_fill, comp_fill, seg_len)[:, None]

    def attention_weights():
        scores = (
            jnp.einsum("sqhd,skhd->shqk", query_heads, all_keys, preferred_element_type=single)
            * scale
        )
        return jax.nn.softmax(jnp.where(allowed, scores, -1e30), axis=-1)

    probs = attention_weights()
    mixed = (
        jnp.einsum("shqk,skhd->sqhd", probs.astype(lowp), all_values, preferred_element_type=single)
        .reshape(rows_here, width)
        .astype(lowp)
    )
    attn_part = jnp.dot(mixed, full_out, preferred_element_type=single)
    after_attn = embedded + head_sum(attn_part)
    ffn_in = rms_norm(after_attn, gain_vals[1]).astype(lowp)
    hidden_pre = jnp.dot(ffn_in, full_up, preferred_element_type=single)
    hidden_act = jax.nn.gelu(hidden_pre).astype(lowp)
    ffn_part = jnp.dot(hidden_act, full_down, preferred_element_type=single)
    after_ffn = after_attn + head_sum(ffn_part)
    final_in = rms_norm(after_ffn, gain_vals[2]).astype(lowp)
    block_rows = math.gcd(rows_here, 512)
    blocks = rows_here // block_rows
    target_local = targets - first_word
    word_index = jnp.arange(vocab_here, dtype=jnp.int32)

    def logit_block(packed):
        inputs, wanted = packed
        logits = jnp.einsum("rd,vd->rv", inputs, full_table, preferred_element_type=single)
        highest = jnp.max(logits, axis=-1)
        summed = jnp.sum(jnp.exp(logits - highest[:, None]), axis=-1)
        hit = jnp.sum(jnp.where(wanted[:, None] == word_index[None, :], logits, 0.0), axis=-1)
        return (logits, highest, summed, hit)

    logits, highest, summed, hit = lax.map(
        logit_block, (final_in.reshape(blocks, block_rows, D), target_local)
    )

    def combine(first, second):
        upper = jnp.maximum(first[0], second[0])
        return (
            upper,
            first[1] * jnp.exp(first[0] - upper) + second[1] * jnp.exp(second[0] - upper),
            first[2] + second[2],
        )

    high_all, sum_all, hit_all = merged((highest, summed, hit), "head", combine)
    log_total = high_all + jnp.log(sum_all)
    counted = target_mask.astype(single)
    loss_local = jnp.sum(counted * (log_total - hit_all))
    count_local = jnp.sum(counted)
    onehot = (target_local[..., None] == word_index).astype(single)
    dlogits = ((jnp.exp(logits - log_total[..., None]) - onehot) * counted[..., None]).astype(lowp)
    dlog_flat = dlogits.reshape(rows_here, vocab_here)
    final_part = jnp.dot(dlog_flat, full_table, preferred_element_type=single)
    table_grad = jnp.einsum("rv,rd->vd", dlog_flat, final_in, preferred_element_type=single)
    final_grad = head_sum(final_part)
    grad_after_ffn, gain_three = norm_back(after_ffn, gain_vals[2], final_grad)
    down_in = grad_after_ffn.astype(lowp)
    act_grad = jnp.einsum("rd,fd->rf", down_in, full_down, preferred_element_type=single)
    down_grad = jnp.einsum("rf,rd->fd", hidden_act, down_in, preferred_element_type=single)
    pre_grad = jax.vjp(jax.nn.gelu, hidden_pre)[1](act_grad)[0].astype(lowp)
    up_grad = jnp.einsum("rd,rf->df", ffn_in, pre_grad, preferred_element_type=single)
    ffn_in_part = jnp.einsum("rf,df->rd", pre_grad, full_up, preferred_element_type=single)
    ffn_in_grad = head_sum(ffn_in_part)
    grad_mid, gain_two = norm_back(after_attn, gain_vals[1], ffn_in_grad)
    grad_after_attn = grad_after_ffn + grad_mid
    attn_in = grad_after_attn.astype(lowp)
    out_grad = jnp.einsum("rw,rd->wd", mixed, attn_in, preferred_element_type=single)
    mixed_grad = (
        jnp.einsum("rd,wd->rw", attn_in, full_out, preferred_element_type=single)
        .astype(lowp)
        .reshape(streams, seg_len, local_heads, DH)
    )
    probs = attention_weights()
    prob_grad = jnp.einsum("sqhd,skhd->shqk", mixed_grad, all_values, preferred_element_type=single)
    score_grad = (probs * (prob_grad - jnp.sum(probs * prob_grad, axis=-1, keepdims=True))).astype(
        lowp
    )
    query_grad = (
        (jnp.einsum("shqk,skhd->sqhd", score_grad, all_keys, preferred_element_type=single) * scale)
        .reshape(rows_here, width)
        .astype(lowp)
    )
    key_grad = (
        jnp.einsum("shqk,sqhd->skhd", score_grad, query_heads, preferred_element_type=single)
        * scale
    ).astype(lowp)
    value_grad = jnp.einsum(
        "shqk,sqhd->skhd", probs.astype(lowp), mixed_grad, preferred_element_type=single
    ).astype(lowp)

    def unsqueeze(grad_heads):
        spread = jnp.einsum(
            "sche,hjde->scjhd", grad_heads, conv_blocks, preferred_element_type=single
        )
        return spread.reshape(streams, RATE * CMEM, width).astype(lowp)

    comp_kg = key_grad[:, :CMEM]
    comp_vg = value_grad[:, :CMEM]
    conv_grad = (
        jnp.einsum("scjhd,sche->hjde", old_blocks(old_keys), comp_kg, preferred_element_type=single)
        + jnp.einsum(
            "scjhd,sche->hjde", old_blocks(old_values), comp_vg, preferred_element_type=single
        )
    ).reshape(local_heads, RATE * DH, DH)
    old_kg = unsqueeze(comp_kg)
    old_vg = unsqueeze(comp_vg)
    mem_kg = key_grad[:, CMEM : CMEM + MEM].reshape(streams, MEM, width)
    mem_vg = value_grad[:, CMEM : CMEM + MEM].reshape(streams, MEM, width)
    seg_kg = key_grad[:, CMEM + MEM :].reshape(rows_here, width)
    seg_vg = value_grad[:, CMEM + MEM :].reshape(rows_here, width)

    def weight_part(inputs, mem_in, old_in, seg_g, mem_g, old_g):
        return (
            jnp.einsum("rd,re->de", inputs, seg_g, preferred_element_type=single)
            + jnp.einsum("smd,sme->de", mem_in, mem_g, preferred_element_type=single)
            + jnp.einsum("smd,sme->de", old_in, old_g, preferred_element_type=single)
        )

    qkv_grad = jnp.stack(
        [
            jnp.einsum("rd,re->de", normed, query_grad, preferred_element_type=single),
            weight_part(normed, mem_normed, old_normed, seg_kg, mem_kg, old_kg),
            weight_part(normed, mem_normed, old_normed, seg_vg, mem_vg, old_vg),
        ]
    )

    def back_in(key_g, value_g):
        return jnp.einsum(
            "...e,de->...d", key_g, full_qkv[1], preferred_element_type=single
        ) + jnp.einsum("...e,de->...d", value_g, full_qkv[2], preferred_element_type=single)

    seg_in_part = back_in(seg_kg, seg_vg) + jnp.einsum(
        "re,de->rd", query_grad, full_qkv[0], preferred_element_type=single
    )
    side_part = gain_only(mem_float, gain_one, back_in(mem_kg, mem_vg)) + gain_only(
        old_float, gain_one, back_in(old_kg, old_vg)
    )
    seg_in_grad, side_gain = head_sum(seg_in_part), lax.psum(side_part, "head")
    grad_embed_norm, gain_first = norm_back(embedded, gain_one, seg_in_grad)
    embed_grad = grad_after_attn + grad_embed_norm
    table_grad = table_grad + jax.ops.segment_sum(
        jnp.where(inside[:, None], embed_grad, 0.0), safe_ids, num_segments=vocab_here
    )
    gains_grad = jnp.stack([gain_first + side_gain, gain_two, gain_three])
    grads = (
        lax.psum_scatter(table_grad.astype(lowp), "dp", scatter_dimension=1, tiled=True).astype(single),
        lax.psum_scatter(qkv_grad.astype(lowp), "dp", scatter_dimension=1, tiled=True).astype(single),
        lax.psum_scatter(out_grad.astype(lowp), "dp", scatter_dimension=1, tiled=True).astype(single),
        lax.psum_scatter(conv_grad, "dp", scatter_dimension=2, tiled=True),
        lax.psum_scatter(up_grad.astype(lowp), "dp", scatter_dimension=0, tiled=True).astype(single),
        lax.psum_scatter(down_grad.astype(lowp), "dp", scatter_dimension=1, tiled=True).astype(single),
        lax.psum_scatter(gains_grad, "dp", scatter_dimension=1, tiled=True),
    )
    weights_now = (table, qkv, wout, wconv, wup, wdown)
    rows_old = (table_rows, qkv_rows, out_rows, conv_rows, up_rows, down_rows)
    cols_old = (table_cols, qkv_cols, out_cols, conv_cols, up_cols, down_cols)
    row_axes = ("head", "dp", "head", "head", "dp", "head")
    col_axes = ("dp", "head", "dp", "dp", "head", "dp")
    row_part = []
    col_part = []
    scalar_list = []
    for index in range(6):
        square = grads[index] * grads[index]
        row_part.append(jnp.sum(square, axis=-1))
        col_part.append(jnp.sum(square, axis=tuple(range(square.ndim - 1))))
        scalar_list.append(jnp.sum(square))
        scalar_list.append(jnp.sum(rows_old[index]) / axis_info[col_axes[index]][0])
    scalar_list.append(loss_local / heads_here)
    scalar_list.append(count_local / heads_here)
    scalar_part = jnp.stack(scalar_list)
    row_e, row_o, row_c, row_d, col_q, col_u = lax.psum(
        (row_part[0], row_part[2], row_part[3], row_part[5], col_part[1], col_part[4]), "dp"
    )
    row_q, row_u, col_e, col_o, col_c, col_d = lax.psum(
        (row_part[1], row_part[4], col_part[0], col_part[2], col_part[3], col_part[5]), "head"
    )
    scalars = lax.psum(scalar_part, ("dp", "head"))
    row_sums = [row_e, row_q, row_o, row_c, row_u, row_d]
    col_sums = [col_e, col_q, col_o, col_c, col_u, col_d]
    loss_all = scalars[12]
    count_all = scalars[13]
    inverse = 1.0 / count_all
    decay = 1.0 - STEP ** (-0.8)
    updates = []
    stats_new = []
    scaled = []
    counts = []
    update_sq = []
    weight_sq = []
    for index in range(6):
        rows_total = rows_old[index].size * axis_info[row_axes[index]][0]
        cols_total = cols_old[index].size * axis_info[col_axes[index]][0]
        grad_scaled = grads[index] * inverse
        rows_new = decay * rows_old[index] + (1.0 - decay) * (
            row_sums[index] * inverse * inverse / cols_total + TINY_SQUARE
        )
        cols_new = decay * cols_old[index] + (1.0 - decay) * (
            col_sums[index] * inverse * inverse / rows_total + TINY_SQUARE
        )
        mean_row = decay * scalars[2 * index + 1] / rows_total + (1.0 - decay) * (
            scalars[2 * index] * inverse * inverse / (rows_total * cols_total) + TINY_SQUARE
        )
        second = rows_new[..., None] * cols_new / mean_row
        direction = grad_scaled * lax.rsqrt(second)
        updates.append(direction)
        stats_new.append((rows_new, cols_new))
        scaled.append(grad_scaled)
        counts.append(rows_total * cols_total)
        update_sq.append(jnp.sum(direction * direction))
        weight_sq.append(jnp.sum(weights_now[index] * weights_now[index]))
    gain_scaled = grads[6] * inverse
    second_new = decay * gains_second + (1.0 - decay) * (gain_scaled * gain_scaled + TINY_SQUARE)
    gain_dir = gain_scaled * lax.rsqrt(second_new)
    for which in range(3):
        update_sq.append(jnp.sum(gain_dir[which] * gain_dir[which]) / heads_here)
        weight_sq.append(jnp.sum(gains[which] * gains[which]) / heads_here)
    update_total, weight_total = lax.psum(
        (jnp.stack(update_sq), jnp.stack(weight_sq)), ("dp", "head")
    )
    results = [loss_all, count_all]
    for index in range(6):
        factor = jnp.maximum(0.001, jnp.sqrt(weight_total[index] / counts[index]))
        denom = jnp.maximum(1.0, jnp.sqrt(update_total[index] / counts[index]) / CLIP_LEVEL)
        new_weight = weights_now[index] - LEARN_RATE * factor * updates[index] / denom
        results += [new_weight, scaled[index], stats_new[index][0], stats_new[index][1]]
    gain_factor = jnp.maximum(0.001, jnp.sqrt(weight_total[6:] / D))[:, None]
    gain_denom = jnp.maximum(1.0, jnp.sqrt(update_total[6:] / D) / CLIP_LEVEL)[:, None]
    results += [gains - LEARN_RATE * gain_factor * gain_dir / gain_denom, gain_scaled, second_new]
    return tuple(results)


def solution(mesh):
    in_specs = (
        P("dp", None),
        P("dp", None),
        P("dp", None),
        P("dp", None, None),
        P("dp", None, None),
        P("dp"),
        P("dp"),
        P("head", "dp"),
        P(None, "dp", "head"),
        P("head", "dp"),
        P("head", None, "dp"),
        P("dp", "head"),
        P("head", "dp"),
        P(None, "dp"),
        P("head"),
        P("dp"),
        P(None, "dp"),
        P("head"),
        P("head"),
        P("dp"),
        P("head", None),
        P("dp"),
        P("dp"),
        P("head"),
        P("head"),
        P("dp"),
        P(None, "dp"),
    )
    out_specs = (
        P(),
        P(),
        P("head", "dp"),
        P("head", "dp"),
        P("head"),
        P("dp"),
        P(None, "dp", "head"),
        P(None, "dp", "head"),
        P(None, "dp"),
        P("head"),
        P("head", "dp"),
        P("head", "dp"),
        P("head"),
        P("dp"),
        P("head", None, "dp"),
        P("head", None, "dp"),
        P("head", None),
        P("dp"),
        P("dp", "head"),
        P("dp", "head"),
        P("dp"),
        P("head"),
        P("head", "dp"),
        P("head", "dp"),
        P("head"),
        P("dp"),
        P(None, "dp"),
        P(None, "dp"),
        P(None, "dp"),
    )
    return jax.shard_map(local, mesh=mesh, in_specs=in_specs, out_specs=out_specs, check_vma=False)
```

```python
import functools

import jax
import jax.numpy as jnp
from jax import lax
from jax.experimental import pallas as pl
from jax.experimental.pallas import tpu as pltpu
from jax.sharding import PartitionSpec as P

D = 1024
H = 8
DH = 128
MEM = 512
CMEM = 512
RATE = 3
STEP = 10


TINY_NORM = 1e-06
TINY_SQUARE = 1e-30
LEARN_RATE = 0.5
CLIP_LEVEL = 1.0

lowp = jnp.bfloat16
single = jnp.float32
NT = (((1,), (1,)), ((), ()))
TN = (((0,), (0,)), ((), ()))
NN = (((1,), (0,)), ((), ()))
MIB = 1024 * 1024


def mm(left, right, dims=NN):
    return lax.dot_general(left, right, dims, preferred_element_type=single)


def swap(value, axis, mask):
    size = lax.axis_size(axis)
    return lax.ppermute(value, axis, [(i, i ^ mask) for i in range(size)])


def after(value, dep):
    return lax.optimization_barrier((value, dep))[0]


def block_order(size):
    return list(range(0, size, 2)) + list(range(1, size, 2))


def gather_blocks(piece, axis):
    size = lax.axis_size("dp")
    near = jnp.concatenate([piece] + [swap(piece, "dp", m) for m in range(2, size, 2)], axis=axis)
    return jnp.concatenate([near, swap(near, "dp", 1)], axis=axis)


def split(value, axis, parts):
    width = value.shape[axis] // parts
    return [lax.slice_in_dim(value, i * width, (i + 1) * width, axis=axis) for i in range(parts)]


def reduce_blocks(own, far, axis):
    size = lax.axis_size("dp")
    total = own + swap(far.astype(lowp), "head", 2).astype(single)
    keep, send = split(total, axis, 2)
    keep = keep + swap(send.astype(lowp), "dp", 1).astype(single)
    pieces = split(keep, axis, size // 2)
    result = pieces[0]
    for i in range(1, size // 2):
        result = result + swap(pieces[i].astype(lowp), "dp", 2 * i).astype(single)
    return result


def reorder(value, mask):
    if mask == 0:
        return value
    order = block_order(lax.axis_size("dp"))
    cols = split(value, 1, len(order))
    return jnp.concatenate([cols[order.index(j ^ mask)] for j in order], axis=1)


def relative(value, x, c):
    value = jnp.where(x == 1, jnp.flip(value, -3), value)
    value = jnp.where(c == 1, jnp.flip(value, -2), value)
    return jnp.swapaxes(value, -3, -2)


def rms(values, gain):
    inv = lax.rsqrt(jnp.mean(values * values, axis=-1, keepdims=True) + TINY_NORM)
    return (values * inv * gain).astype(lowp), inv


def rms_back(values, inv, gain, upstream):
    scaled = gain * upstream
    inner = jnp.sum(scaled * values, axis=-1, keepdims=True) / D
    return scaled * inv - values * (inner * inv * inv * inv)


def vmem(shape=None, index=None):
    if shape is None:
        return pl.BlockSpec(memory_space=pltpu.VMEM)
    return pl.BlockSpec(shape, index)


def smem():
    return pl.BlockSpec(memory_space=pltpu.SMEM)


def params(mib):
    return pltpu.CompilerParams(vmem_limit_bytes=mib * MIB)


def lookup_kernel(first_ref, ids_ref, table_ref, out_ref, tok_ref, row_ref, count_ref, held):
    total = ids_ref.shape[0]
    vocab = table_ref.shape[0]
    first = first_ref[0]

    def group(g, count):
        for j in range(8):
            t = g * 8 + j
            word = ids_ref[t] - first
            inside = jnp.logical_and(word >= 0, word < vocab)
            safe = jnp.where(inside, word, 0)
            flag = jnp.where(inside, 1, 0)
            held[pl.ds(t, 1), :] = table_ref[pl.ds(safe, 1), :] * flag.astype(single)
            tok_ref[count] = t
            row_ref[count] = safe
            count = count + flag
        return count

    count = lax.fori_loop(0, total // 8, group, jnp.int32(0))
    for j in range(8):
        tok_ref[count + j] = total
        row_ref[count + j] = 0
    count_ref[0] = count

    @pl.loop(0, total // 512)
    def _(i):
        rows = pl.ds(pl.multiple_of(i * 512, 512), 512)
        out_ref[rows, :] = held[rows, :].astype(lowp)


def lookup(first, ids, table):
    total = ids.shape[0]
    width = table.shape[1]
    return pl.pallas_call(
        lookup_kernel,
        out_shape=(
            jax.ShapeDtypeStruct((total, width), lowp),
            jax.ShapeDtypeStruct((total + 8,), jnp.int32),
            jax.ShapeDtypeStruct((total + 8,), jnp.int32),
            jax.ShapeDtypeStruct((1,), jnp.int32),
        ),
        in_specs=[smem(), smem(), vmem()],
        out_specs=(vmem(), smem(), smem(), smem()),
        scratch_shapes=[pltpu.VMEM((total, width), single)],
        compiler_params=params(40),
    )(first, ids, table)


def scatter_kernel(count_ref, tok_ref, row_ref, base_ref, grad_ref, out_ref, rows):
    total = grad_ref.shape[0]
    vocab = base_ref.shape[0]

    @pl.loop(0, total // 512)
    def _(i):
        here = pl.ds(pl.multiple_of(i * 512, 512), 512)
        rows[here, :] = grad_ref[here, :].astype(single)

    rows[pl.ds(total, 8), :] = jnp.zeros((8, rows.shape[1]), single)

    @pl.loop(0, vocab // 400)
    def _(i):
        here = pl.ds(pl.multiple_of(i * 400, 400), 400)
        out_ref[here, :] = base_ref[here, :]

    def group(g, carry):
        for j in range(8):
            token = tok_ref[g * 8 + j]
            row = row_ref[g * 8 + j]
            out_ref[pl.ds(row, 1), :] = out_ref[pl.ds(row, 1), :] + rows[pl.ds(token, 1), :]
        return carry

    lax.fori_loop(0, (count_ref[0] + 7) // 8, group, jnp.int32(0))


def scatter(count, tok, row, base, grad):
    total, width = grad.shape
    return pl.pallas_call(
        scatter_kernel,
        out_shape=jax.ShapeDtypeStruct(base.shape, single),
        in_specs=[smem(), smem(), smem(), vmem(), vmem()],
        out_specs=vmem(),
        scratch_shapes=[pltpu.VMEM((total + 8, width), single)],
        compiler_params=params(48),
    )(count, tok, row, base, grad)


def state_kernel(order, width, place_ref, gain_ref, in_ref, out_ref, held):
    rows = in_ref.shape[1]
    values = in_ref[0].astype(single)
    inv = lax.rsqrt(jnp.mean(values * values, axis=-1, keepdims=True) + TINY_NORM)
    for p, j in enumerate(order):
        start = pl.multiple_of((place_ref[1] ^ j) * width, width)
        block = in_ref[0, :, pl.ds(start, width)].astype(single)
        held[p] = block * inv * gain_ref[:, p * width : (p + 1) * width]
    groups = out_ref.shape[0]
    for p in range(len(order)):
        cols = slice(p * width, (p + 1) * width)
        if groups == 1:
            out_ref[0, :, cols] = held[p].astype(lowp)
        else:
            for j in range(groups):
                part = held[p, pl.ds(j, rows // groups, stride=groups), :]
                out_ref[j, :, cols] = part.astype(lowp)


def state_norm(place, gain, states, groups):
    size = lax.axis_size("dp")
    order = block_order(size)
    width = D // size
    count = states.shape[1] // groups
    if width % 128:
        values = lax.dynamic_index_in_dim(states, place[0], 0, keepdims=False).astype(single)
        inv = lax.rsqrt(jnp.mean(values * values, axis=-1, keepdims=True) + TINY_NORM)
        lanes = jnp.arange(D, dtype=jnp.int32)
        blocks = jnp.asarray(order, jnp.int32)[lanes // width] ^ place[1]
        source = blocks * width + lanes % width
        shuffle = (lanes[:, None] == source[None, :]).astype(single)
        moved = jnp.dot(values * inv, shuffle, precision=lax.Precision.HIGHEST)
        out = (moved * gain).astype(lowp)
        return jnp.swapaxes(out.reshape(count, groups, D), 0, 1)
    tile = 128
    return pl.pallas_call(
        functools.partial(state_kernel, order, width),
        out_shape=jax.ShapeDtypeStruct((groups, count, D), lowp),
        grid_spec=pltpu.PrefetchScalarGridSpec(
            num_scalar_prefetch=1,
            grid=(count // tile,),
            in_specs=[
                pl.BlockSpec((1, D), lambda i, s: (0, 0)),
                pl.BlockSpec((1, tile * groups, D), lambda i, s: (s[0], i, 0)),
            ],
            out_specs=pl.BlockSpec((groups, tile, D), lambda i, s: (0, i, 0)),
            scratch_shapes=[pltpu.VMEM((len(order), tile * groups, width), single)],
        ),
        compiler_params=params(24),
    )(place, gain, states)


def compress_kernel(old_ref, weight_ref, conv_ref, comp_ref, raw_ref):
    heads = conv_ref.shape[0]
    sums = [None] * (2 * heads)
    for j in range(RATE):
        raw = mm(old_ref[j], weight_ref[...]).astype(lowp)
        raw_ref[j] = raw
        for n in range(2 * heads):
            piece = raw[:, n * DH : (n + 1) * DH]
            term = mm(piece, conv_ref[n % heads, j * DH : (j + 1) * DH, :])
            sums[n] = term if j == 0 else sums[n] + term
    for n in range(2 * heads):
        comp_ref[:, n * DH : (n + 1) * DH] = sums[n].astype(lowp)


def compress(old3, weight, conv):
    rows = old3.shape[1]
    wide = weight.shape[1]
    tile = 256
    return pl.pallas_call(
        compress_kernel,
        grid=(rows // tile,),
        out_shape=(
            jax.ShapeDtypeStruct((rows, wide), lowp),
            jax.ShapeDtypeStruct((RATE, rows, wide), lowp),
        ),
        in_specs=[
            pl.BlockSpec((RATE, tile, D), lambda i: (0, i, 0)),
            pl.BlockSpec(weight.shape, lambda i: (0, 0)),
            pl.BlockSpec(conv.shape, lambda i: (0, 0, 0)),
        ],
        out_specs=(
            pl.BlockSpec((tile, wide), lambda i: (i, 0)),
            pl.BlockSpec((RATE, tile, wide), lambda i: (0, i, 0)),
        ),
        compiler_params=params(40),
    )(old3, weight, conv)


def expand_kernel(grad_ref, raw_ref, conv_ref, out_ref, conv_out_ref):
    heads = conv_ref.shape[0]
    for h in range(heads):
        for j in range(RATE):
            rows = slice(j * DH, (j + 1) * DH)
            taps = conv_ref[h, rows, :]
            total = None
            for n in (h, heads + h):
                cols = slice(n * DH, (n + 1) * DH)
                grad = grad_ref[:, cols]
                out_ref[j, :, cols] = mm(grad, taps, NT).astype(lowp)
                term = mm(raw_ref[j, :, cols], grad, TN)
                total = term if total is None else total + term
            conv_out_ref[h, rows, :] = total


def expand(grad, raw, conv):
    return pl.pallas_call(
        expand_kernel,
        out_shape=(
            jax.ShapeDtypeStruct(raw.shape, lowp),
            jax.ShapeDtypeStruct(conv.shape, single),
        ),
        in_specs=[vmem()] * 3,
        out_specs=(vmem(), vmem()),
        compiler_params=params(40),
    )(grad, raw, conv)


def masked_scores(info_ref, query, keys):
    rows = query.shape[0]
    scale = DH ** (-0.5)
    result = []
    for which, key in enumerate(keys):
        slots = key.shape[0]
        col = lax.broadcasted_iota(jnp.int32, (rows, slots), 1)
        if which < 2:
            seen = col >= slots - info_ref[which]
        else:
            row = lax.broadcasted_iota(jnp.int32, (rows, slots), 0)
            shift = info_ref[2]
            row = row + shift
            col = col + shift
            row = jnp.where(row >= slots, row - slots, row)
            col = jnp.where(col >= slots, col - slots, col)
            seen = col <= row
        result.append(jnp.where(seen, mm(query, key, NT) * scale, -1e30))
    return result


def attend_kernel(info_ref, q_ref, ks_ref, vs_ref, kc_ref, vc_ref, km_ref, vm_ref, out_ref, lse_ref):
    query = q_ref[...]
    scores = masked_scores(info_ref, query, [kc_ref[...], km_ref[...], ks_ref[...]])
    top = functools.reduce(jnp.maximum, [jnp.max(s, axis=-1, keepdims=True) for s in scores])
    total = 0.0
    mixed = 0.0
    for score, value in zip(scores, (vc_ref, vm_ref, vs_ref)):
        weight = jnp.exp(score - top)
        total = total + jnp.sum(weight, axis=-1, keepdims=True)
        mixed = mixed + mm(weight.astype(lowp), value[...])
    out_ref[...] = (mixed / total).astype(lowp)
    lse_ref[0] = top + jnp.log(total)


def attend_back_kernel(
    info_ref, q_ref, ks_ref, vs_ref, kc_ref, vc_ref, km_ref, vm_ref, lse_ref, up_ref,
    seg_ref, comp_ref, mem_ref,
):
    head = pl.program_id(0)
    wide = pl.num_programs(0) * DH
    scale = DH ** (-0.5)
    query = q_ref[...]
    upstream = up_ref[...]
    keys = [kc_ref[...], km_ref[...], ks_ref[...]]
    scores = masked_scores(info_ref, query, keys)
    probs = [jnp.exp(s - lse_ref[0]) for s in scores]
    prob_grads = [mm(upstream, v[...], NT) for v in (vc_ref, vm_ref, vs_ref)]
    inner = 0.0
    for p, g in zip(probs, prob_grads):
        inner = inner + jnp.sum(p * g, axis=-1, keepdims=True)
    here = pl.ds(pl.multiple_of(head * DH, DH), DH)
    second = pl.ds(pl.multiple_of(wide + head * DH, DH), DH)
    third = pl.ds(pl.multiple_of(2 * wide + head * DH, DH), DH)
    query_grad = 0.0
    places = ((comp_ref, here, second), (mem_ref, here, second), (seg_ref, second, third))
    for p, g, key, (ref, key_at, value_at) in zip(probs, prob_grads, keys, places):
        score_grad = (p * (g - inner)).astype(lowp)
        query_grad = query_grad + mm(score_grad, key)
        ref[:, key_at] = (mm(score_grad, query, TN) * scale).astype(lowp)
        ref[:, value_at] = mm(p.astype(lowp), upstream, TN).astype(lowp)
    seg_ref[:, here] = (query_grad * scale).astype(lowp)


def head_specs(seg, comp, mem, heads):
    def cols(array, first):
        return pl.BlockSpec((array.shape[0], DH), lambda h: (0, first + h))

    return [
        smem(),
        cols(seg, 0),
        cols(seg, heads),
        cols(seg, 2 * heads),
        cols(comp, 0),
        cols(comp, heads),
        cols(mem, 0),
        cols(mem, heads),
    ]


def attend(info, seg, comp, mem):
    rows = seg.shape[0]
    heads = comp.shape[1] // (2 * DH)
    return pl.pallas_call(
        attend_kernel,
        grid=(heads,),
        out_shape=(
            jax.ShapeDtypeStruct((rows, heads * DH), lowp),
            jax.ShapeDtypeStruct((heads, rows, 1), single),
        ),
        in_specs=head_specs(seg, comp, mem, heads),
        out_specs=(
            pl.BlockSpec((rows, DH), lambda h: (0, h)),
            pl.BlockSpec((1, rows, 1), lambda h: (h, 0, 0)),
        ),
        compiler_params=params(48),
    )(info, seg, seg, seg, comp, comp, mem, mem)


def attend_back(info, seg, comp, mem, lse, upstream):
    rows = seg.shape[0]
    heads = comp.shape[1] // (2 * DH)
    whole = lambda h: (0, 0)
    return pl.pallas_call(
        attend_back_kernel,
        grid=(heads,),
        out_shape=(
            jax.ShapeDtypeStruct(seg.shape, lowp),
            jax.ShapeDtypeStruct(comp.shape, lowp),
            jax.ShapeDtypeStruct(mem.shape, lowp),
        ),
        in_specs=head_specs(seg, comp, mem, heads)
        + [
            pl.BlockSpec((1, rows, 1), lambda h: (h, 0, 0)),
            pl.BlockSpec((rows, DH), lambda h: (0, h)),
        ],
        out_specs=(
            pl.BlockSpec(seg.shape, whole),
            pl.BlockSpec(comp.shape, whole),
            pl.BlockSpec(mem.shape, whole),
        ),
        compiler_params=params(56),
    )(info, seg, seg, seg, comp, comp, mem, mem, lse, upstream)


def columns_of(rows):
    tall = jnp.concatenate([rows, jnp.zeros((120, rows.shape[1]), single)], axis=0)
    return jnp.transpose(tall)


def logits_kernel(words, info_ref, in_ref, table_ref, out_ref, stat_ref):
    logits = mm(in_ref[...], table_ref[...], NT)
    wanted = columns_of(info_ref[...])[:, 0:1].astype(jnp.int32)
    col = lax.broadcasted_iota(jnp.int32, logits.shape, 1)
    hit = jnp.sum(jnp.where(col == wanted, logits, 0.0), axis=-1, keepdims=True)
    logits = jnp.where(col < words, logits, -1e30)
    top = jnp.max(logits, axis=-1, keepdims=True)
    raised = jnp.exp(logits - top)
    total = jnp.sum(raised, axis=-1, keepdims=True)
    out_ref[...] = raised.astype(lowp)
    lane = lax.broadcasted_iota(jnp.int32, (logits.shape[0], 128), 1)
    packed = jnp.where(lane == 0, top, jnp.where(lane == 1, total, jnp.where(lane == 2, hit, 0.0)))
    stat_ref[...] = jnp.transpose(packed)[:8]


def logits_part(words, info, inputs, table):
    rows = inputs.shape[0]
    slots = table.shape[0]
    tile = 256
    return pl.pallas_call(
        functools.partial(logits_kernel, words),
        grid=(rows // tile,),
        out_shape=(
            jax.ShapeDtypeStruct((rows, slots), lowp),
            jax.ShapeDtypeStruct((8, rows), single),
        ),
        in_specs=[
            pl.BlockSpec((8, tile), lambda i: (0, i)),
            pl.BlockSpec((tile, D), lambda i: (i, 0)),
            pl.BlockSpec(table.shape, lambda i: (0, 0)),
        ],
        out_specs=(
            pl.BlockSpec((tile, slots), lambda i: (i, 0)),
            pl.BlockSpec((8, tile), lambda i: (0, i)),
        ),
        compiler_params=params(40),
    )(info, inputs, table)


def logits_back_kernel(info_ref, in_ref, table_ref, out_ref, grad_ref):
    info = columns_of(info_ref[...])
    wanted = info[:, 0:1].astype(jnp.int32)
    counted = info[:, 1:2]
    factor = info[:, 2:3]
    raised = in_ref[...].astype(single)
    col = lax.broadcasted_iota(jnp.int32, raised.shape, 1)
    grads = (raised * factor - jnp.where(col == wanted, counted, 0.0)).astype(lowp)
    out_ref[...] = grads
    grad_ref[...] = mm(grads, table_ref[...]).astype(lowp)


def logits_back(info, raised, table):
    rows, slots = raised.shape
    tile = 256
    return pl.pallas_call(
        logits_back_kernel,
        grid=(rows // tile,),
        out_shape=(
            jax.ShapeDtypeStruct((rows, slots), lowp),
            jax.ShapeDtypeStruct((rows, D), lowp),
        ),
        in_specs=[
            pl.BlockSpec((8, tile), lambda i: (0, i)),
            pl.BlockSpec((tile, slots), lambda i: (i, 0)),
            pl.BlockSpec(table.shape, lambda i: (0, 0)),
        ],
        out_specs=(
            pl.BlockSpec((tile, slots), lambda i: (i, 0)),
            pl.BlockSpec((tile, D), lambda i: (i, 0)),
        ),
        compiler_params=params(40),
    )(info, raised, table)


def table_grad_kernel(count, *refs):
    grads = refs[:count]
    inputs = refs[count : 2 * count]
    keep_ref, send_ref = refs[2 * count :]
    total = mm(grads[0][...], inputs[0][...], TN)
    for i in range(1, count):
        total = total + mm(grads[i][...], inputs[i][...], TN)
    half = keep_ref.shape[1]
    keep_ref[...] = total[:, :half]
    send_ref[...] = total[:, half:].astype(send_ref.dtype)


def table_grad_part(grads, inputs):
    count = len(grads)
    rows, slots = grads[0].shape
    block = min(256, slots)
    return pl.pallas_call(
        functools.partial(table_grad_kernel, count),
        grid=(slots // block,),
        out_shape=(
            jax.ShapeDtypeStruct((slots, D // 2), single),
            jax.ShapeDtypeStruct((slots, D // 2), lowp),
        ),
        in_specs=[pl.BlockSpec((rows, block), lambda i: (0, i))] * count
        + [pl.BlockSpec((rows, D), lambda i: (0, 0))] * count,
        out_specs=(
            pl.BlockSpec((block, D // 2), lambda i: (i, 0)),
            pl.BlockSpec((block, D // 2), lambda i: (i, 0)),
        ),
        compiler_params=params(56),
    )(*grads, *inputs)


def local(
    ids,
    targets,
    target_mask,
    memory,
    old_states,
    mem_fill,
    comp_fill,
    table,
    qkv,
    wout,
    wconv,
    wup,
    wdown,
    gains,
    table_rows,
    table_cols,
    qkv_rows,
    qkv_cols,
    out_rows,
    out_cols,
    conv_rows,
    conv_cols,
    up_rows,
    up_cols,
    down_rows,
    down_cols,
    gains_second,
):
    dp_size, head_size = lax.axis_size("dp"), lax.axis_size("head")
    d, h = lax.axis_index("dp"), lax.axis_index("head")
    x, c = h // 2, h % 2
    order = block_order(dp_size)
    reach = dp_size // 2
    streams, seg_len = ids.shape
    half = seg_len // 2
    per_group = streams * seg_len
    vocab, width = table.shape
    assert head_size == 4 and streams == 2

    flat = jnp.concatenate(
        [
            ids.astype(single).reshape(-1),
            targets.astype(single).reshape(-1),
            target_mask.astype(single).reshape(-1),
            gains.astype(lowp).astype(single).reshape(-1),
        ]
    )
    room = -flat.shape[0] % 1024
    flat = jnp.concatenate([flat, jnp.zeros((room,), single)]).reshape(1, -1, 128)
    small = gather_blocks(flat, 0).reshape(dp_size, -1)

    def field(i):
        raw = small[:, i * per_group : (i + 1) * per_group]
        return relative(raw.reshape(dp_size, 2, 2, half), x, c)

    ids_all = jnp.transpose(field(0), (1, 2, 0, 3)).reshape(-1).astype(jnp.int32)
    targets_all = field(1)
    mask_all = field(2)
    gain_blocks = small[:, 3 * per_group : 3 * per_group + 3 * width].reshape(dp_size, 3, width)
    gain_vals = jnp.swapaxes(gain_blocks, 0, 1).reshape(3, 1, D)
    count_all = jnp.sum(small[:, 2 * per_group : 3 * per_group])

    low_qkv = qkv.astype(lowp)
    own_qkv = gather_blocks(low_qkv, 1)
    full_qkv = jnp.concatenate([own_qkv, swap(own_qkv, "head", 2)], axis=2)
    low_conv = wconv.astype(lowp)
    near_conv = gather_blocks(low_conv, 2)
    conv_lanes = jnp.arange(DH, dtype=jnp.int32)
    conv_width = DH // dp_size
    conv_natural = (jnp.asarray(order, jnp.int32)[conv_lanes // conv_width] ^ d) * conv_width
    conv_natural = conv_natural + conv_lanes % conv_width
    conv_shuffle = (conv_natural[:, None] == conv_lanes[None, :]).astype(lowp)
    near_conv = mm(near_conv.reshape(-1, DH), conv_shuffle).astype(lowp).reshape(near_conv.shape)
    full_conv = jnp.concatenate([near_conv, swap(near_conv, "head", 2)], axis=0)

    low_out = after(wout.astype(lowp), own_qkv)
    own_out = gather_blocks(low_out, 1)
    full_out = jnp.concatenate([own_out, swap(own_out, "head", 2)], axis=0)
    low_up = after(wup.astype(lowp), own_out)
    own_up = gather_blocks(low_up, 0)
    full_up = jnp.concatenate([own_up, swap(own_up, "head", 2)], axis=1)
    low_down = after(wdown.astype(lowp), own_up)
    own_down = gather_blocks(low_down, 1)
    full_down = jnp.concatenate([own_down, swap(own_down, "head", 2)], axis=0)

    words = vocab // reach
    z = d // 2
    low_table = after(table.astype(lowp), own_down)
    near_table = []
    for m in range(0, dp_size, 2):
        part = lax.dynamic_slice_in_dim(low_table, (z ^ (m // 2)) * words, words, 0)
        near_table.append(part if m == 0 else swap(part, "dp", m))
    near_table = jnp.concatenate(near_table, axis=1)
    loss_table = jnp.concatenate([near_table, swap(near_table, "dp", 1)], axis=1)
    slots = -(-words // 256) * 256
    loss_table = jnp.concatenate([loss_table, jnp.zeros((slots - words, D), lowp)], axis=0)

    first_word = h * vocab
    looked, tok_list, row_list, list_count = lookup(first_word.reshape(1), ids_all, table)
    looked = looked.reshape(2, -1, width)
    looked = looked[0] + swap(looked[1], "head", 1)
    looked = looked.reshape(2, -1, width)
    looked = looked[0] + swap(looked[1], "head", 2)
    looked = looked.reshape(dp_size, half, width)
    pieces = [looked[p] if p == 0 else swap(looked[p], "dp", m) for p, m in enumerate(order)]
    embedded = jnp.concatenate(pieces, axis=1).astype(single)
    normed, inv_first = rms(embedded, gain_vals[0])
    normed = jnp.concatenate([normed, swap(normed, "head", 1)], axis=0)

    place = jnp.stack([x, d])
    mem_normed = state_norm(place, gain_vals[0], memory, 1)[0]
    old_normed = state_norm(place, gain_vals[0], old_states, RATE)
    key_value = jnp.concatenate([full_qkv[1], full_qkv[2]], axis=1)
    all_three = jnp.concatenate([full_qkv[0], key_value], axis=1)
    comp, old_raw = compress(old_normed, key_value, full_conv)
    mem = mm(mem_normed, key_value).astype(lowp)
    seg = mm(normed, all_three).astype(lowp)
    info = jnp.stack(
        [
            lax.dynamic_index_in_dim(comp_fill, x, 0, keepdims=False),
            lax.dynamic_index_in_dim(mem_fill, x, 0, keepdims=False),
            c * half,
        ]
    ).astype(jnp.int32)
    mixed, lse = attend(info, seg, comp, mem)

    def core_sum(part):
        return part[:half] + swap(part[half:].astype(lowp), "head", 1).astype(single)

    def core_both(part):
        return jnp.concatenate([part, swap(part, "head", 1)], axis=0)

    after_attn = embedded + core_sum(mm(mixed, full_out))
    ffn_in, inv_second = rms(after_attn, gain_vals[1])
    ffn_in = core_both(ffn_in)
    hidden_pre = mm(ffn_in, full_up)
    hidden_act = jax.nn.gelu(hidden_pre).astype(lowp)
    after_ffn = after_attn + core_sum(mm(hidden_act, full_down))
    final_in, inv_third = rms(after_ffn, gain_vals[2])

    word_start = first_word + z * words
    chunks = []
    infos = []
    for m in range(0, dp_size, 2):
        piece = final_in if m == 0 else swap(reorder(final_in, m), "dp", m)
        pair = jnp.concatenate([piece, swap(piece, "head", 2)], axis=0)
        chunks.append(core_both(pair))
        wanted = targets_all[m // 2].reshape(-1) - word_start.astype(single)
        wanted = jnp.where((wanted >= 0) & (wanted < words), wanted, -1.0)
        counted = mask_all[m // 2].reshape(-1)
        infos.append((wanted, counted))
    blank = jnp.zeros((per_group,), single)
    raised = []
    stats = []
    for chunk, (wanted, counted) in zip(chunks, infos):
        packed = jnp.stack([wanted] + [blank] * 7)
        out, stat = logits_part(words, packed, chunk, loss_table)
        raised.append(out)
        stats.append(stat)
    own_stats = jnp.stack([stat[:3] for stat in stats], axis=1)

    def combine(first, second):
        top = jnp.maximum(first[0], second[0])
        total = first[1] * jnp.exp(first[0] - top) + second[1] * jnp.exp(second[0] - top)
        return jnp.stack([top, total, first[2] + second[2]])

    grid4 = own_stats.reshape(3, reach, 2, 2, half)
    other = swap(grid4, "head", 1)
    grid4 = combine(grid4, jnp.flip(other, 2))
    other = swap(grid4, "head", 2)
    grid4 = combine(grid4, jnp.flip(other, 3))
    step = 1
    while step < reach:
        other = swap(grid4, "dp", 2 * step)
        index = [i ^ step for i in range(reach)]
        other = jnp.stack([other[:, i] for i in index], axis=1)
        grid4 = combine(grid4, other)
        step *= 2
    merged = grid4.reshape(3, reach, per_group)
    log_total = merged[0] + jnp.log(merged[1])
    own_loss = infos[0][1][:half] * (log_total[0, :half] - merged[2, 0, :half])
    loss_local = jnp.sum(own_loss)

    dlogits = [None] * reach
    final_grad = None
    for i in list(range(1, reach)) + [0]:
        wanted, counted = infos[i]
        factor = jnp.exp(own_stats[0, i] - log_total[i]) * counted
        packed = jnp.stack([wanted, counted, factor] + [blank] * 5)
        dlogits[i], part = logits_back(packed, raised[i], loss_table)
        rows = per_group // 2
        part = part[:rows].astype(single) + swap(part[rows:], "head", 1).astype(single)
        rows = rows // 2
        part = part[:rows] + swap(part[rows:].astype(lowp), "head", 2).astype(single)
        if i:
            part = reorder(swap(part.astype(lowp), "dp", 2 * i), 2 * i).astype(single)
        final_grad = part if final_grad is None else final_grad + part

    keep, send = table_grad_part(dlogits[:4], chunks[:4])
    for start in range(4, reach, 4):
        more = table_grad_part(dlogits[start : start + 4], chunks[start : start + 4])
        keep = keep + more[0]
        send = (send.astype(single) + more[1].astype(single)).astype(lowp)
    keep = keep + swap(send.astype(lowp), "dp", 1).astype(single)
    table_base = jnp.zeros((vocab, width), single)
    for i, part in enumerate(split(keep[:words], 1, reach)):
        part = part if i == 0 else swap(part.astype(lowp), "dp", 2 * i).astype(single)
        table_base = lax.dynamic_update_slice_in_dim(table_base, part, (z ^ i) * words, 0)

    grad_after_ffn = rms_back(after_ffn, inv_third, gain_vals[2], final_grad)
    down_in = core_both(grad_after_ffn.astype(lowp))
    act_grad = mm(down_in, full_down, NT)
    pre_grad = jax.vjp(jax.nn.gelu, hidden_pre)[1](act_grad)[0].astype(lowp)
    ffn_in_grad = core_sum(mm(pre_grad, full_up, NT))
    grad_after_attn = grad_after_ffn + rms_back(after_attn, inv_second, gain_vals[1], ffn_in_grad)
    attn_in = core_both(grad_after_attn.astype(lowp))

    mixed_grad = mm(attn_in, full_out, NT).astype(lowp)
    seg_grad, comp_grad, mem_grad = attend_back(info, seg, comp, mem, lse, mixed_grad)
    seg_in_grad = core_sum(mm(seg_grad, all_three, NT))
    embed_grad = grad_after_attn + rms_back(embedded, inv_first, gain_vals[0], seg_in_grad)
    pieces = [
        part if m == 0 else swap(part, "dp", m)
        for part, m in zip(split(embed_grad.astype(lowp), 1, dp_size), order)
    ]
    rows_grad = jnp.stack(pieces)
    rows_grad = jnp.stack([rows_grad, swap(rows_grad, "head", 2)])
    rows_grad = jnp.stack([rows_grad, swap(rows_grad, "head", 1)]).reshape(-1, width)

    old_grad, conv_sum = expand(comp_grad, old_raw, full_conv)
    seg_sum = mm(normed, seg_grad, TN)
    side_sum = mm(mem_normed, mem_grad, TN) + mm(
        old_normed.reshape(-1, D), old_grad.reshape(-1, old_grad.shape[-1]), TN
    )
    wide = seg_sum.shape[1] // 3
    own = wide // 2

    def three(first):
        def cols(array, base):
            return array[:, base + first : base + first + own]

        return jnp.stack(
            [
                cols(seg_sum, 0),
                cols(seg_sum, wide) + cols(side_sum, 0),
                cols(seg_sum, 2 * wide) + cols(side_sum, wide),
            ]
        )

    def in_order(value):
        moved = mm(value.astype(lowp).reshape(-1, DH), conv_shuffle, NT)
        return moved.reshape(value.shape)

    heads_own = wconv.shape[0]
    hidden_own = wup.shape[1]
    down_sum = mm(hidden_act, down_in, TN)
    up_sum = mm(ffn_in, pre_grad, TN)
    out_sum = mm(mixed, attn_in, TN)
    down_grad = reduce_blocks(down_sum[:hidden_own], down_sum[hidden_own:], 1)
    up_grad = reduce_blocks(up_sum[:, :hidden_own], up_sum[:, hidden_own:], 0)
    out_grad = reduce_blocks(out_sum[: wout.shape[0]], out_sum[wout.shape[0] :], 1)
    qkv_grad = reduce_blocks(three(0), three(own), 1)
    conv_grad = reduce_blocks(in_order(conv_sum[:heads_own]), in_order(conv_sum[heads_own:]), 2)
    table_grad = scatter(list_count, tok_list, row_list, table_base, rows_grad)

    gains_low = gains.astype(lowp).astype(single)
    gain_part = jnp.stack(
        [
            jnp.sum(low_qkv.astype(single) * qkv_grad, axis=(0, 2)),
            jnp.sum(wup.astype(lowp).astype(single) * up_grad, axis=1),
            jnp.sum(table.astype(lowp).astype(single) * table_base, axis=0),
        ]
    )

    grads = (table_grad, qkv_grad, out_grad, conv_grad, up_grad, down_grad)
    weights_now = (table, qkv, wout, wconv, wup, wdown)
    rows_old = (table_rows, qkv_rows, out_rows, conv_rows, up_rows, down_rows)
    cols_old = (table_cols, qkv_cols, out_cols, conv_cols, up_cols, down_cols)
    sizes = {"dp": dp_size, "head": head_size}
    row_axes = ("head", "dp", "head", "head", "dp", "head")
    col_axes = ("dp", "head", "dp", "dp", "head", "dp")

    def pack(arrays):
        joined = jnp.concatenate([a.reshape(-1) for a in arrays])
        return jnp.concatenate([joined, jnp.zeros((-joined.shape[0] % 1024,), single)])

    def unpack(joined, arrays):
        result = []
        start = 0
        for a in arrays:
            result.append(joined[start : start + a.size].reshape(a.shape))
            start += a.size
        return result

    def sum_over(arrays, axis):
        joined = pack(arrays)
        mask = 1
        while mask < sizes[axis]:
            joined = joined + swap(joined, axis, mask)
            mask *= 2
        return unpack(joined, arrays)

    row_part = []
    col_part = []
    scalar_list = []
    for index in range(6):
        square = grads[index] * grads[index]
        row_part.append(jnp.sum(square, axis=-1))
        col_part.append(jnp.sum(square, axis=tuple(range(square.ndim - 1))))
        scalar_list.append(jnp.sum(square))
        scalar_list.append(jnp.sum(rows_old[index]) / sizes[col_axes[index]])
    for weight in weights_now:
        scalar_list.append(jnp.sum(weight * weight))
    for which in range(3):
        scalar_list.append(jnp.sum(gains[which] * gains[which]) / head_size)
    scalar_list.append(loss_local)
    scalars = jnp.stack(scalar_list)
    row_q, row_u, col_e, col_o, col_c, col_d, gain_raw, scalars = sum_over(
        [row_part[1], row_part[4], col_part[0], col_part[2], col_part[3], col_part[5], gain_part, scalars],
        "head",
    )
    row_e, row_o, row_c, row_d, col_q, col_u, scalars = sum_over(
        [row_part[0], row_part[2], row_part[3], row_part[5], col_part[1], col_part[4], scalars], "dp"
    )
    row_sums = [row_e, row_q, row_o, row_c, row_u, row_d]
    col_sums = [col_e, col_q, col_o, col_c, col_u, col_d]
    weight_total = scalars[12:21]
    loss_all = scalars[21]
    inverse = 1.0 / count_all
    decay = 1.0 - STEP ** (-0.8)
    updates = []
    stats_new = []
    scaled = []
    counts = []
    update_sq = []
    for index in range(6):
        rows_total = rows_old[index].size * sizes[row_axes[index]]
        cols_total = cols_old[index].size * sizes[col_axes[index]]
        grad_scaled = grads[index] * inverse
        rows_new = decay * rows_old[index] + (1.0 - decay) * (
            row_sums[index] * inverse * inverse / cols_total + TINY_SQUARE
        )
        cols_new = decay * cols_old[index] + (1.0 - decay) * (
            col_sums[index] * inverse * inverse / rows_total + TINY_SQUARE
        )
        mean_row = decay * scalars[2 * index + 1] / rows_total + (1.0 - decay) * (
            scalars[2 * index] * inverse * inverse / (rows_total * cols_total) + TINY_SQUARE
        )
        second = rows_new[..., None] * cols_new / mean_row
        direction = grad_scaled * lax.rsqrt(second)
        updates.append(direction)
        stats_new.append((rows_new, cols_new))
        scaled.append(grad_scaled)
        counts.append(rows_total * cols_total)
        update_sq.append(jnp.sum(direction * direction))
    gain_scaled = gain_raw / gains_low * inverse
    second_new = decay * gains_second + (1.0 - decay) * (gain_scaled * gain_scaled + TINY_SQUARE)
    gain_dir = gain_scaled * lax.rsqrt(second_new)
    for which in range(3):
        update_sq.append(jnp.sum(gain_dir[which] * gain_dir[which]) / head_size)
    update_total = sum_over(sum_over([jnp.stack(update_sq)], "head"), "dp")[0]
    results = [loss_all, count_all]
    for index in range(6):
        factor = jnp.maximum(0.001, jnp.sqrt(weight_total[index] / counts[index]))
        denom = jnp.maximum(1.0, jnp.sqrt(update_total[index] / counts[index]) / CLIP_LEVEL)
        new_weight = weights_now[index] - LEARN_RATE * factor * updates[index] / denom
        results += [new_weight, scaled[index], stats_new[index][0], stats_new[index][1]]
    gain_factor = jnp.maximum(0.001, jnp.sqrt(weight_total[6:] / D))[:, None]
    gain_denom = jnp.maximum(1.0, jnp.sqrt(update_total[6:] / D) / CLIP_LEVEL)[:, None]
    results += [gains - LEARN_RATE * gain_factor * gain_dir / gain_denom, gain_scaled, second_new]
    return tuple(results)


def solution(mesh):
    in_specs = (
        P("dp", None),
        P("dp", None),
        P("dp", None),
        P("dp", None, None),
        P("dp", None, None),
        P("dp"),
        P("dp"),
        P("head", "dp"),
        P(None, "dp", "head"),
        P("head", "dp"),
        P("head", None, "dp"),
        P("dp", "head"),
        P("head", "dp"),
        P(None, "dp"),
        P("head"),
        P("dp"),
        P(None, "dp"),
        P("head"),
        P("head"),
        P("dp"),
        P("head", None),
        P("dp"),
        P("dp"),
        P("head"),
        P("head"),
        P("dp"),
        P(None, "dp"),
    )
    out_specs = (
        P(),
        P(),
        P("head", "dp"),
        P("head", "dp"),
        P("head"),
        P("dp"),
        P(None, "dp", "head"),
        P(None, "dp", "head"),
        P(None, "dp"),
        P("head"),
        P("head", "dp"),
        P("head", "dp"),
        P("head"),
        P("dp"),
        P("head", None, "dp"),
        P("head", None, "dp"),
        P("head", None),
        P("dp"),
        P("dp", "head"),
        P("dp", "head"),
        P("dp"),
        P("head"),
        P("head", "dp"),
        P("head", "dp"),
        P("head"),
        P("dp"),
        P(None, "dp"),
        P(None, "dp"),
        P(None, "dp"),
    )
    return jax.shard_map(local, mesh=mesh, in_specs=in_specs, out_specs=out_specs, check_vma=False)
```

```python
import functools

import jax
import jax.numpy as jnp
from jax import lax
from jax.experimental import pallas as pl
from jax.experimental.pallas import tpu as pltpu
from jax.sharding import PartitionSpec as P

D = 1024
H = 8
DH = 128
MEM = 512
CMEM = 512
RATE = 3
STEP = 10


TINY_NORM = 1e-06
TINY_SQUARE = 1e-30
LEARN_RATE = 0.5
CLIP_LEVEL = 1.0

lowp = jnp.bfloat16
single = jnp.float32
NT = (((1,), (1,)), ((), ()))
TN = (((0,), (0,)), ((), ()))
NN = (((1,), (0,)), ((), ()))
MIB = 1024 * 1024


def mm(left, right, dims=NN):
    return lax.dot_general(left, right, dims, preferred_element_type=single)


def swap(value, axis, mask):
    size = lax.axis_size(axis)
    return lax.ppermute(value, axis, [(i, i ^ mask) for i in range(size)])


def after(value, dep):
    return lax.optimization_barrier((value, dep))[0]


def block_order(size):
    order = [0]
    step = size // 2
    while step:
        order = order + [j + step for j in order]
        step //= 2
    return order


def gather_blocks(piece, axis):
    mask = lax.axis_size("dp") // 2
    while mask:
        piece = jnp.concatenate([piece, swap(piece, "dp", mask)], axis=axis)
        mask //= 2
    return piece


def split(value, axis, parts):
    width = value.shape[axis] // parts
    return [lax.slice_in_dim(value, i * width, (i + 1) * width, axis=axis) for i in range(parts)]


def reduce_blocks(keep, send, mask=1):
    total = keep + swap(send.astype(lowp), "dp", mask).astype(single)
    mask *= 2
    if mask == lax.axis_size("dp"):
        return total
    return reduce_blocks(*split(total, 1, 2), mask)


def reorder(value, mask):
    order = block_order(lax.axis_size("dp"))
    cols = split(value, 1, len(order))
    return jnp.concatenate([cols[order.index(j ^ mask)] for j in order], axis=1)


def relative(value, x, c):
    value = jnp.where(x == 1, jnp.flip(value, -3), value)
    value = jnp.where(c == 1, jnp.flip(value, -2), value)
    return jnp.swapaxes(value, -3, -2)


def rms(values, gain):
    inv = lax.rsqrt(jnp.mean(values * values, axis=-1, keepdims=True) + TINY_NORM)
    return (values * inv * gain).astype(lowp), inv


def rms_back(values, inv, gain, upstream):
    scaled = gain * upstream
    inner = jnp.sum(scaled * values, axis=-1, keepdims=True) / D
    return scaled * inv - values * (inner * inv * inv * inv)


def vmem(shape=None, index=None):
    if shape is None:
        return pl.BlockSpec(memory_space=pltpu.VMEM)
    return pl.BlockSpec(shape, index)


def smem():
    return pl.BlockSpec(memory_space=pltpu.SMEM)


def params(mib):
    return pltpu.CompilerParams(vmem_limit_bytes=mib * MIB)


def cost(flops, size, exps=0):
    return pl.CostEstimate(flops=flops, bytes_accessed=size, transcendentals=exps)


def lookup_kernel(row_ref, table_ref, out_ref, tab, held, sem):
    total = row_ref.shape[0]
    vocab = table_ref.shape[0]
    copy = pltpu.make_async_copy(table_ref, tab.at[pl.ds(0, vocab)], sem)
    copy.start()
    tab[pl.ds(vocab, 8), :] = jnp.zeros((8, tab.shape[1]), single)
    copy.wait()

    @pl.loop(0, total // 16)
    def _(g):
        for j in range(16):
            t = g * 16 + j
            held[pl.ds(t, 1), :] = tab[pl.ds(row_ref[t], 1), :]

    @pl.loop(0, total // 512)
    def _(i):
        rows = pl.ds(pl.multiple_of(i * 512, 512), 512)
        out_ref[rows, :] = held[rows, :].astype(lowp)


def lookup(rows, table):
    total = rows.shape[0]
    vocab, width = table.shape
    return pl.pallas_call(
        lookup_kernel,
        out_shape=jax.ShapeDtypeStruct((total, width), lowp),
        in_specs=[smem(), pl.BlockSpec(memory_space=pl.ANY)],
        out_specs=vmem(),
        scratch_shapes=[
            pltpu.VMEM((vocab + 8, width), single),
            pltpu.VMEM((total, width), single),
            pltpu.SemaphoreType.DMA(()),
        ],
        compiler_params=params(60),
        cost_estimate=cost(0, 30 * MIB),
    )(rows, table)


def list_kernel(vocab, row_ref, tok_ref, out_ref, count_ref):
    total = row_ref.shape[0]

    def group(g, count):
        for j in range(8):
            t = g * 8 + j
            row = row_ref[t]
            tok_ref[count] = t
            out_ref[count] = row
            count = count + jnp.where(row < vocab, 1, 0)
        return count

    count = lax.fori_loop(0, total // 8, group, jnp.int32(0))
    for j in range(8):
        tok_ref[count + j] = total
        out_ref[count + j] = 0
    count_ref[0] = count


def own_list(rows, vocab):
    total = rows.shape[0]
    return pl.pallas_call(
        functools.partial(list_kernel, vocab),
        out_shape=(
            jax.ShapeDtypeStruct((total + 8,), jnp.int32),
            jax.ShapeDtypeStruct((total + 8,), jnp.int32),
            jax.ShapeDtypeStruct((1,), jnp.int32),
        ),
        in_specs=[smem()],
        out_specs=(smem(), smem(), smem()),
        cost_estimate=cost(0, 40 * MIB),
    )(rows)


def place_kernel(order, place_ref, in_ref, gain_ref, out_ref, norm_ref, held):
    width = in_ref.shape[2]
    for p, j in enumerate(order):
        block = in_ref[pl.ds(place_ref[1] ^ j, 1)][0]
        out_ref[:, p * width : (p + 1) * width] = block
        held[:, p * width : (p + 1) * width] = block.astype(single)
    values = held[...]
    inv = lax.rsqrt(jnp.mean(values * values, axis=-1, keepdims=True) + TINY_NORM)
    norm_ref[...] = (values * inv * gain_ref[...]).astype(lowp)


def place_embedding(place, blocks, gain):
    rows = blocks.shape[1]
    return pl.pallas_call(
        functools.partial(place_kernel, block_order(blocks.shape[0])),
        out_shape=(jax.ShapeDtypeStruct((rows, D), lowp), jax.ShapeDtypeStruct((rows, D), lowp)),
        in_specs=[smem(), vmem(), vmem()],
        out_specs=(vmem(), vmem()),
        scratch_shapes=[pltpu.VMEM((rows, D), single)],
        compiler_params=params(60),
        cost_estimate=cost(0, 3 * MIB),
    )(place, blocks, gain)


def embed_back_kernel(order, place_ref, in_ref, gain_ref, keep_ref, more_ref, grad_ref, out_ref, held):
    values = in_ref[...].astype(single)
    inv = lax.rsqrt(jnp.mean(values * values, axis=-1, keepdims=True) + TINY_NORM)
    upstream = keep_ref[...] + more_ref[...].astype(single)
    held[...] = grad_ref[...] + rms_back(values, inv, gain_ref[...], upstream)
    width = out_ref.shape[2]
    for p, j in enumerate(order):
        block = held[:, p * width : (p + 1) * width].astype(lowp)
        out_ref[pl.ds(place_ref[1] ^ j, 1)] = block[None]


def embed_back(place, values, gain, keep, more, grad):
    rows = values.shape[0]
    size = lax.axis_size("dp")
    return pl.pallas_call(
        functools.partial(embed_back_kernel, block_order(size)),
        out_shape=jax.ShapeDtypeStruct((size, rows, D // size), lowp),
        in_specs=[smem()] + [vmem()] * 5,
        out_specs=vmem(),
        scratch_shapes=[pltpu.VMEM((rows, D), single)],
        compiler_params=params(60),
        cost_estimate=cost(0, 4 * MIB),
    )(place, values, gain, keep, more, grad)


def scatter_kernel(count_ref, tok_ref, row_ref, base_ref, grad_ref, out_ref, rows):
    total = grad_ref.shape[0]
    vocab = base_ref.shape[0]

    @pl.loop(0, total // 512)
    def _(i):
        here = pl.ds(pl.multiple_of(i * 512, 512), 512)
        rows[here, :] = grad_ref[here, :].astype(single)

    rows[pl.ds(total, 8), :] = jnp.zeros((8, rows.shape[1]), single)

    @pl.loop(0, vocab // 400)
    def _(i):
        here = pl.ds(pl.multiple_of(i * 400, 400), 400)
        out_ref[here, :] = base_ref[here, :]

    def group(g, carry):
        for j in range(8):
            token = tok_ref[g * 8 + j]
            row = row_ref[g * 8 + j]
            out_ref[pl.ds(row, 1), :] = out_ref[pl.ds(row, 1), :] + rows[pl.ds(token, 1), :]
        return carry

    lax.fori_loop(0, (count_ref[0] + 7) // 8, group, jnp.int32(0))


def scatter(count, tok, row, base, grad):
    total, width = grad.shape
    return pl.pallas_call(
        scatter_kernel,
        out_shape=jax.ShapeDtypeStruct(base.shape, single),
        in_specs=[smem(), smem(), smem(), vmem(), vmem()],
        out_specs=vmem(),
        scratch_shapes=[pltpu.VMEM((total + 8, width), single)],
        compiler_params=params(60),
        cost_estimate=cost(0, 30 * MIB),
    )(count, tok, row, base, grad)


def state_kernel(order, width, place_ref, gain_ref, in_ref, out_ref, held):
    rows = in_ref.shape[1]
    values = in_ref[0].astype(single)
    inv = lax.rsqrt(jnp.mean(values * values, axis=-1, keepdims=True) + TINY_NORM)
    for p, j in enumerate(order):
        start = pl.multiple_of((place_ref[1] ^ j) * width, width)
        block = in_ref[0, :, pl.ds(start, width)].astype(single)
        held[p] = block * inv * gain_ref[:, p * width : (p + 1) * width]
    groups = out_ref.shape[0]
    for p in range(len(order)):
        cols = slice(p * width, (p + 1) * width)
        if groups == 1:
            out_ref[0, :, cols] = held[p].astype(lowp)
        else:
            for j in range(groups):
                part = held[p, pl.ds(j, rows // groups, stride=groups), :]
                out_ref[j, :, cols] = part.astype(lowp)


def state_norm(place, gain, states, groups):
    size = lax.axis_size("dp")
    order = block_order(size)
    width = D // size
    count = states.shape[1] // groups
    if width % 128:
        values = lax.dynamic_index_in_dim(states, place[0], 0, keepdims=False).astype(single)
        inv = lax.rsqrt(jnp.mean(values * values, axis=-1, keepdims=True) + TINY_NORM)
        lanes = jnp.arange(D, dtype=jnp.int32)
        blocks = jnp.asarray(order, jnp.int32)[lanes // width] ^ place[1]
        source = blocks * width + lanes % width
        shuffle = (lanes[:, None] == source[None, :]).astype(single)
        moved = jnp.dot(values * inv, shuffle, precision=lax.Precision.HIGHEST)
        out = (moved * gain).astype(lowp)
        return jnp.swapaxes(out.reshape(count, groups, D), 0, 1)
    tile = 128
    return pl.pallas_call(
        functools.partial(state_kernel, order, width),
        out_shape=jax.ShapeDtypeStruct((groups, count, D), lowp),
        grid_spec=pltpu.PrefetchScalarGridSpec(
            num_scalar_prefetch=1,
            grid=(count // tile,),
            in_specs=[
                pl.BlockSpec((1, D), lambda i, s: (0, 0)),
                pl.BlockSpec((1, tile * groups, D), lambda i, s: (s[0], i, 0)),
            ],
            out_specs=pl.BlockSpec((groups, tile, D), lambda i, s: (0, i, 0)),
            scratch_shapes=[pltpu.VMEM((len(order), tile * groups, width), single)],
        ),
        compiler_params=params(60),
        cost_estimate=cost(0, 4 * count * groups * D),
    )(place, gain, states)


def compress_kernel(old_ref, weight_ref, conv_ref, comp_ref, raw_ref):
    heads = conv_ref.shape[0]
    sums = [None] * (2 * heads)
    for j in range(RATE):
        raw = mm(old_ref[j], weight_ref[...], NT).astype(lowp)
        raw_ref[j] = raw
        for n in range(2 * heads):
            piece = raw[:, n * DH : (n + 1) * DH]
            term = mm(piece, conv_ref[n % heads, j * DH : (j + 1) * DH, :])
            sums[n] = term if j == 0 else sums[n] + term
    for n in range(2 * heads):
        comp_ref[:, n * DH : (n + 1) * DH] = sums[n].astype(lowp)


def compress(old3, weight, conv):
    rows = old3.shape[1]
    wide = weight.shape[0]
    tile = 256
    return pl.pallas_call(
        compress_kernel,
        grid=(rows // tile,),
        out_shape=(
            jax.ShapeDtypeStruct((rows, wide), lowp),
            jax.ShapeDtypeStruct((RATE, rows, wide), lowp),
        ),
        in_specs=[
            pl.BlockSpec((RATE, tile, D), lambda i: (0, i, 0)),
            pl.BlockSpec(weight.shape, lambda i: (0, 0)),
            pl.BlockSpec(conv.shape, lambda i: (0, 0, 0)),
        ],
        out_specs=(
            pl.BlockSpec((tile, wide), lambda i: (i, 0)),
            pl.BlockSpec((RATE, tile, wide), lambda i: (0, i, 0)),
        ),
        compiler_params=params(60),
        cost_estimate=cost(4 * RATE * rows * D * D, 12 * MIB),
    )(old3, weight, conv)


def expand_kernel(grad_ref, raw_ref, conv_ref, out_ref, conv_out_ref):
    heads = conv_ref.shape[0]
    for h in range(heads):
        for j in range(RATE):
            rows = slice(j * DH, (j + 1) * DH)
            taps = conv_ref[h, rows, :]
            total = None
            for n in (h, heads + h):
                cols = slice(n * DH, (n + 1) * DH)
                grad = grad_ref[:, cols]
                out_ref[j, :, cols] = mm(grad, taps, NT).astype(lowp)
                term = mm(raw_ref[j, :, cols], grad, TN)
                total = term if total is None else total + term
            conv_out_ref[h, rows, :] = total


def expand(grad, raw, conv):
    return pl.pallas_call(
        expand_kernel,
        out_shape=(
            jax.ShapeDtypeStruct(raw.shape, lowp),
            jax.ShapeDtypeStruct(conv.shape, single),
        ),
        in_specs=[vmem()] * 3,
        out_specs=(vmem(), vmem()),
        compiler_params=params(60),
        cost_estimate=cost(2000 * MIB, 10 * MIB),
    )(grad, raw, conv)


def masked_scores(info_ref, query, keys):
    rows = query.shape[0]
    scale = DH ** (-0.5)
    result = []
    for which, key in enumerate(keys):
        slots = key.shape[0]
        col = lax.broadcasted_iota(jnp.int32, (rows, slots), 1)
        if which < 2:
            seen = col >= slots - info_ref[which]
        else:
            row = lax.broadcasted_iota(jnp.int32, (rows, slots), 0)
            shift = info_ref[2]
            row = row + shift
            col = col + shift
            row = jnp.where(row >= slots, row - slots, row)
            col = jnp.where(col >= slots, col - slots, col)
            seen = col <= row
        result.append(jnp.where(seen, mm(query, key, NT) * scale, -1e30))
    return result


def attend_kernel(info_ref, q_ref, ks_ref, vs_ref, kc_ref, vc_ref, km_ref, vm_ref, out_ref, lse_ref):
    query = q_ref[...]
    scores = masked_scores(info_ref, query, [kc_ref[...], km_ref[...], ks_ref[...]])
    top = functools.reduce(jnp.maximum, [jnp.max(s, axis=-1, keepdims=True) for s in scores])
    total = 0.0
    mixed = 0.0
    for score, value in zip(scores, (vc_ref, vm_ref, vs_ref)):
        weight = jnp.exp(score - top)
        total = total + jnp.sum(weight, axis=-1, keepdims=True)
        mixed = mixed + mm(weight.astype(lowp), value[...])
    out_ref[...] = (mixed / total).astype(lowp)
    lse_ref[0] = top + jnp.log(total)


def attend_back_kernel(
    info_ref, q_ref, ks_ref, vs_ref, kc_ref, vc_ref, km_ref, vm_ref, lse_ref, up_ref,
    seg_ref, comp_ref, mem_ref,
):
    head = pl.program_id(0)
    wide = pl.num_programs(0) * DH
    scale = DH ** (-0.5)
    query = q_ref[...]
    upstream = up_ref[...]
    keys = [kc_ref[...], km_ref[...], ks_ref[...]]
    scores = masked_scores(info_ref, query, keys)
    probs = [jnp.exp(s - lse_ref[0]) for s in scores]
    prob_grads = [mm(upstream, v[...], NT) for v in (vc_ref, vm_ref, vs_ref)]
    inner = 0.0
    for p, g in zip(probs, prob_grads):
        inner = inner + jnp.sum(p * g, axis=-1, keepdims=True)
    here = pl.ds(pl.multiple_of(head * DH, DH), DH)
    second = pl.ds(pl.multiple_of(wide + head * DH, DH), DH)
    third = pl.ds(pl.multiple_of(2 * wide + head * DH, DH), DH)
    query_grad = 0.0
    places = ((comp_ref, here, second), (mem_ref, here, second), (seg_ref, second, third))
    for p, g, key, (ref, key_at, value_at) in zip(probs, prob_grads, keys, places):
        score_grad = (p * (g - inner)).astype(lowp)
        query_grad = query_grad + mm(score_grad, key)
        ref[:, key_at] = (mm(score_grad, query, TN) * scale).astype(lowp)
        ref[:, value_at] = mm(p.astype(lowp), upstream, TN).astype(lowp)
    seg_ref[:, here] = (query_grad * scale).astype(lowp)


def head_specs(query, seg, comp, mem, heads):
    def cols(array, first):
        return pl.BlockSpec((array.shape[0], DH), lambda h: (0, first + h))

    return [
        smem(),
        cols(query, 0),
        cols(seg, 0),
        cols(seg, heads),
        cols(comp, 0),
        cols(comp, heads),
        cols(mem, 0),
        cols(mem, heads),
    ]


def attend(info, query, seg, comp, mem):
    rows = seg.shape[0]
    heads = comp.shape[1] // (2 * DH)
    return pl.pallas_call(
        attend_kernel,
        grid=(heads,),
        out_shape=(
            jax.ShapeDtypeStruct((rows, heads * DH), lowp),
            jax.ShapeDtypeStruct((heads, rows, 1), single),
        ),
        in_specs=head_specs(query, seg, comp, mem, heads),
        out_specs=(
            pl.BlockSpec((rows, DH), lambda h: (0, h)),
            pl.BlockSpec((1, rows, 1), lambda h: (h, 0, 0)),
        ),
        compiler_params=params(60),
        cost_estimate=cost(7000 * MIB, 6 * MIB),
    )(info, query, seg, seg, comp, comp, mem, mem)


def attend_back(info, query, seg, comp, mem, lse, upstream):
    rows = seg.shape[0]
    heads = comp.shape[1] // (2 * DH)
    whole = lambda h: (0, 0)
    return pl.pallas_call(
        attend_back_kernel,
        grid=(heads,),
        out_shape=(
            jax.ShapeDtypeStruct((rows, 3 * heads * DH), lowp),
            jax.ShapeDtypeStruct(comp.shape, lowp),
            jax.ShapeDtypeStruct(mem.shape, lowp),
        ),
        in_specs=head_specs(query, seg, comp, mem, heads)
        + [
            pl.BlockSpec((1, rows, 1), lambda h: (h, 0, 0)),
            pl.BlockSpec((rows, DH), lambda h: (0, h)),
        ],
        out_specs=(
            pl.BlockSpec((rows, 3 * heads * DH), whole),
            pl.BlockSpec(comp.shape, whole),
            pl.BlockSpec(mem.shape, whole),
        ),
        compiler_params=params(60),
        cost_estimate=cost(11000 * MIB, 9 * MIB),
    )(info, query, seg, seg, comp, comp, mem, mem, lse, upstream)


def columns_of(rows):
    tall = jnp.concatenate([rows, jnp.zeros((120, rows.shape[1]), single)], axis=0)
    return jnp.transpose(tall)


def logits_kernel(words, info_ref, in_ref, table_ref, out_ref, stat_ref):
    logits = mm(in_ref[...], table_ref[...], NT)
    wanted = columns_of(info_ref[...])[:, 0:1].astype(jnp.int32)
    col = lax.broadcasted_iota(jnp.int32, logits.shape, 1)
    hit = jnp.sum(jnp.where(col == wanted, logits, 0.0), axis=-1, keepdims=True)
    logits = jnp.where(col < words, logits, -1e30)
    top = jnp.max(logits, axis=-1, keepdims=True)
    raised = jnp.exp(logits - top)
    total = jnp.sum(raised, axis=-1, keepdims=True)
    out_ref[...] = raised.astype(lowp)
    lane = lax.broadcasted_iota(jnp.int32, (logits.shape[0], 128), 1)
    packed = jnp.where(lane == 0, top, jnp.where(lane == 1, total, jnp.where(lane == 2, hit, 0.0)))
    stat_ref[...] = jnp.transpose(packed)[:8]


def logits_part(words, info, inputs, table):
    rows = inputs.shape[0]
    slots = table.shape[0]
    tile = 256
    return pl.pallas_call(
        functools.partial(logits_kernel, words),
        grid=(rows // tile,),
        out_shape=(
            jax.ShapeDtypeStruct((rows, slots), lowp),
            jax.ShapeDtypeStruct((8, rows), single),
        ),
        in_specs=[
            pl.BlockSpec((8, tile), lambda i: (0, i)),
            pl.BlockSpec((tile, D), lambda i: (i, 0)),
            pl.BlockSpec(table.shape, lambda i: (0, 0)),
        ],
        out_specs=(
            pl.BlockSpec((tile, slots), lambda i: (i, 0)),
            pl.BlockSpec((8, tile), lambda i: (0, i)),
        ),
        compiler_params=params(60),
        cost_estimate=cost(4 * rows * slots * D, 10 * MIB),
    )(info, inputs, table)


def logits_back_kernel(info_ref, factor_ref, in_ref, table_ref, out_ref, grad_ref):
    info = columns_of(info_ref[...])
    wanted = info[:, 0:1].astype(jnp.int32)
    counted = info[:, 1:2]
    factor = columns_of(factor_ref[...])[:, 0:1]
    raised = in_ref[...].astype(single)
    col = lax.broadcasted_iota(jnp.int32, raised.shape, 1)
    grads = (raised * factor - jnp.where(col == wanted, counted, 0.0)).astype(lowp)
    out_ref[...] = grads
    grad_ref[...] = mm(grads, table_ref[...]).astype(lowp)


def logits_back(info, factor, raised, table):
    rows, slots = raised.shape
    tile = 256
    return pl.pallas_call(
        logits_back_kernel,
        grid=(rows // tile,),
        out_shape=(
            jax.ShapeDtypeStruct((rows, slots), lowp),
            jax.ShapeDtypeStruct((rows, D), lowp),
        ),
        in_specs=[
            pl.BlockSpec((8, tile), lambda i: (0, i)),
            pl.BlockSpec((8, tile), lambda i: (0, i)),
            pl.BlockSpec((tile, slots), lambda i: (i, 0)),
            pl.BlockSpec(table.shape, lambda i: (0, 0)),
        ],
        out_specs=(
            pl.BlockSpec((tile, slots), lambda i: (i, 0)),
            pl.BlockSpec((tile, D), lambda i: (i, 0)),
        ),
        compiler_params=params(60),
        cost_estimate=cost(4 * rows * slots * D, 12 * MIB),
    )(info, factor, raised, table)


def halves(total, keep_ref, send_ref):
    half = keep_ref.shape[1]
    keep_ref[...] = total[:, :half]
    send_ref[...] = total[:, half:].astype(send_ref.dtype)


def table_grad_kernel(count, *refs):
    grads = refs[:count]
    inputs = refs[count : 2 * count]
    total = mm(grads[0][...], inputs[0][...], TN)
    for i in range(1, count):
        total = total + mm(grads[i][...], inputs[i][...], TN)
    halves(total, *refs[2 * count :])


def table_grad_part(grads, inputs):
    count = len(grads)
    rows = sum(g.shape[0] for g in grads)
    slots = grads[0].shape[1]
    block = 256
    if rows > 4096:
        total = sum(mm(g, v, TN) for g, v in zip(grads, inputs))
        keep, send = split(total, 1, 2)
        return keep, send.astype(lowp)
    return pl.pallas_call(
        functools.partial(table_grad_kernel, count),
        grid=(slots // block,),
        out_shape=(
            jax.ShapeDtypeStruct((slots, D // 2), single),
            jax.ShapeDtypeStruct((slots, D // 2), lowp),
        ),
        in_specs=[pl.BlockSpec((g.shape[0], block), lambda i: (0, i)) for g in grads]
        + [pl.BlockSpec(v.shape, lambda i: (0, 0)) for v in inputs],
        out_specs=(
            pl.BlockSpec((block, D // 2), lambda i: (i, 0)),
            pl.BlockSpec((block, D // 2), lambda i: (i, 0)),
        ),
        compiler_params=params(60),
        cost_estimate=cost(3 * rows * slots * D, 30 * MIB),
    )(*grads, *inputs)


def hidden_grad_kernel(blocks, pre_ref, act_ref, in_ref, down_ref, keep_ref, send_ref):
    step = pl.program_id(0)

    @pl.when(step < blocks)
    def _():
        halves(mm(pre_ref[...], in_ref[...], TN), keep_ref, send_ref)

    @pl.when(step >= blocks)
    def _():
        halves(mm(act_ref[...], down_ref[...], TN), keep_ref, send_ref)


def hidden_grads(pre_grad, hidden_act, ffn_in, down_in):
    rows, hidden = pre_grad.shape
    block = 256
    blocks = hidden // block
    return pl.pallas_call(
        functools.partial(hidden_grad_kernel, blocks),
        grid=(2 * blocks,),
        out_shape=(
            jax.ShapeDtypeStruct((2 * hidden, D // 2), single),
            jax.ShapeDtypeStruct((2 * hidden, D // 2), lowp),
        ),
        in_specs=[
            pl.BlockSpec((rows, block), lambda i: (0, jnp.minimum(i, blocks - 1))),
            pl.BlockSpec((rows, block), lambda i: (0, jnp.maximum(i - blocks, 0))),
            pl.BlockSpec((rows, D), lambda i: (0, 0)),
            pl.BlockSpec((rows, D), lambda i: (0, 0)),
        ],
        out_specs=(
            pl.BlockSpec((block, D // 2), lambda i: (i, 0)),
            pl.BlockSpec((block, D // 2), lambda i: (i, 0)),
        ),
        compiler_params=params(60),
        cost_estimate=cost(6 * rows * hidden * D, 16 * MIB),
    )(pre_grad, hidden_act, ffn_in, down_in)


def attn_grad_kernel(
    seg_ref, mixed_ref, mem_ref, old_ref, normed_ref, up_ref, mem_in_ref, old_in_ref, far_ref, own_ref
):
    step = pl.program_id(0)
    which = step % 4

    def give(total):
        @pl.when(step < 4)
        def _():
            far_ref[...] = total.astype(lowp)

        @pl.when(step >= 4)
        def _():
            own_ref[...] = total

    @pl.when(which == 0)
    def _():
        give(mm(seg_ref[...], normed_ref[...], TN))

    @pl.when(which == 3)
    def _():
        give(mm(mixed_ref[...], up_ref[...], TN))

    @pl.when(jnp.logical_and(which > 0, which < 3))
    def _():
        total = mm(seg_ref[...], normed_ref[...], TN)
        total = total + mm(mem_ref[...], mem_in_ref[...], TN)
        give(total + mm(old_ref[...], old_in_ref[...], TN))


def attn_grads(seg_grad, mixed, mem_grad, old_grad, normed, attn_in, mem_in, old_in):
    block = mixed.shape[1] // 2

    def side(i):
        return 1 - i // 4

    def whole(array):
        return pl.BlockSpec(array.shape, lambda i: (0, 0))

    return pl.pallas_call(
        attn_grad_kernel,
        grid=(8,),
        out_shape=(
            jax.ShapeDtypeStruct((4 * block, D), lowp),
            jax.ShapeDtypeStruct((4 * block, D), single),
        ),
        in_specs=[
            pl.BlockSpec(
                (seg_grad.shape[0], block), lambda i: (0, jnp.minimum(i % 4, 2) * 2 + side(i))
            ),
            pl.BlockSpec((mixed.shape[0], block), lambda i: (0, side(i))),
            pl.BlockSpec(
                (mem_grad.shape[0], block), lambda i: (0, jnp.clip(i % 4 - 1, 0, 1) * 2 + side(i))
            ),
            pl.BlockSpec(
                (old_grad.shape[0], block), lambda i: (0, jnp.clip(i % 4 - 1, 0, 1) * 2 + side(i))
            ),
            whole(normed),
            whole(attn_in),
            whole(mem_in),
            whole(old_in),
        ],
        out_specs=(
            pl.BlockSpec((block, D), lambda i: (jnp.minimum(i, 3), 0)),
            pl.BlockSpec((block, D), lambda i: (jnp.maximum(i - 4, 0), 0)),
        ),
        compiler_params=params(60),
        cost_estimate=cost(9000 * MIB, 20 * MIB),
    )(seg_grad, mixed, mem_grad, old_grad, normed, attn_in, mem_in, old_in)


def local(
    ids,
    targets,
    target_mask,
    memory,
    old_states,
    mem_fill,
    comp_fill,
    table,
    qkv,
    wout,
    wconv,
    wup,
    wdown,
    gains,
    table_rows,
    table_cols,
    qkv_rows,
    qkv_cols,
    out_rows,
    out_cols,
    conv_rows,
    conv_cols,
    up_rows,
    up_cols,
    down_rows,
    down_cols,
    gains_second,
):
    dp_size, head_size = lax.axis_size("dp"), lax.axis_size("head")
    d, h = lax.axis_index("dp"), lax.axis_index("head")
    x, c = h // 2, h % 2
    order = block_order(dp_size)
    reach = dp_size // 2
    streams, seg_len = ids.shape
    half = seg_len // 2
    per_group = streams * seg_len
    vocab, width = table.shape
    assert head_size == 4 and streams == 2

    flat = jnp.concatenate(
        [
            ids.astype(single).reshape(-1),
            targets.astype(single).reshape(-1),
            target_mask.astype(single).reshape(-1),
            gains.astype(lowp).astype(single).reshape(-1),
        ]
    )
    room = -flat.shape[0] % 1024
    flat = jnp.concatenate([flat, jnp.zeros((room,), single)]).reshape(1, -1, 128)
    small = gather_blocks(flat, 0).reshape(dp_size, -1)
    place = jnp.stack([x, d])

    def field(raw):
        return relative(raw.reshape(-1, 2, 2, half), x, c)

    ids_all = small[:, :per_group]
    position = [order.index(j) for j in range(dp_size)]
    ids_all = jnp.take(ids_all, jnp.asarray(position, jnp.int32)[jnp.arange(dp_size) ^ d], axis=0)
    ids_all = jnp.transpose(field(ids_all), (1, 2, 0, 3)).reshape(-1).astype(jnp.int32)
    table_rows_all = ids_all - h * vocab
    inside = (table_rows_all >= 0) & (table_rows_all < vocab)
    table_rows_all = jnp.where(inside, table_rows_all, vocab)
    targets_all = field(small[:reach, per_group : 2 * per_group])
    mask_all = field(small[:reach, 2 * per_group : 3 * per_group])
    gain_blocks = small[:, 3 * per_group : 3 * per_group + 3 * width].reshape(dp_size, 3, width)
    gain_vals = jnp.swapaxes(gain_blocks, 0, 1).reshape(3, 1, D)
    count_all = jnp.sum(small[:, 2 * per_group : 3 * per_group])

    heads_own = wconv.shape[0]
    wide = qkv.shape[2]
    conv_rows_own = wconv.size // width
    low_qkv = qkv.astype(lowp)
    pack_one = jnp.concatenate(
        [
            jnp.swapaxes(low_qkv, 1, 2).reshape(3 * wide, width),
            wout.astype(lowp),
            wconv.astype(lowp).reshape(conv_rows_own, width),
        ]
    )
    own_one = gather_blocks(after(pack_one, small), 1)
    far_one = swap(own_one, "head", 2)
    near_rows = split(own_one[: 4 * wide], 0, 4)
    far_rows = split(far_one[: 4 * wide], 0, 4)
    query_weight = jnp.concatenate([near_rows[0], far_rows[0]])
    pair_weight = jnp.concatenate([near_rows[1], far_rows[1], near_rows[2], far_rows[2]])
    full_out = jnp.concatenate([near_rows[3], far_rows[3]])

    conv_lanes = jnp.arange(DH, dtype=jnp.int32)
    conv_width = DH // dp_size
    conv_natural = (jnp.asarray(order, jnp.int32)[conv_lanes // conv_width] ^ d) * conv_width
    conv_natural = conv_natural + conv_lanes % conv_width
    conv_shuffle = (conv_natural[:, None] == conv_lanes[None, :]).astype(lowp)
    taps = heads_own * RATE * DH

    def conv_natural_order(rows):
        value = jnp.swapaxes(rows.reshape(conv_rows_own, dp_size, width), 0, 1)
        value = jnp.swapaxes(value.reshape(dp_size, taps, conv_width), 0, 1)
        moved = mm(value.reshape(taps, DH), conv_shuffle).astype(lowp)
        return moved.reshape(heads_own, RATE * DH, DH)

    def conv_block_order(value):
        moved = mm(value.astype(lowp).reshape(taps, DH), conv_shuffle, NT).astype(lowp)
        moved = jnp.swapaxes(moved.reshape(taps, dp_size, conv_width), 0, 1)
        moved = jnp.swapaxes(moved.reshape(dp_size, conv_rows_own, width), 0, 1)
        return moved.reshape(conv_rows_own, D)

    full_conv = jnp.concatenate(
        [conv_natural_order(own_one[4 * wide :]), conv_natural_order(far_one[4 * wide :])]
    )

    hidden_own = wup.shape[1]
    pack_two = jnp.concatenate([wup.astype(lowp).T, wdown.astype(lowp)])
    own_two = gather_blocks(after(pack_two, own_one), 1)
    full_up, full_down = split(own_two, 0, 2)

    words = vocab // reach
    z = d // 2
    low_table = after(table.astype(lowp), own_two)
    near_table = []
    for m in order[:reach]:
        part = lax.dynamic_slice_in_dim(low_table, (z ^ (m // 2)) * words, words, 0)
        near_table.append(part if m == 0 else swap(part, "dp", m))
    near_table = jnp.concatenate(near_table, axis=1)
    loss_table = jnp.concatenate([near_table, swap(near_table, "dp", 1)], axis=1)
    slots = -(-words // 256) * 256
    loss_table = jnp.concatenate([loss_table, jnp.zeros((slots - words, D), lowp)], axis=0)

    own_half, far_half = split(table_rows_all, 0, 2)
    looked_far = swap(lookup(far_half, table), "head", 1)
    looked = (lookup(own_half, table) + looked_far).reshape(2, -1, width)
    looked = looked[0] + swap(looked[1], "head", 2)
    looked = lax.all_to_all(looked.reshape(dp_size, half, width), "dp", 0, 0)
    embedded_low, normed = place_embedding(place, looked, gain_vals[0])
    embedded = embedded_low.astype(single)
    normed = jnp.concatenate([normed, swap(normed, "head", 1)], axis=0)

    mem_normed = state_norm(place, gain_vals[0], memory, 1)[0]
    old_normed = state_norm(place, gain_vals[0], old_states, RATE)
    comp, old_raw = compress(old_normed, pair_weight, full_conv)
    mem = mm(mem_normed, pair_weight, NT).astype(lowp)
    query = mm(normed, query_weight, NT).astype(lowp)
    seg = mm(normed, pair_weight, NT).astype(lowp)
    info = jnp.stack(
        [
            lax.dynamic_index_in_dim(comp_fill, x, 0, keepdims=False),
            lax.dynamic_index_in_dim(mem_fill, x, 0, keepdims=False),
            c * half,
        ]
    ).astype(jnp.int32)
    mixed, lse = attend(info, query, seg, comp, mem)

    def core_sum(part):
        rows = part.shape[0] // 2
        return part[:rows] + swap(part[rows:].astype(lowp), "head", 1).astype(single)

    def core_both(part):
        return jnp.concatenate([part, swap(part, "head", 1)], axis=0)

    def group_sum(part):
        part = core_sum(part)
        rows = part.shape[0] // 2
        return part[:rows] + swap(part[rows:].astype(lowp), "head", 2).astype(single)

    def group_both(part):
        return core_both(jnp.concatenate([part, swap(part, "head", 2)], axis=0))

    after_attn = embedded + core_sum(mm(mixed, full_out))
    ffn_in, inv_second = rms(after_attn, gain_vals[1])
    ffn_in = group_both(ffn_in)
    hidden_pre = mm(ffn_in, full_up, NT)
    hidden_act = jax.nn.gelu(hidden_pre).astype(lowp)
    after_ffn = after_attn + group_sum(mm(hidden_act, full_down))
    final_in, inv_third = rms(after_ffn, gain_vals[2])

    word_start = (h * vocab + z * words).astype(single)
    wanted_all = targets_all - word_start
    wanted_all = jnp.where((wanted_all >= 0) & (wanted_all < words), wanted_all, -1.0)
    groups = [(0, 1)]
    pieces = [final_in]
    mask = dp_size // 2
    while mask > 1:
        joined = jnp.concatenate(pieces) if len(pieces) > 1 else pieces[0]
        pieces.append(swap(reorder(joined, mask), "dp", mask))
        groups.append((groups[-1][1], 2 * groups[-1][1]))
        mask //= 2
    info_all = jnp.stack([wanted_all, mask_all] + [jnp.zeros_like(mask_all)] * 6)
    chunks = []
    infos = []
    raised = []
    stats = []
    for (first, last), piece in zip(groups, pieces):
        chunk = group_both(piece)
        packed = jnp.transpose(info_all[:, first:last], (0, 2, 3, 1, 4)).reshape(8, -1)
        out, stat = logits_part(words, packed, chunk, loss_table)
        chunks.append(chunk)
        infos.append(packed)
        raised.append(out)
        stats.append(stat[:3].reshape(3, 2, 2, last - first, half))
    own_stats = jnp.concatenate(stats, axis=3)

    def combine(first, second):
        top = jnp.maximum(first[0], second[0])
        total = first[1] * jnp.exp(first[0] - top) + second[1] * jnp.exp(second[0] - top)
        return jnp.stack([top, total, first[2] + second[2]])

    merged = own_stats
    merged = combine(merged, jnp.flip(swap(merged, "head", 1), 1))
    merged = combine(merged, jnp.flip(swap(merged, "head", 2), 2))
    mask = 2
    while mask < dp_size:
        other = split(swap(merged, "dp", mask), 3, reach)
        other = [other[order.index(j ^ mask)] for j in order[:reach]]
        merged = combine(merged, jnp.concatenate(other, axis=3))
        mask *= 2
    log_total = merged[0] + jnp.log(merged[1])
    loss_local = jnp.sum(mask_all[0, 0, 0] * (log_total[0, 0, 0] - merged[2, 0, 0, 0]))
    factor_all = jnp.exp(own_stats[0] - log_total)

    dlogits = [None] * len(groups)
    parts = []
    for i in reversed(range(len(groups))):
        first, last = groups[i]
        factor = factor_all[:, :, first:last].reshape(1, -1) * infos[i][1:2]
        factor = jnp.broadcast_to(factor, infos[i].shape)
        dlogits[i], part = logits_back(infos[i], factor, raised[i], loss_table)
        parts.append(group_sum(part.astype(single)))
    mask = 2
    total = jnp.zeros(())
    for i in range(len(groups) - 1):
        moved = swap(reorder(parts[0].astype(lowp), mask), "dp", mask).astype(single)
        rest = []
        start = 0
        for part in reversed(parts[1:]):
            rest.append(part + moved[start : start + part.shape[0]])
            start += part.shape[0]
        parts = rest[::-1]
        mask *= 2
    final_grad = parts[0]

    keep, send = table_grad_part(dlogits, chunks)
    keep = keep + swap(send, "dp", 1).astype(single)
    table_base = jnp.zeros((vocab, width), single)
    for m, part in zip(order[:reach], split(keep[:words], 1, reach)):
        part = part if m == 0 else swap(part.astype(lowp), "dp", m).astype(single)
        table_base = lax.dynamic_update_slice_in_dim(table_base, part, (z ^ (m // 2)) * words, 0)

    grad_after_ffn = rms_back(after_ffn, inv_third, gain_vals[2], final_grad)
    down_in = group_both(grad_after_ffn.astype(lowp))
    act_grad = mm(down_in, full_down, NT)
    pre_grad = jax.vjp(jax.nn.gelu, hidden_pre)[1](act_grad)[0].astype(lowp)
    ffn_in_grad = group_sum(mm(pre_grad, full_up))
    grad_after_attn = grad_after_ffn + rms_back(after_attn, inv_second, gain_vals[1], ffn_in_grad)
    attn_in = core_both(grad_after_attn.astype(lowp))

    mixed_grad = mm(attn_in, full_out, NT).astype(lowp)
    seg_grad, comp_grad, mem_grad = attend_back(info, query, seg, comp, mem, lse, mixed_grad)
    seg_in = mm(seg_grad, jnp.concatenate([query_weight, pair_weight]))
    rows_grad = embed_back(
        place,
        embedded_low,
        gain_vals[0],
        seg_in[:half],
        swap(seg_in[half:].astype(lowp), "head", 1),
        grad_after_attn,
    )
    rows_grad = lax.all_to_all(rows_grad, "dp", 0, 0)
    rows_grad = jnp.stack([rows_grad, swap(rows_grad, "head", 2)])
    rows_grad = jnp.stack([rows_grad, swap(rows_grad, "head", 1)]).reshape(-1, width)

    two = reduce_blocks(*hidden_grads(pre_grad, hidden_act, ffn_in, down_in))
    up_grad = two[:hidden_own].T
    down_grad = two[hidden_own:]
    old_grad, conv_sum = expand(comp_grad, old_raw, full_conv)
    far_sum, own_sum = attn_grads(
        seg_grad,
        mixed,
        mem_grad,
        old_grad.reshape(-1, old_grad.shape[-1]),
        normed,
        attn_in,
        mem_normed,
        old_normed.reshape(-1, D),
    )
    far_sum = jnp.concatenate([far_sum, conv_block_order(conv_sum[heads_own:])])
    own_sum = jnp.concatenate([own_sum, conv_block_order(conv_sum[:heads_own]).astype(single)])
    one = own_sum + swap(far_sum, "head", 2).astype(single)
    one = reduce_blocks(*split(one, 1, 2))
    qkv_grad = jnp.swapaxes(one[: 3 * wide].reshape(3, wide, width), 1, 2)
    out_grad = one[3 * wide : 4 * wide]
    conv_grad = one[4 * wide :].reshape(wconv.shape)
    tok_list, row_list, list_count = own_list(after(table_rows_all, final_in), vocab)
    table_grad = scatter(list_count, tok_list, row_list, table_base, rows_grad)

    gains_low = gains.astype(lowp).astype(single)
    gain_part = jnp.stack(
        [
            jnp.sum(low_qkv.astype(single) * qkv_grad, axis=(0, 2)),
            jnp.sum(wup.astype(lowp).astype(single) * up_grad, axis=1),
            jnp.sum(table.astype(lowp).astype(single) * table_base, axis=0),
        ]
    )

    grads = (table_grad, qkv_grad, out_grad, conv_grad, up_grad, down_grad)
    weights_now = (table, qkv, wout, wconv, wup, wdown)
    rows_old = (table_rows, qkv_rows, out_rows, conv_rows, up_rows, down_rows)
    cols_old = (table_cols, qkv_cols, out_cols, conv_cols, up_cols, down_cols)
    sizes = {"dp": dp_size, "head": head_size}
    row_axes = ("head", "dp", "head", "head", "dp", "head")
    col_axes = ("dp", "head", "dp", "dp", "head", "dp")

    def sum_over_dp(joined):
        mask = 1
        while mask < dp_size:
            joined = joined + swap(joined, "dp", mask)
            mask *= 2
        return joined

    row_part = []
    col_part = []
    scalar_list = []
    for index in range(6):
        square = grads[index] * grads[index]
        row_part.append(jnp.sum(square, axis=-1))
        col_part.append(jnp.sum(square, axis=tuple(range(square.ndim - 1))))
        scalar_list.append(jnp.sum(square))
        scalar_list.append(jnp.sum(rows_old[index]) / sizes[col_axes[index]])
    for weight in weights_now:
        scalar_list.append(jnp.sum(weight * weight))
    for which in range(3):
        scalar_list.append(jnp.sum(gains[which] * gains[which]) / head_size)
    scalar_list.append(loss_local)
    row_q, row_u, col_e, col_o, col_c, col_d, gain_raw, scalars = lax.psum(
        (
            row_part[1],
            row_part[4],
            col_part[0],
            col_part[2],
            col_part[3],
            col_part[5],
            gain_part,
            jnp.stack(scalar_list),
        ),
        "head",
    )
    members = [col_part[4], row_part[5], row_part[3], row_part[2], col_part[1], scalars, row_part[0]]
    joined = jnp.concatenate([m.reshape(-1) for m in members])
    joined = sum_over_dp(jnp.concatenate([joined, jnp.zeros((-joined.shape[0] % 1024,), single)]))
    sums = []
    start = 0
    for member in members:
        sums.append(joined[start : start + member.size].reshape(member.shape))
        start += member.size
    col_u, row_d, row_c, row_o, col_q, scalars, row_e = sums
    row_sums = [row_e, row_q, row_o, row_c, row_u, row_d]
    col_sums = [col_e, col_q, col_o, col_c, col_u, col_d]
    weight_total = scalars[12:21]
    loss_all = scalars[21]
    inverse = 1.0 / count_all
    decay = 1.0 - STEP ** (-0.8)
    updates = []
    stats_new = []
    scaled = []
    counts = []
    update_sq = []
    for index in range(6):
        rows_total = rows_old[index].size * sizes[row_axes[index]]
        cols_total = cols_old[index].size * sizes[col_axes[index]]
        grad_scaled = grads[index] * inverse
        rows_new = decay * rows_old[index] + (1.0 - decay) * (
            row_sums[index] * inverse * inverse / cols_total + TINY_SQUARE
        )
        cols_new = decay * cols_old[index] + (1.0 - decay) * (
            col_sums[index] * inverse * inverse / rows_total + TINY_SQUARE
        )
        mean_row = decay * scalars[2 * index + 1] / rows_total + (1.0 - decay) * (
            scalars[2 * index] * inverse * inverse / (rows_total * cols_total) + TINY_SQUARE
        )
        second = rows_new[..., None] * cols_new / mean_row
        direction = grad_scaled * lax.rsqrt(second)
        updates.append(direction)
        stats_new.append((rows_new, cols_new))
        scaled.append(grad_scaled)
        counts.append(rows_total * cols_total)
        update_sq.append(jnp.sum(direction * direction))
    gain_scaled = gain_raw / gains_low * inverse
    second_new = decay * gains_second + (1.0 - decay) * (gain_scaled * gain_scaled + TINY_SQUARE)
    gain_dir = gain_scaled * lax.rsqrt(second_new)
    for which in range(3):
        update_sq.append(jnp.sum(gain_dir[which] * gain_dir[which]) / head_size)
    update_total = jnp.concatenate([jnp.stack(update_sq), jnp.zeros((1024 - 9,), single)])
    update_total = sum_over_dp(lax.psum(update_total, "head"))[:9]
    results = [loss_all, count_all]
    for index in range(6):
        factor = jnp.maximum(0.001, jnp.sqrt(weight_total[index] / counts[index]))
        denom = jnp.maximum(1.0, jnp.sqrt(update_total[index] / counts[index]) / CLIP_LEVEL)
        new_weight = weights_now[index] - LEARN_RATE * factor * updates[index] / denom
        results += [new_weight, scaled[index], stats_new[index][0], stats_new[index][1]]
    gain_factor = jnp.maximum(0.001, jnp.sqrt(weight_total[6:] / D))[:, None]
    gain_denom = jnp.maximum(1.0, jnp.sqrt(update_total[6:] / D) / CLIP_LEVEL)[:, None]
    results += [gains - LEARN_RATE * gain_factor * gain_dir / gain_denom, gain_scaled, second_new]
    return tuple(results)


def solution(mesh):
    in_specs = (
        P("dp", None),
        P("dp", None),
        P("dp", None),
        P("dp", None, None),
        P("dp", None, None),
        P("dp"),
        P("dp"),
        P("head", "dp"),
        P(None, "dp", "head"),
        P("head", "dp"),
        P("head", None, "dp"),
        P("dp", "head"),
        P("head", "dp"),
        P(None, "dp"),
        P("head"),
        P("dp"),
        P(None, "dp"),
        P("head"),
        P("head"),
        P("dp"),
        P("head", None),
        P("dp"),
        P("dp"),
        P("head"),
        P("head"),
        P("dp"),
        P(None, "dp"),
    )
    out_specs = (
        P(),
        P(),
        P("head", "dp"),
        P("head", "dp"),
        P("head"),
        P("dp"),
        P(None, "dp", "head"),
        P(None, "dp", "head"),
        P(None, "dp"),
        P("head"),
        P("head", "dp"),
        P("head", "dp"),
        P("head"),
        P("dp"),
        P("head", None, "dp"),
        P("head", None, "dp"),
        P("head", None),
        P("dp"),
        P("dp", "head"),
        P("dp", "head"),
        P("dp"),
        P("head"),
        P("head", "dp"),
        P("head", "dp"),
        P("head"),
        P("dp"),
        P(None, "dp"),
        P(None, "dp"),
        P(None, "dp"),
    )
    return jax.shard_map(local, mesh=mesh, in_specs=in_specs, out_specs=out_specs, check_vma=False)
```

```python
import functools

import jax
import jax.numpy as jnp
from jax import lax
from jax.experimental import pallas as pl
from jax.experimental.pallas import tpu as pltpu
from jax.sharding import PartitionSpec as P

D = 1024
H = 8
DH = 128
MEM = 512
CMEM = 512
RATE = 3
STEP = 10


TINY_NORM = 1e-06
TINY_SQUARE = 1e-30
LEARN_RATE = 0.5
CLIP_LEVEL = 1.0

lowp = jnp.bfloat16
single = jnp.float32
NT = (((1,), (1,)), ((), ()))
TN = (((0,), (0,)), ((), ()))
NN = (((1,), (0,)), ((), ()))
MIB = 1024 * 1024


def mm(left, right, dims=NN):
    return lax.dot_general(left, right, dims, preferred_element_type=single)


def swap(value, axis, mask):
    size = lax.axis_size(axis)
    return lax.ppermute(value, axis, [(i, i ^ mask) for i in range(size)])


def after(value, *deps):
    return lax.optimization_barrier((value, *deps))[0]


def together(*values):
    return lax.optimization_barrier(values)


def block_order(size):
    order = [0]
    step = size // 2
    while step:
        order = order + [j + step for j in order]
        step //= 2
    return order


def gather_blocks(piece, axis, start=None):
    steps = []
    mask = lax.axis_size("dp") // 2
    while mask:
        piece = jnp.concatenate([piece, swap(piece, "dp", mask)], axis=axis)
        steps.append(piece)
        mask //= 2
    return piece, steps


def split(value, axis, parts):
    width = value.shape[axis] // parts
    return [lax.slice_in_dim(value, i * width, (i + 1) * width, axis=axis) for i in range(parts)]


def reduce_blocks(keep, send, mask=1):
    total = keep + swap(send.astype(lowp), "dp", mask).astype(single)
    mask *= 2
    if mask == lax.axis_size("dp"):
        return total
    return reduce_blocks(*split(total, 1, 2), mask)


def reorder(value, mask):
    order = block_order(lax.axis_size("dp"))
    cols = split(value, 1, len(order))
    return jnp.concatenate([cols[order.index(j ^ mask)] for j in order], axis=1)


def relative(value, x, c):
    value = jnp.where(x == 1, jnp.flip(value, -3), value)
    value = jnp.where(c == 1, jnp.flip(value, -2), value)
    return jnp.swapaxes(value, -3, -2)


def rms(values, gain):
    inv = lax.rsqrt(jnp.mean(values * values, axis=-1, keepdims=True) + TINY_NORM)
    return (values * inv * gain).astype(lowp), inv


def rms_back(values, inv, gain, upstream):
    scaled = gain * upstream
    inner = jnp.sum(scaled * values, axis=-1, keepdims=True) / D
    return scaled * inv - values * (inner * inv * inv * inv)


def vmem(shape=None, index=None):
    if shape is None:
        return pl.BlockSpec(memory_space=pltpu.VMEM)
    return pl.BlockSpec(shape, index)


def smem():
    return pl.BlockSpec(memory_space=pltpu.SMEM)


def params(mib):
    return pltpu.CompilerParams(vmem_limit_bytes=mib * MIB)


def cost(flops, size, exps=0):
    return pl.CostEstimate(
        flops=int(0.4 * flops), bytes_accessed=int(0.4 * size), transcendentals=exps
    )


def lookup_kernel(row_ref, table_ref, out_ref, tab, held, sem):
    total = row_ref.shape[0]
    vocab = table_ref.shape[0]
    copy = pltpu.make_async_copy(table_ref, tab.at[pl.ds(0, vocab)], sem)
    copy.start()
    tab[pl.ds(vocab, 8), :] = jnp.zeros((8, tab.shape[1]), single)
    copy.wait()

    @pl.loop(0, total // 16)
    def _(g):
        for j in range(16):
            t = g * 16 + j
            held[pl.ds(t, 1), :] = tab[pl.ds(row_ref[t], 1), :]

    @pl.loop(0, total // 512)
    def _(i):
        rows = pl.ds(pl.multiple_of(i * 512, 512), 512)
        out_ref[rows, :] = held[rows, :].astype(lowp)


def lookup(rows, table):
    total = rows.shape[0]
    vocab, width = table.shape
    return pl.pallas_call(
        lookup_kernel,
        name="lookup",
        out_shape=jax.ShapeDtypeStruct((total, width), lowp),
        in_specs=[smem(), pl.BlockSpec(memory_space=pl.ANY)],
        out_specs=vmem(),
        scratch_shapes=[
            pltpu.VMEM((vocab + 8, width), single),
            pltpu.VMEM((total, width), single),
            pltpu.SemaphoreType.DMA(()),
        ],
        compiler_params=params(60),
        cost_estimate=cost(0, 30 * MIB),
    )(rows, table)


def list_kernel(code_ref, out_ref, count_ref):
    total = code_ref.shape[0]

    def group(g, count):
        for j in range(16):
            code = code_ref[g * 16 + j]
            out_ref[count] = code
            count = count + jnp.where(code >= 0, 1, 0)
        return count

    count_ref[0] = lax.fori_loop(0, total // 16, group, jnp.int32(0))


def own_list(codes):
    total = codes.shape[0]
    return pl.pallas_call(
        list_kernel,
        name="own_list",
        out_shape=(
            jax.ShapeDtypeStruct((total + 8,), jnp.int32),
            jax.ShapeDtypeStruct((1,), jnp.int32),
        ),
        in_specs=[smem()],
        out_specs=(smem(), smem()),
        cost_estimate=cost(0, 60 * MIB),
    )(codes)


def place_kernel(order, place_ref, in_ref, gain_ref, out_ref, norm_ref, held):
    width = in_ref.shape[2]
    for p, j in enumerate(order):
        block = in_ref[pl.ds(place_ref[1] ^ j, 1)][0]
        out_ref[:, p * width : (p + 1) * width] = block
        held[:, p * width : (p + 1) * width] = block.astype(single)
    values = held[...]
    inv = lax.rsqrt(jnp.mean(values * values, axis=-1, keepdims=True) + TINY_NORM)
    norm_ref[...] = (values * inv * gain_ref[...]).astype(lowp)


def place_embedding(place, blocks, gain):
    rows = blocks.shape[1]
    return pl.pallas_call(
        functools.partial(place_kernel, block_order(blocks.shape[0])),
        name="place_embedding",
        out_shape=(jax.ShapeDtypeStruct((rows, D), lowp), jax.ShapeDtypeStruct((rows, D), lowp)),
        in_specs=[smem(), vmem(), vmem()],
        out_specs=(vmem(), vmem()),
        scratch_shapes=[pltpu.VMEM((rows, D), single)],
        compiler_params=params(60),
        cost_estimate=cost(0, 3 * MIB),
    )(place, blocks, gain)


def embed_back_kernel(order, place_ref, in_ref, gain_ref, keep_ref, more_ref, grad_ref, out_ref, held):
    values = in_ref[...].astype(single)
    inv = lax.rsqrt(jnp.mean(values * values, axis=-1, keepdims=True) + TINY_NORM)
    upstream = keep_ref[...] + more_ref[...].astype(single)
    held[...] = grad_ref[...] + rms_back(values, inv, gain_ref[...], upstream)
    width = out_ref.shape[2]
    for p, j in enumerate(order):
        block = held[:, p * width : (p + 1) * width].astype(lowp)
        out_ref[pl.ds(place_ref[1] ^ j, 1)] = block[None]


def embed_back(place, values, gain, keep, more, grad):
    rows = values.shape[0]
    size = lax.axis_size("dp")
    return pl.pallas_call(
        functools.partial(embed_back_kernel, block_order(size)),
        name="embed_back",
        out_shape=jax.ShapeDtypeStruct((size, rows, D // size), lowp),
        in_specs=[smem()] + [vmem()] * 5,
        out_specs=vmem(),
        scratch_shapes=[pltpu.VMEM((rows, D), single)],
        compiler_params=params(60),
        cost_estimate=cost(0, 4 * MIB),
    )(place, values, gain, keep, more, grad)


def scatter_kernel(bits, count_ref, code_ref, base_ref, grad_ref, out_ref, rows):
    total = grad_ref.shape[0]
    vocab = base_ref.shape[0]

    @pl.loop(0, total // 512)
    def _(i):
        here = pl.ds(pl.multiple_of(i * 512, 512), 512)
        rows[here, :] = grad_ref[here, :].astype(single)

    rows[pl.ds(total, 8), :] = jnp.zeros((8, rows.shape[1]), single)

    @pl.loop(0, vocab // 400)
    def _(i):
        here = pl.ds(pl.multiple_of(i * 400, 400), 400)
        out_ref[here, :] = base_ref[here, :]

    count = count_ref[0]

    def group(g, carry):
        for j in range(8):
            index = g * 8 + j
            code = jnp.where(index < count, code_ref[index], total << bits)
            token = lax.shift_right_logical(code, bits)
            row = code & ((1 << bits) - 1)
            out_ref[pl.ds(row, 1), :] = out_ref[pl.ds(row, 1), :] + rows[pl.ds(token, 1), :]
        return carry

    lax.fori_loop(0, (count + 7) // 8, group, jnp.int32(0))


def scatter(bits, count, codes, base, grad):
    total, width = grad.shape
    return pl.pallas_call(
        functools.partial(scatter_kernel, bits),
        name="scatter",
        out_shape=jax.ShapeDtypeStruct(base.shape, single),
        in_specs=[smem(), smem(), vmem(), vmem()],
        out_specs=vmem(),
        scratch_shapes=[pltpu.VMEM((total + 8, width), single)],
        compiler_params=params(60),
        cost_estimate=cost(0, 30 * MIB),
    )(count, codes, base, grad)


def state_kernel(order, width, place_ref, gain_ref, in_ref, out_ref, held):
    rows = in_ref.shape[1]
    values = in_ref[0].astype(single)
    inv = lax.rsqrt(jnp.mean(values * values, axis=-1, keepdims=True) + TINY_NORM)
    for p, j in enumerate(order):
        start = pl.multiple_of((place_ref[1] ^ j) * width, width)
        block = in_ref[0, :, pl.ds(start, width)].astype(single)
        held[p] = block * inv * gain_ref[:, p * width : (p + 1) * width]
    groups = out_ref.shape[0]
    for p in range(len(order)):
        cols = slice(p * width, (p + 1) * width)
        if groups == 1:
            out_ref[0, :, cols] = held[p].astype(lowp)
        else:
            for j in range(groups):
                part = held[p, pl.ds(j, rows // groups, stride=groups), :]
                out_ref[j, :, cols] = part.astype(lowp)


def state_norm(place, gain, states, groups):
    size = lax.axis_size("dp")
    order = block_order(size)
    width = D // size
    streams = states.shape[0]
    count = states.shape[1] // groups
    if width % 128:
        values = jnp.where(place[0] == 1, jnp.flip(states, 0), states).astype(single).reshape(-1, D)
        inv = lax.rsqrt(jnp.mean(values * values, axis=-1, keepdims=True) + TINY_NORM)
        lanes = jnp.arange(D, dtype=jnp.int32)
        blocks = jnp.asarray(order, jnp.int32)[lanes // width] ^ place[1]
        source = blocks * width + lanes % width
        shuffle = (lanes[:, None] == source[None, :]).astype(single)
        moved = jnp.dot(values * inv, shuffle, precision=lax.Precision.HIGHEST)
        out = (moved * gain).astype(lowp)
        return jnp.swapaxes(out.reshape(streams * count, groups, D), 0, 1)
    tile = 128
    return pl.pallas_call(
        functools.partial(state_kernel, order, width),
        name="state_norm",
        out_shape=jax.ShapeDtypeStruct((groups, streams * count, D), lowp),
        grid_spec=pltpu.PrefetchScalarGridSpec(
            num_scalar_prefetch=1,
            grid=(streams, count // tile),
            in_specs=[
                pl.BlockSpec((1, D), lambda n, i, s: (0, 0)),
                pl.BlockSpec((1, tile * groups, D), lambda n, i, s: (s[0] ^ n, i, 0)),
            ],
            out_specs=pl.BlockSpec(
                (groups, tile, D), lambda n, i, s: (0, n * (count // tile) + i, 0)
            ),
            scratch_shapes=[pltpu.VMEM((len(order), tile * groups, width), single)],
        ),
        compiler_params=params(60),
        cost_estimate=cost(0, 4 * streams * count * groups * D),
    )(place, gain, states)


def compress_kernel(old_ref, key_ref, value_ref, conv_ref, comp_ref, raw_ref):
    heads = conv_ref.shape[0]
    wide = heads * DH
    for part, weight_ref in enumerate((key_ref, value_ref)):
        sums = [None] * heads
        for j in range(RATE):
            raw = mm(old_ref[j], weight_ref[...], NT).astype(lowp)
            raw_ref[j, :, part * wide : (part + 1) * wide] = raw
            for n in range(heads):
                piece = raw[:, n * DH : (n + 1) * DH]
                term = mm(piece, conv_ref[n, j * DH : (j + 1) * DH, :])
                sums[n] = term if j == 0 else sums[n] + term
        for n in range(heads):
            first = part * wide + n * DH
            comp_ref[:, first : first + DH] = sums[n].astype(lowp)


def compress(old3, weights, conv):
    rows = old3.shape[1]
    wide = conv.shape[0] * DH
    tile = 256
    return pl.pallas_call(
        compress_kernel,
        name="compress",
        grid=(rows // tile,),
        out_shape=(
            jax.ShapeDtypeStruct((rows, 2 * wide), lowp),
            jax.ShapeDtypeStruct((RATE, rows, 2 * wide), lowp),
        ),
        in_specs=[
            pl.BlockSpec((RATE, tile, D), lambda i: (0, i, 0)),
            pl.BlockSpec((wide, D), lambda i: (1, 0)),
            pl.BlockSpec((wide, D), lambda i: (2, 0)),
            pl.BlockSpec(conv.shape, lambda i: (0, 0, 0)),
        ],
        out_specs=(
            pl.BlockSpec((tile, 2 * wide), lambda i: (i, 0)),
            pl.BlockSpec((RATE, tile, 2 * wide), lambda i: (0, i, 0)),
        ),
        compiler_params=params(60),
        cost_estimate=cost(4 * RATE * rows * wide * D, 12 * MIB),
    )(old3, weights, weights, conv)


def expand_kernel(grad_ref, raw_ref, conv_ref, out_ref, conv_out_ref):
    heads = conv_ref.shape[0]
    for h in range(heads):
        for j in range(RATE):
            rows = slice(j * DH, (j + 1) * DH)
            taps = conv_ref[h, rows, :]
            total = None
            for n in (h, heads + h):
                cols = slice(n * DH, (n + 1) * DH)
                grad = grad_ref[:, cols]
                out_ref[j, :, cols] = mm(grad, taps, NT).astype(lowp)
                term = mm(raw_ref[j, :, cols], grad, TN)
                total = term if total is None else total + term
            conv_out_ref[h, rows, :] = total


def expand(grad, raw, conv):
    return pl.pallas_call(
        expand_kernel,
        name="expand",
        out_shape=(
            jax.ShapeDtypeStruct(raw.shape, lowp),
            jax.ShapeDtypeStruct(conv.shape, single),
        ),
        in_specs=[vmem()] * 3,
        out_specs=(vmem(), vmem()),
        compiler_params=params(60),
        cost_estimate=cost(2000 * MIB, 12 * MIB),
    )(grad, raw, conv)


def masked_scores(info_ref, query, keys):
    rows = query.shape[0]
    scale = DH ** (-0.5)
    result = []
    for which, key in enumerate(keys):
        slots = key.shape[0]
        col = lax.broadcasted_iota(jnp.int32, (rows, slots), 1)
        if which < 2:
            seen = col >= slots - info_ref[2 * pl.program_id(0) + which]
        else:
            row = lax.broadcasted_iota(jnp.int32, (rows, slots), 0)
            shift = info_ref[4]
            row = row + shift
            col = col + shift
            row = jnp.where(row >= slots, row - slots, row)
            col = jnp.where(col >= slots, col - slots, col)
            seen = col <= row
        result.append(jnp.where(seen, mm(query, key, NT) * scale, -1e30))
    return result


def rows_of(ref):
    return ref[...].reshape(-1, ref.shape[-1])


def attend_kernel(info_ref, q_ref, ks_ref, vs_ref, kc_ref, vc_ref, km_ref, vm_ref, out_ref, lse_ref):
    query = rows_of(q_ref)
    scores = masked_scores(info_ref, query, [kc_ref[...], km_ref[...], rows_of(ks_ref)])
    top = functools.reduce(jnp.maximum, [jnp.max(s, axis=-1, keepdims=True) for s in scores])
    total = 0.0
    mixed = 0.0
    for score, value in zip(scores, (vc_ref[...], vm_ref[...], rows_of(vs_ref))):
        weight = jnp.exp(score - top)
        total = total + jnp.sum(weight, axis=-1, keepdims=True)
        mixed = mixed + mm(weight.astype(lowp), value)
    out_ref[...] = (mixed / total).astype(lowp).reshape(out_ref.shape)
    lse_ref[0, 0] = top + jnp.log(total)


def attend_back_kernel(
    info_ref, q_ref, ks_ref, vs_ref, kc_ref, vc_ref, km_ref, vm_ref, lse_ref, up_ref,
    seg_ref, comp_ref, mem_ref,
):
    head = pl.program_id(1)
    wide = pl.num_programs(1) * DH
    scale = DH ** (-0.5)
    query = rows_of(q_ref)
    upstream = rows_of(up_ref)
    keys = [kc_ref[...], km_ref[...], rows_of(ks_ref)]
    scores = masked_scores(info_ref, query, keys)
    probs = [jnp.exp(s - lse_ref[0, 0]) for s in scores]
    prob_grads = [
        mm(upstream, v, NT) for v in (vc_ref[...], vm_ref[...], rows_of(vs_ref))
    ]
    inner = 0.0
    for p, g in zip(probs, prob_grads):
        inner = inner + jnp.sum(p * g, axis=-1, keepdims=True)
    here = pl.ds(pl.multiple_of(head * DH, DH), DH)
    second = pl.ds(pl.multiple_of(wide + head * DH, DH), DH)
    third = pl.ds(pl.multiple_of(2 * wide + head * DH, DH), DH)
    query_grad = 0.0
    places = ((comp_ref, here, second), (mem_ref, here, second), (seg_ref, second, third))
    for p, g, key, (ref, key_at, value_at) in zip(probs, prob_grads, keys, places):
        score_grad = (p * (g - inner)).astype(lowp)
        query_grad = query_grad + mm(score_grad, key)
        shape = ref.shape[:-1] + (DH,)
        key_grad = (mm(score_grad, query, TN) * scale).astype(lowp)
        value_grad = mm(p.astype(lowp), upstream, TN).astype(lowp)
        ref[..., key_at] = key_grad.reshape(shape)
        ref[..., value_at] = value_grad.reshape(shape)
    shape = seg_ref.shape[:-1] + (DH,)
    seg_ref[..., here] = (query_grad * scale).astype(lowp).reshape(shape)


def head_specs(seg, comp, mem, heads):
    streams = seg.shape[1]

    def of_seg(first):
        return pl.BlockSpec((2, 1, seg.shape[2], DH), lambda n, h: (0, n, 0, first + h))

    def cols(array, first):
        return pl.BlockSpec((array.shape[0] // streams, DH), lambda n, h: (n, first + h))

    return [
        smem(),
        of_seg(0),
        of_seg(heads),
        of_seg(2 * heads),
        cols(comp, 0),
        cols(comp, heads),
        cols(mem, 0),
        cols(mem, heads),
    ]


def attend(info, seg, comp, mem):
    _, streams, half, _ = seg.shape
    heads = comp.shape[1] // (2 * DH)
    return pl.pallas_call(
        attend_kernel,
        name="attend",
        grid=(streams, heads),
        out_shape=(
            jax.ShapeDtypeStruct((2, streams, half, heads * DH), lowp),
            jax.ShapeDtypeStruct((streams, heads, 2 * half, 1), single),
        ),
        in_specs=head_specs(seg, comp, mem, heads),
        out_specs=(
            pl.BlockSpec((2, 1, half, DH), lambda n, h: (0, n, 0, h)),
            pl.BlockSpec((1, 1, 2 * half, 1), lambda n, h: (n, h, 0, 0)),
        ),
        compiler_params=params(60),
        cost_estimate=cost(7000 * MIB, 6 * MIB),
    )(info, seg, seg, seg, comp, comp, mem, mem)


def attend_back(info, seg, comp, mem, lse, upstream):
    _, streams, half, wide = seg.shape
    heads = comp.shape[1] // (2 * DH)
    slots = comp.shape[0] // streams
    kept = mem.shape[0] // streams
    return pl.pallas_call(
        attend_back_kernel,
        name="attend_back",
        grid=(streams, heads),
        out_shape=(
            jax.ShapeDtypeStruct(seg.shape, lowp),
            jax.ShapeDtypeStruct(comp.shape, lowp),
            jax.ShapeDtypeStruct(mem.shape, lowp),
        ),
        in_specs=head_specs(seg, comp, mem, heads)
        + [
            pl.BlockSpec((1, 1, 2 * half, 1), lambda n, h: (n, h, 0, 0)),
            pl.BlockSpec((2, 1, half, DH), lambda n, h: (0, n, 0, h)),
        ],
        out_specs=(
            pl.BlockSpec((2, 1, half, wide), lambda n, h: (0, n, 0, 0)),
            pl.BlockSpec((slots, comp.shape[1]), lambda n, h: (n, 0)),
            pl.BlockSpec((kept, mem.shape[1]), lambda n, h: (n, 0)),
        ),
        compiler_params=params(60),
        cost_estimate=cost(11000 * MIB, 9 * MIB),
    )(info, seg, seg, seg, comp, comp, mem, mem, lse, upstream)


def columns_of(rows):
    tall = jnp.concatenate([rows, jnp.zeros((120, rows.shape[1]), single)], axis=0)
    return jnp.transpose(tall)


def logits_kernel(words, info_ref, in_ref, table_ref, out_ref, stat_ref):
    logits = mm(in_ref[...], table_ref[...], NT)
    wanted = columns_of(info_ref[...])[:, 0:1].astype(jnp.int32)
    col = lax.broadcasted_iota(jnp.int32, logits.shape, 1)
    hit = jnp.sum(jnp.where(col == wanted, logits, 0.0), axis=-1, keepdims=True)
    logits = jnp.where(col < words, logits, -1e30)
    top = jnp.max(logits, axis=-1, keepdims=True)
    raised = jnp.exp(logits - top)
    total = jnp.sum(raised, axis=-1, keepdims=True)
    out_ref[...] = raised.astype(lowp)
    lane = lax.broadcasted_iota(jnp.int32, (logits.shape[0], 128), 1)
    packed = jnp.where(lane == 0, top, jnp.where(lane == 1, total, jnp.where(lane == 2, hit, 0.0)))
    stat_ref[...] = jnp.transpose(packed)[:8]


def logits_part(words, info, inputs, table):
    rows = inputs.shape[0]
    slots = table.shape[0]
    tile = 256
    return pl.pallas_call(
        functools.partial(logits_kernel, words),
        name="logits_part",
        grid=(rows // tile,),
        out_shape=(
            jax.ShapeDtypeStruct((rows, slots), lowp),
            jax.ShapeDtypeStruct((8, rows), single),
        ),
        in_specs=[
            pl.BlockSpec((8, tile), lambda i: (0, i)),
            pl.BlockSpec((tile, D), lambda i: (i, 0)),
            pl.BlockSpec(table.shape, lambda i: (0, 0)),
        ],
        out_specs=(
            pl.BlockSpec((tile, slots), lambda i: (i, 0)),
            pl.BlockSpec((8, tile), lambda i: (0, i)),
        ),
        compiler_params=params(60),
        cost_estimate=cost(4 * rows * slots * D, 10 * MIB),
    )(info, inputs, table)


def logits_back_kernel(info_ref, factor_ref, in_ref, table_ref, out_ref, grad_ref):
    info = columns_of(info_ref[...])
    wanted = info[:, 0:1].astype(jnp.int32)
    counted = info[:, 1:2]
    factor = columns_of(factor_ref[...])[:, 0:1]
    raised = in_ref[...].astype(single)
    col = lax.broadcasted_iota(jnp.int32, raised.shape, 1)
    grads = (raised * factor - jnp.where(col == wanted, counted, 0.0)).astype(lowp)
    out_ref[...] = grads
    grad_ref[...] = mm(grads, table_ref[...]).astype(lowp)


def logits_back(info, factor, raised, table):
    rows, slots = raised.shape
    tile = 256
    return pl.pallas_call(
        logits_back_kernel,
        name="logits_back",
        grid=(rows // tile,),
        out_shape=(
            jax.ShapeDtypeStruct((rows, slots), lowp),
            jax.ShapeDtypeStruct((rows, D), lowp),
        ),
        in_specs=[
            pl.BlockSpec((8, tile), lambda i: (0, i)),
            pl.BlockSpec((8, tile), lambda i: (0, i)),
            pl.BlockSpec((tile, slots), lambda i: (i, 0)),
            pl.BlockSpec(table.shape, lambda i: (0, 0)),
        ],
        out_specs=(
            pl.BlockSpec((tile, slots), lambda i: (i, 0)),
            pl.BlockSpec((tile, D), lambda i: (i, 0)),
        ),
        compiler_params=params(60),
        cost_estimate=cost(4 * rows * slots * D, 12 * MIB),
    )(info, factor, raised, table)


def halves(total, keep_ref, send_ref):
    half = keep_ref.shape[1]
    keep_ref[...] = total[:, :half]
    send_ref[...] = total[:, half:].astype(send_ref.dtype)


def table_grad_kernel(count, *refs):
    grads = refs[:count]
    inputs = refs[count : 2 * count]
    total = mm(grads[0][...], inputs[0][...], TN)
    for i in range(1, count):
        total = total + mm(grads[i][...], inputs[i][...], TN)
    halves(total, *refs[2 * count :])


def table_grad_part(grads, inputs):
    count = len(grads)
    rows = sum(g.shape[0] for g in grads)
    slots = grads[0].shape[1]
    block = 256
    if rows > 4096:
        total = sum(mm(g, v, TN) for g, v in zip(grads, inputs))
        keep, send = split(total, 1, 2)
        return keep, send.astype(lowp)
    return pl.pallas_call(
        functools.partial(table_grad_kernel, count),
        name="table_grad_part",
        grid=(slots // block,),
        out_shape=(
            jax.ShapeDtypeStruct((slots, D // 2), single),
            jax.ShapeDtypeStruct((slots, D // 2), lowp),
        ),
        in_specs=[pl.BlockSpec((g.shape[0], block), lambda i: (0, i)) for g in grads]
        + [pl.BlockSpec(v.shape, lambda i: (0, 0)) for v in inputs],
        out_specs=(
            pl.BlockSpec((block, D // 2), lambda i: (i, 0)),
            pl.BlockSpec((block, D // 2), lambda i: (i, 0)),
        ),
        compiler_params=params(60),
        cost_estimate=cost(3 * rows * slots * D, 30 * MIB),
    )(*grads, *inputs)


def hidden_grad_kernel(blocks, pre_ref, act_ref, in_ref, down_ref, keep_ref, send_ref):
    step = pl.program_id(0)

    @pl.when(step < blocks)
    def _():
        halves(mm(pre_ref[...], in_ref[...], TN), keep_ref, send_ref)

    @pl.when(step >= blocks)
    def _():
        halves(mm(act_ref[...], down_ref[...], TN), keep_ref, send_ref)


def hidden_grads(pre_grad, hidden_act, ffn_in, down_in):
    rows, hidden = pre_grad.shape
    block = 256
    blocks = hidden // block
    return pl.pallas_call(
        functools.partial(hidden_grad_kernel, blocks),
        name="hidden_grads",
        grid=(2 * blocks,),
        out_shape=(
            jax.ShapeDtypeStruct((2 * hidden, D // 2), single),
            jax.ShapeDtypeStruct((2 * hidden, D // 2), lowp),
        ),
        in_specs=[
            pl.BlockSpec((rows, block), lambda i: (0, jnp.minimum(i, blocks - 1))),
            pl.BlockSpec((rows, block), lambda i: (0, jnp.maximum(i - blocks, 0))),
            pl.BlockSpec((rows, D), lambda i: (0, 0)),
            pl.BlockSpec((rows, D), lambda i: (0, 0)),
        ],
        out_specs=(
            pl.BlockSpec((block, D // 2), lambda i: (i, 0)),
            pl.BlockSpec((block, D // 2), lambda i: (i, 0)),
        ),
        compiler_params=params(60),
        cost_estimate=cost(6 * rows * hidden * D, 16 * MIB),
    )(pre_grad, hidden_act, ffn_in, down_in)


def attn_grad_kernel(
    seg_ref, mixed_ref, mem_ref, old_ref, normed_ref, up_ref, mem_in_ref, old_in_ref, keep_ref, send_ref
):
    which = pl.program_id(0)

    @pl.when(which == 0)
    def _():
        halves(mm(seg_ref[...], normed_ref[...], TN), keep_ref, send_ref)

    @pl.when(which == 3)
    def _():
        halves(mm(mixed_ref[...], up_ref[...], TN), keep_ref, send_ref)

    @pl.when(jnp.logical_and(which > 0, which < 3))
    def _():
        total = mm(seg_ref[...], normed_ref[...], TN)
        total = total + mm(mem_ref[...], mem_in_ref[...], TN)
        total = total + mm(old_ref[...], old_in_ref[...], TN)
        halves(total, keep_ref, send_ref)


def attn_grads(seg_grad, mixed, mem_grad, old_grad, normed, attn_in, mem_in, old_in):
    block = mixed.shape[1]

    def whole(array):
        return pl.BlockSpec(array.shape, lambda i: (0, 0))

    return pl.pallas_call(
        attn_grad_kernel,
        name="attn_grads",
        grid=(4,),
        out_shape=(
            jax.ShapeDtypeStruct((4 * block, D // 2), single),
            jax.ShapeDtypeStruct((4 * block, D // 2), lowp),
        ),
        in_specs=[
            pl.BlockSpec((seg_grad.shape[0], block), lambda i: (0, jnp.minimum(i, 2))),
            whole(mixed),
            pl.BlockSpec((mem_grad.shape[0], block), lambda i: (0, jnp.clip(i - 1, 0, 1))),
            pl.BlockSpec((old_grad.shape[0], block), lambda i: (0, jnp.clip(i - 1, 0, 1))),
            whole(normed),
            whole(attn_in),
            whole(mem_in),
            whole(old_in),
        ],
        out_specs=(
            pl.BlockSpec((block, D // 2), lambda i: (i, 0)),
            pl.BlockSpec((block, D // 2), lambda i: (i, 0)),
        ),
        compiler_params=params(60),
        cost_estimate=cost(9000 * MIB, 24 * MIB),
    )(seg_grad, mixed, mem_grad, old_grad, normed, attn_in, mem_in, old_in)


def scalar_row(values, length=128):
    lane = jnp.arange(length, dtype=jnp.int32)
    row = jnp.zeros((length,), single)
    for i, value in enumerate(values):
        row = jnp.where(lane == i, value, row)
    return row


def local(
    ids,
    targets,
    target_mask,
    memory,
    old_states,
    mem_fill,
    comp_fill,
    table,
    qkv,
    wout,
    wconv,
    wup,
    wdown,
    gains,
    table_rows,
    table_cols,
    qkv_rows,
    qkv_cols,
    out_rows,
    out_cols,
    conv_rows,
    conv_cols,
    up_rows,
    up_cols,
    down_rows,
    down_cols,
    gains_second,
):
    dp_size, head_size = lax.axis_size("dp"), lax.axis_size("head")
    d, h = lax.axis_index("dp"), lax.axis_index("head")
    x, c = h // 2, h % 2
    order = block_order(dp_size)
    reach = dp_size // 2
    streams, seg_len = ids.shape
    half = seg_len // 2
    per_group = streams * seg_len
    vocab, width = table.shape
    assert head_size == 4 and streams == 2

    weights_now = (table, qkv, wout, wconv, wup, wdown)
    rows_old = (table_rows, qkv_rows, out_rows, conv_rows, up_rows, down_rows)
    cols_old = (table_cols, qkv_cols, out_cols, conv_cols, up_cols, down_cols)
    sizes = {"dp": dp_size, "head": head_size}
    row_axes = ("head", "dp", "head", "head", "dp", "head")
    col_axes = ("dp", "head", "dp", "dp", "head", "dp")
    early = [jnp.sum(old) / sizes[axis] for old, axis in zip(rows_old, col_axes)]
    early += [jnp.sum(weight * weight) for weight in weights_now]
    gain_sums = jnp.sum(gains * gains, axis=1) / head_size
    early = scalar_row(early + [gain_sums[0], gain_sums[1], gain_sums[2]])

    flat = jnp.concatenate(
        [
            ids.astype(single).reshape(-1),
            targets.astype(single).reshape(-1),
            target_mask.astype(single).reshape(-1),
            gains.astype(lowp).astype(single).reshape(-1),
        ]
    )
    room = -flat.shape[0] % 1024
    flat = jnp.concatenate([flat, jnp.zeros((room,), single)]).reshape(1, -1, 128)
    small, small_steps = gather_blocks(flat, 0)
    small = small.reshape(dp_size, -1)
    place = jnp.stack([x, d])

    def field(raw):
        return relative(raw.reshape(-1, 2, 2, half), x, c)

    ids_all = small[:, :per_group]
    position = [order.index(j) for j in range(dp_size)]
    ids_all = jnp.take(ids_all, jnp.asarray(position, jnp.int32)[jnp.arange(dp_size) ^ d], axis=0)
    ids_all = jnp.transpose(field(ids_all), (1, 2, 0, 3)).reshape(-1).astype(jnp.int32)
    table_rows_all = ids_all - h * vocab
    inside = (table_rows_all >= 0) & (table_rows_all < vocab)
    bits = vocab.bit_length()
    token_codes = (jnp.arange(ids_all.shape[0], dtype=jnp.int32) << bits) | table_rows_all
    token_codes = jnp.where(inside, token_codes, -1)
    table_rows_all = jnp.where(inside, table_rows_all, vocab)
    targets_all = field(small[:reach, per_group : 2 * per_group])
    mask_all = field(small[:reach, 2 * per_group : 3 * per_group])
    gain_blocks = small[:, 3 * per_group : 3 * per_group + 3 * width].reshape(dp_size, 3, width)
    gain_vals = jnp.swapaxes(gain_blocks, 0, 1).reshape(3, 1, D)
    count_all = jnp.sum(small[:, 2 * per_group : 3 * per_group])

    heads_own = wconv.shape[0]
    wide = qkv.shape[2]
    conv_rows_own = wconv.size // width
    low_qkv = qkv.astype(lowp)
    pack_one = jnp.concatenate(
        [
            jnp.swapaxes(low_qkv, 1, 2).reshape(3 * wide, width),
            wout.astype(lowp),
            wconv.astype(lowp).reshape(conv_rows_own, width),
        ]
    )
    own_one, steps_one = gather_blocks(after(pack_one, small_steps[0]), 1)
    conv_lanes = jnp.arange(DH, dtype=jnp.int32)
    conv_width = DH // dp_size
    conv_natural = (jnp.asarray(order, jnp.int32)[conv_lanes // conv_width] ^ d) * conv_width
    conv_natural = conv_natural + conv_lanes % conv_width
    conv_shuffle = (conv_natural[:, None] == conv_lanes[None, :]).astype(lowp)
    taps = heads_own * RATE * DH

    def conv_natural_order(rows):
        value = jnp.swapaxes(rows.reshape(conv_rows_own, dp_size, width), 0, 1)
        value = jnp.swapaxes(value.reshape(dp_size, taps, conv_width), 0, 1)
        moved = mm(value.reshape(taps, DH), conv_shuffle).astype(lowp)
        return moved.reshape(heads_own, RATE * DH, DH)

    def conv_block_order(value):
        moved = mm(value.astype(lowp).reshape(taps, DH), conv_shuffle, NT).astype(lowp)
        moved = jnp.swapaxes(moved.reshape(taps, dp_size, conv_width), 0, 1)
        moved = jnp.swapaxes(moved.reshape(dp_size, conv_rows_own, width), 0, 1)
        return moved.reshape(conv_rows_own, D)

    full_conv = conv_natural_order(own_one[4 * wide :])

    hidden_own = wup.shape[1]
    pack_two = jnp.concatenate([wup.astype(lowp).T, wdown.astype(lowp)])
    own_two, steps_two = gather_blocks(after(pack_two, steps_one[0]), 1)

    words = vocab // reach
    z = d // 2
    low_table = after(table.astype(lowp), steps_two[-2])
    near_table = []
    for m in order[:reach]:
        part = lax.dynamic_slice_in_dim(low_table, (z ^ (m // 2)) * words, words, 0)
        near_table.append(part if m == 0 else swap(part, "dp", m))
    near_table = jnp.concatenate(near_table, axis=1)
    far_table = swap(after(near_table, own_two), "dp", 1)
    slots = -(-words // 256) * 256

    own_half, far_half = split(table_rows_all, 0, 2)
    looked_far = swap(lookup(far_half, table), "head", 1)
    looked = (lookup(after(own_half, steps_one[0]), table) + looked_far).reshape(2, -1, width)
    looked = looked[0] + swap(looked[1], "head", 2)
    looked = lax.all_to_all(looked.reshape(dp_size, half, width), "dp", 0, 0)
    embedded_low, normed = place_embedding(place, after(looked, steps_two[0]), gain_vals[0])
    embedded = embedded_low.astype(single)

    mem_normed = state_norm(place, gain_vals[0], memory, 1)[0]
    old_normed = state_norm(after(place, steps_one[1]), gain_vals[0], old_states, RATE)
    comp_counts = jnp.where(x == 1, jnp.flip(comp_fill), comp_fill)
    mem_counts = jnp.where(x == 1, jnp.flip(mem_fill), mem_fill)
    info = jnp.stack([comp_counts[0], mem_counts[0], comp_counts[1], mem_counts[1], c * half])
    info = info.astype(jnp.int32)

    def core_sum(part):
        rows = part.shape[0] // 2
        more = swap(part[rows:].astype(lowp), "head", 1)
        return part[:rows].astype(single) + more.astype(single)

    def core_both(part):
        return jnp.concatenate([part, swap(part, "head", 1)], axis=0)

    def group_sum(part, beside=()):
        part = core_sum(part)
        rows = part.shape[0] // 2
        more = swap(part[rows:].astype(lowp), "head", 2)
        more, *beside = together(more, *beside)
        part = part[:rows] + more.astype(single)
        return (part, beside) if beside else part

    def group_both(part, beside=()):
        far, *beside = together(swap(part, "head", 2), *beside)
        both = core_both(jnp.concatenate([part, far], axis=0))
        return (both, beside) if beside else both

    normed = group_both(normed)
    in_weight = own_one[: 3 * wide]
    comp, old_raw = compress(old_normed, own_one, full_conv)
    mem = mm(mem_normed, own_one[wide : 3 * wide], NT).astype(lowp)
    seg = mm(normed, in_weight, NT).astype(lowp).reshape(2, streams, half, 3 * wide)
    mixed, lse = attend(info, after(seg, steps_two[1]), comp, mem)
    mixed = mixed.reshape(-1, wide)
    attn_sum, (full_up, full_down) = group_sum(
        mm(mixed, own_one[3 * wide : 4 * wide]), split(own_two, 0, 2)
    )
    after_attn = embedded + attn_sum
    ffn_in, inv_second = rms(after_attn, gain_vals[1])
    ffn_in, (near_table,) = group_both(ffn_in, (near_table,))
    hidden_pre = mm(ffn_in, full_up, NT)
    hidden_act = jax.nn.gelu(hidden_pre).astype(lowp)
    ffn_sum, (far_table,) = group_sum(mm(hidden_act, full_down), (far_table,))
    after_ffn = after_attn + ffn_sum
    loss_table = jnp.concatenate([near_table, far_table], axis=1)
    loss_table = jnp.concatenate([loss_table, jnp.zeros((slots - words, D), lowp)], axis=0)
    final_in, inv_third = rms(after_ffn, gain_vals[2])

    word_start = (h * vocab + z * words).astype(single)
    wanted_all = targets_all - word_start
    wanted_all = jnp.where((wanted_all >= 0) & (wanted_all < words), wanted_all, -1.0)
    info_all = jnp.stack([wanted_all, mask_all] + [jnp.zeros_like(mask_all)] * 6)
    info_all = jnp.transpose(info_all, (1, 0, 2, 3, 4)).reshape(reach, 8, per_group)
    pieces = [final_in]
    chunks = []
    raised = []
    stats = []

    def next_chunk():
        i = len(chunks)
        if i < 2:
            chunks.append(group_both(pieces[i]))
        else:
            chunk, (stats[i - 2],) = group_both(pieces[i], (stats[i - 2],))
            chunks.append(chunk)
        out, stat = logits_part(words, info_all[i], chunks[i], loss_table)
        raised.append(out)
        stats.append(stat)

    mask = dp_size // 2
    while mask > 1:
        joined = jnp.concatenate(pieces) if len(pieces) > 1 else pieces[0]
        moved = swap(reorder(joined, mask), "dp", mask)
        if len(pieces) == 1:
            next_chunk()
            moved, own_codes, own_count, early = together(
                moved, *own_list(after(token_codes, final_in)), early
            )
        elif len(pieces) == 2:
            moved, stats[0] = together(moved, stats[0])
        pieces += split(moved, 0, len(pieces))
        mask //= 2
    while len(chunks) < reach:
        next_chunk()
    stats = [stat[:3].reshape(3, 1, 2, 2, half) for stat in stats]
    own_stats = jnp.concatenate(stats, axis=1)

    def combine(first, second):
        top = jnp.maximum(first[0], second[0])
        total = first[1] * jnp.exp(first[0] - top) + second[1] * jnp.exp(second[0] - top)
        return jnp.stack([top, total, first[2] + second[2]])

    merged = own_stats
    merged = combine(merged, jnp.flip(swap(merged, "head", 1), 2))
    merged = combine(merged, jnp.flip(swap(merged, "head", 2), 3))
    mask = 2
    while mask < dp_size:
        other = split(swap(merged, "dp", mask), 1, reach)
        other = [other[order.index(j ^ mask)] for j in order[:reach]]
        merged = combine(merged, jnp.concatenate(other, axis=1))
        mask *= 2
    log_total = merged[0] + jnp.log(merged[1])
    loss_local = jnp.sum(mask_all[0, 0, 0] * (log_total[0, 0, 0] - merged[2, 0, 0, 0]))
    factor_all = jnp.exp(own_stats[0] - log_total)

    factor_all = factor_all.reshape(reach, 1, per_group) * info_all[:, 1:2]
    factor_all = jnp.broadcast_to(factor_all, info_all.shape)
    dlogits = [None] * reach
    parts = [None] * reach
    for i in reversed(range(reach)):
        factor = factor_all[i]
        if i + 2 < reach:
            factor = after(factor, parts[i + 2])
        dlogits[i], part = logits_back(info_all[i], factor, raised[i], loss_table)
        parts[i] = group_sum(part)
    table_parts = table_grad_part(dlogits, chunks)
    mask = 2
    while len(parts) > 1:
        count = len(parts) // 2
        moved = jnp.concatenate([part.astype(lowp) for part in parts[count:]])
        moved = swap(reorder(moved, mask), "dp", mask)
        if mask == 2:
            moved, *table_parts = together(moved, *table_parts)
        moved = split(moved.astype(single), 0, count)
        parts = [part + more for part, more in zip(parts, moved)]
        mask *= 2
    final_grad = parts[0]

    keep, send = table_parts
    moved_table = swap(send, "dp", 1)

    grad_after_ffn = rms_back(after_ffn, inv_third, gain_vals[2], final_grad)
    down_in = group_both(grad_after_ffn.astype(lowp))
    act_grad = mm(down_in, full_down, NT)
    pre_grad = jax.vjp(jax.nn.gelu, hidden_pre)[1](act_grad)[0].astype(lowp)
    two = hidden_grads(pre_grad, hidden_act, ffn_in, down_in)
    ffn_in_grad, (*two, moved_table) = group_sum(mm(pre_grad, full_up), (*two, moved_table))
    two_moved = swap(two[1], "dp", 1)
    keep = keep + moved_table.astype(single)
    table_pieces = split(keep[:words], 1, reach)
    for i in range(1, reach):
        table_pieces[i] = swap(table_pieces[i].astype(lowp), "dp", order[i])
    grad_after_attn = grad_after_ffn + rms_back(after_attn, inv_second, gain_vals[1], ffn_in_grad)
    attn_in = group_both(grad_after_attn.astype(lowp))

    mixed_grad = mm(attn_in, own_one[3 * wide : 4 * wide], NT).astype(lowp)
    mixed_grad = mixed_grad.reshape(2, streams, half, wide)
    seg_grad, comp_grad, mem_grad = attend_back(info, seg, comp, mem, lse, mixed_grad)
    seg_grad = seg_grad.reshape(-1, 3 * wide)
    seg_in = core_sum(mm(seg_grad, in_weight))
    seg_in_far = swap(seg_in[half:].astype(lowp), "head", 2)
    seg_in_far, two_moved, *table_pieces = together(seg_in_far, two_moved, *table_pieces)
    table_base = jnp.zeros((vocab, width), single)
    for m, part in zip(order[:reach], table_pieces):
        part = part.astype(single)
        table_base = lax.dynamic_update_slice_in_dim(table_base, part, (z ^ (m // 2)) * words, 0)
    rows_grad = embed_back(
        place,
        embedded_low,
        gain_vals[0],
        seg_in[:half],
        seg_in_far,
        grad_after_attn,
    )
    rows_grad = lax.all_to_all(rows_grad, "dp", 0, 0)
    rows_grad = jnp.stack([rows_grad, swap(rows_grad, "head", 2)])
    rows_grad = jnp.stack([rows_grad, swap(rows_grad, "head", 1)]).reshape(-1, width)

    two = two[0] + two_moved.astype(single)
    two = reduce_blocks(*split(two, 1, 2), 2)
    up_grad = two[:hidden_own].T
    down_grad = two[hidden_own:]
    old_grad, conv_sum = expand(comp_grad, old_raw, full_conv)
    one = attn_grads(
        seg_grad,
        mixed,
        mem_grad,
        old_grad.reshape(-1, old_grad.shape[-1]),
        normed,
        attn_in,
        mem_normed,
        old_normed.reshape(-1, D),
    )
    conv_sum = split(conv_block_order(conv_sum), 1, 2)
    one = [jnp.concatenate([part, more.astype(part.dtype)]) for part, more in zip(one, conv_sum)]
    one = reduce_blocks(*one)
    qkv_grad = jnp.swapaxes(one[: 3 * wide].reshape(3, wide, width), 1, 2)
    out_grad = one[3 * wide : 4 * wide]
    conv_grad = one[4 * wide :].reshape(wconv.shape)
    table_grad = scatter(bits, own_count, own_codes, table_base, rows_grad)

    gains_low = gains.astype(lowp).astype(single)
    gain_part = jnp.stack(
        [
            jnp.sum(low_qkv.astype(single) * qkv_grad, axis=(0, 2)),
            jnp.sum(wup.astype(lowp).astype(single) * up_grad, axis=1),
            jnp.sum(table.astype(lowp).astype(single) * table_base, axis=0),
        ]
    )

    grads = (table_grad, qkv_grad, out_grad, conv_grad, up_grad, down_grad)
    def sum_over_dp(joined):
        mask = 1
        while mask < dp_size:
            joined = joined + swap(joined, "dp", mask)
            mask *= 2
        return joined

    row_part = []
    col_part = []
    for grad in grads:
        square = grad * grad
        row_part.append(jnp.sum(square, axis=-1))
        col_part.append(jnp.sum(square, axis=tuple(range(square.ndim - 1))))
    row_q, row_u, col_e, col_o, col_c, col_d, gain_raw, early = lax.psum(
        (
            row_part[1],
            row_part[4],
            col_part[0],
            col_part[2],
            col_part[3],
            col_part[5],
            gain_part,
            early + scalar_row([0.0] * 15 + [loss_local]),
        ),
        "head",
    )
    lanes = [col_e, jnp.sum(row_q, axis=0), col_o]
    lanes += [jnp.concatenate([col_c, jnp.zeros((width - col_c.shape[0],), single)]), row_u, col_d]
    members = [col_part[4], row_part[5], row_part[3], row_part[2], col_part[1], *lanes, row_part[0], early]
    joined = jnp.concatenate([m.reshape(-1) for m in members])
    joined = sum_over_dp(jnp.concatenate([joined, jnp.zeros((-joined.shape[0] % 1024,), single)]))
    sums = []
    start = 0
    for member in members:
        sums.append(joined[start : start + member.size].reshape(member.shape))
        start += member.size
    col_u, row_d, row_c, row_o, col_q, *lanes, row_e, early = sums
    square_total = [jnp.sum(lane) for lane in lanes]
    row_sums = [row_e, row_q, row_o, row_c, row_u, row_d]
    col_sums = [col_e, col_q, col_o, col_c, col_u, col_d]
    weight_total = early[6:15]
    loss_all = early[15]
    inverse = 1.0 / count_all
    decay = 1.0 - STEP ** (-0.8)
    updates = []
    stats_new = []
    scaled = []
    counts = []
    update_sq = []
    for index in range(6):
        rows_total = rows_old[index].size * sizes[row_axes[index]]
        cols_total = cols_old[index].size * sizes[col_axes[index]]
        grad_scaled = grads[index] * inverse
        rows_new = decay * rows_old[index] + (1.0 - decay) * (
            row_sums[index] * inverse * inverse / cols_total + TINY_SQUARE
        )
        cols_new = decay * cols_old[index] + (1.0 - decay) * (
            col_sums[index] * inverse * inverse / rows_total + TINY_SQUARE
        )
        mean_row = decay * early[index] / rows_total + (1.0 - decay) * (
            square_total[index] * inverse * inverse / (rows_total * cols_total) + TINY_SQUARE
        )
        second = rows_new[..., None] * cols_new / mean_row
        direction = grad_scaled * lax.rsqrt(second)
        updates.append(direction)
        stats_new.append((rows_new, cols_new))
        scaled.append(grad_scaled)
        counts.append(rows_total * cols_total)
        update_sq.append(jnp.sum(direction * direction))
    gain_scaled = gain_raw / gains_low * inverse
    second_new = decay * gains_second + (1.0 - decay) * (gain_scaled * gain_scaled + TINY_SQUARE)
    gain_dir = gain_scaled * lax.rsqrt(second_new)
    for which in range(3):
        update_sq.append(jnp.sum(gain_dir[which] * gain_dir[which]) / head_size)
    update_total = scalar_row(update_sq, 1024)
    for mask in (1, 2):
        update_total = update_total + swap(update_total, "head", mask)
    update_total = sum_over_dp(update_total)[:9]
    results = [loss_all, count_all]
    for index in range(6):
        factor = jnp.maximum(0.001, jnp.sqrt(weight_total[index] / counts[index]))
        denom = jnp.maximum(1.0, jnp.sqrt(update_total[index] / counts[index]) / CLIP_LEVEL)
        new_weight = weights_now[index] - LEARN_RATE * factor * updates[index] / denom
        results += [new_weight, scaled[index], stats_new[index][0], stats_new[index][1]]
    gain_factor = jnp.maximum(0.001, jnp.sqrt(weight_total[6:] / D))[:, None]
    gain_denom = jnp.maximum(1.0, jnp.sqrt(update_total[6:] / D) / CLIP_LEVEL)[:, None]
    results += [gains - LEARN_RATE * gain_factor * gain_dir / gain_denom, gain_scaled, second_new]
    return tuple(results)


def solution(mesh):
    in_specs = (
        P("dp", None),
        P("dp", None),
        P("dp", None),
        P("dp", None, None),
        P("dp", None, None),
        P("dp"),
        P("dp"),
        P("head", "dp"),
        P(None, "dp", "head"),
        P("head", "dp"),
        P("head", None, "dp"),
        P("dp", "head"),
        P("head", "dp"),
        P(None, "dp"),
        P("head"),
        P("dp"),
        P(None, "dp"),
        P("head"),
        P("head"),
        P("dp"),
        P("head", None),
        P("dp"),
        P("dp"),
        P("head"),
        P("head"),
        P("dp"),
        P(None, "dp"),
    )
    out_specs = (
        P(),
        P(),
        P("head", "dp"),
        P("head", "dp"),
        P("head"),
        P("dp"),
        P(None, "dp", "head"),
        P(None, "dp", "head"),
        P(None, "dp"),
        P("head"),
        P("head", "dp"),
        P("head", "dp"),
        P("head"),
        P("dp"),
        P("head", None, "dp"),
        P("head", None, "dp"),
        P("head", None),
        P("dp"),
        P("dp", "head"),
        P("dp", "head"),
        P("dp"),
        P("head"),
        P("head", "dp"),
        P("head", "dp"),
        P("head"),
        P("dp"),
        P(None, "dp"),
        P(None, "dp"),
        P(None, "dp"),
    )
    return jax.shard_map(local, mesh=mesh, in_specs=in_specs, out_specs=out_specs, check_vma=False)
```

```python
import functools

import jax
import jax.numpy as jnp
from jax import lax
from jax.experimental import pallas as pl
from jax.experimental.pallas import tpu as pltpu
from jax.sharding import PartitionSpec as P

D = 1024
H = 8
DH = 128
MEM = 512
CMEM = 512
RATE = 3
STEP = 10


TINY_NORM = 1e-06
TINY_SQUARE = 1e-30
LEARN_RATE = 0.5
CLIP_LEVEL = 1.0

lowp = jnp.bfloat16
single = jnp.float32
NT = (((1,), (1,)), ((), ()))
TN = (((0,), (0,)), ((), ()))
NN = (((1,), (0,)), ((), ()))
MIB = 1024 * 1024


def mm(left, right, dims=NN):
    return lax.dot_general(left, right, dims, preferred_element_type=single)


def swap(value, axis, mask):
    size = lax.axis_size(axis)
    return lax.ppermute(value, axis, [(i, i ^ mask) for i in range(size)])


def after(value, *deps):
    return lax.optimization_barrier((value, *deps))[0]


def together(*values):
    return lax.optimization_barrier(values)


def block_order(size):
    order = [0]
    step = size // 2
    while step:
        order = order + [j + step for j in order]
        step //= 2
    return order


def gather_blocks(piece, axis, beside=()):
    steps = []
    mask = lax.axis_size("dp") // 2
    while mask:
        moved = swap(piece, "dp", mask)
        if not steps and beside:
            moved, *beside = together(moved, *beside)
        piece = jnp.concatenate([piece, moved], axis=axis)
        steps.append(piece)
        mask //= 2
    return piece, steps, beside


def split(value, axis, parts):
    width = value.shape[axis] // parts
    return [lax.slice_in_dim(value, i * width, (i + 1) * width, axis=axis) for i in range(parts)]


def reduce_blocks(keep, send, mask=1):
    total = keep + swap(send.astype(lowp), "dp", mask).astype(single)
    mask *= 2
    if mask == lax.axis_size("dp"):
        return total
    return reduce_blocks(*split(total, 1, 2), mask)


def reorder(value, mask):
    order = block_order(lax.axis_size("dp"))
    cols = split(value, 1, len(order))
    return jnp.concatenate([cols[order.index(j ^ mask)] for j in order], axis=1)


def relative(value, x, c):
    value = jnp.where(x == 1, jnp.flip(value, -3), value)
    value = jnp.where(c == 1, jnp.flip(value, -2), value)
    return jnp.swapaxes(value, -3, -2)


def rms(values, gain):
    inv = lax.rsqrt(jnp.mean(values * values, axis=-1, keepdims=True) + TINY_NORM)
    return (values * inv * gain).astype(lowp), inv


def rms_back(values, inv, gain, upstream):
    scaled = gain * upstream
    inner = jnp.sum(scaled * values, axis=-1, keepdims=True) / D
    return scaled * inv - values * (inner * inv * inv * inv)


def vmem(shape=None, index=None):
    if shape is None:
        return pl.BlockSpec(memory_space=pltpu.VMEM)
    return pl.BlockSpec(shape, index)


def smem():
    return pl.BlockSpec(memory_space=pltpu.SMEM)


def params(mib):
    return pltpu.CompilerParams(vmem_limit_bytes=mib * MIB)


def cost(flops, size, exps=0):
    return pl.CostEstimate(
        flops=int(0.02 * flops), bytes_accessed=int(0.02 * size), transcendentals=exps
    )


def lookup_kernel(row_ref, table_ref, out_ref, tab, held, sem):
    total = row_ref.shape[0]
    vocab = table_ref.shape[0]
    copy = pltpu.make_async_copy(table_ref, tab.at[pl.ds(0, vocab)], sem)
    copy.start()
    tab[pl.ds(vocab, 8), :] = jnp.zeros((8, tab.shape[1]), single)
    copy.wait()

    @pl.loop(0, total // 16)
    def _(g):
        for j in range(16):
            t = g * 16 + j
            held[pl.ds(t, 1), :] = tab[pl.ds(row_ref[t], 1), :]

    @pl.loop(0, total // 512)
    def _(i):
        rows = pl.ds(pl.multiple_of(i * 512, 512), 512)
        out_ref[rows, :] = held[rows, :].astype(lowp)


def lookup(rows, table):
    total = rows.shape[0]
    vocab, width = table.shape
    return pl.pallas_call(
        lookup_kernel,
        name="lookup",
        out_shape=jax.ShapeDtypeStruct((total, width), lowp),
        in_specs=[smem(), pl.BlockSpec(memory_space=pl.ANY)],
        out_specs=vmem(),
        scratch_shapes=[
            pltpu.VMEM((vocab + 8, width), single),
            pltpu.VMEM((total, width), single),
            pltpu.SemaphoreType.DMA(()),
        ],
        compiler_params=params(60),
        cost_estimate=cost(0, 30 * MIB),
    )(rows, table)


def list_kernel(code_ref, out_ref, count_ref):
    total = code_ref.shape[0]

    def group(g, count):
        for j in range(16):
            code = code_ref[g * 16 + j]
            out_ref[count] = code
            count = count + jnp.where(code >= 0, 1, 0)
        return count

    count_ref[0] = lax.fori_loop(0, total // 16, group, jnp.int32(0))


def own_list(codes):
    total = codes.shape[0]
    return pl.pallas_call(
        list_kernel,
        name="own_list",
        out_shape=(
            jax.ShapeDtypeStruct((total + 8,), jnp.int32),
            jax.ShapeDtypeStruct((1,), jnp.int32),
        ),
        in_specs=[smem()],
        out_specs=(smem(), smem()),
        cost_estimate=cost(0, 60 * MIB),
    )(codes)


def place_kernel(order, place_ref, in_ref, gain_ref, out_ref, norm_ref, held):
    width = in_ref.shape[2]
    for p, j in enumerate(order):
        block = in_ref[pl.ds(place_ref[1] ^ j, 1)][0]
        out_ref[:, p * width : (p + 1) * width] = block
        held[:, p * width : (p + 1) * width] = block.astype(single)
    values = held[...]
    inv = lax.rsqrt(jnp.mean(values * values, axis=-1, keepdims=True) + TINY_NORM)
    norm_ref[...] = (values * inv * gain_ref[...]).astype(lowp)


def place_embedding(place, blocks, gain):
    rows = blocks.shape[1]
    return pl.pallas_call(
        functools.partial(place_kernel, block_order(blocks.shape[0])),
        name="place_embedding",
        out_shape=(jax.ShapeDtypeStruct((rows, D), lowp), jax.ShapeDtypeStruct((rows, D), lowp)),
        in_specs=[smem(), vmem(), vmem()],
        out_specs=(vmem(), vmem()),
        scratch_shapes=[pltpu.VMEM((rows, D), single)],
        compiler_params=params(60),
        cost_estimate=cost(0, 3 * MIB),
    )(place, blocks, gain)


def embed_back_kernel(order, place_ref, in_ref, gain_ref, keep_ref, more_ref, grad_ref, out_ref, held):
    values = in_ref[...].astype(single)
    inv = lax.rsqrt(jnp.mean(values * values, axis=-1, keepdims=True) + TINY_NORM)
    upstream = keep_ref[...] + more_ref[...].astype(single)
    held[...] = grad_ref[...] + rms_back(values, inv, gain_ref[...], upstream)
    width = out_ref.shape[2]
    for p, j in enumerate(order):
        block = held[:, p * width : (p + 1) * width].astype(lowp)
        out_ref[pl.ds(place_ref[1] ^ j, 1)] = block[None]


def embed_back(place, values, gain, keep, more, grad):
    rows = values.shape[0]
    size = lax.axis_size("dp")
    return pl.pallas_call(
        functools.partial(embed_back_kernel, block_order(size)),
        name="embed_back",
        out_shape=jax.ShapeDtypeStruct((size, rows, D // size), lowp),
        in_specs=[smem()] + [vmem()] * 5,
        out_specs=vmem(),
        scratch_shapes=[pltpu.VMEM((rows, D), single)],
        compiler_params=params(60),
        cost_estimate=cost(0, 4 * MIB),
    )(place, values, gain, keep, more, grad)


def scatter_kernel(bits, count_ref, code_ref, base_ref, grad_ref, out_ref, rows):
    total = grad_ref.shape[0]
    vocab = base_ref.shape[0]

    @pl.loop(0, total // 512)
    def _(i):
        here = pl.ds(pl.multiple_of(i * 512, 512), 512)
        rows[here, :] = grad_ref[here, :].astype(single)

    rows[pl.ds(total, 8), :] = jnp.zeros((8, rows.shape[1]), single)

    @pl.loop(0, vocab // 400)
    def _(i):
        here = pl.ds(pl.multiple_of(i * 400, 400), 400)
        out_ref[here, :] = base_ref[here, :]

    count = count_ref[0]

    def group(g, carry):
        for j in range(8):
            index = g * 8 + j
            code = jnp.where(index < count, code_ref[index], total << bits)
            token = lax.shift_right_logical(code, bits)
            row = code & ((1 << bits) - 1)
            out_ref[pl.ds(row, 1), :] = out_ref[pl.ds(row, 1), :] + rows[pl.ds(token, 1), :]
        return carry

    lax.fori_loop(0, (count + 7) // 8, group, jnp.int32(0))


def scatter(bits, count, codes, base, grad):
    total, width = grad.shape
    return pl.pallas_call(
        functools.partial(scatter_kernel, bits),
        name="scatter",
        out_shape=jax.ShapeDtypeStruct(base.shape, single),
        in_specs=[smem(), smem(), vmem(), vmem()],
        out_specs=vmem(),
        scratch_shapes=[pltpu.VMEM((total + 8, width), single)],
        compiler_params=params(60),
        cost_estimate=cost(0, 30 * MIB),
    )(count, codes, base, grad)


def state_kernel(order, width, place_ref, gain_ref, in_ref, out_ref, held):
    rows = in_ref.shape[1]
    values = in_ref[0].astype(single)
    inv = lax.rsqrt(jnp.mean(values * values, axis=-1, keepdims=True) + TINY_NORM)
    for p, j in enumerate(order):
        start = pl.multiple_of((place_ref[1] ^ j) * width, width)
        block = in_ref[0, :, pl.ds(start, width)].astype(single)
        held[p] = block * inv * gain_ref[:, p * width : (p + 1) * width]
    groups = out_ref.shape[0]
    for p in range(len(order)):
        cols = slice(p * width, (p + 1) * width)
        if groups == 1:
            out_ref[0, :, cols] = held[p].astype(lowp)
        else:
            for j in range(groups):
                part = held[p, pl.ds(j, rows // groups, stride=groups), :]
                out_ref[j, :, cols] = part.astype(lowp)


def state_norm(place, gain, states, groups):
    size = lax.axis_size("dp")
    order = block_order(size)
    width = D // size
    streams = states.shape[0]
    count = states.shape[1] // groups
    if width % 128:
        values = jnp.where(place[0] == 1, jnp.flip(states, 0), states).astype(single).reshape(-1, D)
        inv = lax.rsqrt(jnp.mean(values * values, axis=-1, keepdims=True) + TINY_NORM)
        lanes = jnp.arange(D, dtype=jnp.int32)
        blocks = jnp.asarray(order, jnp.int32)[lanes // width] ^ place[1]
        source = blocks * width + lanes % width
        shuffle = (lanes[:, None] == source[None, :]).astype(single)
        moved = jnp.dot(values * inv, shuffle, precision=lax.Precision.HIGHEST)
        out = (moved * gain).astype(lowp)
        return jnp.swapaxes(out.reshape(streams * count, groups, D), 0, 1)
    tile = 128
    return pl.pallas_call(
        functools.partial(state_kernel, order, width),
        name="state_norm",
        out_shape=jax.ShapeDtypeStruct((groups, streams * count, D), lowp),
        grid_spec=pltpu.PrefetchScalarGridSpec(
            num_scalar_prefetch=1,
            grid=(streams, count // tile),
            in_specs=[
                pl.BlockSpec((1, D), lambda n, i, s: (0, 0)),
                pl.BlockSpec((1, tile * groups, D), lambda n, i, s: (s[0] ^ n, i, 0)),
            ],
            out_specs=pl.BlockSpec(
                (groups, tile, D), lambda n, i, s: (0, n * (count // tile) + i, 0)
            ),
            scratch_shapes=[pltpu.VMEM((len(order), tile * groups, width), single)],
        ),
        compiler_params=params(60),
        cost_estimate=cost(0, 4 * streams * count * groups * D),
    )(place, gain, states)


def compress_kernel(old_ref, key_ref, value_ref, conv_ref, comp_ref, raw_ref):
    heads = conv_ref.shape[0]
    wide = heads * DH
    for part, weight_ref in enumerate((key_ref, value_ref)):
        sums = [None] * heads
        for j in range(RATE):
            raw = mm(old_ref[j], weight_ref[...], NT).astype(lowp)
            raw_ref[j, :, part * wide : (part + 1) * wide] = raw
            for n in range(heads):
                piece = raw[:, n * DH : (n + 1) * DH]
                term = mm(piece, conv_ref[n, j * DH : (j + 1) * DH, :])
                sums[n] = term if j == 0 else sums[n] + term
        for n in range(heads):
            first = part * wide + n * DH
            comp_ref[:, first : first + DH] = sums[n].astype(lowp)


def compress(old3, weights, conv):
    rows = old3.shape[1]
    wide = conv.shape[0] * DH
    tile = 256
    return pl.pallas_call(
        compress_kernel,
        name="compress",
        grid=(rows // tile,),
        out_shape=(
            jax.ShapeDtypeStruct((rows, 2 * wide), lowp),
            jax.ShapeDtypeStruct((RATE, rows, 2 * wide), lowp),
        ),
        in_specs=[
            pl.BlockSpec((RATE, tile, D), lambda i: (0, i, 0)),
            pl.BlockSpec((wide, D), lambda i: (1, 0)),
            pl.BlockSpec((wide, D), lambda i: (2, 0)),
            pl.BlockSpec(conv.shape, lambda i: (0, 0, 0)),
        ],
        out_specs=(
            pl.BlockSpec((tile, 2 * wide), lambda i: (i, 0)),
            pl.BlockSpec((RATE, tile, 2 * wide), lambda i: (0, i, 0)),
        ),
        compiler_params=params(60),
        cost_estimate=cost(4 * RATE * rows * wide * D, 12 * MIB),
    )(old3, weights, weights, conv)


def expand_kernel(grad_ref, raw_ref, conv_ref, out_ref, conv_out_ref):
    heads = conv_ref.shape[0]
    for h in range(heads):
        for j in range(RATE):
            rows = slice(j * DH, (j + 1) * DH)
            taps = conv_ref[h, rows, :]
            total = None
            for n in (h, heads + h):
                cols = slice(n * DH, (n + 1) * DH)
                grad = grad_ref[:, cols]
                out_ref[j, :, cols] = mm(grad, taps, NT).astype(lowp)
                term = mm(raw_ref[j, :, cols], grad, TN)
                total = term if total is None else total + term
            conv_out_ref[h, rows, :] = total


def expand(grad, raw, conv):
    return pl.pallas_call(
        expand_kernel,
        name="expand",
        out_shape=(
            jax.ShapeDtypeStruct(raw.shape, lowp),
            jax.ShapeDtypeStruct(conv.shape, single),
        ),
        in_specs=[vmem()] * 3,
        out_specs=(vmem(), vmem()),
        compiler_params=params(60),
        cost_estimate=cost(2000 * MIB, 12 * MIB),
    )(grad, raw, conv)


def masked_scores(info_ref, query, keys):
    rows = query.shape[0]
    scale = DH ** (-0.5)
    result = []
    for which, key in enumerate(keys):
        slots = key.shape[0]
        col = lax.broadcasted_iota(jnp.int32, (rows, slots), 1)
        if which < 2:
            seen = col >= slots - info_ref[2 * pl.program_id(0) + which]
        else:
            row = lax.broadcasted_iota(jnp.int32, (rows, slots), 0)
            shift = info_ref[4]
            row = row + shift
            col = col + shift
            row = jnp.where(row >= slots, row - slots, row)
            col = jnp.where(col >= slots, col - slots, col)
            seen = col <= row
        result.append(jnp.where(seen, mm(query, key, NT) * scale, -1e30))
    return result


def rows_of(ref):
    return ref[...].reshape(-1, ref.shape[-1])


def attend_kernel(info_ref, q_ref, ks_ref, vs_ref, kc_ref, vc_ref, km_ref, vm_ref, out_ref, lse_ref):
    query = rows_of(q_ref)
    scores = masked_scores(info_ref, query, [kc_ref[...], km_ref[...], rows_of(ks_ref)])
    top = functools.reduce(jnp.maximum, [jnp.max(s, axis=-1, keepdims=True) for s in scores])
    total = 0.0
    mixed = 0.0
    for score, value in zip(scores, (vc_ref[...], vm_ref[...], rows_of(vs_ref))):
        weight = jnp.exp(score - top)
        total = total + jnp.sum(weight, axis=-1, keepdims=True)
        mixed = mixed + mm(weight.astype(lowp), value)
    out_ref[...] = (mixed / total).astype(lowp).reshape(out_ref.shape)
    lse_ref[0, 0] = top + jnp.log(total)


def attend_back_kernel(
    info_ref, q_ref, ks_ref, vs_ref, kc_ref, vc_ref, km_ref, vm_ref, lse_ref, up_ref,
    seg_ref, comp_ref, mem_ref,
):
    head = pl.program_id(1)
    wide = pl.num_programs(1) * DH
    scale = DH ** (-0.5)
    query = rows_of(q_ref)
    upstream = rows_of(up_ref)
    keys = [kc_ref[...], km_ref[...], rows_of(ks_ref)]
    scores = masked_scores(info_ref, query, keys)
    probs = [jnp.exp(s - lse_ref[0, 0]) for s in scores]
    prob_grads = [
        mm(upstream, v, NT) for v in (vc_ref[...], vm_ref[...], rows_of(vs_ref))
    ]
    inner = 0.0
    for p, g in zip(probs, prob_grads):
        inner = inner + jnp.sum(p * g, axis=-1, keepdims=True)
    here = pl.ds(pl.multiple_of(head * DH, DH), DH)
    second = pl.ds(pl.multiple_of(wide + head * DH, DH), DH)
    third = pl.ds(pl.multiple_of(2 * wide + head * DH, DH), DH)
    query_grad = 0.0
    places = ((comp_ref, here, second), (mem_ref, here, second), (seg_ref, second, third))
    for p, g, key, (ref, key_at, value_at) in zip(probs, prob_grads, keys, places):
        score_grad = (p * (g - inner)).astype(lowp)
        query_grad = query_grad + mm(score_grad, key)
        shape = ref.shape[:-1] + (DH,)
        key_grad = (mm(score_grad, query, TN) * scale).astype(lowp)
        value_grad = mm(p.astype(lowp), upstream, TN).astype(lowp)
        ref[..., key_at] = key_grad.reshape(shape)
        ref[..., value_at] = value_grad.reshape(shape)
    shape = seg_ref.shape[:-1] + (DH,)
    seg_ref[..., here] = (query_grad * scale).astype(lowp).reshape(shape)


def head_specs(seg, comp, mem, heads):
    streams = seg.shape[1]

    def of_seg(first):
        return pl.BlockSpec((2, 1, seg.shape[2], DH), lambda n, h: (0, n, 0, first + h))

    def cols(array, first):
        return pl.BlockSpec((array.shape[0] // streams, DH), lambda n, h: (n, first + h))

    return [
        smem(),
        of_seg(0),
        of_seg(heads),
        of_seg(2 * heads),
        cols(comp, 0),
        cols(comp, heads),
        cols(mem, 0),
        cols(mem, heads),
    ]


def attend(info, seg, comp, mem):
    _, streams, half, _ = seg.shape
    heads = comp.shape[1] // (2 * DH)
    return pl.pallas_call(
        attend_kernel,
        name="attend",
        grid=(streams, heads),
        out_shape=(
            jax.ShapeDtypeStruct((2, streams, half, heads * DH), lowp),
            jax.ShapeDtypeStruct((streams, heads, 2 * half, 1), single),
        ),
        in_specs=head_specs(seg, comp, mem, heads),
        out_specs=(
            pl.BlockSpec((2, 1, half, DH), lambda n, h: (0, n, 0, h)),
            pl.BlockSpec((1, 1, 2 * half, 1), lambda n, h: (n, h, 0, 0)),
        ),
        compiler_params=params(60),
        cost_estimate=cost(7000 * MIB, 6 * MIB),
    )(info, seg, seg, seg, comp, comp, mem, mem)


def attend_back(info, seg, comp, mem, lse, upstream):
    _, streams, half, wide = seg.shape
    heads = comp.shape[1] // (2 * DH)
    slots = comp.shape[0] // streams
    kept = mem.shape[0] // streams
    return pl.pallas_call(
        attend_back_kernel,
        name="attend_back",
        grid=(streams, heads),
        out_shape=(
            jax.ShapeDtypeStruct(seg.shape, lowp),
            jax.ShapeDtypeStruct(comp.shape, lowp),
            jax.ShapeDtypeStruct(mem.shape, lowp),
        ),
        in_specs=head_specs(seg, comp, mem, heads)
        + [
            pl.BlockSpec((1, 1, 2 * half, 1), lambda n, h: (n, h, 0, 0)),
            pl.BlockSpec((2, 1, half, DH), lambda n, h: (0, n, 0, h)),
        ],
        out_specs=(
            pl.BlockSpec((2, 1, half, wide), lambda n, h: (0, n, 0, 0)),
            pl.BlockSpec((slots, comp.shape[1]), lambda n, h: (n, 0)),
            pl.BlockSpec((kept, mem.shape[1]), lambda n, h: (n, 0)),
        ),
        compiler_params=params(60),
        cost_estimate=cost(11000 * MIB, 9 * MIB),
    )(info, seg, seg, seg, comp, comp, mem, mem, lse, upstream)


def columns_of(rows):
    tall = jnp.concatenate([rows, jnp.zeros((120, rows.shape[1]), single)], axis=0)
    return jnp.transpose(tall)


def logits_kernel(words, tiles, info_ref, pair_ref, near_ref, table_ref, out_ref, stat_ref, held):
    step = pl.program_id(0)

    @pl.when(step < tiles)
    def _():
        held[...] = pair_ref[...]

    @pl.when(step >= tiles)
    def _():
        held[...] = near_ref[...]

    logits = mm(held[...], table_ref[...], NT)
    wanted = columns_of(info_ref[...])[:, 0:1].astype(jnp.int32)
    col = lax.broadcasted_iota(jnp.int32, logits.shape, 1)
    hit = jnp.sum(jnp.where(col == wanted, logits, 0.0), axis=-1, keepdims=True)
    logits = jnp.where(col < words, logits, -1e30)
    top = jnp.max(logits, axis=-1, keepdims=True)
    raised = jnp.exp(logits - top)
    total = jnp.sum(raised, axis=-1, keepdims=True)
    out_ref[...] = raised.astype(lowp)
    lane = lax.broadcasted_iota(jnp.int32, (logits.shape[0], 128), 1)
    packed = jnp.where(lane == 0, top, jnp.where(lane == 1, total, jnp.where(lane == 2, hit, 0.0)))
    stat_ref[...] = jnp.transpose(packed)[:8]


def logits_part(words, info, pair, near, table):
    rows = pair.shape[0] + near.shape[0]
    slots = table.shape[0]
    tile = 256
    tiles = pair.shape[0] // tile
    return pl.pallas_call(
        functools.partial(logits_kernel, words, tiles),
        name="logits_part",
        grid=(2 * tiles,),
        out_shape=(
            jax.ShapeDtypeStruct((rows, slots), lowp),
            jax.ShapeDtypeStruct((8, rows), single),
        ),
        in_specs=[
            pl.BlockSpec((8, tile), lambda i: (0, i)),
            pl.BlockSpec((tile, D), lambda i: (jnp.minimum(i, tiles - 1), 0)),
            pl.BlockSpec((tile, D), lambda i: (jnp.maximum(i - tiles, 0), 0)),
            pl.BlockSpec(table.shape, lambda i: (0, 0)),
        ],
        out_specs=(
            pl.BlockSpec((tile, slots), lambda i: (i, 0)),
            pl.BlockSpec((8, tile), lambda i: (0, i)),
        ),
        scratch_shapes=[pltpu.VMEM((tile, D), lowp)],
        compiler_params=params(60),
        cost_estimate=cost(4 * rows * slots * D, 10 * MIB),
    )(info, pair, near, table)


def logits_back_kernel(tiles, info_ref, factor_ref, in_ref, table_ref, out_ref, keep_ref, send_ref):
    step = pl.program_id(0)
    info = columns_of(info_ref[...])
    wanted = info[:, 0:1].astype(jnp.int32)
    counted = info[:, 1:2]
    factor = columns_of(factor_ref[...])[:, 0:1]
    raised = in_ref[...].astype(single)
    col = lax.broadcasted_iota(jnp.int32, raised.shape, 1)
    grads = (raised * factor - jnp.where(col == wanted, counted, 0.0)).astype(lowp)
    out_ref[...] = grads
    total = mm(grads, table_ref[...]).astype(lowp)

    @pl.when(step < tiles)
    def _():
        send_ref[...] = total

    @pl.when(step >= tiles)
    def _():
        keep_ref[...] = total


def logits_back(info, factor, raised, table):
    rows, slots = raised.shape
    tile = 256
    tiles = rows // (2 * tile)

    def at(i):
        return (i + tiles) % (2 * tiles)

    return pl.pallas_call(
        functools.partial(logits_back_kernel, tiles),
        name="logits_back",
        grid=(2 * tiles,),
        out_shape=(
            jax.ShapeDtypeStruct((rows, slots), lowp),
            jax.ShapeDtypeStruct((rows // 2, D), lowp),
            jax.ShapeDtypeStruct((rows // 2, D), lowp),
        ),
        in_specs=[
            pl.BlockSpec((8, tile), lambda i: (0, at(i))),
            pl.BlockSpec((8, tile), lambda i: (0, at(i))),
            pl.BlockSpec((tile, slots), lambda i: (at(i), 0)),
            pl.BlockSpec(table.shape, lambda i: (0, 0)),
        ],
        out_specs=(
            pl.BlockSpec((tile, slots), lambda i: (at(i), 0)),
            pl.BlockSpec((tile, D), lambda i: (jnp.maximum(i - tiles, 0), 0)),
            pl.BlockSpec((tile, D), lambda i: (jnp.minimum(i, tiles - 1), 0)),
        ),
        compiler_params=params(60),
        cost_estimate=cost(4 * rows * slots * D, 12 * MIB),
    )(info, factor, raised, table)


def halves(total, keep_ref, send_ref):
    half = keep_ref.shape[1]
    keep_ref[...] = total[:, :half]
    send_ref[...] = total[:, half:].astype(send_ref.dtype)


def table_grad_kernel(count, *refs):
    total = None
    for i in range(count):
        rows = refs[count + 2 * i].shape[0]
        for j in range(2):
            term = mm(refs[i][j * rows : (j + 1) * rows, :], refs[count + 2 * i + j][...], TN)
            total = term if total is None else total + term
    halves(total, *refs[3 * count :])


def table_grad_part(grads, inputs):
    count = len(grads)
    rows = sum(g.shape[0] for g in grads)
    slots = grads[0].shape[1]
    block = 256
    if rows > 4096:
        total = sum(mm(g, jnp.concatenate(v), TN) for g, v in zip(grads, inputs))
        keep, send = split(total, 1, 2)
        return keep, send.astype(lowp)
    inputs = [part for pair in inputs for part in pair]
    return pl.pallas_call(
        functools.partial(table_grad_kernel, count),
        name="table_grad_part",
        grid=(slots // block,),
        out_shape=(
            jax.ShapeDtypeStruct((slots, D // 2), single),
            jax.ShapeDtypeStruct((slots, D // 2), lowp),
        ),
        in_specs=[pl.BlockSpec((g.shape[0], block), lambda i: (0, i)) for g in grads]
        + [pl.BlockSpec(v.shape, lambda i: (0, 0)) for v in inputs],
        out_specs=(
            pl.BlockSpec((block, D // 2), lambda i: (i, 0)),
            pl.BlockSpec((block, D // 2), lambda i: (i, 0)),
        ),
        compiler_params=params(60),
        cost_estimate=cost(3 * rows * slots * D, 30 * MIB),
    )(*grads, *inputs)


def hidden_grad_kernel(blocks, pre_ref, act_ref, in_ref, down_ref, keep_ref, send_ref):
    step = pl.program_id(0)

    @pl.when(step < blocks)
    def _():
        halves(mm(pre_ref[...], in_ref[...], TN), keep_ref, send_ref)

    @pl.when(step >= blocks)
    def _():
        halves(mm(act_ref[...], down_ref[...], TN), keep_ref, send_ref)


def hidden_grads(pre_grad, hidden_act, ffn_in, down_in):
    rows, hidden = pre_grad.shape
    block = 256
    blocks = hidden // block
    return pl.pallas_call(
        functools.partial(hidden_grad_kernel, blocks),
        name="hidden_grads",
        grid=(2 * blocks,),
        out_shape=(
            jax.ShapeDtypeStruct((2 * hidden, D // 2), single),
            jax.ShapeDtypeStruct((2 * hidden, D // 2), lowp),
        ),
        in_specs=[
            pl.BlockSpec((rows, block), lambda i: (0, jnp.minimum(i, blocks - 1))),
            pl.BlockSpec((rows, block), lambda i: (0, jnp.maximum(i - blocks, 0))),
            pl.BlockSpec((rows, D), lambda i: (0, 0)),
            pl.BlockSpec((rows, D), lambda i: (0, 0)),
        ],
        out_specs=(
            pl.BlockSpec((block, D // 2), lambda i: (i, 0)),
            pl.BlockSpec((block, D // 2), lambda i: (i, 0)),
        ),
        compiler_params=params(60),
        cost_estimate=cost(6 * rows * hidden * D, 16 * MIB),
    )(pre_grad, hidden_act, ffn_in, down_in)


def attn_grad_kernel(
    seg_ref, mixed_ref, mem_ref, old_ref, normed_ref, up_ref, mem_in_ref, old_in_ref, keep_ref, send_ref
):
    which = pl.program_id(0)

    @pl.when(which == 0)
    def _():
        halves(mm(seg_ref[...], normed_ref[...], TN), keep_ref, send_ref)

    @pl.when(which == 3)
    def _():
        halves(mm(mixed_ref[...], up_ref[...], TN), keep_ref, send_ref)

    @pl.when(jnp.logical_and(which > 0, which < 3))
    def _():
        total = mm(seg_ref[...], normed_ref[...], TN)
        total = total + mm(mem_ref[...], mem_in_ref[...], TN)
        total = total + mm(old_ref[...], old_in_ref[...], TN)
        halves(total, keep_ref, send_ref)


def attn_grads(seg_grad, mixed, mem_grad, old_grad, normed, attn_in, mem_in, old_in):
    block = mixed.shape[1]

    def whole(array):
        return pl.BlockSpec(array.shape, lambda i: (0, 0))

    return pl.pallas_call(
        attn_grad_kernel,
        name="attn_grads",
        grid=(4,),
        out_shape=(
            jax.ShapeDtypeStruct((4 * block, D // 2), single),
            jax.ShapeDtypeStruct((4 * block, D // 2), lowp),
        ),
        in_specs=[
            pl.BlockSpec((seg_grad.shape[0], block), lambda i: (0, jnp.minimum(i, 2))),
            whole(mixed),
            pl.BlockSpec((mem_grad.shape[0], block), lambda i: (0, jnp.clip(i - 1, 0, 1))),
            pl.BlockSpec((old_grad.shape[0], block), lambda i: (0, jnp.clip(i - 1, 0, 1))),
            whole(normed),
            whole(attn_in),
            whole(mem_in),
            whole(old_in),
        ],
        out_specs=(
            pl.BlockSpec((block, D // 2), lambda i: (i, 0)),
            pl.BlockSpec((block, D // 2), lambda i: (i, 0)),
        ),
        compiler_params=params(60),
        cost_estimate=cost(9000 * MIB, 24 * MIB),
    )(seg_grad, mixed, mem_grad, old_grad, normed, attn_in, mem_in, old_in)


def scalar_row(values, length=128):
    lane = jnp.arange(length, dtype=jnp.int32)
    row = jnp.zeros((length,), single)
    for i, value in enumerate(values):
        row = jnp.where(lane == i, value, row)
    return row


def local(
    ids,
    targets,
    target_mask,
    memory,
    old_states,
    mem_fill,
    comp_fill,
    table,
    qkv,
    wout,
    wconv,
    wup,
    wdown,
    gains,
    table_rows,
    table_cols,
    qkv_rows,
    qkv_cols,
    out_rows,
    out_cols,
    conv_rows,
    conv_cols,
    up_rows,
    up_cols,
    down_rows,
    down_cols,
    gains_second,
):
    dp_size, head_size = lax.axis_size("dp"), lax.axis_size("head")
    d, h = lax.axis_index("dp"), lax.axis_index("head")
    x, c = h // 2, h % 2
    order = block_order(dp_size)
    reach = dp_size // 2
    streams, seg_len = ids.shape
    half = seg_len // 2
    per_group = streams * seg_len
    vocab, width = table.shape
    assert head_size == 4 and streams == 2

    weights_now = (table, qkv, wout, wconv, wup, wdown)
    rows_old = (table_rows, qkv_rows, out_rows, conv_rows, up_rows, down_rows)
    cols_old = (table_cols, qkv_cols, out_cols, conv_cols, up_cols, down_cols)
    sizes = {"dp": dp_size, "head": head_size}
    row_axes = ("head", "dp", "head", "head", "dp", "head")
    col_axes = ("dp", "head", "dp", "dp", "head", "dp")
    early = [jnp.sum(old) / sizes[axis] for old, axis in zip(rows_old, col_axes)]
    early += [jnp.sum(weight * weight) for weight in weights_now]
    gain_sums = jnp.sum(gains * gains, axis=1) / head_size
    early = scalar_row(early + [gain_sums[0], gain_sums[1], gain_sums[2]])

    flat = jnp.concatenate(
        [
            ids.astype(single).reshape(-1),
            targets.astype(single).reshape(-1),
            target_mask.astype(single).reshape(-1),
            gains.astype(lowp).astype(single).reshape(-1),
        ]
    )
    room = -flat.shape[0] % 1024
    flat = jnp.concatenate([flat, jnp.zeros((room,), single)]).reshape(1, -1, 128)
    small, small_steps, _ = gather_blocks(flat, 0)
    small = small.reshape(dp_size, -1)
    place = jnp.stack([x, d])

    def field(raw):
        return relative(raw.reshape(-1, 2, 2, half), x, c)

    ids_all = small[:, :per_group]
    position = [order.index(j) for j in range(dp_size)]
    ids_all = jnp.take(ids_all, jnp.asarray(position, jnp.int32)[jnp.arange(dp_size) ^ d], axis=0)
    ids_all = jnp.transpose(field(ids_all), (1, 2, 0, 3)).reshape(-1).astype(jnp.int32)
    table_rows_all = ids_all - h * vocab
    inside = (table_rows_all >= 0) & (table_rows_all < vocab)
    bits = vocab.bit_length()
    token_codes = (jnp.arange(ids_all.shape[0], dtype=jnp.int32) << bits) | table_rows_all
    token_codes = jnp.where(inside, token_codes, -1)
    table_rows_all = jnp.where(inside, table_rows_all, vocab)
    targets_all = field(small[:reach, per_group : 2 * per_group])
    mask_all = field(small[:reach, 2 * per_group : 3 * per_group])
    gain_blocks = small[:, 3 * per_group : 3 * per_group + 3 * width].reshape(dp_size, 3, width)
    gain_vals = jnp.swapaxes(gain_blocks, 0, 1).reshape(3, 1, D)
    count_all = jnp.sum(small[:, 2 * per_group : 3 * per_group])

    heads_own = wconv.shape[0]
    wide = qkv.shape[2]
    conv_rows_own = wconv.size // width
    low_qkv = qkv.astype(lowp)
    pack_one = jnp.concatenate(
        [
            jnp.swapaxes(low_qkv, 1, 2).reshape(3 * wide, width),
            wout.astype(lowp),
            wconv.astype(lowp).reshape(conv_rows_own, width),
        ]
    )
    own_half, far_half = split(table_rows_all, 0, 2)
    looked_far = lookup(far_half, table)
    looked_own = lookup(own_half, table)
    own_one, steps_one, (looked_far, looked_own) = gather_blocks(
        after(pack_one, small_steps[0]), 1, (looked_far, looked_own)
    )
    mem_normed = state_norm(place, gain_vals[0], memory, 1)[0]
    old_normed = state_norm(place, gain_vals[0], old_states, RATE)
    own_one, mem_normed, old_normed = together(own_one, mem_normed, old_normed)
    conv_lanes = jnp.arange(DH, dtype=jnp.int32)
    conv_width = DH // dp_size
    conv_natural = (jnp.asarray(order, jnp.int32)[conv_lanes // conv_width] ^ d) * conv_width
    conv_natural = conv_natural + conv_lanes % conv_width
    conv_shuffle = (conv_natural[:, None] == conv_lanes[None, :]).astype(lowp)
    taps = heads_own * RATE * DH

    def conv_natural_order(rows):
        value = jnp.swapaxes(rows.reshape(conv_rows_own, dp_size, width), 0, 1)
        value = jnp.swapaxes(value.reshape(dp_size, taps, conv_width), 0, 1)
        moved = mm(value.reshape(taps, DH), conv_shuffle).astype(lowp)
        return moved.reshape(heads_own, RATE * DH, DH)

    def conv_block_order(value):
        moved = mm(value.astype(lowp).reshape(taps, DH), conv_shuffle, NT).astype(lowp)
        moved = jnp.swapaxes(moved.reshape(taps, dp_size, conv_width), 0, 1)
        moved = jnp.swapaxes(moved.reshape(dp_size, conv_rows_own, width), 0, 1)
        return moved.reshape(conv_rows_own, D)

    full_conv = conv_natural_order(own_one[4 * wide :])

    hidden_own = wup.shape[1]
    pack_two = jnp.concatenate([wup.astype(lowp).T, wdown.astype(lowp)])
    own_two, steps_two, _ = gather_blocks(after(pack_two, steps_one[0]), 1)

    words = vocab // reach
    z = d // 2
    z_groups = [[2 * i + b for i in range(reach)] for b in range(2)]
    low_table = after(table.astype(lowp), steps_two[0]).reshape(reach, words, width)
    low_table = lax.all_to_all(low_table, "dp", 0, 0, axis_index_groups=z_groups)
    slots = -(-words // 256) * 256

    looked = (looked_own + swap(looked_far, "head", 1)).reshape(2, -1, width)
    looked = looked[0] + swap(looked[1], "head", 2)
    looked = lax.all_to_all(looked.reshape(dp_size, half, width), "dp", 0, 0)
    embedded_low, normed = place_embedding(place, looked, gain_vals[0])
    embedded = embedded_low.astype(single)

    comp_counts = jnp.where(x == 1, jnp.flip(comp_fill), comp_fill)
    mem_counts = jnp.where(x == 1, jnp.flip(mem_fill), mem_fill)
    info = jnp.stack([comp_counts[0], mem_counts[0], comp_counts[1], mem_counts[1], c * half])
    info = info.astype(jnp.int32)

    def core_sum(keep, send):
        more = swap(send.astype(lowp), "head", 1)
        return keep.astype(single) + more.astype(single)

    def group_sum(part, beside=()):
        keep, send = split(part, 0, 2) if not isinstance(part, (tuple, list)) else part
        keep, send = split(core_sum(keep, send), 0, 2)
        more, *beside = together(swap(send.astype(lowp), "head", 2), *beside)
        part = keep + more.astype(single)
        return (part, beside) if beside else part

    def group_both(part, beside=()):
        far, *beside = together(swap(part, "head", 2), *beside)
        pair = jnp.concatenate([part, far], axis=0)
        both = (pair, swap(pair, "head", 1))
        return (both, beside) if beside else both

    normed = jnp.concatenate(group_both(normed))
    in_weight = own_one[: 3 * wide]
    comp, old_raw = compress(old_normed, own_one, full_conv)
    mem = mm(mem_normed, own_one[wide : 3 * wide], NT).astype(lowp)
    seg = mm(normed, in_weight, NT).astype(lowp).reshape(2, streams, half, 3 * wide)
    mixed, lse = attend(info, after(seg, steps_two[1]), comp, mem)
    mixed, low_parts = together(mixed.reshape(-1, wide), low_table)
    near_table = [
        lax.dynamic_index_in_dim(low_parts, z ^ (m // 2), 0, keepdims=False) for m in order[:reach]
    ]
    near_table = jnp.concatenate(near_table, axis=1)
    full_up, full_down = split(own_two, 0, 2)
    attn_sum, (full_up, full_down, near_table) = group_sum(
        mm(mixed, own_one[3 * wide : 4 * wide]), (full_up, full_down, near_table)
    )
    far_table = swap(near_table, "dp", 1)
    loss_table = jnp.concatenate([near_table, far_table], axis=1)
    loss_table = jnp.concatenate([loss_table, jnp.zeros((slots - words, D), lowp)], axis=0)
    after_attn = embedded + attn_sum
    ffn_in, inv_second = rms(after_attn, gain_vals[1])
    ffn_in = jnp.concatenate(group_both(ffn_in))
    hidden_pre = mm(ffn_in, full_up, NT)
    hidden_act = jax.nn.gelu(hidden_pre).astype(lowp)
    ffn_sum, (loss_table,) = group_sum(mm(hidden_act, full_down), (loss_table,))
    after_ffn = after_attn + ffn_sum
    final_in, inv_third = rms(after_ffn, gain_vals[2])

    word_start = (h * vocab + z * words).astype(single)
    wanted_all = targets_all - word_start
    wanted_all = jnp.where((wanted_all >= 0) & (wanted_all < words), wanted_all, -1.0)
    info_all = jnp.stack([wanted_all, mask_all] + [jnp.zeros_like(mask_all)] * 6)
    info_all = jnp.transpose(info_all, (1, 0, 2, 3, 4)).reshape(reach, 8, per_group)
    pieces = [final_in]
    chunks = []
    raised = []
    stats = []

    def next_chunk():
        i = len(chunks)
        if i < 2:
            chunks.append(group_both(pieces[i]))
        else:
            chunk, (stats[i - 2],) = group_both(pieces[i], (stats[i - 2],))
            chunks.append(chunk)
        out, stat = logits_part(words, info_all[i], *chunks[i], loss_table)
        raised.append(out)
        stats.append(stat)

    mask = dp_size // 2
    while mask > 1:
        joined = jnp.concatenate(pieces) if len(pieces) > 1 else pieces[0]
        moved = swap(reorder(joined, mask), "dp", mask)
        if len(pieces) == 1:
            next_chunk()
            moved, own_codes, own_count, early = together(
                moved, *own_list(after(token_codes, final_in)), early
            )
        elif len(pieces) == 2:
            moved, stats[0] = together(moved, stats[0])
        pieces += split(moved, 0, len(pieces))
        mask //= 2
    while len(chunks) < reach:
        next_chunk()
    stats = [stat[:3].reshape(3, 1, 2, 2, half) for stat in stats]
    own_stats = jnp.concatenate(stats, axis=1)

    def combine(first, second):
        top = jnp.maximum(first[0], second[0])
        total = first[1] * jnp.exp(first[0] - top) + second[1] * jnp.exp(second[0] - top)
        return jnp.stack([top, total, first[2] + second[2]])

    merged = own_stats
    merged = combine(merged, jnp.flip(swap(merged, "head", 1), 2))
    merged = combine(merged, jnp.flip(swap(merged, "head", 2), 3))
    mask = 2
    while mask < dp_size:
        other = split(swap(merged, "dp", mask), 1, reach)
        other = [other[order.index(j ^ mask)] for j in order[:reach]]
        merged = combine(merged, jnp.concatenate(other, axis=1))
        mask *= 2
    log_total = merged[0] + jnp.log(merged[1])
    loss_local = jnp.sum(mask_all[0, 0, 0] * (log_total[0, 0, 0] - merged[2, 0, 0, 0]))
    factor_all = jnp.exp(own_stats[0] - log_total)

    factor_all = factor_all.reshape(reach, 1, per_group) * info_all[:, 1:2]
    factor_all = jnp.broadcast_to(factor_all, info_all.shape)
    dlogits = [None] * reach
    parts = [None] * reach
    for i in reversed(range(reach)):
        dlogits[i], *part = logits_back(info_all[i], factor_all[i], raised[i], loss_table)
        parts[i] = group_sum(part)
    dlogits[0] = after(dlogits[0], parts[min(1, reach - 1)])
    table_parts = table_grad_part(dlogits, chunks)
    mask = 2
    while len(parts) > 1:
        count = len(parts) // 2
        moved = jnp.concatenate([part.astype(lowp) for part in parts[count:]])
        moved = swap(reorder(moved, mask), "dp", mask)
        if mask == 2:
            moved, *table_parts = together(moved, *table_parts)
        moved = split(moved.astype(single), 0, count)
        parts = [part + more for part, more in zip(parts, moved)]
        mask *= 2
    final_grad = parts[0]

    keep, send = table_parts
    moved_table = swap(send, "dp", 1)

    grad_after_ffn = rms_back(after_ffn, inv_third, gain_vals[2], final_grad)
    down_in, (moved_table,) = group_both(grad_after_ffn.astype(lowp), (moved_table,))
    down_in = jnp.concatenate(down_in)
    act_grad = mm(down_in, full_down, NT)
    pre_grad = jax.vjp(jax.nn.gelu, hidden_pre)[1](act_grad)[0].astype(lowp)
    two = hidden_grads(pre_grad, hidden_act, ffn_in, down_in)
    ffn_in_grad, two = group_sum(mm(pre_grad, full_up), two)
    two_moved = swap(two[1], "dp", 1)
    keep = keep + moved_table.astype(single)
    table_pieces = jnp.stack(split(keep[:words].astype(lowp), 1, reach))
    position = [order.index(2 * i) for i in range(reach)]
    position = jnp.asarray(position, jnp.int32)[jnp.arange(reach) ^ z]
    table_pieces = jnp.concatenate(
        [lax.dynamic_index_in_dim(table_pieces, position[i], 0) for i in range(reach)]
    )
    table_pieces = lax.all_to_all(table_pieces, "dp", 0, 0, axis_index_groups=z_groups)
    grad_after_attn = grad_after_ffn + rms_back(after_attn, inv_second, gain_vals[1], ffn_in_grad)
    attn_in = jnp.concatenate(group_both(grad_after_attn.astype(lowp)))

    mixed_grad = mm(attn_in, own_one[3 * wide : 4 * wide], NT).astype(lowp)
    mixed_grad = mixed_grad.reshape(2, streams, half, wide)
    seg_grad, comp_grad, mem_grad = attend_back(info, seg, comp, mem, lse, mixed_grad)
    seg_grad, table_pieces = together(seg_grad.reshape(-1, 3 * wide), table_pieces)
    seg_in = core_sum(*split(mm(seg_grad, in_weight), 0, 2))
    seg_in_far = swap(seg_in[half:].astype(lowp), "head", 2)
    old_grad, conv_sum = expand(comp_grad, old_raw, full_conv)
    one = attn_grads(
        seg_grad,
        mixed,
        mem_grad,
        old_grad.reshape(-1, old_grad.shape[-1]),
        normed,
        attn_in,
        mem_normed,
        old_normed.reshape(-1, D),
    )
    seg_in_far, two_moved, *one = together(seg_in_far, two_moved, *one)
    table_base = table_pieces.astype(single).reshape(vocab, width)
    rows_grad = embed_back(
        place,
        embedded_low,
        gain_vals[0],
        seg_in[:half],
        seg_in_far,
        grad_after_attn,
    )
    rows_grad = lax.all_to_all(rows_grad, "dp", 0, 0)
    two = two[0] + two_moved.astype(single)
    two_keep, two_send = split(two, 1, 2)
    two_send, rows_grad = together(swap(two_send.astype(lowp), "dp", 2), rows_grad)
    two = two_keep + two_send.astype(single)
    rows_grad = jnp.stack([rows_grad, swap(rows_grad, "head", 2)])
    rows_grad = jnp.stack([rows_grad, swap(rows_grad, "head", 1)]).reshape(-1, width)

    two = reduce_blocks(*split(two, 1, 2), 4)
    up_grad = two[:hidden_own].T
    down_grad = two[hidden_own:]
    conv_sum = split(conv_block_order(conv_sum), 1, 2)
    one = [jnp.concatenate([part, more.astype(part.dtype)]) for part, more in zip(one, conv_sum)]
    one = reduce_blocks(*one)
    qkv_grad = jnp.swapaxes(one[: 3 * wide].reshape(3, wide, width), 1, 2)
    out_grad = one[3 * wide : 4 * wide]
    conv_grad = one[4 * wide :].reshape(wconv.shape)
    table_grad = scatter(bits, own_count, own_codes, table_base, rows_grad)

    gains_low = gains.astype(lowp).astype(single)
    gain_part = jnp.stack(
        [
            jnp.sum(low_qkv.astype(single) * qkv_grad, axis=(0, 2)),
            jnp.sum(wup.astype(lowp).astype(single) * up_grad, axis=1),
            jnp.sum(table.astype(lowp).astype(single) * table_base, axis=0),
        ]
    )

    grads = (table_grad, qkv_grad, out_grad, conv_grad, up_grad, down_grad)
    def sum_over_dp(joined):
        mask = 1
        while mask < dp_size:
            joined = joined + swap(joined, "dp", mask)
            mask *= 2
        return joined

    row_part = []
    col_part = []
    for grad in grads:
        square = grad * grad
        row_part.append(jnp.sum(square, axis=-1))
        col_part.append(jnp.sum(square, axis=tuple(range(square.ndim - 1))))
    row_q, row_u, col_e, col_o, col_c, col_d, gain_raw, early = lax.psum(
        (
            row_part[1],
            row_part[4],
            col_part[0],
            col_part[2],
            col_part[3],
            col_part[5],
            gain_part,
            early + scalar_row([0.0] * 15 + [loss_local]),
        ),
        "head",
    )
    lanes = [col_e, jnp.sum(row_q, axis=0), col_o]
    lanes += [jnp.concatenate([col_c, jnp.zeros((width - col_c.shape[0],), single)]), row_u, col_d]
    members = [col_part[4], row_part[5], row_part[3], row_part[2], col_part[1], *lanes, row_part[0], early]
    joined = jnp.concatenate([m.reshape(-1) for m in members])
    joined = sum_over_dp(jnp.concatenate([joined, jnp.zeros((-joined.shape[0] % 1024,), single)]))
    sums = []
    start = 0
    for member in members:
        sums.append(joined[start : start + member.size].reshape(member.shape))
        start += member.size
    col_u, row_d, row_c, row_o, col_q, *lanes, row_e, early = sums
    square_total = [jnp.sum(lane) for lane in lanes]
    row_sums = [row_e, row_q, row_o, row_c, row_u, row_d]
    col_sums = [col_e, col_q, col_o, col_c, col_u, col_d]
    weight_total = early[6:15]
    loss_all = early[15]
    inverse = 1.0 / count_all
    decay = 1.0 - STEP ** (-0.8)
    updates = []
    stats_new = []
    scaled = []
    counts = []
    update_sq = []
    for index in range(6):
        rows_total = rows_old[index].size * sizes[row_axes[index]]
        cols_total = cols_old[index].size * sizes[col_axes[index]]
        grad_scaled = grads[index] * inverse
        rows_new = decay * rows_old[index] + (1.0 - decay) * (
            row_sums[index] * inverse * inverse / cols_total + TINY_SQUARE
        )
        cols_new = decay * cols_old[index] + (1.0 - decay) * (
            col_sums[index] * inverse * inverse / rows_total + TINY_SQUARE
        )
        mean_row = decay * early[index] / rows_total + (1.0 - decay) * (
            square_total[index] * inverse * inverse / (rows_total * cols_total) + TINY_SQUARE
        )
        second = rows_new[..., None] * cols_new / mean_row
        direction = grad_scaled * lax.rsqrt(second)
        updates.append(direction)
        stats_new.append((rows_new, cols_new))
        scaled.append(grad_scaled)
        counts.append(rows_total * cols_total)
        update_sq.append(jnp.sum(direction * direction))
    gain_scaled = gain_raw / gains_low * inverse
    second_new = decay * gains_second + (1.0 - decay) * (gain_scaled * gain_scaled + TINY_SQUARE)
    gain_dir = gain_scaled * lax.rsqrt(second_new)
    for which in range(3):
        update_sq.append(jnp.sum(gain_dir[which] * gain_dir[which]) / head_size)
    update_total = after(scalar_row(update_sq, 1024), loss_all)
    for mask in (1, 2):
        update_total = update_total + swap(update_total, "head", mask)
    update_total = sum_over_dp(update_total)[:9]
    results = [loss_all, count_all]
    for index in range(6):
        factor = jnp.maximum(0.001, jnp.sqrt(weight_total[index] / counts[index]))
        denom = jnp.maximum(1.0, jnp.sqrt(update_total[index] / counts[index]) / CLIP_LEVEL)
        new_weight = weights_now[index] - LEARN_RATE * factor * updates[index] / denom
        results += [new_weight, scaled[index], stats_new[index][0], stats_new[index][1]]
    gain_factor = jnp.maximum(0.001, jnp.sqrt(weight_total[6:] / D))[:, None]
    gain_denom = jnp.maximum(1.0, jnp.sqrt(update_total[6:] / D) / CLIP_LEVEL)[:, None]
    results += [gains - LEARN_RATE * gain_factor * gain_dir / gain_denom, gain_scaled, second_new]
    return tuple(results)


def solution(mesh):
    in_specs = (
        P("dp", None),
        P("dp", None),
        P("dp", None),
        P("dp", None, None),
        P("dp", None, None),
        P("dp"),
        P("dp"),
        P("head", "dp"),
        P(None, "dp", "head"),
        P("head", "dp"),
        P("head", None, "dp"),
        P("dp", "head"),
        P("head", "dp"),
        P(None, "dp"),
        P("head"),
        P("dp"),
        P(None, "dp"),
        P("head"),
        P("head"),
        P("dp"),
        P("head", None),
        P("dp"),
        P("dp"),
        P("head"),
        P("head"),
        P("dp"),
        P(None, "dp"),
    )
    out_specs = (
        P(),
        P(),
        P("head", "dp"),
        P("head", "dp"),
        P("head"),
        P("dp"),
        P(None, "dp", "head"),
        P(None, "dp", "head"),
        P(None, "dp"),
        P("head"),
        P("head", "dp"),
        P("head", "dp"),
        P("head"),
        P("dp"),
        P("head", None, "dp"),
        P("head", None, "dp"),
        P("head", None),
        P("dp"),
        P("dp", "head"),
        P("dp", "head"),
        P("dp"),
        P("head"),
        P("head", "dp"),
        P("head", "dp"),
        P("head"),
        P("dp"),
        P(None, "dp"),
        P(None, "dp"),
        P(None, "dp"),
    )
    return jax.shard_map(local, mesh=mesh, in_specs=in_specs, out_specs=out_specs, check_vma=False)
```

```python
import functools

import jax
import jax.numpy as jnp
from jax import lax
from jax.experimental import pallas as pl
from jax.experimental.pallas import tpu as pltpu
from jax.sharding import PartitionSpec as P

D = 1024
H = 8
DH = 128
MEM = 512
CMEM = 512
RATE = 3
STEP = 10


TINY_NORM = 1e-06
TINY_SQUARE = 1e-30
LEARN_RATE = 0.5
CLIP_LEVEL = 1.0

lowp = jnp.bfloat16
single = jnp.float32
NT = (((1,), (1,)), ((), ()))
TN = (((0,), (0,)), ((), ()))
NN = (((1,), (0,)), ((), ()))
MIB = 1024 * 1024


def mm(left, right, dims=NN):
    return lax.dot_general(left, right, dims, preferred_element_type=single)


def swap(value, axis, mask):
    size = lax.axis_size(axis)
    return lax.ppermute(value, axis, [(i, i ^ mask) for i in range(size)])


def after(value, *deps):
    return lax.optimization_barrier((value, *deps))[0]


def together(*values):
    return lax.optimization_barrier(values)


def block_order(size):
    order = [0]
    step = size // 2
    while step:
        order = order + [j + step for j in order]
        step //= 2
    return order


def gather_blocks(piece, axis, beside=()):
    steps = []
    mask = lax.axis_size("dp") // 2
    while mask:
        moved = swap(piece, "dp", mask)
        if len(steps) < len(beside):
            moved = beside[len(steps)](moved)
        piece = jnp.concatenate([piece, moved], axis=axis)
        steps.append(piece)
        mask //= 2
    return piece, steps


def split(value, axis, parts):
    width = value.shape[axis] // parts
    return [lax.slice_in_dim(value, i * width, (i + 1) * width, axis=axis) for i in range(parts)]


def reduce_blocks(keep, send, beside=(), mask=1):
    moved = swap(send.astype(lowp), "dp", mask)
    if beside:
        moved = beside[0](moved)
    total = keep + moved.astype(single)
    mask *= 2
    if mask == lax.axis_size("dp"):
        return total
    return reduce_blocks(*split(total, 1, 2), beside[1:], mask)


def reorder(value, mask):
    order = block_order(lax.axis_size("dp"))
    cols = split(value, 1, len(order))
    return jnp.concatenate([cols[order.index(j ^ mask)] for j in order], axis=1)


def relative(value, x, c):
    value = jnp.where(x == 1, jnp.flip(value, -3), value)
    value = jnp.where(c == 1, jnp.flip(value, -2), value)
    return jnp.swapaxes(value, -3, -2)


def rms(values, gain):
    inv = lax.rsqrt(jnp.mean(values * values, axis=-1, keepdims=True) + TINY_NORM)
    return (values * inv * gain).astype(lowp), inv


def rms_back(values, inv, gain, upstream):
    scaled = gain * upstream
    inner = jnp.sum(scaled * values, axis=-1, keepdims=True) / D
    return scaled * inv - values * (inner * inv * inv * inv)


def vmem(shape=None, index=None):
    if shape is None:
        return pl.BlockSpec(memory_space=pltpu.VMEM)
    return pl.BlockSpec(shape, index)


def smem():
    return pl.BlockSpec(memory_space=pltpu.SMEM)


def params(mib):
    return pltpu.CompilerParams(vmem_limit_bytes=mib * MIB)


def cost(flops, size, exps=0):
    return pl.CostEstimate(
        flops=int(0.02 * flops), bytes_accessed=int(0.02 * size), transcendentals=exps
    )


def lookup_kernel(row_ref, table_ref, out_ref, tab, held, sem):
    total = row_ref.shape[0]
    vocab = table_ref.shape[0]
    copy = pltpu.make_async_copy(table_ref, tab.at[pl.ds(0, vocab)], sem)
    copy.start()
    tab[pl.ds(vocab, 8), :] = jnp.zeros((8, tab.shape[1]), single)
    copy.wait()

    @pl.loop(0, total // 16)
    def _(g):
        for j in range(16):
            t = g * 16 + j
            held[pl.ds(t, 1), :] = tab[pl.ds(row_ref[t], 1), :]

    @pl.loop(0, total // 512)
    def _(i):
        rows = pl.ds(pl.multiple_of(i * 512, 512), 512)
        out_ref[rows, :] = held[rows, :].astype(lowp)


def lookup(rows, table):
    total = rows.shape[0]
    vocab, width = table.shape
    return pl.pallas_call(
        lookup_kernel,
        name="lookup",
        out_shape=jax.ShapeDtypeStruct((total, width), lowp),
        in_specs=[smem(), pl.BlockSpec(memory_space=pl.ANY)],
        out_specs=vmem(),
        scratch_shapes=[
            pltpu.VMEM((vocab + 8, width), single),
            pltpu.VMEM((total, width), single),
            pltpu.SemaphoreType.DMA(()),
        ],
        compiler_params=params(60),
        cost_estimate=cost(0, 30 * MIB),
    )(rows, table)


def list_kernel(code_ref, out_ref, count_ref):
    total = code_ref.shape[0]

    def group(g, count):
        for j in range(16):
            code = code_ref[g * 16 + j]
            out_ref[count] = code
            count = count + jnp.where(code >= 0, 1, 0)
        return count

    count_ref[0] = lax.fori_loop(0, total // 16, group, jnp.int32(0))


def own_list(codes):
    total = codes.shape[0]
    return pl.pallas_call(
        list_kernel,
        name="own_list",
        out_shape=(
            jax.ShapeDtypeStruct((total + 8,), jnp.int32),
            jax.ShapeDtypeStruct((1,), jnp.int32),
        ),
        in_specs=[smem()],
        out_specs=(smem(), smem()),
        cost_estimate=cost(0, 60 * MIB),
    )(codes)


def place_kernel(order, place_ref, in_ref, gain_ref, out_ref, norm_ref, held):
    width = in_ref.shape[2]
    for p, j in enumerate(order):
        block = in_ref[pl.ds(place_ref[1] ^ j, 1)][0]
        out_ref[:, p * width : (p + 1) * width] = block
        held[:, p * width : (p + 1) * width] = block.astype(single)
    values = held[...]
    inv = lax.rsqrt(jnp.mean(values * values, axis=-1, keepdims=True) + TINY_NORM)
    norm_ref[...] = (values * inv * gain_ref[...]).astype(lowp)


def place_embedding(place, blocks, gain):
    rows = blocks.shape[1]
    return pl.pallas_call(
        functools.partial(place_kernel, block_order(blocks.shape[0])),
        name="place_embedding",
        out_shape=(jax.ShapeDtypeStruct((rows, D), lowp), jax.ShapeDtypeStruct((rows, D), lowp)),
        in_specs=[smem(), vmem(), vmem()],
        out_specs=(vmem(), vmem()),
        scratch_shapes=[pltpu.VMEM((rows, D), single)],
        compiler_params=params(60),
        cost_estimate=cost(0, 3 * MIB),
    )(place, blocks, gain)


def embed_back_kernel(order, place_ref, in_ref, gain_ref, keep_ref, more_ref, grad_ref, out_ref, held):
    values = in_ref[...].astype(single)
    inv = lax.rsqrt(jnp.mean(values * values, axis=-1, keepdims=True) + TINY_NORM)
    upstream = keep_ref[...] + more_ref[...].astype(single)
    held[...] = grad_ref[...] + rms_back(values, inv, gain_ref[...], upstream)
    width = out_ref.shape[2]
    for p, j in enumerate(order):
        block = held[:, p * width : (p + 1) * width].astype(lowp)
        out_ref[pl.ds(place_ref[1] ^ j, 1)] = block[None]


def embed_back(place, values, gain, keep, more, grad):
    rows = values.shape[0]
    size = lax.axis_size("dp")
    return pl.pallas_call(
        functools.partial(embed_back_kernel, block_order(size)),
        name="embed_back",
        out_shape=jax.ShapeDtypeStruct((size, rows, D // size), lowp),
        in_specs=[smem()] + [vmem()] * 5,
        out_specs=vmem(),
        scratch_shapes=[pltpu.VMEM((rows, D), single)],
        compiler_params=params(60),
        cost_estimate=cost(0, 4 * MIB),
    )(place, values, gain, keep, more, grad)


def scatter_kernel(bits, count_ref, code_ref, base_ref, grad_ref, out_ref, rows):
    total = grad_ref.shape[0]
    vocab = base_ref.shape[0]

    @pl.loop(0, total // 512)
    def _(i):
        here = pl.ds(pl.multiple_of(i * 512, 512), 512)
        rows[here, :] = grad_ref[here, :].astype(single)

    rows[pl.ds(total, 8), :] = jnp.zeros((8, rows.shape[1]), single)

    @pl.loop(0, vocab // 400)
    def _(i):
        here = pl.ds(pl.multiple_of(i * 400, 400), 400)
        out_ref[here, :] = base_ref[here, :]

    count = count_ref[0]

    def group(g, carry):
        for j in range(8):
            index = g * 8 + j
            code = jnp.where(index < count, code_ref[index], total << bits)
            token = lax.shift_right_logical(code, bits)
            row = code & ((1 << bits) - 1)
            out_ref[pl.ds(row, 1), :] = out_ref[pl.ds(row, 1), :] + rows[pl.ds(token, 1), :]
        return carry

    lax.fori_loop(0, (count + 7) // 8, group, jnp.int32(0))


def scatter(bits, count, codes, base, grad):
    total, width = grad.shape
    return pl.pallas_call(
        functools.partial(scatter_kernel, bits),
        name="scatter",
        out_shape=jax.ShapeDtypeStruct(base.shape, single),
        in_specs=[smem(), smem(), vmem(), vmem()],
        out_specs=vmem(),
        scratch_shapes=[pltpu.VMEM((total + 8, width), single)],
        compiler_params=params(60),
        cost_estimate=cost(0, 30 * MIB),
    )(count, codes, base, grad)


def state_kernel(order, width, place_ref, gain_ref, in_ref, out_ref, held):
    rows = in_ref.shape[1]
    values = in_ref[0].astype(single)
    inv = lax.rsqrt(jnp.mean(values * values, axis=-1, keepdims=True) + TINY_NORM)
    for p, j in enumerate(order):
        start = pl.multiple_of((place_ref[1] ^ j) * width, width)
        block = in_ref[0, :, pl.ds(start, width)].astype(single)
        held[p] = block * inv * gain_ref[:, p * width : (p + 1) * width]
    groups = out_ref.shape[0]
    for p in range(len(order)):
        cols = slice(p * width, (p + 1) * width)
        if groups == 1:
            out_ref[0, :, cols] = held[p].astype(lowp)
        else:
            for j in range(groups):
                part = held[p, pl.ds(j, rows // groups, stride=groups), :]
                out_ref[j, :, cols] = part.astype(lowp)


def state_norm(place, gain, states, groups):
    size = lax.axis_size("dp")
    order = block_order(size)
    width = D // size
    streams = states.shape[0]
    count = states.shape[1] // groups
    if width % 128:
        values = jnp.where(place[0] == 1, jnp.flip(states, 0), states).astype(single).reshape(-1, D)
        inv = lax.rsqrt(jnp.mean(values * values, axis=-1, keepdims=True) + TINY_NORM)
        lanes = jnp.arange(D, dtype=jnp.int32)
        blocks = jnp.asarray(order, jnp.int32)[lanes // width] ^ place[1]
        source = blocks * width + lanes % width
        shuffle = (lanes[:, None] == source[None, :]).astype(single)
        moved = jnp.dot(values * inv, shuffle, precision=lax.Precision.HIGHEST)
        out = (moved * gain).astype(lowp)
        return jnp.swapaxes(out.reshape(streams * count, groups, D), 0, 1)
    tile = 128
    return pl.pallas_call(
        functools.partial(state_kernel, order, width),
        name="state_norm",
        out_shape=jax.ShapeDtypeStruct((groups, streams * count, D), lowp),
        grid_spec=pltpu.PrefetchScalarGridSpec(
            num_scalar_prefetch=1,
            grid=(streams, count // tile),
            in_specs=[
                pl.BlockSpec((1, D), lambda n, i, s: (0, 0)),
                pl.BlockSpec((1, tile * groups, D), lambda n, i, s: (s[0] ^ n, i, 0)),
            ],
            out_specs=pl.BlockSpec(
                (groups, tile, D), lambda n, i, s: (0, n * (count // tile) + i, 0)
            ),
            scratch_shapes=[pltpu.VMEM((len(order), tile * groups, width), single)],
        ),
        compiler_params=params(60),
        cost_estimate=cost(0, 4 * streams * count * groups * D),
    )(place, gain, states)


def compress_kernel(old_ref, key_ref, value_ref, conv_ref, comp_ref, raw_ref):
    heads = conv_ref.shape[0]
    wide = heads * DH
    for part, weight_ref in enumerate((key_ref, value_ref)):
        sums = [None] * heads
        for j in range(RATE):
            raw = mm(old_ref[j], weight_ref[...], NT).astype(lowp)
            raw_ref[j, :, part * wide : (part + 1) * wide] = raw
            for n in range(heads):
                piece = raw[:, n * DH : (n + 1) * DH]
                term = mm(piece, conv_ref[n, j * DH : (j + 1) * DH, :])
                sums[n] = term if j == 0 else sums[n] + term
        for n in range(heads):
            first = part * wide + n * DH
            comp_ref[:, first : first + DH] = sums[n].astype(lowp)


def compress(old3, weights, conv):
    rows = old3.shape[1]
    wide = conv.shape[0] * DH
    tile = 256
    return pl.pallas_call(
        compress_kernel,
        name="compress",
        grid=(rows // tile,),
        out_shape=(
            jax.ShapeDtypeStruct((rows, 2 * wide), lowp),
            jax.ShapeDtypeStruct((RATE, rows, 2 * wide), lowp),
        ),
        in_specs=[
            pl.BlockSpec((RATE, tile, D), lambda i: (0, i, 0)),
            pl.BlockSpec((wide, D), lambda i: (1, 0)),
            pl.BlockSpec((wide, D), lambda i: (2, 0)),
            pl.BlockSpec(conv.shape, lambda i: (0, 0, 0)),
        ],
        out_specs=(
            pl.BlockSpec((tile, 2 * wide), lambda i: (i, 0)),
            pl.BlockSpec((RATE, tile, 2 * wide), lambda i: (0, i, 0)),
        ),
        compiler_params=params(60),
        cost_estimate=cost(4 * RATE * rows * wide * D, 12 * MIB),
    )(old3, weights, weights, conv)


def expand_kernel(grad_ref, raw_ref, conv_ref, out_ref, conv_out_ref):
    heads = conv_ref.shape[0]
    for h in range(heads):
        for j in range(RATE):
            rows = slice(j * DH, (j + 1) * DH)
            taps = conv_ref[h, rows, :]
            total = None
            for n in (h, heads + h):
                cols = slice(n * DH, (n + 1) * DH)
                grad = grad_ref[:, cols]
                out_ref[j, :, cols] = mm(grad, taps, NT).astype(lowp)
                term = mm(raw_ref[j, :, cols], grad, TN)
                total = term if total is None else total + term
            conv_out_ref[h, rows, :] = total


def expand(grad, raw, conv):
    return pl.pallas_call(
        expand_kernel,
        name="expand",
        out_shape=(
            jax.ShapeDtypeStruct(raw.shape, lowp),
            jax.ShapeDtypeStruct(conv.shape, single),
        ),
        in_specs=[vmem()] * 3,
        out_specs=(vmem(), vmem()),
        compiler_params=params(60),
        cost_estimate=cost(2000 * MIB, 12 * MIB),
    )(grad, raw, conv)


def masked_scores(info_ref, query, keys):
    rows = query.shape[0]
    scale = DH ** (-0.5)
    result = []
    for which, key in enumerate(keys):
        slots = key.shape[0]
        col = lax.broadcasted_iota(jnp.int32, (rows, slots), 1)
        if which < 2:
            seen = col >= slots - info_ref[2 * pl.program_id(0) + which]
        else:
            row = lax.broadcasted_iota(jnp.int32, (rows, slots), 0)
            shift = info_ref[4]
            row = row + shift
            col = col + shift
            row = jnp.where(row >= slots, row - slots, row)
            col = jnp.where(col >= slots, col - slots, col)
            seen = col <= row
        result.append(jnp.where(seen, mm(query, key, NT) * scale, -1e30))
    return result


def rows_of(ref):
    return ref[...].reshape(-1, ref.shape[-1])


def attend_kernel(info_ref, q_ref, ks_ref, vs_ref, kc_ref, vc_ref, km_ref, vm_ref, out_ref, lse_ref):
    query = rows_of(q_ref)
    scores = masked_scores(info_ref, query, [kc_ref[...], km_ref[...], rows_of(ks_ref)])
    top = functools.reduce(jnp.maximum, [jnp.max(s, axis=-1, keepdims=True) for s in scores])
    total = 0.0
    mixed = 0.0
    for score, value in zip(scores, (vc_ref[...], vm_ref[...], rows_of(vs_ref))):
        weight = jnp.exp(score - top)
        total = total + jnp.sum(weight, axis=-1, keepdims=True)
        mixed = mixed + mm(weight.astype(lowp), value)
    out_ref[...] = (mixed / total).astype(lowp).reshape(out_ref.shape)
    lse_ref[0, 0] = top + jnp.log(total)


def attend_back_kernel(
    info_ref, q_ref, ks_ref, vs_ref, kc_ref, vc_ref, km_ref, vm_ref, lse_ref, up_ref,
    seg_ref, comp_ref, mem_ref,
):
    head = pl.program_id(1)
    wide = pl.num_programs(1) * DH
    scale = DH ** (-0.5)
    query = rows_of(q_ref)
    upstream = rows_of(up_ref)
    keys = [kc_ref[...], km_ref[...], rows_of(ks_ref)]
    scores = masked_scores(info_ref, query, keys)
    probs = [jnp.exp(s - lse_ref[0, 0]) for s in scores]
    prob_grads = [
        mm(upstream, v, NT) for v in (vc_ref[...], vm_ref[...], rows_of(vs_ref))
    ]
    inner = 0.0
    for p, g in zip(probs, prob_grads):
        inner = inner + jnp.sum(p * g, axis=-1, keepdims=True)
    here = pl.ds(pl.multiple_of(head * DH, DH), DH)
    second = pl.ds(pl.multiple_of(wide + head * DH, DH), DH)
    third = pl.ds(pl.multiple_of(2 * wide + head * DH, DH), DH)
    query_grad = 0.0
    places = ((comp_ref, here, second), (mem_ref, here, second), (seg_ref, second, third))
    for p, g, key, (ref, key_at, value_at) in zip(probs, prob_grads, keys, places):
        score_grad = (p * (g - inner)).astype(lowp)
        query_grad = query_grad + mm(score_grad, key)
        shape = ref.shape[:-1] + (DH,)
        key_grad = (mm(score_grad, query, TN) * scale).astype(lowp)
        value_grad = mm(p.astype(lowp), upstream, TN).astype(lowp)
        ref[..., key_at] = key_grad.reshape(shape)
        ref[..., value_at] = value_grad.reshape(shape)
    shape = seg_ref.shape[:-1] + (DH,)
    seg_ref[..., here] = (query_grad * scale).astype(lowp).reshape(shape)


def head_specs(seg, comp, mem, heads):
    streams = seg.shape[1]

    def of_seg(first):
        return pl.BlockSpec((2, 1, seg.shape[2], DH), lambda n, h: (0, n, 0, first + h))

    def cols(array, first):
        return pl.BlockSpec((array.shape[0] // streams, DH), lambda n, h: (n, first + h))

    return [
        smem(),
        of_seg(0),
        of_seg(heads),
        of_seg(2 * heads),
        cols(comp, 0),
        cols(comp, heads),
        cols(mem, 0),
        cols(mem, heads),
    ]


def attend(info, seg, comp, mem):
    _, streams, half, _ = seg.shape
    heads = comp.shape[1] // (2 * DH)
    return pl.pallas_call(
        attend_kernel,
        name="attend",
        grid=(streams, heads),
        out_shape=(
            jax.ShapeDtypeStruct((2, streams, half, heads * DH), lowp),
            jax.ShapeDtypeStruct((streams, heads, 2 * half, 1), single),
        ),
        in_specs=head_specs(seg, comp, mem, heads),
        out_specs=(
            pl.BlockSpec((2, 1, half, DH), lambda n, h: (0, n, 0, h)),
            pl.BlockSpec((1, 1, 2 * half, 1), lambda n, h: (n, h, 0, 0)),
        ),
        compiler_params=params(60),
        cost_estimate=cost(7000 * MIB, 6 * MIB),
    )(info, seg, seg, seg, comp, comp, mem, mem)


def attend_back(info, seg, comp, mem, lse, upstream):
    _, streams, half, wide = seg.shape
    heads = comp.shape[1] // (2 * DH)
    slots = comp.shape[0] // streams
    kept = mem.shape[0] // streams
    return pl.pallas_call(
        attend_back_kernel,
        name="attend_back",
        grid=(streams, heads),
        out_shape=(
            jax.ShapeDtypeStruct(seg.shape, lowp),
            jax.ShapeDtypeStruct(comp.shape, lowp),
            jax.ShapeDtypeStruct(mem.shape, lowp),
        ),
        in_specs=head_specs(seg, comp, mem, heads)
        + [
            pl.BlockSpec((1, 1, 2 * half, 1), lambda n, h: (n, h, 0, 0)),
            pl.BlockSpec((2, 1, half, DH), lambda n, h: (0, n, 0, h)),
        ],
        out_specs=(
            pl.BlockSpec((2, 1, half, wide), lambda n, h: (0, n, 0, 0)),
            pl.BlockSpec((slots, comp.shape[1]), lambda n, h: (n, 0)),
            pl.BlockSpec((kept, mem.shape[1]), lambda n, h: (n, 0)),
        ),
        compiler_params=params(60),
        cost_estimate=cost(11000 * MIB, 9 * MIB),
    )(info, seg, seg, seg, comp, comp, mem, mem, lse, upstream)


def columns_of(rows):
    tall = jnp.concatenate([rows, jnp.zeros((120, rows.shape[1]), single)], axis=0)
    return jnp.transpose(tall)


def logits_kernel(words, tiles, info_ref, pair_ref, near_ref, table_ref, out_ref, stat_ref, held):
    step = pl.program_id(0)

    @pl.when(step < tiles)
    def _():
        held[...] = pair_ref[...]

    @pl.when(step >= tiles)
    def _():
        held[...] = near_ref[...]

    logits = mm(held[...], table_ref[...], NT)
    wanted = columns_of(info_ref[...])[:, 0:1].astype(jnp.int32)
    col = lax.broadcasted_iota(jnp.int32, logits.shape, 1)
    hit = jnp.sum(jnp.where(col == wanted, logits, 0.0), axis=-1, keepdims=True)
    logits = jnp.where(col < words, logits, -1e30)
    top = jnp.max(logits, axis=-1, keepdims=True)
    raised = jnp.exp(logits - top)
    total = jnp.sum(raised, axis=-1, keepdims=True)
    out_ref[...] = raised.astype(lowp)
    lane = lax.broadcasted_iota(jnp.int32, (logits.shape[0], 128), 1)
    packed = jnp.where(lane == 0, top, jnp.where(lane == 1, total, jnp.where(lane == 2, hit, 0.0)))
    stat_ref[...] = jnp.transpose(packed)[:8]


def logits_part(words, info, pair, near, table):
    rows = pair.shape[0] + near.shape[0]
    slots = table.shape[0]
    tile = 256
    tiles = pair.shape[0] // tile
    return pl.pallas_call(
        functools.partial(logits_kernel, words, tiles),
        name="logits_part",
        grid=(2 * tiles,),
        out_shape=(
            jax.ShapeDtypeStruct((rows, slots), lowp),
            jax.ShapeDtypeStruct((8, rows), single),
        ),
        in_specs=[
            pl.BlockSpec((8, tile), lambda i: (0, i)),
            pl.BlockSpec((tile, D), lambda i: (jnp.minimum(i, tiles - 1), 0)),
            pl.BlockSpec((tile, D), lambda i: (jnp.maximum(i - tiles, 0), 0)),
            pl.BlockSpec(table.shape, lambda i: (0, 0)),
        ],
        out_specs=(
            pl.BlockSpec((tile, slots), lambda i: (i, 0)),
            pl.BlockSpec((8, tile), lambda i: (0, i)),
        ),
        scratch_shapes=[pltpu.VMEM((tile, D), lowp)],
        compiler_params=params(60),
        cost_estimate=cost(4 * rows * slots * D, 10 * MIB),
    )(info, pair, near, table)


def logits_back_kernel(tiles, info_ref, factor_ref, in_ref, table_ref, out_ref, keep_ref, send_ref):
    step = pl.program_id(0)
    info = columns_of(info_ref[...])
    wanted = info[:, 0:1].astype(jnp.int32)
    counted = info[:, 1:2]
    factor = columns_of(factor_ref[...])[:, 0:1]
    raised = in_ref[...].astype(single)
    col = lax.broadcasted_iota(jnp.int32, raised.shape, 1)
    grads = (raised * factor - jnp.where(col == wanted, counted, 0.0)).astype(lowp)
    out_ref[...] = grads
    total = mm(grads, table_ref[...]).astype(lowp)

    @pl.when(step < tiles)
    def _():
        send_ref[...] = total

    @pl.when(step >= tiles)
    def _():
        keep_ref[...] = total


def logits_back(info, factor, raised, table):
    rows, slots = raised.shape
    tile = 256
    tiles = rows // (2 * tile)

    def at(i):
        return (i + tiles) % (2 * tiles)

    return pl.pallas_call(
        functools.partial(logits_back_kernel, tiles),
        name="logits_back",
        grid=(2 * tiles,),
        out_shape=(
            jax.ShapeDtypeStruct((rows, slots), lowp),
            jax.ShapeDtypeStruct((rows // 2, D), lowp),
            jax.ShapeDtypeStruct((rows // 2, D), lowp),
        ),
        in_specs=[
            pl.BlockSpec((8, tile), lambda i: (0, at(i))),
            pl.BlockSpec((8, tile), lambda i: (0, at(i))),
            pl.BlockSpec((tile, slots), lambda i: (at(i), 0)),
            pl.BlockSpec(table.shape, lambda i: (0, 0)),
        ],
        out_specs=(
            pl.BlockSpec((tile, slots), lambda i: (at(i), 0)),
            pl.BlockSpec((tile, D), lambda i: (jnp.maximum(i - tiles, 0), 0)),
            pl.BlockSpec((tile, D), lambda i: (jnp.minimum(i, tiles - 1), 0)),
        ),
        compiler_params=params(60),
        cost_estimate=cost(4 * rows * slots * D, 12 * MIB),
    )(info, factor, raised, table)


def halves(total, keep_ref, send_ref):
    half = keep_ref.shape[1]
    keep_ref[...] = total[:, :half]
    send_ref[...] = total[:, half:].astype(send_ref.dtype)


def table_grad_kernel(count, *refs):
    total = None
    for i in range(count):
        rows = refs[count + 2 * i].shape[0]
        for j in range(2):
            term = mm(refs[i][j * rows : (j + 1) * rows, :], refs[count + 2 * i + j][...], TN)
            total = term if total is None else total + term
    halves(total, *refs[3 * count :])


def table_grad_part(grads, inputs, part):
    count = len(grads)
    rows = sum(g.shape[0] for g in grads)
    slots = grads[0].shape[1] // 2
    block = 256
    first = part * (slots // block)
    if rows > 4096:
        total = sum(
            mm(split(g, 1, 2)[part], jnp.concatenate(v), TN) for g, v in zip(grads, inputs)
        )
        keep, send = split(total, 1, 2)
        return keep, send.astype(lowp)
    inputs = [half for pair in inputs for half in pair]
    return pl.pallas_call(
        functools.partial(table_grad_kernel, count),
        name="table_grad_part",
        grid=(slots // block,),
        out_shape=(
            jax.ShapeDtypeStruct((slots, D // 2), single),
            jax.ShapeDtypeStruct((slots, D // 2), lowp),
        ),
        in_specs=[pl.BlockSpec((g.shape[0], block), lambda i: (0, first + i)) for g in grads]
        + [pl.BlockSpec(v.shape, lambda i: (0, 0)) for v in inputs],
        out_specs=(
            pl.BlockSpec((block, D // 2), lambda i: (i, 0)),
            pl.BlockSpec((block, D // 2), lambda i: (i, 0)),
        ),
        compiler_params=params(60),
        cost_estimate=cost(3 * rows * slots * D, 30 * MIB),
    )(*grads, *inputs)


def hidden_grad_kernel(blocks, pre_ref, act_ref, in_ref, down_ref, keep_ref, send_ref):
    step = pl.program_id(0)

    @pl.when(step < blocks)
    def _():
        halves(mm(pre_ref[...], in_ref[...], TN), keep_ref, send_ref)

    @pl.when(step >= blocks)
    def _():
        halves(mm(act_ref[...], down_ref[...], TN), keep_ref, send_ref)


def hidden_grads(pre_grad, hidden_act, ffn_in, down_in):
    rows, hidden = pre_grad.shape
    block = 256
    blocks = hidden // block
    return pl.pallas_call(
        functools.partial(hidden_grad_kernel, blocks),
        name="hidden_grads",
        grid=(2 * blocks,),
        out_shape=(
            jax.ShapeDtypeStruct((2 * hidden, D // 2), single),
            jax.ShapeDtypeStruct((2 * hidden, D // 2), lowp),
        ),
        in_specs=[
            pl.BlockSpec((rows, block), lambda i: (0, jnp.minimum(i, blocks - 1))),
            pl.BlockSpec((rows, block), lambda i: (0, jnp.maximum(i - blocks, 0))),
            pl.BlockSpec((rows, D), lambda i: (0, 0)),
            pl.BlockSpec((rows, D), lambda i: (0, 0)),
        ],
        out_specs=(
            pl.BlockSpec((block, D // 2), lambda i: (i, 0)),
            pl.BlockSpec((block, D // 2), lambda i: (i, 0)),
        ),
        compiler_params=params(60),
        cost_estimate=cost(6 * rows * hidden * D, 16 * MIB),
    )(pre_grad, hidden_act, ffn_in, down_in)


def attn_grad_kernel(
    seg_ref, mixed_ref, mem_ref, old_ref, normed_ref, up_ref, mem_in_ref, old_in_ref, keep_ref, send_ref
):
    which = pl.program_id(0)

    @pl.when(which == 0)
    def _():
        halves(mm(seg_ref[...], normed_ref[...], TN), keep_ref, send_ref)

    @pl.when(which == 3)
    def _():
        halves(mm(mixed_ref[...], up_ref[...], TN), keep_ref, send_ref)

    @pl.when(jnp.logical_and(which > 0, which < 3))
    def _():
        total = mm(seg_ref[...], normed_ref[...], TN)
        total = total + mm(mem_ref[...], mem_in_ref[...], TN)
        total = total + mm(old_ref[...], old_in_ref[...], TN)
        halves(total, keep_ref, send_ref)


def attn_grads(seg_grad, mixed, mem_grad, old_grad, normed, attn_in, mem_in, old_in):
    block = mixed.shape[1]

    def whole(array):
        return pl.BlockSpec(array.shape, lambda i: (0, 0))

    return pl.pallas_call(
        attn_grad_kernel,
        name="attn_grads",
        grid=(4,),
        out_shape=(
            jax.ShapeDtypeStruct((4 * block, D // 2), single),
            jax.ShapeDtypeStruct((4 * block, D // 2), lowp),
        ),
        in_specs=[
            pl.BlockSpec((seg_grad.shape[0], block), lambda i: (0, jnp.minimum(i, 2))),
            whole(mixed),
            pl.BlockSpec((mem_grad.shape[0], block), lambda i: (0, jnp.clip(i - 1, 0, 1))),
            pl.BlockSpec((old_grad.shape[0], block), lambda i: (0, jnp.clip(i - 1, 0, 1))),
            whole(normed),
            whole(attn_in),
            whole(mem_in),
            whole(old_in),
        ],
        out_specs=(
            pl.BlockSpec((block, D // 2), lambda i: (i, 0)),
            pl.BlockSpec((block, D // 2), lambda i: (i, 0)),
        ),
        compiler_params=params(60),
        cost_estimate=cost(9000 * MIB, 24 * MIB),
    )(seg_grad, mixed, mem_grad, old_grad, normed, attn_in, mem_in, old_in)


def scalar_row(values, length=128):
    lane = jnp.arange(length, dtype=jnp.int32)
    row = jnp.zeros((length,), single)
    for i, value in enumerate(values):
        row = jnp.where(lane == i, value, row)
    return row


def local(
    ids,
    targets,
    target_mask,
    memory,
    old_states,
    mem_fill,
    comp_fill,
    table,
    qkv,
    wout,
    wconv,
    wup,
    wdown,
    gains,
    table_rows,
    table_cols,
    qkv_rows,
    qkv_cols,
    out_rows,
    out_cols,
    conv_rows,
    conv_cols,
    up_rows,
    up_cols,
    down_rows,
    down_cols,
    gains_second,
):
    dp_size, head_size = lax.axis_size("dp"), lax.axis_size("head")
    d, h = lax.axis_index("dp"), lax.axis_index("head")
    x, c = h // 2, h % 2
    order = block_order(dp_size)
    reach = dp_size // 2
    streams, seg_len = ids.shape
    half = seg_len // 2
    per_group = streams * seg_len
    vocab, width = table.shape
    assert head_size == 4 and streams == 2

    weights_now = (table, qkv, wout, wconv, wup, wdown)
    rows_old = (table_rows, qkv_rows, out_rows, conv_rows, up_rows, down_rows)
    cols_old = (table_cols, qkv_cols, out_cols, conv_cols, up_cols, down_cols)
    sizes = {"dp": dp_size, "head": head_size}
    row_axes = ("head", "dp", "head", "head", "dp", "head")
    col_axes = ("dp", "head", "dp", "dp", "head", "dp")
    early = [jnp.sum(old) / sizes[axis] for old, axis in zip(rows_old, col_axes)]
    early += [jnp.sum(weight * weight) for weight in weights_now]
    gain_sums = jnp.sum(gains * gains, axis=1) / head_size
    early = scalar_row(early + [gain_sums[0], gain_sums[1], gain_sums[2]])

    flat = jnp.concatenate(
        [
            ids.astype(single).reshape(-1),
            targets.astype(single).reshape(-1),
            target_mask.astype(single).reshape(-1),
            gains.astype(lowp).astype(single).reshape(-1),
        ]
    )
    room = -flat.shape[0] % 1024
    flat = jnp.concatenate([flat, jnp.zeros((room,), single)]).reshape(1, -1, 128)
    small, small_steps = gather_blocks(flat, 0)
    small = small.reshape(dp_size, -1)
    place = jnp.stack([x, d])

    def field(raw):
        return relative(raw.reshape(-1, 2, 2, half), x, c)

    ids_all = small[:, :per_group]
    position = [order.index(j) for j in range(dp_size)]
    ids_all = jnp.take(ids_all, jnp.asarray(position, jnp.int32)[jnp.arange(dp_size) ^ d], axis=0)
    ids_all = jnp.transpose(field(ids_all), (1, 2, 0, 3)).reshape(-1).astype(jnp.int32)
    table_rows_all = ids_all - h * vocab
    inside = (table_rows_all >= 0) & (table_rows_all < vocab)
    bits = vocab.bit_length()
    token_codes = (jnp.arange(ids_all.shape[0], dtype=jnp.int32) << bits) | table_rows_all
    token_codes = jnp.where(inside, token_codes, -1)
    table_rows_all = jnp.where(inside, table_rows_all, vocab)
    targets_all = field(small[:reach, per_group : 2 * per_group])
    mask_all = field(small[:reach, 2 * per_group : 3 * per_group])
    gain_blocks = small[:, 3 * per_group : 3 * per_group + 3 * width].reshape(dp_size, 3, width)
    gain_vals = jnp.swapaxes(gain_blocks, 0, 1).reshape(3, 1, D)
    count_all = jnp.sum(small[:, 2 * per_group : 3 * per_group])

    heads_own = wconv.shape[0]
    wide = qkv.shape[2]
    conv_rows_own = wconv.size // width
    low_qkv = qkv.astype(lowp)
    pack_one = jnp.concatenate(
        [
            jnp.swapaxes(low_qkv, 1, 2).reshape(3 * wide, width),
            wout.astype(lowp),
            wconv.astype(lowp).reshape(conv_rows_own, width),
        ]
    )
    own_half, far_half = split(table_rows_all, 0, 2)
    kept = {}

    def beside_lookup(moved):
        moved, kept["far"], kept["own"] = together(
            moved, lookup(far_half, table), lookup(own_half, table)
        )
        return moved

    def beside_memory(moved):
        looked = (kept["own"] + swap(kept["far"], "head", 1)).reshape(2, -1, width)
        mem_normed = state_norm(place, gain_vals[0], memory, 1)[0]
        moved, more, kept["mem"] = together(moved, swap(looked[1], "head", 2), mem_normed)
        looked = (looked[0] + more).reshape(dp_size, half, width)
        kept["looked"] = lax.all_to_all(looked, "dp", 0, 0)
        return moved

    own_one, steps_one = gather_blocks(
        after(pack_one, small_steps[0]), 1, (beside_lookup, beside_memory)
    )
    conv_lanes = jnp.arange(DH, dtype=jnp.int32)
    conv_width = DH // dp_size
    conv_natural = (jnp.asarray(order, jnp.int32)[conv_lanes // conv_width] ^ d) * conv_width
    conv_natural = conv_natural + conv_lanes % conv_width
    conv_shuffle = (conv_natural[:, None] == conv_lanes[None, :]).astype(lowp)
    taps = heads_own * RATE * DH

    def conv_natural_order(rows):
        value = jnp.swapaxes(rows.reshape(conv_rows_own, dp_size, width), 0, 1)
        value = jnp.swapaxes(value.reshape(dp_size, taps, conv_width), 0, 1)
        moved = mm(value.reshape(taps, DH), conv_shuffle).astype(lowp)
        return moved.reshape(heads_own, RATE * DH, DH)

    def conv_block_order(value):
        moved = mm(value.astype(lowp).reshape(taps, DH), conv_shuffle, NT).astype(lowp)
        moved = jnp.swapaxes(moved.reshape(taps, dp_size, conv_width), 0, 1)
        moved = jnp.swapaxes(moved.reshape(dp_size, conv_rows_own, width), 0, 1)
        return moved.reshape(conv_rows_own, D)

    full_conv = conv_natural_order(own_one[4 * wide :])

    hidden_own = wup.shape[1]
    pack_two = jnp.concatenate([wup.astype(lowp).T, wdown.astype(lowp)])

    def beside_old(moved):
        old_normed = state_norm(place, gain_vals[0], old_states, RATE)
        moved, kept["looked"], kept["old"] = together(moved, kept["looked"], old_normed)
        return moved

    def beside_compress(moved):
        moved, *kept["comp"] = together(moved, *compress(kept["old"], own_one, full_conv))
        return moved

    own_two, steps_two = gather_blocks(
        after(pack_two, steps_one[1]), 1, (beside_old, beside_compress)
    )
    mem_normed, old_normed = kept["mem"], kept["old"]
    comp, old_raw = kept["comp"]

    words = vocab // reach
    z = d // 2
    z_groups = [[2 * i + b for i in range(reach)] for b in range(2)]
    low_table = after(table.astype(lowp), steps_two[1]).reshape(reach, words, width)
    low_table = lax.all_to_all(low_table, "dp", 0, 0, axis_index_groups=z_groups)
    slots = -(-words // 256) * 256

    embedded_low, normed = place_embedding(place, kept["looked"], gain_vals[0])
    embedded = embedded_low.astype(single)

    comp_counts = jnp.where(x == 1, jnp.flip(comp_fill), comp_fill)
    mem_counts = jnp.where(x == 1, jnp.flip(mem_fill), mem_fill)
    info = jnp.stack([comp_counts[0], mem_counts[0], comp_counts[1], mem_counts[1], c * half])
    info = info.astype(jnp.int32)

    def core_sum(keep, send):
        more = swap(send.astype(lowp), "head", 1)
        return keep.astype(single) + more.astype(single)

    def stream_sum(part, beside=()):
        keep, send = split(part, 0, 2)
        more, *beside = together(swap(send.astype(lowp), "head", 2), *beside)
        part = keep + more.astype(single)
        return (part, beside) if beside else part

    def group_sum(part, beside=()):
        return stream_sum(core_sum(*split(part, 0, 2)), beside)

    def group_both(part, beside=()):
        far, *beside = together(swap(part, "head", 2), *beside)
        pair = jnp.concatenate([part, far], axis=0)
        both = (pair, swap(pair, "head", 1))
        return (both, beside) if beside else both

    normed = jnp.concatenate(group_both(normed))
    in_weight = own_one[: 3 * wide]
    mem = mm(mem_normed, own_one[wide : 3 * wide], NT).astype(lowp)
    seg = mm(normed, in_weight, NT).astype(lowp).reshape(2, streams, half, 3 * wide)
    mixed, lse = attend(info, seg, comp, mem)
    mixed = mixed.reshape(-1, wide)
    attn_sum, (own_codes, own_count, own_two, low_table) = group_sum(
        mm(mixed, own_one[3 * wide : 4 * wide]),
        (*own_list(after(token_codes, mixed)), own_two, low_table),
    )
    after_attn = embedded + attn_sum
    ffn_in, inv_second = rms(after_attn, gain_vals[1])
    ffn_in = jnp.concatenate(group_both(ffn_in))
    full_up, full_down = split(own_two, 0, 2)
    near_table = [
        lax.dynamic_index_in_dim(low_table, z ^ (m // 2), 0, keepdims=False) for m in order[:reach]
    ]
    near_table = jnp.concatenate(near_table, axis=1)
    far_table = swap(near_table, "dp", 1)
    loss_table = jnp.concatenate([near_table, far_table], axis=1)
    loss_table = jnp.concatenate([loss_table, jnp.zeros((slots - words, D), lowp)], axis=0)
    hidden_pre = mm(ffn_in, full_up, NT)
    hidden_act = jax.nn.gelu(hidden_pre).astype(lowp)
    after_ffn = after_attn + group_sum(mm(hidden_act, full_down))
    final_in, inv_third = rms(after_ffn, gain_vals[2])

    word_start = (h * vocab + z * words).astype(single)
    wanted_all = targets_all - word_start
    wanted_all = jnp.where((wanted_all >= 0) & (wanted_all < words), wanted_all, -1.0)
    info_all = jnp.stack([wanted_all, mask_all] + [jnp.zeros_like(mask_all)] * 6)
    info_all = jnp.transpose(info_all, (1, 0, 2, 3, 4)).reshape(reach, 8, per_group)
    pieces = [final_in]
    chunks = []
    raised = []
    stats = []

    def next_chunk():
        i = len(chunks)
        if i == 0:
            chunks.append(group_both(pieces[i]))
        else:
            chunk, (stats[i - 1],) = group_both(pieces[i], (stats[i - 1],))
            chunks.append(chunk)
        out, stat = logits_part(words, info_all[i], *chunks[i], loss_table)
        raised.append(out)
        stats.append(stat)

    mask = dp_size // 2
    while mask > 1:
        joined = jnp.concatenate(pieces) if len(pieces) > 1 else pieces[0]
        moved = swap(reorder(joined, mask), "dp", mask)
        if len(pieces) == 1:
            moved, loss_table, early = together(moved, loss_table, early)
            next_chunk()
        elif len(pieces) == 2:
            moved, stats[0] = together(moved, stats[0])
        pieces += split(moved, 0, len(pieces))
        mask //= 2
    while len(chunks) < reach:
        next_chunk()
    stats = [stat[:3].reshape(3, 1, 2, 2, half) for stat in stats]
    own_stats = jnp.concatenate(stats, axis=1)

    def combine(first, second):
        top = jnp.maximum(first[0], second[0])
        total = first[1] * jnp.exp(first[0] - top) + second[1] * jnp.exp(second[0] - top)
        return jnp.stack([top, total, first[2] + second[2]])

    merged = own_stats
    merged = combine(merged, jnp.flip(swap(merged, "head", 1), 2))
    merged = combine(merged, jnp.flip(swap(merged, "head", 2), 3))
    mask = 2
    while mask < dp_size:
        other = split(swap(merged, "dp", mask), 1, reach)
        other = [other[order.index(j ^ mask)] for j in order[:reach]]
        merged = combine(merged, jnp.concatenate(other, axis=1))
        mask *= 2
    log_total = merged[0] + jnp.log(merged[1])
    loss_local = jnp.sum(mask_all[0, 0, 0] * (log_total[0, 0, 0] - merged[2, 0, 0, 0]))
    factor_all = jnp.exp(own_stats[0] - log_total)

    factor_all = factor_all.reshape(reach, 1, per_group) * info_all[:, 1:2]
    factor_all = jnp.broadcast_to(factor_all, info_all.shape)
    dlogits = [None] * reach
    parts = [None] * reach
    for i in reversed(range(reach)):
        dlogits[i], *core = logits_back(info_all[i], factor_all[i], raised[i], loss_table)
        if i + 1 < reach:
            parts[i + 1], (dlogits[i], *core) = stream_sum(parts[i + 1], (dlogits[i], *core))
        parts[i] = core_sum(*core)
    parts[0] = stream_sum(parts[0])
    table_parts = []
    mask = 2
    while len(parts) > 1:
        count = len(parts) // 2
        moved = jnp.concatenate([part.astype(lowp) for part in parts[count:]])
        moved = swap(reorder(moved, mask), "dp", mask)
        if len(table_parts) < 2:
            more = table_grad_part(dlogits, chunks, len(table_parts))
            moved, *more = together(moved, *more, *[part[1] for part in table_parts])
            table_parts = [(part[0], done) for part, done in zip(table_parts, more[2:])]
            table_parts.append((more[0], swap(more[1], "dp", 1)))
        moved = split(moved.astype(single), 0, count)
        parts = [part + more for part, more in zip(parts, moved)]
        mask *= 2
    final_grad = parts[0]

    grad_after_ffn = rms_back(after_ffn, inv_third, gain_vals[2], final_grad)
    moved_table = [part[1] for part in table_parts]
    down_in, (moved_table[1],) = group_both(grad_after_ffn.astype(lowp), (moved_table[1],))
    down_in = jnp.concatenate(down_in)
    act_grad = mm(down_in, full_down, NT)
    pre_grad = jax.vjp(jax.nn.gelu, hidden_pre)[1](act_grad)[0].astype(lowp)
    two = hidden_grads(pre_grad, hidden_act, ffn_in, down_in)
    ffn_in_grad, two = group_sum(mm(pre_grad, full_up), two)
    keep = [part + more.astype(single) for (part, _), more in zip(table_parts, moved_table)]
    keep = jnp.concatenate(keep)
    table_pieces = jnp.stack(split(keep[:words].astype(lowp), 1, reach))
    position = [order.index(2 * i) for i in range(reach)]
    position = jnp.asarray(position, jnp.int32)[jnp.arange(reach) ^ z]
    table_pieces = jnp.concatenate(
        [lax.dynamic_index_in_dim(table_pieces, position[i], 0) for i in range(reach)]
    )
    table_pieces = lax.all_to_all(table_pieces, "dp", 0, 0, axis_index_groups=z_groups)
    grad_after_attn = grad_after_ffn + rms_back(after_attn, inv_second, gain_vals[1], ffn_in_grad)
    attn_in = jnp.concatenate(group_both(grad_after_attn.astype(lowp)))

    mixed_grad = mm(attn_in, own_one[3 * wide : 4 * wide], NT).astype(lowp)
    mixed_grad = mixed_grad.reshape(2, streams, half, wide)
    def beside_attend(moved):
        grads = attend_back(info, seg, comp, mem, lse, mixed_grad)
        moved, kept["table"], *kept["grads"] = together(moved, table_pieces, *grads)
        return moved

    def beside_sums(moved):
        seg_grad, comp_grad, mem_grad = kept["grads"]
        seg_grad = seg_grad.reshape(-1, 3 * wide)
        seg_in = core_sum(*split(mm(seg_grad, in_weight), 0, 2))
        seg_in_far = swap(seg_in[half:].astype(lowp), "head", 2)
        old_grad, conv_sum = expand(comp_grad, old_raw, full_conv)
        sums = attn_grads(
            seg_grad,
            mixed,
            mem_grad,
            old_grad.reshape(-1, old_grad.shape[-1]),
            normed,
            attn_in,
            mem_normed,
            old_normed.reshape(-1, D),
        )
        conv_sum = split(conv_block_order(conv_sum), 1, 2)
        sums = [jnp.concatenate([part, more.astype(part.dtype)]) for part, more in zip(sums, conv_sum)]
        moved, seg_in_far, *kept["sums"] = together(moved, seg_in_far, *sums)
        rows_grad = embed_back(
            place, embedded_low, gain_vals[0], seg_in[:half], seg_in_far, grad_after_attn
        )
        kept["rows"] = lax.all_to_all(rows_grad, "dp", 0, 0)
        return moved

    def beside_rows(moved):
        moved, kept["rows"] = together(moved, kept["rows"])
        return moved

    def beside_streams(moved):
        moved, far = together(moved, swap(kept["rows"], "head", 2))
        kept["rows"] = jnp.stack([kept["rows"], far])
        return moved

    two = reduce_blocks(*two, (beside_attend, beside_sums))
    one = reduce_blocks(*kept["sums"], (beside_rows, beside_streams))
    rows_grad = kept["rows"]
    rows_grad = jnp.stack([rows_grad, swap(rows_grad, "head", 1)]).reshape(-1, width)
    table_base = kept["table"].astype(single).reshape(vocab, width)

    up_grad = two[:hidden_own].T
    down_grad = two[hidden_own:]
    qkv_grad = jnp.swapaxes(one[: 3 * wide].reshape(3, wide, width), 1, 2)
    out_grad = one[3 * wide : 4 * wide]
    conv_grad = one[4 * wide :].reshape(wconv.shape)
    table_grad = scatter(bits, own_count, own_codes, table_base, rows_grad)

    gains_low = gains.astype(lowp).astype(single)
    gain_part = jnp.stack(
        [
            jnp.sum(low_qkv.astype(single) * qkv_grad, axis=(0, 2)),
            jnp.sum(wup.astype(lowp).astype(single) * up_grad, axis=1),
            jnp.sum(table.astype(lowp).astype(single) * table_base, axis=0),
        ]
    )

    grads = (table_grad, qkv_grad, out_grad, conv_grad, up_grad, down_grad)
    def sum_over_dp(joined):
        mask = 1
        while mask < dp_size:
            joined = joined + swap(joined, "dp", mask)
            mask *= 2
        return joined

    row_part = []
    col_part = []
    for grad in grads:
        square = grad * grad
        row_part.append(jnp.sum(square, axis=-1))
        col_part.append(jnp.sum(square, axis=tuple(range(square.ndim - 1))))
    row_q, row_u, col_e, col_o, col_c, col_d, gain_raw, early = lax.psum(
        (
            row_part[1],
            row_part[4],
            col_part[0],
            col_part[2],
            col_part[3],
            col_part[5],
            gain_part,
            early + scalar_row([0.0] * 15 + [loss_local]),
        ),
        "head",
    )
    lanes = [col_e, jnp.sum(row_q, axis=0), col_o]
    lanes += [jnp.concatenate([col_c, jnp.zeros((width - col_c.shape[0],), single)]), row_u, col_d]
    members = [col_part[4], row_part[5], row_part[3], row_part[2], col_part[1], *lanes, row_part[0], early]
    joined = jnp.concatenate([m.reshape(-1) for m in members])
    joined = sum_over_dp(jnp.concatenate([joined, jnp.zeros((-joined.shape[0] % 1024,), single)]))
    sums = []
    start = 0
    for member in members:
        sums.append(joined[start : start + member.size].reshape(member.shape))
        start += member.size
    col_u, row_d, row_c, row_o, col_q, *lanes, row_e, early = sums
    square_total = [jnp.sum(lane) for lane in lanes]
    row_sums = [row_e, row_q, row_o, row_c, row_u, row_d]
    col_sums = [col_e, col_q, col_o, col_c, col_u, col_d]
    weight_total = early[6:15]
    loss_all = early[15]
    inverse = 1.0 / count_all
    decay = 1.0 - STEP ** (-0.8)
    updates = []
    stats_new = []
    scaled = []
    counts = []
    update_sq = []
    for index in range(6):
        rows_total = rows_old[index].size * sizes[row_axes[index]]
        cols_total = cols_old[index].size * sizes[col_axes[index]]
        grad_scaled = grads[index] * inverse
        rows_new = decay * rows_old[index] + (1.0 - decay) * (
            row_sums[index] * inverse * inverse / cols_total + TINY_SQUARE
        )
        cols_new = decay * cols_old[index] + (1.0 - decay) * (
            col_sums[index] * inverse * inverse / rows_total + TINY_SQUARE
        )
        mean_row = decay * early[index] / rows_total + (1.0 - decay) * (
            square_total[index] * inverse * inverse / (rows_total * cols_total) + TINY_SQUARE
        )
        second = rows_new[..., None] * cols_new / mean_row
        direction = grad_scaled * lax.rsqrt(second)
        updates.append(direction)
        stats_new.append((rows_new, cols_new))
        scaled.append(grad_scaled)
        counts.append(rows_total * cols_total)
        update_sq.append(jnp.sum(direction * direction))
    gain_scaled = gain_raw / gains_low * inverse
    second_new = decay * gains_second + (1.0 - decay) * (gain_scaled * gain_scaled + TINY_SQUARE)
    gain_dir = gain_scaled * lax.rsqrt(second_new)
    for which in range(3):
        update_sq.append(jnp.sum(gain_dir[which] * gain_dir[which]) / head_size)
    update_total = after(scalar_row(update_sq, 1024), loss_all)
    for mask in (1, 2):
        update_total = update_total + swap(update_total, "head", mask)
    update_total = sum_over_dp(update_total)[:9]
    results = [loss_all, count_all]
    for index in range(6):
        factor = jnp.maximum(0.001, jnp.sqrt(weight_total[index] / counts[index]))
        denom = jnp.maximum(1.0, jnp.sqrt(update_total[index] / counts[index]) / CLIP_LEVEL)
        new_weight = weights_now[index] - LEARN_RATE * factor * updates[index] / denom
        results += [new_weight, scaled[index], stats_new[index][0], stats_new[index][1]]
    gain_factor = jnp.maximum(0.001, jnp.sqrt(weight_total[6:] / D))[:, None]
    gain_denom = jnp.maximum(1.0, jnp.sqrt(update_total[6:] / D) / CLIP_LEVEL)[:, None]
    results += [gains - LEARN_RATE * gain_factor * gain_dir / gain_denom, gain_scaled, second_new]
    return tuple(results)


def solution(mesh):
    in_specs = (
        P("dp", None),
        P("dp", None),
        P("dp", None),
        P("dp", None, None),
        P("dp", None, None),
        P("dp"),
        P("dp"),
        P("head", "dp"),
        P(None, "dp", "head"),
        P("head", "dp"),
        P("head", None, "dp"),
        P("dp", "head"),
        P("head", "dp"),
        P(None, "dp"),
        P("head"),
        P("dp"),
        P(None, "dp"),
        P("head"),
        P("head"),
        P("dp"),
        P("head", None),
        P("dp"),
        P("dp"),
        P("head"),
        P("head"),
        P("dp"),
        P(None, "dp"),
    )
    out_specs = (
        P(),
        P(),
        P("head", "dp"),
        P("head", "dp"),
        P("head"),
        P("dp"),
        P(None, "dp", "head"),
        P(None, "dp", "head"),
        P(None, "dp"),
        P("head"),
        P("head", "dp"),
        P("head", "dp"),
        P("head"),
        P("dp"),
        P("head", None, "dp"),
        P("head", None, "dp"),
        P("head", None),
        P("dp"),
        P("dp", "head"),
        P("dp", "head"),
        P("dp"),
        P("head"),
        P("head", "dp"),
        P("head", "dp"),
        P("head"),
        P("dp"),
        P(None, "dp"),
        P(None, "dp"),
        P(None, "dp"),
    )
    return jax.shard_map(local, mesh=mesh, in_specs=in_specs, out_specs=out_specs, check_vma=False)
```

```python
import functools

import jax
import jax.numpy as jnp
from jax import lax
from jax.experimental import pallas as pl
from jax.experimental.pallas import tpu as pltpu
from jax.sharding import PartitionSpec as P

D = 1024
H = 8
DH = 128
MEM = 512
CMEM = 512
RATE = 3
STEP = 10


TINY_NORM = 1e-06
TINY_SQUARE = 1e-30
LEARN_RATE = 0.5
CLIP_LEVEL = 1.0

lowp = jnp.bfloat16
single = jnp.float32
NT = (((1,), (1,)), ((), ()))
TN = (((0,), (0,)), ((), ()))
NN = (((1,), (0,)), ((), ()))
MIB = 1024 * 1024


def mm(left, right, dims=NN):
    return lax.dot_general(left, right, dims, preferred_element_type=single)


def swap(value, axis, mask):
    size = lax.axis_size(axis)
    return lax.ppermute(value, axis, [(i, i ^ mask) for i in range(size)])


def after(value, *deps):
    return lax.optimization_barrier((value, *deps))[0]


def together(*values):
    return lax.optimization_barrier(values)


def block_order(size):
    order = [0]
    step = size // 2
    while step:
        order = order + [j + step for j in order]
        step //= 2
    return order


def gather_blocks(piece, axis, beside=(), stop=0):
    steps = []
    mask = lax.axis_size("dp") // 2
    while mask > stop:
        moved = swap(piece, "dp", mask)
        if len(steps) < len(beside):
            moved = beside[len(steps)](moved)
        piece = jnp.concatenate([piece, moved], axis=axis)
        steps.append(piece)
        mask //= 2
    return piece, steps


def split(value, axis, parts):
    width = value.shape[axis] // parts
    return [lax.slice_in_dim(value, i * width, (i + 1) * width, axis=axis) for i in range(parts)]


def reduce_blocks(keep, send, beside=(), mask=1):
    moved = swap(send.astype(lowp), "dp", mask)
    if beside:
        moved = beside[0](moved)
    total = keep + moved.astype(single)
    mask *= 2
    if mask == lax.axis_size("dp"):
        return total
    return reduce_blocks(*split(total, 1, 2), beside[1:], mask)


def reorder_kernel(sources, in_ref, out_ref):
    width = in_ref.shape[1] // len(sources)
    for p, q in enumerate(sources):
        out_ref[:, p * width : (p + 1) * width] = in_ref[:, q * width : (q + 1) * width]


def reorder(value, mask):
    order = block_order(lax.axis_size("dp"))
    sources = [order.index(j ^ mask) for j in order]
    if value.shape[1] // len(order) % 128:
        cols = split(value, 1, len(order))
        return jnp.concatenate([cols[q] for q in sources], axis=1)
    return pl.pallas_call(
        functools.partial(reorder_kernel, sources),
        name="reorder",
        out_shape=jax.ShapeDtypeStruct(value.shape, value.dtype),
        in_specs=[vmem()],
        out_specs=vmem(),
        compiler_params=params(60),
        cost_estimate=cost(0, 2 * MIB),
    )(value)


def relative(value, x, c):
    value = jnp.where(x == 1, jnp.flip(value, -3), value)
    value = jnp.where(c == 1, jnp.flip(value, -2), value)
    return jnp.swapaxes(value, -3, -2)


def rms(values, gain):
    inv = lax.rsqrt(jnp.mean(values * values, axis=-1, keepdims=True) + TINY_NORM)
    return (values * inv * gain).astype(lowp), inv


def rms_back(values, inv, gain, upstream):
    scaled = gain * upstream
    inner = jnp.sum(scaled * values, axis=-1, keepdims=True) / D
    return scaled * inv - values * (inner * inv * inv * inv)


def vmem(shape=None, index=None):
    if shape is None:
        return pl.BlockSpec(memory_space=pltpu.VMEM)
    return pl.BlockSpec(shape, index)


def smem():
    return pl.BlockSpec(memory_space=pltpu.SMEM)


def params(mib):
    return pltpu.CompilerParams(vmem_limit_bytes=mib * MIB)


def cost(flops, size, exps=0):
    return pl.CostEstimate(
        flops=int(0.02 * flops), bytes_accessed=int(0.02 * size), transcendentals=exps
    )


def lookup_kernel(row_ref, table_ref, out_ref, tab, held, sem):
    total = row_ref.shape[0]
    vocab = table_ref.shape[0]
    copy = pltpu.make_async_copy(table_ref, tab.at[pl.ds(0, vocab)], sem)
    copy.start()
    tab[pl.ds(vocab, 8), :] = jnp.zeros((8, tab.shape[1]), single)
    copy.wait()

    @pl.loop(0, total // 16)
    def _(g):
        for j in range(16):
            t = g * 16 + j
            held[pl.ds(t, 1), :] = tab[pl.ds(row_ref[t], 1), :]

    @pl.loop(0, total // 512)
    def _(i):
        rows = pl.ds(pl.multiple_of(i * 512, 512), 512)
        out_ref[rows, :] = held[rows, :].astype(lowp)


def lookup(rows, table):
    total = rows.shape[0]
    vocab, width = table.shape
    return pl.pallas_call(
        lookup_kernel,
        name="lookup",
        out_shape=jax.ShapeDtypeStruct((total, width), lowp),
        in_specs=[smem(), pl.BlockSpec(memory_space=pl.ANY)],
        out_specs=vmem(),
        scratch_shapes=[
            pltpu.VMEM((vocab + 8, width), single),
            pltpu.VMEM((total, width), single),
            pltpu.SemaphoreType.DMA(()),
        ],
        compiler_params=params(60),
        cost_estimate=cost(0, 30 * MIB),
    )(rows, table)


def list_kernel(code_ref, out_ref, count_ref):
    total = code_ref.shape[0]

    def group(g, count):
        for j in range(16):
            code = code_ref[g * 16 + j]
            out_ref[count] = code
            count = count + jnp.where(code >= 0, 1, 0)
        return count

    count_ref[0] = lax.fori_loop(0, total // 16, group, jnp.int32(0))


def own_list(codes):
    total = codes.shape[0]
    return pl.pallas_call(
        list_kernel,
        name="own_list",
        out_shape=(
            jax.ShapeDtypeStruct((total + 8,), jnp.int32),
            jax.ShapeDtypeStruct((1,), jnp.int32),
        ),
        in_specs=[smem()],
        out_specs=(smem(), smem()),
        cost_estimate=cost(0, 60 * MIB),
    )(codes)


def place_kernel(order, place_ref, in_ref, gain_ref, out_ref, norm_ref, held):
    width = in_ref.shape[2]
    for p, j in enumerate(order):
        block = in_ref[pl.ds(place_ref[1] ^ j, 1)][0]
        out_ref[:, p * width : (p + 1) * width] = block
        held[:, p * width : (p + 1) * width] = block.astype(single)
    values = held[...]
    inv = lax.rsqrt(jnp.mean(values * values, axis=-1, keepdims=True) + TINY_NORM)
    norm_ref[...] = (values * inv * gain_ref[...]).astype(lowp)


def place_embedding(place, blocks, gain):
    rows = blocks.shape[1]
    return pl.pallas_call(
        functools.partial(place_kernel, block_order(blocks.shape[0])),
        name="place_embedding",
        out_shape=(jax.ShapeDtypeStruct((rows, D), lowp), jax.ShapeDtypeStruct((rows, D), lowp)),
        in_specs=[smem(), vmem(), vmem()],
        out_specs=(vmem(), vmem()),
        scratch_shapes=[pltpu.VMEM((rows, D), single)],
        compiler_params=params(60),
        cost_estimate=cost(0, 3 * MIB),
    )(place, blocks, gain)


def embed_back_kernel(order, place_ref, in_ref, gain_ref, keep_ref, more_ref, grad_ref, out_ref, held):
    values = in_ref[...].astype(single)
    inv = lax.rsqrt(jnp.mean(values * values, axis=-1, keepdims=True) + TINY_NORM)
    upstream = keep_ref[...] + more_ref[...].astype(single)
    held[...] = grad_ref[...] + rms_back(values, inv, gain_ref[...], upstream)
    width = out_ref.shape[2]
    for p, j in enumerate(order):
        block = held[:, p * width : (p + 1) * width].astype(lowp)
        out_ref[pl.ds(place_ref[1] ^ j, 1)] = block[None]


def embed_back(place, values, gain, keep, more, grad):
    rows = values.shape[0]
    size = lax.axis_size("dp")
    return pl.pallas_call(
        functools.partial(embed_back_kernel, block_order(size)),
        name="embed_back",
        out_shape=jax.ShapeDtypeStruct((size, rows, D // size), lowp),
        in_specs=[smem()] + [vmem()] * 5,
        out_specs=vmem(),
        scratch_shapes=[pltpu.VMEM((rows, D), single)],
        compiler_params=params(60),
        cost_estimate=cost(0, 4 * MIB),
    )(place, values, gain, keep, more, grad)


def scatter_kernel(bits, count_ref, code_ref, base_ref, grad_ref, out_ref, rows):
    total = grad_ref.shape[0]
    vocab = base_ref.shape[0]

    @pl.loop(0, total // 512)
    def _(i):
        here = pl.ds(pl.multiple_of(i * 512, 512), 512)
        rows[here, :] = grad_ref[here, :].astype(single)

    rows[pl.ds(total, 8), :] = jnp.zeros((8, rows.shape[1]), single)

    @pl.loop(0, vocab // 400)
    def _(i):
        here = pl.ds(pl.multiple_of(i * 400, 400), 400)
        out_ref[here, :] = base_ref[here, :]

    count = count_ref[0]

    def group(g, carry):
        for j in range(8):
            index = g * 8 + j
            code = jnp.where(index < count, code_ref[index], total << bits)
            token = lax.shift_right_logical(code, bits)
            row = code & ((1 << bits) - 1)
            out_ref[pl.ds(row, 1), :] = out_ref[pl.ds(row, 1), :] + rows[pl.ds(token, 1), :]
        return carry

    lax.fori_loop(0, (count + 7) // 8, group, jnp.int32(0))


def scatter(bits, count, codes, base, grad):
    total, width = grad.shape
    return pl.pallas_call(
        functools.partial(scatter_kernel, bits),
        name="scatter",
        out_shape=jax.ShapeDtypeStruct(base.shape, single),
        in_specs=[smem(), smem(), vmem(), vmem()],
        out_specs=vmem(),
        scratch_shapes=[pltpu.VMEM((total + 8, width), single)],
        compiler_params=params(60),
        cost_estimate=cost(0, 30 * MIB),
    )(count, codes, base, grad)


def state_kernel(order, width, place_ref, gain_ref, in_ref, out_ref, held):
    rows = in_ref.shape[1]
    values = in_ref[0].astype(single)
    inv = lax.rsqrt(jnp.mean(values * values, axis=-1, keepdims=True) + TINY_NORM)
    for p, j in enumerate(order):
        start = pl.multiple_of((place_ref[1] ^ j) * width, width)
        block = in_ref[0, :, pl.ds(start, width)].astype(single)
        held[p] = block * inv * gain_ref[:, p * width : (p + 1) * width]
    groups = out_ref.shape[0]
    for p in range(len(order)):
        cols = slice(p * width, (p + 1) * width)
        if groups == 1:
            out_ref[0, :, cols] = held[p].astype(lowp)
        else:
            for j in range(groups):
                part = held[p, pl.ds(j, rows // groups, stride=groups), :]
                out_ref[j, :, cols] = part.astype(lowp)


def state_norm(place, gain, states, groups):
    size = lax.axis_size("dp")
    order = block_order(size)
    width = D // size
    streams = states.shape[0]
    count = states.shape[1] // groups
    if width % 128:
        values = jnp.where(place[0] == 1, jnp.flip(states, 0), states).astype(single).reshape(-1, D)
        inv = lax.rsqrt(jnp.mean(values * values, axis=-1, keepdims=True) + TINY_NORM)
        lanes = jnp.arange(D, dtype=jnp.int32)
        blocks = jnp.asarray(order, jnp.int32)[lanes // width] ^ place[1]
        source = blocks * width + lanes % width
        shuffle = (lanes[:, None] == source[None, :]).astype(single)
        moved = jnp.dot(values * inv, shuffle, precision=lax.Precision.HIGHEST)
        out = (moved * gain).astype(lowp)
        return jnp.swapaxes(out.reshape(streams * count, groups, D), 0, 1)
    tile = 128
    return pl.pallas_call(
        functools.partial(state_kernel, order, width),
        name="state_norm",
        out_shape=jax.ShapeDtypeStruct((groups, streams * count, D), lowp),
        grid_spec=pltpu.PrefetchScalarGridSpec(
            num_scalar_prefetch=1,
            grid=(streams, count // tile),
            in_specs=[
                pl.BlockSpec((1, D), lambda n, i, s: (0, 0)),
                pl.BlockSpec((1, tile * groups, D), lambda n, i, s: (s[0] ^ n, i, 0)),
            ],
            out_specs=pl.BlockSpec(
                (groups, tile, D), lambda n, i, s: (0, n * (count // tile) + i, 0)
            ),
            scratch_shapes=[pltpu.VMEM((len(order), tile * groups, width), single)],
        ),
        compiler_params=params(60),
        cost_estimate=cost(0, 4 * streams * count * groups * D),
    )(place, gain, states)


def compress_kernel(old_ref, key_ref, value_ref, conv_ref, comp_ref, raw_ref):
    heads = conv_ref.shape[0]
    wide = heads * DH
    for part, weight_ref in enumerate((key_ref, value_ref)):
        sums = [None] * heads
        for j in range(RATE):
            raw = mm(old_ref[j], weight_ref[...], NT).astype(lowp)
            raw_ref[j, :, part * wide : (part + 1) * wide] = raw
            for n in range(heads):
                piece = raw[:, n * DH : (n + 1) * DH]
                term = mm(piece, conv_ref[n, j * DH : (j + 1) * DH, :])
                sums[n] = term if j == 0 else sums[n] + term
        for n in range(heads):
            first = part * wide + n * DH
            comp_ref[:, first : first + DH] = sums[n].astype(lowp)


def compress(old3, weights, conv):
    rows = old3.shape[1]
    wide = conv.shape[0] * DH
    tile = 256
    return pl.pallas_call(
        compress_kernel,
        name="compress",
        grid=(rows // tile,),
        out_shape=(
            jax.ShapeDtypeStruct((rows, 2 * wide), lowp),
            jax.ShapeDtypeStruct((RATE, rows, 2 * wide), lowp),
        ),
        in_specs=[
            pl.BlockSpec((RATE, tile, D), lambda i: (0, i, 0)),
            pl.BlockSpec((wide, D), lambda i: (1, 0)),
            pl.BlockSpec((wide, D), lambda i: (2, 0)),
            pl.BlockSpec(conv.shape, lambda i: (0, 0, 0)),
        ],
        out_specs=(
            pl.BlockSpec((tile, 2 * wide), lambda i: (i, 0)),
            pl.BlockSpec((RATE, tile, 2 * wide), lambda i: (0, i, 0)),
        ),
        compiler_params=params(60),
        cost_estimate=cost(4 * RATE * rows * wide * D, 12 * MIB),
    )(old3, weights, weights, conv)


def expand_kernel(grad_ref, raw_ref, conv_ref, out_ref, conv_out_ref):
    heads = conv_ref.shape[0]
    for h in range(heads):
        for j in range(RATE):
            rows = slice(j * DH, (j + 1) * DH)
            taps = conv_ref[h, rows, :]
            total = None
            for n in (h, heads + h):
                cols = slice(n * DH, (n + 1) * DH)
                grad = grad_ref[:, cols]
                out_ref[j, :, cols] = mm(grad, taps, NT).astype(lowp)
                term = mm(raw_ref[j, :, cols], grad, TN)
                total = term if total is None else total + term
            conv_out_ref[h, rows, :] = total


def expand(grad, raw, conv):
    return pl.pallas_call(
        expand_kernel,
        name="expand",
        out_shape=(
            jax.ShapeDtypeStruct(raw.shape, lowp),
            jax.ShapeDtypeStruct(conv.shape, single),
        ),
        in_specs=[vmem()] * 3,
        out_specs=(vmem(), vmem()),
        compiler_params=params(60),
        cost_estimate=cost(2000 * MIB, 12 * MIB),
    )(grad, raw, conv)


def masked_scores(info_ref, query, keys):
    rows = query.shape[0]
    scale = DH ** (-0.5)
    result = []
    for which, key in enumerate(keys):
        slots = key.shape[0]
        col = lax.broadcasted_iota(jnp.int32, (rows, slots), 1)
        if which < 2:
            seen = col >= slots - info_ref[2 * pl.program_id(0) + which]
        else:
            row = lax.broadcasted_iota(jnp.int32, (rows, slots), 0)
            shift = info_ref[4]
            row = row + shift
            col = col + shift
            row = jnp.where(row >= slots, row - slots, row)
            col = jnp.where(col >= slots, col - slots, col)
            seen = col <= row
        result.append(jnp.where(seen, mm(query, key, NT) * scale, -1e30))
    return result


def rows_of(ref):
    return ref[...].reshape(-1, ref.shape[-1])


def attend_kernel(info_ref, q_ref, ks_ref, vs_ref, kc_ref, vc_ref, km_ref, vm_ref, out_ref, lse_ref):
    query = rows_of(q_ref)
    scores = masked_scores(info_ref, query, [kc_ref[...], km_ref[...], rows_of(ks_ref)])
    top = functools.reduce(jnp.maximum, [jnp.max(s, axis=-1, keepdims=True) for s in scores])
    total = 0.0
    mixed = 0.0
    for score, value in zip(scores, (vc_ref[...], vm_ref[...], rows_of(vs_ref))):
        weight = jnp.exp(score - top)
        total = total + jnp.sum(weight, axis=-1, keepdims=True)
        mixed = mixed + mm(weight.astype(lowp), value)
    out_ref[...] = (mixed / total).astype(lowp).reshape(out_ref.shape)
    lse_ref[0, 0] = top + jnp.log(total)


def attend_back_kernel(
    info_ref, q_ref, ks_ref, vs_ref, kc_ref, vc_ref, km_ref, vm_ref, lse_ref, up_ref,
    seg_ref, comp_ref, mem_ref,
):
    head = pl.program_id(1)
    wide = pl.num_programs(1) * DH
    scale = DH ** (-0.5)
    query = rows_of(q_ref)
    upstream = rows_of(up_ref)
    keys = [kc_ref[...], km_ref[...], rows_of(ks_ref)]
    scores = masked_scores(info_ref, query, keys)
    probs = [jnp.exp(s - lse_ref[0, 0]) for s in scores]
    prob_grads = [
        mm(upstream, v, NT) for v in (vc_ref[...], vm_ref[...], rows_of(vs_ref))
    ]
    inner = 0.0
    for p, g in zip(probs, prob_grads):
        inner = inner + jnp.sum(p * g, axis=-1, keepdims=True)
    here = pl.ds(pl.multiple_of(head * DH, DH), DH)
    second = pl.ds(pl.multiple_of(wide + head * DH, DH), DH)
    third = pl.ds(pl.multiple_of(2 * wide + head * DH, DH), DH)
    query_grad = 0.0
    places = ((comp_ref, here, second), (mem_ref, here, second), (seg_ref, second, third))
    for p, g, key, (ref, key_at, value_at) in zip(probs, prob_grads, keys, places):
        score_grad = (p * (g - inner)).astype(lowp)
        query_grad = query_grad + mm(score_grad, key)
        shape = ref.shape[:-1] + (DH,)
        key_grad = (mm(score_grad, query, TN) * scale).astype(lowp)
        value_grad = mm(p.astype(lowp), upstream, TN).astype(lowp)
        ref[..., key_at] = key_grad.reshape(shape)
        ref[..., value_at] = value_grad.reshape(shape)
    shape = seg_ref.shape[:-1] + (DH,)
    seg_ref[..., here] = (query_grad * scale).astype(lowp).reshape(shape)


def head_specs(seg, comp, mem, heads):
    streams = seg.shape[1]

    def of_seg(first):
        return pl.BlockSpec((2, 1, seg.shape[2], DH), lambda n, h: (0, n, 0, first + h))

    def cols(array, first):
        return pl.BlockSpec((array.shape[0] // streams, DH), lambda n, h: (n, first + h))

    return [
        smem(),
        of_seg(0),
        of_seg(heads),
        of_seg(2 * heads),
        cols(comp, 0),
        cols(comp, heads),
        cols(mem, 0),
        cols(mem, heads),
    ]


def attend(info, seg, comp, mem):
    _, streams, half, _ = seg.shape
    heads = comp.shape[1] // (2 * DH)
    return pl.pallas_call(
        attend_kernel,
        name="attend",
        grid=(streams, heads),
        out_shape=(
            jax.ShapeDtypeStruct((2, streams, half, heads * DH), lowp),
            jax.ShapeDtypeStruct((streams, heads, 2 * half, 1), single),
        ),
        in_specs=head_specs(seg, comp, mem, heads),
        out_specs=(
            pl.BlockSpec((2, 1, half, DH), lambda n, h: (0, n, 0, h)),
            pl.BlockSpec((1, 1, 2 * half, 1), lambda n, h: (n, h, 0, 0)),
        ),
        compiler_params=params(60),
        cost_estimate=cost(7000 * MIB, 6 * MIB),
    )(info, seg, seg, seg, comp, comp, mem, mem)


def attend_back(info, seg, comp, mem, lse, upstream):
    _, streams, half, wide = seg.shape
    heads = comp.shape[1] // (2 * DH)
    slots = comp.shape[0] // streams
    kept = mem.shape[0] // streams
    return pl.pallas_call(
        attend_back_kernel,
        name="attend_back",
        grid=(streams, heads),
        out_shape=(
            jax.ShapeDtypeStruct(seg.shape, lowp),
            jax.ShapeDtypeStruct(comp.shape, lowp),
            jax.ShapeDtypeStruct(mem.shape, lowp),
        ),
        in_specs=head_specs(seg, comp, mem, heads)
        + [
            pl.BlockSpec((1, 1, 2 * half, 1), lambda n, h: (n, h, 0, 0)),
            pl.BlockSpec((2, 1, half, DH), lambda n, h: (0, n, 0, h)),
        ],
        out_specs=(
            pl.BlockSpec((2, 1, half, wide), lambda n, h: (0, n, 0, 0)),
            pl.BlockSpec((slots, comp.shape[1]), lambda n, h: (n, 0)),
            pl.BlockSpec((kept, mem.shape[1]), lambda n, h: (n, 0)),
        ),
        compiler_params=params(60),
        cost_estimate=cost(11000 * MIB, 9 * MIB),
    )(info, seg, seg, seg, comp, comp, mem, mem, lse, upstream)


def columns_of(rows):
    tall = jnp.concatenate([rows, jnp.zeros((120, rows.shape[1]), single)], axis=0)
    return jnp.transpose(tall)


def logits_kernel(words, tiles, info_ref, pair_ref, near_ref, table_ref, out_ref, stat_ref, held):
    step = pl.program_id(0)

    @pl.when(step < tiles)
    def _():
        held[...] = pair_ref[...]

    @pl.when(step >= tiles)
    def _():
        held[...] = near_ref[...]

    logits = mm(held[...], table_ref[...], NT)
    wanted = columns_of(info_ref[...])[:, 0:1].astype(jnp.int32)
    col = lax.broadcasted_iota(jnp.int32, logits.shape, 1)
    hit = jnp.sum(jnp.where(col == wanted, logits, 0.0), axis=-1, keepdims=True)
    logits = jnp.where(col < words, logits, -1e30)
    top = jnp.max(logits, axis=-1, keepdims=True)
    raised = jnp.exp(logits - top)
    total = jnp.sum(raised, axis=-1, keepdims=True)
    out_ref[...] = raised.astype(lowp)
    lane = lax.broadcasted_iota(jnp.int32, (logits.shape[0], 128), 1)
    packed = jnp.where(lane == 0, top, jnp.where(lane == 1, total, jnp.where(lane == 2, hit, 0.0)))
    stat_ref[...] = jnp.transpose(packed)[:8]


def logits_part(words, info, pair, near, table):
    rows = pair.shape[0] + near.shape[0]
    slots = table.shape[0]
    tile = 256
    tiles = pair.shape[0] // tile
    return pl.pallas_call(
        functools.partial(logits_kernel, words, tiles),
        name="logits_part",
        grid=(2 * tiles,),
        out_shape=(
            jax.ShapeDtypeStruct((rows, slots), lowp),
            jax.ShapeDtypeStruct((8, rows), single),
        ),
        in_specs=[
            pl.BlockSpec((8, tile), lambda i: (0, i)),
            pl.BlockSpec((tile, D), lambda i: (jnp.minimum(i, tiles - 1), 0)),
            pl.BlockSpec((tile, D), lambda i: (jnp.maximum(i - tiles, 0), 0)),
            pl.BlockSpec(table.shape, lambda i: (0, 0)),
        ],
        out_specs=(
            pl.BlockSpec((tile, slots), lambda i: (i, 0)),
            pl.BlockSpec((8, tile), lambda i: (0, i)),
        ),
        scratch_shapes=[pltpu.VMEM((tile, D), lowp)],
        compiler_params=params(60),
        cost_estimate=cost(4 * rows * slots * D, 10 * MIB),
    )(info, pair, near, table)


def logits_back_kernel(tiles, info_ref, factor_ref, in_ref, table_ref, out_ref, keep_ref, send_ref):
    step = pl.program_id(0)
    info = columns_of(info_ref[...])
    wanted = info[:, 0:1].astype(jnp.int32)
    counted = info[:, 1:2]
    factor = columns_of(factor_ref[...])[:, 0:1]
    raised = in_ref[...].astype(single)
    col = lax.broadcasted_iota(jnp.int32, raised.shape, 1)
    grads = (raised * factor - jnp.where(col == wanted, counted, 0.0)).astype(lowp)
    out_ref[...] = grads
    total = mm(grads, table_ref[...]).astype(lowp)

    @pl.when(step < tiles)
    def _():
        send_ref[...] = total

    @pl.when(step >= tiles)
    def _():
        keep_ref[...] = total


def logits_back(info, factor, raised, table):
    rows, slots = raised.shape
    tile = 256
    tiles = rows // (2 * tile)

    def at(i):
        return (i + tiles) % (2 * tiles)

    return pl.pallas_call(
        functools.partial(logits_back_kernel, tiles),
        name="logits_back",
        grid=(2 * tiles,),
        out_shape=(
            jax.ShapeDtypeStruct((rows, slots), lowp),
            jax.ShapeDtypeStruct((rows // 2, D), lowp),
            jax.ShapeDtypeStruct((rows // 2, D), lowp),
        ),
        in_specs=[
            pl.BlockSpec((8, tile), lambda i: (0, at(i))),
            pl.BlockSpec((8, tile), lambda i: (0, at(i))),
            pl.BlockSpec((tile, slots), lambda i: (at(i), 0)),
            pl.BlockSpec(table.shape, lambda i: (0, 0)),
        ],
        out_specs=(
            pl.BlockSpec((tile, slots), lambda i: (at(i), 0)),
            pl.BlockSpec((tile, D), lambda i: (jnp.maximum(i - tiles, 0), 0)),
            pl.BlockSpec((tile, D), lambda i: (jnp.minimum(i, tiles - 1), 0)),
        ),
        compiler_params=params(60),
        cost_estimate=cost(4 * rows * slots * D, 12 * MIB),
    )(info, factor, raised, table)


def halves(total, keep_ref, send_ref):
    half = keep_ref.shape[1]
    keep_ref[...] = total[:, :half]
    send_ref[...] = total[:, half:].astype(send_ref.dtype)


def table_grad_kernel(count, *refs):
    total = None
    for i in range(count):
        rows = refs[count + 2 * i].shape[0]
        for j in range(2):
            term = mm(refs[i][j * rows : (j + 1) * rows, :], refs[count + 2 * i + j][...], TN)
            total = term if total is None else total + term
    halves(total, *refs[3 * count :])


def table_grad_part(grads, inputs):
    count = len(grads)
    rows = sum(g.shape[0] for g in grads)
    slots = grads[0].shape[1]
    block = 256
    if rows > 4096:
        total = sum(
            mm(g, jnp.concatenate(v), TN) for g, v in zip(grads, inputs)
        )
        keep, send = split(total, 1, 2)
        return keep, send.astype(lowp)
    inputs = [half for pair in inputs for half in pair]
    return pl.pallas_call(
        functools.partial(table_grad_kernel, count),
        name="table_grad_part",
        grid=(slots // block,),
        out_shape=(
            jax.ShapeDtypeStruct((slots, D // 2), single),
            jax.ShapeDtypeStruct((slots, D // 2), lowp),
        ),
        in_specs=[pl.BlockSpec((g.shape[0], block), lambda i: (0, i)) for g in grads]
        + [pl.BlockSpec(v.shape, lambda i: (0, 0)) for v in inputs],
        out_specs=(
            pl.BlockSpec((block, D // 2), lambda i: (i, 0)),
            pl.BlockSpec((block, D // 2), lambda i: (i, 0)),
        ),
        compiler_params=params(60),
        cost_estimate=cost(3 * rows * slots * D, 30 * MIB),
    )(*grads, *inputs)


def hidden_grad_kernel(blocks, pre_ref, act_ref, in_ref, down_ref, keep_ref, send_ref):
    step = pl.program_id(0)

    @pl.when(step < blocks)
    def _():
        halves(mm(pre_ref[...], in_ref[...], TN), keep_ref, send_ref)

    @pl.when(step >= blocks)
    def _():
        halves(mm(act_ref[...], down_ref[...], TN), keep_ref, send_ref)


def hidden_grads(pre_grad, hidden_act, ffn_in, down_in):
    rows, hidden = pre_grad.shape
    block = 256
    blocks = hidden // block
    return pl.pallas_call(
        functools.partial(hidden_grad_kernel, blocks),
        name="hidden_grads",
        grid=(2 * blocks,),
        out_shape=(
            jax.ShapeDtypeStruct((2 * hidden, D // 2), single),
            jax.ShapeDtypeStruct((2 * hidden, D // 2), lowp),
        ),
        in_specs=[
            pl.BlockSpec((rows, block), lambda i: (0, jnp.minimum(i, blocks - 1))),
            pl.BlockSpec((rows, block), lambda i: (0, jnp.maximum(i - blocks, 0))),
            pl.BlockSpec((rows, D), lambda i: (0, 0)),
            pl.BlockSpec((rows, D), lambda i: (0, 0)),
        ],
        out_specs=(
            pl.BlockSpec((block, D // 2), lambda i: (i, 0)),
            pl.BlockSpec((block, D // 2), lambda i: (i, 0)),
        ),
        compiler_params=params(60),
        cost_estimate=cost(6 * rows * hidden * D, 16 * MIB),
    )(pre_grad, hidden_act, ffn_in, down_in)


def attn_grad_kernel(
    seg_ref, mixed_ref, mem_ref, old_ref, normed_ref, up_ref, mem_in_ref, old_in_ref, keep_ref, send_ref
):
    which = pl.program_id(0)

    @pl.when(which == 0)
    def _():
        halves(mm(seg_ref[...], normed_ref[...], TN), keep_ref, send_ref)

    @pl.when(which == 3)
    def _():
        halves(mm(mixed_ref[...], up_ref[...], TN), keep_ref, send_ref)

    @pl.when(jnp.logical_and(which > 0, which < 3))
    def _():
        total = mm(seg_ref[...], normed_ref[...], TN)
        total = total + mm(mem_ref[...], mem_in_ref[...], TN)
        total = total + mm(old_ref[...], old_in_ref[...], TN)
        halves(total, keep_ref, send_ref)


def attn_grads(seg_grad, mixed, mem_grad, old_grad, normed, attn_in, mem_in, old_in):
    block = mixed.shape[1]

    def whole(array):
        return pl.BlockSpec(array.shape, lambda i: (0, 0))

    return pl.pallas_call(
        attn_grad_kernel,
        name="attn_grads",
        grid=(4,),
        out_shape=(
            jax.ShapeDtypeStruct((4 * block, D // 2), single),
            jax.ShapeDtypeStruct((4 * block, D // 2), lowp),
        ),
        in_specs=[
            pl.BlockSpec((seg_grad.shape[0], block), lambda i: (0, jnp.minimum(i, 2))),
            whole(mixed),
            pl.BlockSpec((mem_grad.shape[0], block), lambda i: (0, jnp.clip(i - 1, 0, 1))),
            pl.BlockSpec((old_grad.shape[0], block), lambda i: (0, jnp.clip(i - 1, 0, 1))),
            whole(normed),
            whole(attn_in),
            whole(mem_in),
            whole(old_in),
        ],
        out_specs=(
            pl.BlockSpec((block, D // 2), lambda i: (i, 0)),
            pl.BlockSpec((block, D // 2), lambda i: (i, 0)),
        ),
        compiler_params=params(60),
        cost_estimate=cost(9000 * MIB, 24 * MIB),
    )(seg_grad, mixed, mem_grad, old_grad, normed, attn_in, mem_in, old_in)


def scalar_row(values, length=128):
    lane = jnp.arange(length, dtype=jnp.int32)
    row = jnp.zeros((length,), single)
    for i, value in enumerate(values):
        row = jnp.where(lane == i, value, row)
    return row


def local(
    ids,
    targets,
    target_mask,
    memory,
    old_states,
    mem_fill,
    comp_fill,
    table,
    qkv,
    wout,
    wconv,
    wup,
    wdown,
    gains,
    table_rows,
    table_cols,
    qkv_rows,
    qkv_cols,
    out_rows,
    out_cols,
    conv_rows,
    conv_cols,
    up_rows,
    up_cols,
    down_rows,
    down_cols,
    gains_second,
):
    dp_size, head_size = lax.axis_size("dp"), lax.axis_size("head")
    d, h = lax.axis_index("dp"), lax.axis_index("head")
    x, c = h // 2, h % 2
    order = block_order(dp_size)
    reach = dp_size // 2
    streams, seg_len = ids.shape
    half = seg_len // 2
    per_group = streams * seg_len
    vocab, width = table.shape
    assert head_size == 4 and streams == 2

    weights_now = (table, qkv, wout, wconv, wup, wdown)
    rows_old = (table_rows, qkv_rows, out_rows, conv_rows, up_rows, down_rows)
    cols_old = (table_cols, qkv_cols, out_cols, conv_cols, up_cols, down_cols)
    sizes = {"dp": dp_size, "head": head_size}
    row_axes = ("head", "dp", "head", "head", "dp", "head")
    col_axes = ("dp", "head", "dp", "dp", "head", "dp")

    def early_sums(dep):
        _, *tied = together(dep, *rows_old, *weights_now, gains)
        sums = [jnp.sum(old) / sizes[axis] for old, axis in zip(tied[:6], col_axes)]
        sums += [jnp.sum(weight * weight) for weight in tied[6:12]]
        gain_sums = jnp.sum(tied[12] * tied[12], axis=1) / head_size
        return scalar_row(sums + [gain_sums[0], gain_sums[1], gain_sums[2]])

    def core_sum(keep, send):
        more = swap(send.astype(lowp), "head", 1)
        return keep.astype(single) + more.astype(single)

    def stream_sum(part, beside=()):
        keep, send = split(part, 0, 2)
        more, *beside = together(swap(send.astype(lowp), "head", 2), *beside)
        part = keep + more.astype(single)
        return (part, beside) if beside else part

    def group_sum(part, beside=()):
        return stream_sum(core_sum(*split(part, 0, 2)), beside)

    def group_both(part, beside=()):
        far, *beside = together(swap(part, "head", 2), *beside)
        pair = jnp.concatenate([part, far], axis=0)
        both = (pair, swap(pair, "head", 1))
        return (both, beside) if beside else both

    flat = jnp.concatenate(
        [
            ids.astype(single).reshape(-1),
            targets.astype(single).reshape(-1),
            target_mask.astype(single).reshape(-1),
            gains.astype(lowp).astype(single).reshape(-1),
        ]
    )
    room = -flat.shape[0] % 1024
    flat = jnp.concatenate([flat, jnp.zeros((room,), single)]).reshape(1, -1, 128)
    small, small_steps = gather_blocks(flat, 0)
    small = small.reshape(dp_size, -1)
    place = jnp.stack([x, d])

    def field(raw):
        return relative(raw.reshape(-1, 2, 2, half), x, c)

    ids_all = small[:, :per_group]
    position = [order.index(j) for j in range(dp_size)]
    ids_all = jnp.take(ids_all, jnp.asarray(position, jnp.int32)[jnp.arange(dp_size) ^ d], axis=0)
    ids_all = jnp.transpose(field(ids_all), (1, 2, 0, 3)).reshape(-1).astype(jnp.int32)
    table_rows_all = ids_all - h * vocab
    inside = (table_rows_all >= 0) & (table_rows_all < vocab)
    bits = vocab.bit_length()
    token_codes = (jnp.arange(ids_all.shape[0], dtype=jnp.int32) << bits) | table_rows_all
    token_codes = jnp.where(inside, token_codes, -1)
    table_rows_all = jnp.where(inside, table_rows_all, vocab)
    targets_all = field(small[:reach, per_group : 2 * per_group])
    mask_all = field(small[:reach, 2 * per_group : 3 * per_group])
    gain_blocks = small[:, 3 * per_group : 3 * per_group + 3 * width].reshape(dp_size, 3, width)
    gain_vals = jnp.swapaxes(gain_blocks, 0, 1).reshape(3, 1, D)
    count_all = jnp.sum(small[:, 2 * per_group : 3 * per_group])

    heads_own = wconv.shape[0]
    wide = qkv.shape[2]
    conv_rows_own = wconv.size // width
    low_qkv = qkv.astype(lowp)
    pack_one = jnp.concatenate(
        [
            jnp.swapaxes(low_qkv, 1, 2).reshape(3 * wide, width),
            wout.astype(lowp),
            wconv.astype(lowp).reshape(conv_rows_own, width),
        ]
    )
    own_half, far_half = split(table_rows_all, 0, 2)
    kept = {}

    def beside_lookup(moved):
        moved, kept["far"], kept["own"] = together(
            moved, lookup(far_half, table), lookup(own_half, table)
        )
        return moved

    def beside_memory(moved):
        looked = (kept["own"] + swap(kept["far"], "head", 1)).reshape(2, -1, width)
        mem_normed = state_norm(place, gain_vals[0], memory, 1)[0]
        moved, more, kept["mem"] = together(moved, swap(looked[1], "head", 2), mem_normed)
        looked = (looked[0] + more).reshape(dp_size, half, width)
        kept["looked"] = lax.all_to_all(looked, "dp", 0, 0)
        return moved

    own_one, steps_one = gather_blocks(
        after(pack_one, small_steps[0]), 1, (beside_lookup, beside_memory)
    )
    conv_lanes = jnp.arange(DH, dtype=jnp.int32)
    conv_width = DH // dp_size
    conv_natural = (jnp.asarray(order, jnp.int32)[conv_lanes // conv_width] ^ d) * conv_width
    conv_natural = conv_natural + conv_lanes % conv_width
    conv_shuffle = (conv_natural[:, None] == conv_lanes[None, :]).astype(lowp)
    taps = heads_own * RATE * DH

    def conv_natural_order(rows):
        value = jnp.swapaxes(rows.reshape(conv_rows_own, dp_size, width), 0, 1)
        value = jnp.swapaxes(value.reshape(dp_size, taps, conv_width), 0, 1)
        moved = mm(value.reshape(taps, DH), conv_shuffle).astype(lowp)
        return moved.reshape(heads_own, RATE * DH, DH)

    def conv_block_order(value):
        moved = mm(value.astype(lowp).reshape(taps, DH), conv_shuffle, NT).astype(lowp)
        moved = jnp.swapaxes(moved.reshape(taps, dp_size, conv_width), 0, 1)
        moved = jnp.swapaxes(moved.reshape(dp_size, conv_rows_own, width), 0, 1)
        return moved.reshape(conv_rows_own, D)

    full_conv = conv_natural_order(own_one[4 * wide :])

    hidden_own = wup.shape[1]
    pack_two = jnp.concatenate([wup.astype(lowp).T, wdown.astype(lowp)])

    old_normed = state_norm(place, gain_vals[0], old_states, RATE)

    def beside_old(moved):
        moved, looked, kept["old"] = together(moved, kept["looked"], old_normed)
        kept["embedded"], kept["normed"] = place_embedding(place, looked, gain_vals[0])
        return moved

    def beside_compress(moved):
        moved, *kept["comp"] = together(moved, *compress(kept["old"], own_one, full_conv))
        return moved

    near_two, steps_two = gather_blocks(
        after(pack_two, steps_one[1]), 1, (beside_old, beside_compress), 1
    )
    near_up, near_down = split(near_two, 0, 2)
    far_up, far_down = swap(near_up, "dp", 1), swap(near_down, "dp", 1)
    mem_normed, old_normed = kept["mem"], kept["old"]
    embedded_low = kept["embedded"]
    embedded = embedded_low.astype(single)
    normed = jnp.concatenate(group_both(kept["normed"]))
    comp, old_raw = kept["comp"]

    words = vocab // reach
    z = d // 2
    z_groups = [[2 * i + b for i in range(reach)] for b in range(2)]
    slots = -(-words // 256) * 256


    comp_counts = jnp.where(x == 1, jnp.flip(comp_fill), comp_fill)
    mem_counts = jnp.where(x == 1, jnp.flip(mem_fill), mem_fill)
    info = [comp_counts[0], mem_counts[0], comp_counts[1], mem_counts[1], c * half]
    lane = jnp.arange(8, dtype=jnp.int32)
    info = sum(jnp.where(lane == i, value, 0) for i, value in enumerate(info)).astype(jnp.int32)

    in_weight = own_one[: 3 * wide]
    mem = mm(mem_normed, own_one[wide : 3 * wide], NT).astype(lowp)
    seg = mm(normed, in_weight, NT).astype(lowp).reshape(2, streams, half, 3 * wide)
    low_table = after(table.astype(lowp), seg).reshape(reach, words, width)
    low_table = lax.all_to_all(low_table, "dp", 0, 0, axis_index_groups=z_groups)
    mixed, lse = attend(info, seg, comp, mem)
    mixed = mixed.reshape(-1, wide)
    attn_sum, (early, far_up) = group_sum(
        mm(mixed, own_one[3 * wide : 4 * wide]), (early_sums(mixed), far_up)
    )
    after_attn = embedded + attn_sum
    ffn_in, inv_second = rms(after_attn, gain_vals[1])
    ffn_in, (far_down, low_table) = group_both(ffn_in, (far_down, low_table))
    near_table = [
        lax.dynamic_index_in_dim(low_table, z ^ (m // 2), 0, keepdims=False) for m in order[:reach]
    ]
    near_table = jnp.concatenate(near_table, axis=1)
    ffn_in = jnp.concatenate(ffn_in)
    full_up = jnp.concatenate([near_up, far_up], axis=1)
    full_down = jnp.concatenate([near_down, far_down], axis=1)
    far_table = swap(near_table, "dp", 1)
    loss_table = jnp.concatenate([near_table, far_table], axis=1)
    loss_table = jnp.concatenate([loss_table, jnp.zeros((slots - words, D), lowp)], axis=0)
    hidden_pre = mm(ffn_in, full_up, NT)
    hidden_act = jax.nn.gelu(hidden_pre).astype(lowp)
    after_ffn = after_attn + group_sum(mm(hidden_act, full_down))
    final_in, inv_third = rms(after_ffn, gain_vals[2])

    word_start = (h * vocab + z * words).astype(single)
    wanted_all = targets_all - word_start
    wanted_all = jnp.where((wanted_all >= 0) & (wanted_all < words), wanted_all, -1.0)
    info_all = jnp.stack([wanted_all, mask_all] + [jnp.zeros_like(mask_all)] * 6)
    info_all = jnp.transpose(info_all, (1, 0, 2, 3, 4)).reshape(reach, 8, per_group)
    pieces = [final_in]
    chunks = []
    raised = []
    stats = []

    def next_chunk():
        i = len(chunks)
        if i == 0:
            chunks.append(group_both(pieces[i]))
        else:
            chunk, (stats[i - 1],) = group_both(pieces[i], (stats[i - 1],))
            chunks.append(chunk)
        out, stat = logits_part(words, info_all[i], *chunks[i], loss_table)
        raised.append(out)
        stats.append(stat)

    mask = dp_size // 2
    while mask > 1:
        joined = jnp.concatenate(pieces) if len(pieces) > 1 else pieces[0]
        moved = swap(reorder(joined, mask), "dp", mask)
        if len(pieces) == 1:
            moved, own_codes, own_count = together(
                moved, *own_list(after(token_codes, final_in))
            )
            next_chunk()
        elif len(pieces) == 2:
            moved, stats[0] = together(moved, stats[0])
        pieces += split(moved, 0, len(pieces))
        mask //= 2
    while len(chunks) < reach:
        next_chunk()
    stats = [stat[:3].reshape(3, 1, 2, 2, half) for stat in stats]
    own_stats = jnp.concatenate(stats, axis=1)

    def combine(first, second):
        top = jnp.maximum(first[0], second[0])
        total = first[1] * jnp.exp(first[0] - top) + second[1] * jnp.exp(second[0] - top)
        return jnp.stack([top, total, first[2] + second[2]])

    merged = own_stats
    merged = combine(merged, jnp.flip(swap(merged, "head", 1), 2))
    merged = combine(merged, jnp.flip(swap(merged, "head", 2), 3))
    mask = 2
    while mask < dp_size:
        other = split(swap(merged, "dp", mask), 1, reach)
        other = [other[order.index(j ^ mask)] for j in order[:reach]]
        merged = combine(merged, jnp.concatenate(other, axis=1))
        mask *= 2
    log_total = merged[0] + jnp.log(merged[1])
    loss_local = jnp.sum(mask_all[0, 0, 0] * (log_total[0, 0, 0] - merged[2, 0, 0, 0]))
    factor_all = jnp.exp(own_stats[0] - log_total)

    factor_all = factor_all.reshape(reach, 1, per_group) * info_all[:, 1:2]
    factor_all = jnp.broadcast_to(factor_all, info_all.shape)
    dlogits = [None] * reach
    parts = [None] * reach
    for i in reversed(range(reach)):
        dlogits[i], *core = logits_back(info_all[i], factor_all[i], raised[i], loss_table)
        if i + 1 < reach:
            parts[i + 1], (dlogits[i], *core) = stream_sum(parts[i + 1], (dlogits[i], *core))
        parts[i] = core_sum(*core)
    parts[0] = stream_sum(parts[0])
    table_parts = []
    mask = 2
    while len(parts) > 1:
        count = len(parts) // 2
        moved = jnp.concatenate([part.astype(lowp) for part in parts[count:]])
        moved = swap(reorder(moved, mask), "dp", mask)
        if mask == 2:
            moved, dlogits[0] = together(moved, dlogits[0])
        elif mask == 4:
            moved, *table_parts = together(moved, *table_grad_part(dlogits, chunks))
        moved = split(moved.astype(single), 0, count)
        parts = [part + more for part, more in zip(parts, moved)]
        mask *= 2
    final_grad = parts[0]

    grad_after_ffn = rms_back(after_ffn, inv_third, gain_vals[2], final_grad)
    moved_table = swap(table_parts[1], "dp", 1)
    down_in = group_both(grad_after_ffn.astype(lowp))
    down_in = jnp.concatenate(down_in)
    act_grad = mm(down_in, full_down, NT)
    pre_grad = jax.vjp(jax.nn.gelu, hidden_pre)[1](act_grad)[0].astype(lowp)
    two = hidden_grads(pre_grad, hidden_act, ffn_in, down_in)
    ffn_in_grad, (*two, moved_table) = group_sum(mm(pre_grad, full_up), (*two, moved_table))
    keep = table_parts[0] + moved_table.astype(single)
    table_pieces = jnp.stack(split(keep[:words].astype(lowp), 1, reach))
    position = [order.index(2 * i) for i in range(reach)]
    position = jnp.asarray(position, jnp.int32)[jnp.arange(reach) ^ z]
    table_pieces = jnp.concatenate(
        [lax.dynamic_index_in_dim(table_pieces, position[i], 0) for i in range(reach)]
    )
    table_pieces = lax.all_to_all(table_pieces, "dp", 0, 0, axis_index_groups=z_groups)
    grad_after_attn = grad_after_ffn + rms_back(after_attn, inv_second, gain_vals[1], ffn_in_grad)
    attn_in = jnp.concatenate(group_both(grad_after_attn.astype(lowp)))

    mixed_grad = mm(attn_in, own_one[3 * wide : 4 * wide], NT).astype(lowp)
    mixed_grad = mixed_grad.reshape(2, streams, half, wide)
    seg_grad, comp_grad, mem_grad = attend_back(info, seg, comp, mem, lse, mixed_grad)
    seg_grad = seg_grad.reshape(-1, 3 * wide)

    def beside_expand(moved):
        keep, send = split(mm(seg_grad, in_weight), 0, 2)
        more = swap(send.astype(lowp), "head", 1)
        moved, more, *kept["old"] = together(
            moved, more, *expand(comp_grad, old_raw, full_conv)
        )
        kept["seg_in"] = split(keep + more.astype(single), 0, 2)
        return moved

    def beside_sums(moved):
        seg_in, seg_in_far = kept["seg_in"]
        seg_in_far = swap(seg_in_far.astype(lowp), "head", 2)
        old_grad, conv_sum = kept["old"]
        sums = attn_grads(
            seg_grad,
            mixed,
            mem_grad,
            old_grad.reshape(-1, old_grad.shape[-1]),
            normed,
            attn_in,
            mem_normed,
            old_normed.reshape(-1, D),
        )
        conv_sum = split(conv_block_order(conv_sum), 1, 2)
        sums = [jnp.concatenate([part, more.astype(part.dtype)]) for part, more in zip(sums, conv_sum)]
        moved, kept["table"], seg_in_far, *kept["sums"] = together(
            moved, table_pieces, seg_in_far, *sums
        )
        rows_grad = embed_back(
            place, embedded_low, gain_vals[0], seg_in, seg_in_far, grad_after_attn
        )
        kept["rows"] = lax.all_to_all(rows_grad, "dp", 0, 0)
        return moved

    def beside_rows(moved):
        moved, kept["rows"] = together(moved, kept["rows"])
        return moved

    def beside_streams(moved):
        moved, far = together(moved, swap(kept["rows"], "head", 2))
        kept["rows"] = jnp.stack([kept["rows"], far])
        return moved

    two = reduce_blocks(*two, (beside_expand, beside_sums))
    one = reduce_blocks(*kept["sums"], (beside_rows, beside_streams))
    rows_grad = kept["rows"]
    rows_grad = jnp.stack([rows_grad, swap(rows_grad, "head", 1)]).reshape(-1, width)
    table_base = kept["table"].astype(single).reshape(vocab, width)

    up_grad = two[:hidden_own].T
    down_grad = two[hidden_own:]
    qkv_grad = jnp.swapaxes(one[: 3 * wide].reshape(3, wide, width), 1, 2)
    out_grad = one[3 * wide : 4 * wide]
    conv_grad = one[4 * wide :].reshape(wconv.shape)
    table_grad = scatter(bits, own_count, own_codes, table_base, rows_grad)

    gains_low = gains.astype(lowp).astype(single)
    gain_part = jnp.stack(
        [
            jnp.sum(low_qkv.astype(single) * qkv_grad, axis=(0, 2)),
            jnp.sum(wup.astype(lowp).astype(single) * up_grad, axis=1),
            jnp.sum(table.astype(lowp).astype(single) * table_base, axis=0),
        ]
    )

    grads = (table_grad, qkv_grad, out_grad, conv_grad, up_grad, down_grad)
    def sum_over_dp(joined):
        mask = 1
        while mask < dp_size:
            joined = joined + swap(joined, "dp", mask)
            mask *= 2
        return joined

    row_part = []
    col_part = []
    for grad in grads:
        square = grad * grad
        row_part.append(jnp.sum(square, axis=-1))
        col_part.append(jnp.sum(square, axis=tuple(range(square.ndim - 1))))
    row_q, row_u, col_e, col_o, col_c, col_d, gain_raw, early = lax.psum(
        (
            row_part[1],
            row_part[4],
            col_part[0],
            col_part[2],
            col_part[3],
            col_part[5],
            gain_part,
            early + scalar_row([0.0] * 15 + [loss_local]),
        ),
        "head",
    )
    lanes = [col_e, jnp.sum(row_q, axis=0), col_o]
    lanes += [jnp.concatenate([col_c, jnp.zeros((width - col_c.shape[0],), single)]), row_u, col_d]
    members = [col_part[4], row_part[5], row_part[3], row_part[2], col_part[1], *lanes, row_part[0], early]
    joined = jnp.concatenate([m.reshape(-1) for m in members])
    joined = sum_over_dp(jnp.concatenate([joined, jnp.zeros((-joined.shape[0] % 1024,), single)]))
    sums = []
    start = 0
    for member in members:
        sums.append(joined[start : start + member.size].reshape(member.shape))
        start += member.size
    col_u, row_d, row_c, row_o, col_q, *lanes, row_e, early = sums
    square_total = [jnp.sum(lane) for lane in lanes]
    row_sums = [row_e, row_q, row_o, row_c, row_u, row_d]
    col_sums = [col_e, col_q, col_o, col_c, col_u, col_d]
    weight_total = early[6:15]
    loss_all = early[15]
    inverse = 1.0 / count_all
    decay = 1.0 - STEP ** (-0.8)
    updates = []
    stats_new = []
    scaled = []
    counts = []
    update_sq = []
    for index in range(6):
        rows_total = rows_old[index].size * sizes[row_axes[index]]
        cols_total = cols_old[index].size * sizes[col_axes[index]]
        grad_scaled = grads[index] * inverse
        rows_new = decay * rows_old[index] + (1.0 - decay) * (
            row_sums[index] * inverse * inverse / cols_total + TINY_SQUARE
        )
        cols_new = decay * cols_old[index] + (1.0 - decay) * (
            col_sums[index] * inverse * inverse / rows_total + TINY_SQUARE
        )
        mean_row = decay * early[index] / rows_total + (1.0 - decay) * (
            square_total[index] * inverse * inverse / (rows_total * cols_total) + TINY_SQUARE
        )
        second = rows_new[..., None] * cols_new / mean_row
        direction = grad_scaled * lax.rsqrt(second)
        updates.append(direction)
        stats_new.append((rows_new, cols_new))
        scaled.append(grad_scaled)
        counts.append(rows_total * cols_total)
        update_sq.append(jnp.sum(direction * direction))
    gain_scaled = gain_raw / gains_low * inverse
    second_new = decay * gains_second + (1.0 - decay) * (gain_scaled * gain_scaled + TINY_SQUARE)
    gain_dir = gain_scaled * lax.rsqrt(second_new)
    for which in range(3):
        update_sq.append(jnp.sum(gain_dir[which] * gain_dir[which]) / head_size)
    update_total = after(scalar_row(update_sq, 1024), loss_all)
    for mask in (1, 2):
        update_total = update_total + swap(update_total, "head", mask)
    update_total = sum_over_dp(update_total)[:9]
    results = [loss_all, count_all]
    for index in range(6):
        factor = jnp.maximum(0.001, jnp.sqrt(weight_total[index] / counts[index]))
        denom = jnp.maximum(1.0, jnp.sqrt(update_total[index] / counts[index]) / CLIP_LEVEL)
        new_weight = weights_now[index] - LEARN_RATE * factor * updates[index] / denom
        results += [new_weight, scaled[index], stats_new[index][0], stats_new[index][1]]
    gain_factor = jnp.maximum(0.001, jnp.sqrt(weight_total[6:] / D))[:, None]
    gain_denom = jnp.maximum(1.0, jnp.sqrt(update_total[6:] / D) / CLIP_LEVEL)[:, None]
    results += [gains - LEARN_RATE * gain_factor * gain_dir / gain_denom, gain_scaled, second_new]
    return tuple(results)


def solution(mesh):
    in_specs = (
        P("dp", None),
        P("dp", None),
        P("dp", None),
        P("dp", None, None),
        P("dp", None, None),
        P("dp"),
        P("dp"),
        P("head", "dp"),
        P(None, "dp", "head"),
        P("head", "dp"),
        P("head", None, "dp"),
        P("dp", "head"),
        P("head", "dp"),
        P(None, "dp"),
        P("head"),
        P("dp"),
        P(None, "dp"),
        P("head"),
        P("head"),
        P("dp"),
        P("head", None),
        P("dp"),
        P("dp"),
        P("head"),
        P("head"),
        P("dp"),
        P(None, "dp"),
    )
    out_specs = (
        P(),
        P(),
        P("head", "dp"),
        P("head", "dp"),
        P("head"),
        P("dp"),
        P(None, "dp", "head"),
        P(None, "dp", "head"),
        P(None, "dp"),
        P("head"),
        P("head", "dp"),
        P("head", "dp"),
        P("head"),
        P("dp"),
        P("head", None, "dp"),
        P("head", None, "dp"),
        P("head", None),
        P("dp"),
        P("dp", "head"),
        P("dp", "head"),
        P("dp"),
        P("head"),
        P("head", "dp"),
        P("head", "dp"),
        P("head"),
        P("dp"),
        P(None, "dp"),
        P(None, "dp"),
        P(None, "dp"),
    )
    return jax.shard_map(local, mesh=mesh, in_specs=in_specs, out_specs=out_specs, check_vma=False)
```

```python
import functools

import jax
import jax.numpy as jnp
from jax import lax
from jax.experimental import pallas as pl
from jax.experimental.pallas import tpu as pltpu
from jax.sharding import PartitionSpec as P

D = 1024
H = 8
DH = 128
MEM = 512
CMEM = 512
RATE = 3
STEP = 10


TINY_NORM = 1e-06
TINY_SQUARE = 1e-30
LEARN_RATE = 0.5
CLIP_LEVEL = 1.0

lowp = jnp.bfloat16
single = jnp.float32
NT = (((1,), (1,)), ((), ()))
TN = (((0,), (0,)), ((), ()))
NN = (((1,), (0,)), ((), ()))
MIB = 1024 * 1024


def mm(left, right, dims=NN):
    return lax.dot_general(left, right, dims, preferred_element_type=single)


def swap(value, axis, mask):
    size = lax.axis_size(axis)
    return lax.ppermute(value, axis, [(i, i ^ mask) for i in range(size)])


def after(value, *deps):
    return lax.optimization_barrier((value, *deps))[0]


def together(*values):
    return lax.optimization_barrier(values)


def block_order(size):
    order = [0]
    step = size // 2
    while step:
        order = order + [j + step for j in order]
        step //= 2
    return order


def gather_blocks(piece, axis, beside=(), stop=0):
    steps = []
    mask = lax.axis_size("dp") // 2
    while mask > stop:
        moved = swap(piece, "dp", mask)
        if len(steps) < len(beside):
            moved = beside[len(steps)](moved)
        piece = jnp.concatenate([piece, moved], axis=axis)
        steps.append(piece)
        mask //= 2
    return piece, steps


def split(value, axis, parts):
    width = value.shape[axis] // parts
    return [lax.slice_in_dim(value, i * width, (i + 1) * width, axis=axis) for i in range(parts)]


def reduce_blocks(keep, send, beside=(), mask=1):
    moved = swap(send.astype(lowp), "dp", mask)
    if beside:
        moved = beside[0](moved)
    total = keep + moved.astype(single)
    mask *= 2
    if mask == lax.axis_size("dp"):
        return total
    return reduce_blocks(*split(total, 1, 2), beside[1:], mask)


def reorder_kernel(sources, *refs):
    out_ref = refs[-1]
    width = out_ref.shape[1] // len(sources)
    start = 0
    for in_ref in refs[:-1]:
        rows = slice(start, start + in_ref.shape[0])
        start += in_ref.shape[0]
        for p, q in enumerate(sources):
            block = in_ref[:, q * width : (q + 1) * width]
            out_ref[rows, p * width : (p + 1) * width] = block.astype(out_ref.dtype)


def reorder(values, mask):
    order = block_order(lax.axis_size("dp"))
    sources = [order.index(j ^ mask) for j in order]
    rows = sum(value.shape[0] for value in values)
    if D // len(order) % 128:
        joined = jnp.concatenate([value.astype(lowp) for value in values])
        cols = split(joined, 1, len(order))
        return jnp.concatenate([cols[q] for q in sources], axis=1)
    return pl.pallas_call(
        functools.partial(reorder_kernel, sources),
        name="reorder",
        out_shape=jax.ShapeDtypeStruct((rows, D), lowp),
        in_specs=[vmem()] * len(values),
        out_specs=vmem(),
        compiler_params=params(60),
        cost_estimate=cost(0, 2 * MIB),
    )(*values)


def relative(value, x, c):
    value = jnp.where(x == 1, jnp.flip(value, -3), value)
    value = jnp.where(c == 1, jnp.flip(value, -2), value)
    return jnp.swapaxes(value, -3, -2)


def rms(values, gain):
    inv = lax.rsqrt(jnp.mean(values * values, axis=-1, keepdims=True) + TINY_NORM)
    return (values * inv * gain).astype(lowp), inv


def rms_back(values, inv, gain, upstream):
    scaled = gain * upstream
    inner = jnp.sum(scaled * values, axis=-1, keepdims=True) / D
    return scaled * inv - values * (inner * inv * inv * inv)


def vmem(shape=None, index=None):
    if shape is None:
        return pl.BlockSpec(memory_space=pltpu.VMEM)
    return pl.BlockSpec(shape, index)


def smem():
    return pl.BlockSpec(memory_space=pltpu.SMEM)


def params(mib):
    return pltpu.CompilerParams(vmem_limit_bytes=mib * MIB)


def cost(flops, size, exps=0):
    return pl.CostEstimate(
        flops=int(0.02 * flops), bytes_accessed=int(0.02 * size), transcendentals=exps
    )


def lookup_kernel(row_ref, table_ref, out_ref, tab, held, sem):
    total = row_ref.shape[0]
    vocab = table_ref.shape[0]
    copy = pltpu.make_async_copy(table_ref, tab.at[pl.ds(0, vocab)], sem)
    copy.start()
    tab[pl.ds(vocab, 8), :] = jnp.zeros((8, tab.shape[1]), single)
    copy.wait()

    @pl.loop(0, total // 16)
    def _(g):
        for j in range(16):
            t = g * 16 + j
            held[pl.ds(t, 1), :] = tab[pl.ds(row_ref[t], 1), :]

    @pl.loop(0, total // 512)
    def _(i):
        rows = pl.ds(pl.multiple_of(i * 512, 512), 512)
        out_ref[rows, :] = held[rows, :].astype(lowp)


def lookup(rows, table):
    total = rows.shape[0]
    vocab, width = table.shape
    return pl.pallas_call(
        lookup_kernel,
        name="lookup",
        out_shape=jax.ShapeDtypeStruct((total, width), lowp),
        in_specs=[smem(), pl.BlockSpec(memory_space=pl.ANY)],
        out_specs=vmem(),
        scratch_shapes=[
            pltpu.VMEM((vocab + 8, width), single),
            pltpu.VMEM((total, width), single),
            pltpu.SemaphoreType.DMA(()),
        ],
        compiler_params=params(60),
        cost_estimate=cost(0, 30 * MIB),
    )(rows, table)


def list_kernel(code_ref, out_ref, count_ref):
    total = code_ref.shape[0]

    def group(g, count):
        for j in range(16):
            code = code_ref[g * 16 + j]
            out_ref[count] = code
            count = count + jnp.where(code >= 0, 1, 0)
        return count

    count_ref[0] = lax.fori_loop(0, total // 16, group, jnp.int32(0))


def own_list(codes):
    total = codes.shape[0]
    return pl.pallas_call(
        list_kernel,
        name="own_list",
        out_shape=(
            jax.ShapeDtypeStruct((total + 8,), jnp.int32),
            jax.ShapeDtypeStruct((1,), jnp.int32),
        ),
        in_specs=[smem()],
        out_specs=(smem(), smem()),
        cost_estimate=cost(0, 60 * MIB),
    )(codes)


def place_kernel(order, place_ref, in_ref, gain_ref, out_ref, norm_ref, held):
    width = in_ref.shape[2]
    for p, j in enumerate(order):
        block = in_ref[pl.ds(place_ref[1] ^ j, 1)][0]
        out_ref[:, p * width : (p + 1) * width] = block
        held[:, p * width : (p + 1) * width] = block.astype(single)
    values = held[...]
    inv = lax.rsqrt(jnp.mean(values * values, axis=-1, keepdims=True) + TINY_NORM)
    norm_ref[...] = (values * inv * gain_ref[...]).astype(lowp)


def place_embedding(place, blocks, gain):
    rows = blocks.shape[1]
    return pl.pallas_call(
        functools.partial(place_kernel, block_order(blocks.shape[0])),
        name="place_embedding",
        out_shape=(jax.ShapeDtypeStruct((rows, D), lowp), jax.ShapeDtypeStruct((rows, D), lowp)),
        in_specs=[smem(), vmem(), vmem()],
        out_specs=(vmem(), vmem()),
        scratch_shapes=[pltpu.VMEM((rows, D), single)],
        compiler_params=params(60),
        cost_estimate=cost(0, 3 * MIB),
    )(place, blocks, gain)


def embed_back_kernel(order, place_ref, in_ref, gain_ref, keep_ref, more_ref, grad_ref, out_ref, held):
    values = in_ref[...].astype(single)
    inv = lax.rsqrt(jnp.mean(values * values, axis=-1, keepdims=True) + TINY_NORM)
    upstream = keep_ref[...] + more_ref[...].astype(single)
    held[...] = grad_ref[...] + rms_back(values, inv, gain_ref[...], upstream)
    width = out_ref.shape[2]
    for p, j in enumerate(order):
        block = held[:, p * width : (p + 1) * width].astype(lowp)
        out_ref[pl.ds(place_ref[1] ^ j, 1)] = block[None]


def embed_back(place, values, gain, keep, more, grad):
    rows = values.shape[0]
    size = lax.axis_size("dp")
    return pl.pallas_call(
        functools.partial(embed_back_kernel, block_order(size)),
        name="embed_back",
        out_shape=jax.ShapeDtypeStruct((size, rows, D // size), lowp),
        in_specs=[smem()] + [vmem()] * 5,
        out_specs=vmem(),
        scratch_shapes=[pltpu.VMEM((rows, D), single)],
        compiler_params=params(60),
        cost_estimate=cost(0, 4 * MIB),
    )(place, values, gain, keep, more, grad)


def scatter_kernel(bits, count_ref, code_ref, base_ref, grad_ref, out_ref, rows):
    total = grad_ref.shape[0]
    vocab = base_ref.shape[0]

    @pl.loop(0, total // 512)
    def _(i):
        here = pl.ds(pl.multiple_of(i * 512, 512), 512)
        rows[here, :] = grad_ref[here, :].astype(single)

    rows[pl.ds(total, 8), :] = jnp.zeros((8, rows.shape[1]), single)

    @pl.loop(0, vocab // 400)
    def _(i):
        here = pl.ds(pl.multiple_of(i * 400, 400), 400)
        out_ref[here, :] = base_ref[here, :]

    count = count_ref[0]

    def group(g, carry):
        for j in range(8):
            index = g * 8 + j
            code = jnp.where(index < count, code_ref[index], total << bits)
            token = lax.shift_right_logical(code, bits)
            row = code & ((1 << bits) - 1)
            out_ref[pl.ds(row, 1), :] = out_ref[pl.ds(row, 1), :] + rows[pl.ds(token, 1), :]
        return carry

    lax.fori_loop(0, (count + 7) // 8, group, jnp.int32(0))


def scatter(bits, count, codes, base, grad):
    total, width = grad.shape
    return pl.pallas_call(
        functools.partial(scatter_kernel, bits),
        name="scatter",
        out_shape=jax.ShapeDtypeStruct(base.shape, single),
        in_specs=[smem(), smem(), vmem(), vmem()],
        out_specs=vmem(),
        scratch_shapes=[pltpu.VMEM((total + 8, width), single)],
        compiler_params=params(60),
        cost_estimate=cost(0, 30 * MIB),
    )(count, codes, base, grad)


def state_kernel(order, width, place_ref, gain_ref, in_ref, out_ref, held):
    rows = in_ref.shape[1]
    values = in_ref[0].astype(single)
    inv = lax.rsqrt(jnp.mean(values * values, axis=-1, keepdims=True) + TINY_NORM)
    for p, j in enumerate(order):
        start = pl.multiple_of((place_ref[1] ^ j) * width, width)
        block = in_ref[0, :, pl.ds(start, width)].astype(single)
        held[p] = block * inv * gain_ref[:, p * width : (p + 1) * width]
    groups = out_ref.shape[0]
    for p in range(len(order)):
        cols = slice(p * width, (p + 1) * width)
        if groups == 1:
            out_ref[0, :, cols] = held[p].astype(lowp)
        else:
            for j in range(groups):
                part = held[p, pl.ds(j, rows // groups, stride=groups), :]
                out_ref[j, :, cols] = part.astype(lowp)


def state_norm(place, gain, states, groups):
    size = lax.axis_size("dp")
    order = block_order(size)
    width = D // size
    streams = states.shape[0]
    count = states.shape[1] // groups
    if width % 128:
        values = jnp.where(place[0] == 1, jnp.flip(states, 0), states).astype(single).reshape(-1, D)
        inv = lax.rsqrt(jnp.mean(values * values, axis=-1, keepdims=True) + TINY_NORM)
        lanes = jnp.arange(D, dtype=jnp.int32)
        blocks = jnp.asarray(order, jnp.int32)[lanes // width] ^ place[1]
        source = blocks * width + lanes % width
        shuffle = (lanes[:, None] == source[None, :]).astype(single)
        moved = jnp.dot(values * inv, shuffle, precision=lax.Precision.HIGHEST)
        out = (moved * gain).astype(lowp)
        return jnp.swapaxes(out.reshape(streams * count, groups, D), 0, 1)
    tile = 128
    return pl.pallas_call(
        functools.partial(state_kernel, order, width),
        name="state_norm",
        out_shape=jax.ShapeDtypeStruct((groups, streams * count, D), lowp),
        grid_spec=pltpu.PrefetchScalarGridSpec(
            num_scalar_prefetch=1,
            grid=(streams, count // tile),
            in_specs=[
                pl.BlockSpec((1, D), lambda n, i, s: (0, 0)),
                pl.BlockSpec((1, tile * groups, D), lambda n, i, s: (s[0] ^ n, i, 0)),
            ],
            out_specs=pl.BlockSpec(
                (groups, tile, D), lambda n, i, s: (0, n * (count // tile) + i, 0)
            ),
            scratch_shapes=[pltpu.VMEM((len(order), tile * groups, width), single)],
        ),
        compiler_params=params(60),
        cost_estimate=cost(0, 4 * streams * count * groups * D),
    )(place, gain, states)


def compress_kernel(old_ref, key_ref, value_ref, conv_ref, comp_ref, raw_ref):
    heads = conv_ref.shape[0]
    wide = heads * DH
    for part, weight_ref in enumerate((key_ref, value_ref)):
        sums = [None] * heads
        for j in range(RATE):
            raw = mm(old_ref[j], weight_ref[...], NT).astype(lowp)
            raw_ref[j, :, part * wide : (part + 1) * wide] = raw
            for n in range(heads):
                piece = raw[:, n * DH : (n + 1) * DH]
                term = mm(piece, conv_ref[n, j * DH : (j + 1) * DH, :])
                sums[n] = term if j == 0 else sums[n] + term
        for n in range(heads):
            first = part * wide + n * DH
            comp_ref[:, first : first + DH] = sums[n].astype(lowp)


def compress(old3, weights, conv):
    rows = old3.shape[1]
    wide = conv.shape[0] * DH
    tile = 256
    return pl.pallas_call(
        compress_kernel,
        name="compress",
        grid=(rows // tile,),
        out_shape=(
            jax.ShapeDtypeStruct((rows, 2 * wide), lowp),
            jax.ShapeDtypeStruct((RATE, rows, 2 * wide), lowp),
        ),
        in_specs=[
            pl.BlockSpec((RATE, tile, D), lambda i: (0, i, 0)),
            pl.BlockSpec((wide, D), lambda i: (1, 0)),
            pl.BlockSpec((wide, D), lambda i: (2, 0)),
            pl.BlockSpec(conv.shape, lambda i: (0, 0, 0)),
        ],
        out_specs=(
            pl.BlockSpec((tile, 2 * wide), lambda i: (i, 0)),
            pl.BlockSpec((RATE, tile, 2 * wide), lambda i: (0, i, 0)),
        ),
        compiler_params=params(60),
        cost_estimate=cost(4 * RATE * rows * wide * D, 12 * MIB),
    )(old3, weights, weights, conv)


def expand_kernel(grad_ref, raw_ref, conv_ref, out_ref, conv_out_ref):
    heads = conv_ref.shape[0]
    for h in range(heads):
        for j in range(RATE):
            rows = slice(j * DH, (j + 1) * DH)
            taps = conv_ref[h, rows, :]
            total = None
            for n in (h, heads + h):
                cols = slice(n * DH, (n + 1) * DH)
                grad = grad_ref[:, cols]
                out_ref[j, :, cols] = mm(grad, taps, NT).astype(lowp)
                term = mm(raw_ref[j, :, cols], grad, TN)
                total = term if total is None else total + term
            conv_out_ref[h, rows, :] = total


def expand(grad, raw, conv):
    return pl.pallas_call(
        expand_kernel,
        name="expand",
        out_shape=(
            jax.ShapeDtypeStruct(raw.shape, lowp),
            jax.ShapeDtypeStruct(conv.shape, single),
        ),
        in_specs=[vmem()] * 3,
        out_specs=(vmem(), vmem()),
        compiler_params=params(60),
        cost_estimate=cost(2000 * MIB, 12 * MIB),
    )(grad, raw, conv)


def masked_scores(info_ref, query, keys):
    rows = query.shape[0]
    scale = DH ** (-0.5)
    result = []
    for which, key in enumerate(keys):
        slots = key.shape[0]
        col = lax.broadcasted_iota(jnp.int32, (rows, slots), 1)
        if which < 2:
            seen = col >= slots - info_ref[2 * pl.program_id(0) + which]
        else:
            row = lax.broadcasted_iota(jnp.int32, (rows, slots), 0)
            shift = info_ref[4]
            row = row + shift
            col = col + shift
            row = jnp.where(row >= slots, row - slots, row)
            col = jnp.where(col >= slots, col - slots, col)
            seen = col <= row
        result.append(jnp.where(seen, mm(query, key, NT) * scale, -1e30))
    return result


def rows_of(ref):
    return ref[...].reshape(-1, ref.shape[-1])


def attend_kernel(info_ref, q_ref, ks_ref, vs_ref, kc_ref, vc_ref, km_ref, vm_ref, out_ref, lse_ref):
    query = rows_of(q_ref)
    scores = masked_scores(info_ref, query, [kc_ref[...], km_ref[...], rows_of(ks_ref)])
    top = functools.reduce(jnp.maximum, [jnp.max(s, axis=-1, keepdims=True) for s in scores])
    total = 0.0
    mixed = 0.0
    for score, value in zip(scores, (vc_ref[...], vm_ref[...], rows_of(vs_ref))):
        weight = jnp.exp(score - top)
        total = total + jnp.sum(weight, axis=-1, keepdims=True)
        mixed = mixed + mm(weight.astype(lowp), value)
    out_ref[...] = (mixed / total).astype(lowp).reshape(out_ref.shape)
    lse_ref[0, 0] = top + jnp.log(total)


def attend_back_kernel(
    info_ref, q_ref, ks_ref, vs_ref, kc_ref, vc_ref, km_ref, vm_ref, lse_ref, up_ref,
    seg_ref, comp_ref, mem_ref,
):
    head = pl.program_id(1)
    wide = pl.num_programs(1) * DH
    scale = DH ** (-0.5)
    query = rows_of(q_ref)
    upstream = rows_of(up_ref)
    keys = [kc_ref[...], km_ref[...], rows_of(ks_ref)]
    scores = masked_scores(info_ref, query, keys)
    probs = [jnp.exp(s - lse_ref[0, 0]) for s in scores]
    prob_grads = [
        mm(upstream, v, NT) for v in (vc_ref[...], vm_ref[...], rows_of(vs_ref))
    ]
    inner = 0.0
    for p, g in zip(probs, prob_grads):
        inner = inner + jnp.sum(p * g, axis=-1, keepdims=True)
    here = pl.ds(pl.multiple_of(head * DH, DH), DH)
    second = pl.ds(pl.multiple_of(wide + head * DH, DH), DH)
    third = pl.ds(pl.multiple_of(2 * wide + head * DH, DH), DH)
    query_grad = 0.0
    places = ((comp_ref, here, second), (mem_ref, here, second), (seg_ref, second, third))
    for p, g, key, (ref, key_at, value_at) in zip(probs, prob_grads, keys, places):
        score_grad = (p * (g - inner)).astype(lowp)
        query_grad = query_grad + mm(score_grad, key)
        shape = ref.shape[:-1] + (DH,)
        key_grad = (mm(score_grad, query, TN) * scale).astype(lowp)
        value_grad = mm(p.astype(lowp), upstream, TN).astype(lowp)
        ref[..., key_at] = key_grad.reshape(shape)
        ref[..., value_at] = value_grad.reshape(shape)
    shape = seg_ref.shape[:-1] + (DH,)
    seg_ref[..., here] = (query_grad * scale).astype(lowp).reshape(shape)


def head_specs(seg, comp, mem, heads):
    streams = seg.shape[1]

    def of_seg(first):
        return pl.BlockSpec((2, 1, seg.shape[2], DH), lambda n, h: (0, n, 0, first + h))

    def cols(array, first):
        return pl.BlockSpec((array.shape[0] // streams, DH), lambda n, h: (n, first + h))

    return [
        smem(),
        of_seg(0),
        of_seg(heads),
        of_seg(2 * heads),
        cols(comp, 0),
        cols(comp, heads),
        cols(mem, 0),
        cols(mem, heads),
    ]


def attend(info, seg, comp, mem):
    _, streams, half, _ = seg.shape
    heads = comp.shape[1] // (2 * DH)
    return pl.pallas_call(
        attend_kernel,
        name="attend",
        grid=(streams, heads),
        out_shape=(
            jax.ShapeDtypeStruct((2, streams, half, heads * DH), lowp),
            jax.ShapeDtypeStruct((streams, heads, 2 * half, 1), single),
        ),
        in_specs=head_specs(seg, comp, mem, heads),
        out_specs=(
            pl.BlockSpec((2, 1, half, DH), lambda n, h: (0, n, 0, h)),
            pl.BlockSpec((1, 1, 2 * half, 1), lambda n, h: (n, h, 0, 0)),
        ),
        compiler_params=params(60),
        cost_estimate=cost(7000 * MIB, 6 * MIB),
    )(info, seg, seg, seg, comp, comp, mem, mem)


def attend_back(info, seg, comp, mem, lse, upstream):
    _, streams, half, wide = seg.shape
    heads = comp.shape[1] // (2 * DH)
    slots = comp.shape[0] // streams
    kept = mem.shape[0] // streams
    return pl.pallas_call(
        attend_back_kernel,
        name="attend_back",
        grid=(streams, heads),
        out_shape=(
            jax.ShapeDtypeStruct(seg.shape, lowp),
            jax.ShapeDtypeStruct(comp.shape, lowp),
            jax.ShapeDtypeStruct(mem.shape, lowp),
        ),
        in_specs=head_specs(seg, comp, mem, heads)
        + [
            pl.BlockSpec((1, 1, 2 * half, 1), lambda n, h: (n, h, 0, 0)),
            pl.BlockSpec((2, 1, half, DH), lambda n, h: (0, n, 0, h)),
        ],
        out_specs=(
            pl.BlockSpec((2, 1, half, wide), lambda n, h: (0, n, 0, 0)),
            pl.BlockSpec((slots, comp.shape[1]), lambda n, h: (n, 0)),
            pl.BlockSpec((kept, mem.shape[1]), lambda n, h: (n, 0)),
        ),
        compiler_params=params(60),
        cost_estimate=cost(11000 * MIB, 9 * MIB),
    )(info, seg, seg, seg, comp, comp, mem, mem, lse, upstream)


def columns_of(rows):
    tall = jnp.concatenate([rows, jnp.zeros((120, rows.shape[1]), single)], axis=0)
    return jnp.transpose(tall)


def logits_kernel(words, info_ref, pair_ref, near_ref, left_ref, right_ref, out_ref, stat_ref, held):
    step = pl.program_id(0)

    @pl.when(step == 0)
    def _():
        held[...] = pair_ref[...]

    @pl.when(step == 1)
    def _():
        held[...] = near_ref[...]

    half = left_ref.shape[1]
    slots = left_ref.shape[0]
    logits = mm(held[:, :half], left_ref[...], NT) + mm(held[:, half:], right_ref[...], NT)
    wanted = columns_of(info_ref[0])[:, 0:1].astype(jnp.int32)
    col = lax.broadcasted_iota(jnp.int32, logits.shape, 1)
    hit = jnp.sum(jnp.where(col == wanted, logits, 0.0), axis=-1, keepdims=True)
    edge = slots - 128
    last = jnp.where(col[:, edge:] < words, logits[:, edge:], -1e30)
    top = jnp.max(last, axis=-1, keepdims=True)
    top = jnp.maximum(top, jnp.max(logits[:, :edge], axis=-1, keepdims=True))
    raised = jnp.exp(logits[:, :edge] - top)
    last = jnp.exp(last - top)
    total = jnp.sum(raised, axis=-1, keepdims=True) + jnp.sum(last, axis=-1, keepdims=True)
    out_ref[:, :edge] = raised.astype(lowp)
    out_ref[:, edge:] = last.astype(lowp)
    lane = lax.broadcasted_iota(jnp.int32, (logits.shape[0], 128), 1)
    packed = jnp.where(lane == 0, top, jnp.where(lane == 1, total, jnp.where(lane == 2, hit, 0.0)))
    stat_ref[...] = jnp.transpose(packed)[:8]


def logits_part(words, chunk, info, pair, near, left, right):
    rows = pair.shape[0] + near.shape[0]
    slots = left.shape[0]
    tile = pair.shape[0]
    whole = lambda i: (0, 0)
    return pl.pallas_call(
        functools.partial(logits_kernel, words),
        name="logits_part",
        grid=(2,),
        out_shape=(
            jax.ShapeDtypeStruct((rows, slots), lowp),
            jax.ShapeDtypeStruct((8, rows), single),
        ),
        in_specs=[
            pl.BlockSpec((1, 8, tile), lambda i: (chunk, 0, i)),
            pl.BlockSpec((tile, D), whole),
            pl.BlockSpec((tile, D), whole),
            pl.BlockSpec(left.shape, whole),
            pl.BlockSpec(right.shape, whole),
        ],
        out_specs=(
            pl.BlockSpec((tile, slots), lambda i: (i, 0)),
            pl.BlockSpec((8, tile), lambda i: (0, i)),
        ),
        scratch_shapes=[pltpu.VMEM((tile, D), lowp)],
        compiler_params=params(60),
        cost_estimate=cost(4 * rows * slots * D, 10 * MIB),
    )(info, pair, near, left, right)


def logits_back_kernel(info_ref, factor_ref, in_ref, left_ref, right_ref, out_ref, keep_ref, send_ref):
    step = pl.program_id(0)
    info = columns_of(info_ref[0])
    wanted = info[:, 0:1].astype(jnp.int32)
    counted = info[:, 1:2]
    factor = columns_of(factor_ref[0])[:, 0:1]
    raised = in_ref[...].astype(single)
    col = lax.broadcasted_iota(jnp.int32, raised.shape, 1)
    grads = (raised * factor - jnp.where(col == wanted, counted, 0.0)).astype(lowp)
    out_ref[...] = grads
    half = left_ref.shape[1]
    left = mm(grads, left_ref[...]).astype(lowp)
    right = mm(grads, right_ref[...]).astype(lowp)

    @pl.when(step == 0)
    def _():
        send_ref[:, :half] = left
        send_ref[:, half:] = right

    @pl.when(step == 1)
    def _():
        keep_ref[:, :half] = left
        keep_ref[:, half:] = right


def logits_back(chunk, info, factor, raised, left, right):
    rows, slots = raised.shape
    tile = rows // 2
    whole = lambda i: (0, 0)
    return pl.pallas_call(
        logits_back_kernel,
        name="logits_back",
        grid=(2,),
        out_shape=(
            jax.ShapeDtypeStruct((rows, slots), lowp),
            jax.ShapeDtypeStruct((tile, D), lowp),
            jax.ShapeDtypeStruct((tile, D), lowp),
        ),
        in_specs=[
            pl.BlockSpec((1, 8, tile), lambda i: (chunk, 0, 1 - i)),
            pl.BlockSpec((1, 8, tile), lambda i: (chunk, 0, 1 - i)),
            pl.BlockSpec((tile, slots), lambda i: (1 - i, 0)),
            pl.BlockSpec(left.shape, whole),
            pl.BlockSpec(right.shape, whole),
        ],
        out_specs=(
            pl.BlockSpec((tile, slots), lambda i: (1 - i, 0)),
            pl.BlockSpec((tile, D), whole),
            pl.BlockSpec((tile, D), whole),
        ),
        compiler_params=params(60),
        cost_estimate=cost(4 * rows * slots * D, 12 * MIB),
    )(info, factor, raised, left, right)


def halves(total, keep_ref, send_ref):
    half = keep_ref.shape[1]
    keep_ref[...] = total[:, :half]
    send_ref[...] = total[:, half:].astype(send_ref.dtype)


def table_grad_kernel(count, *refs):
    total = None
    for i in range(count):
        rows = refs[count + 2 * i].shape[0]
        for j in range(2):
            term = mm(refs[i][j * rows : (j + 1) * rows, :], refs[count + 2 * i + j][...], TN)
            total = term if total is None else total + term
    halves(total, *refs[3 * count :])


def table_grad_part(grads, inputs):
    count = len(grads)
    rows = sum(g.shape[0] for g in grads)
    slots = grads[0].shape[1]
    block = 256
    if rows > 4096:
        total = sum(
            mm(g, jnp.concatenate(v), TN) for g, v in zip(grads, inputs)
        )
        keep, send = split(total, 1, 2)
        return keep, send.astype(lowp)
    inputs = [half for pair in inputs for half in pair]
    return pl.pallas_call(
        functools.partial(table_grad_kernel, count),
        name="table_grad_part",
        grid=(slots // block,),
        out_shape=(
            jax.ShapeDtypeStruct((slots, D // 2), single),
            jax.ShapeDtypeStruct((slots, D // 2), lowp),
        ),
        in_specs=[pl.BlockSpec((g.shape[0], block), lambda i: (0, i)) for g in grads]
        + [pl.BlockSpec(v.shape, lambda i: (0, 0)) for v in inputs],
        out_specs=(
            pl.BlockSpec((block, D // 2), lambda i: (i, 0)),
            pl.BlockSpec((block, D // 2), lambda i: (i, 0)),
        ),
        compiler_params=params(60),
        cost_estimate=cost(3 * rows * slots * D, 30 * MIB),
    )(*grads, *inputs)


def hidden_grad_kernel(blocks, pre_ref, act_ref, in_ref, down_ref, keep_ref, send_ref):
    step = pl.program_id(0)

    @pl.when(step < blocks)
    def _():
        halves(mm(pre_ref[...], in_ref[...], TN), keep_ref, send_ref)

    @pl.when(step >= blocks)
    def _():
        halves(mm(act_ref[...], down_ref[...], TN), keep_ref, send_ref)


def hidden_grads(pre_grad, hidden_act, ffn_in, down_in):
    rows, hidden = pre_grad.shape
    block = 256
    blocks = hidden // block
    return pl.pallas_call(
        functools.partial(hidden_grad_kernel, blocks),
        name="hidden_grads",
        grid=(2 * blocks,),
        out_shape=(
            jax.ShapeDtypeStruct((2 * hidden, D // 2), single),
            jax.ShapeDtypeStruct((2 * hidden, D // 2), lowp),
        ),
        in_specs=[
            pl.BlockSpec((rows, block), lambda i: (0, jnp.minimum(i, blocks - 1))),
            pl.BlockSpec((rows, block), lambda i: (0, jnp.maximum(i - blocks, 0))),
            pl.BlockSpec((rows, D), lambda i: (0, 0)),
            pl.BlockSpec((rows, D), lambda i: (0, 0)),
        ],
        out_specs=(
            pl.BlockSpec((block, D // 2), lambda i: (i, 0)),
            pl.BlockSpec((block, D // 2), lambda i: (i, 0)),
        ),
        compiler_params=params(60),
        cost_estimate=cost(6 * rows * hidden * D, 16 * MIB),
    )(pre_grad, hidden_act, ffn_in, down_in)


def attn_grad_kernel(
    seg_ref, mixed_ref, mem_ref, old_ref, normed_ref, up_ref, mem_in_ref, old_in_ref, keep_ref, send_ref
):
    which = pl.program_id(0)

    @pl.when(which == 0)
    def _():
        halves(mm(seg_ref[...], normed_ref[...], TN), keep_ref, send_ref)

    @pl.when(which == 3)
    def _():
        halves(mm(mixed_ref[...], up_ref[...], TN), keep_ref, send_ref)

    @pl.when(jnp.logical_and(which > 0, which < 3))
    def _():
        total = mm(seg_ref[...], normed_ref[...], TN)
        total = total + mm(mem_ref[...], mem_in_ref[...], TN)
        total = total + mm(old_ref[...], old_in_ref[...], TN)
        halves(total, keep_ref, send_ref)


def attn_grads(seg_grad, mixed, mem_grad, old_grad, normed, attn_in, mem_in, old_in):
    block = mixed.shape[1]

    def whole(array):
        return pl.BlockSpec(array.shape, lambda i: (0, 0))

    return pl.pallas_call(
        attn_grad_kernel,
        name="attn_grads",
        grid=(4,),
        out_shape=(
            jax.ShapeDtypeStruct((4 * block, D // 2), single),
            jax.ShapeDtypeStruct((4 * block, D // 2), lowp),
        ),
        in_specs=[
            pl.BlockSpec((seg_grad.shape[0], block), lambda i: (0, jnp.minimum(i, 2))),
            whole(mixed),
            pl.BlockSpec((mem_grad.shape[0], block), lambda i: (0, jnp.clip(i - 1, 0, 1))),
            pl.BlockSpec((old_grad.shape[0], block), lambda i: (0, jnp.clip(i - 1, 0, 1))),
            whole(normed),
            whole(attn_in),
            whole(mem_in),
            whole(old_in),
        ],
        out_specs=(
            pl.BlockSpec((block, D // 2), lambda i: (i, 0)),
            pl.BlockSpec((block, D // 2), lambda i: (i, 0)),
        ),
        compiler_params=params(60),
        cost_estimate=cost(9000 * MIB, 24 * MIB),
    )(seg_grad, mixed, mem_grad, old_grad, normed, attn_in, mem_in, old_in)


def scalar_row(values, length=128):
    lane = jnp.arange(length, dtype=jnp.int32)
    row = jnp.zeros((length,), single)
    for i, value in enumerate(values):
        row = jnp.where(lane == i, value, row)
    return row


def local(
    ids,
    targets,
    target_mask,
    memory,
    old_states,
    mem_fill,
    comp_fill,
    table,
    qkv,
    wout,
    wconv,
    wup,
    wdown,
    gains,
    table_rows,
    table_cols,
    qkv_rows,
    qkv_cols,
    out_rows,
    out_cols,
    conv_rows,
    conv_cols,
    up_rows,
    up_cols,
    down_rows,
    down_cols,
    gains_second,
):
    dp_size, head_size = lax.axis_size("dp"), lax.axis_size("head")
    d, h = lax.axis_index("dp"), lax.axis_index("head")
    x, c = h // 2, h % 2
    order = block_order(dp_size)
    reach = dp_size // 2
    streams, seg_len = ids.shape
    half = seg_len // 2
    per_group = streams * seg_len
    vocab, width = table.shape
    assert head_size == 4 and streams == 2

    weights_now = (table, qkv, wout, wconv, wup, wdown)
    rows_old = (table_rows, qkv_rows, out_rows, conv_rows, up_rows, down_rows)
    cols_old = (table_cols, qkv_cols, out_cols, conv_cols, up_cols, down_cols)
    sizes = {"dp": dp_size, "head": head_size}
    row_axes = ("head", "dp", "head", "head", "dp", "head")
    col_axes = ("dp", "head", "dp", "dp", "head", "dp")

    def early_sums(dep):
        _, *tied = together(dep, *rows_old, *weights_now, gains)
        sums = [jnp.sum(old) / sizes[axis] for old, axis in zip(tied[:6], col_axes)]
        sums += [jnp.sum(weight * weight) for weight in tied[6:12]]
        gain_sums = jnp.sum(tied[12] * tied[12], axis=1) / head_size
        return scalar_row(sums + [gain_sums[0], gain_sums[1], gain_sums[2]])

    def core_sum(keep, send, beside=()):
        more, *beside = together(swap(send.astype(lowp), "head", 1), *beside)
        part = keep.astype(single) + more.astype(single)
        return (part, beside) if beside else part

    def stream_sum(part, beside=()):
        keep, send = split(part, 0, 2)
        more, *beside = together(swap(send.astype(lowp), "head", 2), *beside)
        part = keep + more.astype(single)
        return (part, beside) if beside else part

    def group_sum(part, beside=()):
        return stream_sum(core_sum(*split(part, 0, 2)), beside)

    def group_both(part, beside=()):
        far, *beside = together(swap(part, "head", 2), *beside)
        pair = jnp.concatenate([part, far], axis=0)
        both = (pair, swap(pair, "head", 1))
        return (both, beside) if beside else both

    flat = jnp.concatenate(
        [
            ids.astype(single).reshape(-1),
            targets.astype(single).reshape(-1),
            target_mask.astype(single).reshape(-1),
            gains.astype(lowp).astype(single).reshape(-1),
        ]
    )
    room = -flat.shape[0] % 1024
    flat = jnp.concatenate([flat, jnp.zeros((room,), single)]).reshape(1, -1, 128)
    small, small_steps = gather_blocks(flat, 0)
    small = small.reshape(dp_size, -1)
    place = jnp.stack([x, d])

    def field(raw):
        return relative(raw.reshape(-1, 2, 2, half), x, c)

    ids_all = small[:, :per_group]
    position = [order.index(j) for j in range(dp_size)]
    ids_all = jnp.take(ids_all, jnp.asarray(position, jnp.int32)[jnp.arange(dp_size) ^ d], axis=0)
    ids_all = jnp.transpose(field(ids_all), (1, 2, 0, 3)).reshape(-1).astype(jnp.int32)
    table_rows_all = ids_all - h * vocab
    inside = (table_rows_all >= 0) & (table_rows_all < vocab)
    bits = vocab.bit_length()
    token_codes = (jnp.arange(ids_all.shape[0], dtype=jnp.int32) << bits) | table_rows_all
    token_codes = jnp.where(inside, token_codes, -1)
    table_rows_all = jnp.where(inside, table_rows_all, vocab)
    targets_all = field(small[:reach, per_group : 2 * per_group])
    mask_all = field(small[:reach, 2 * per_group : 3 * per_group])
    gain_blocks = small[:, 3 * per_group : 3 * per_group + 3 * width].reshape(dp_size, 3, width)
    gain_vals = jnp.swapaxes(gain_blocks, 0, 1).reshape(3, 1, D)
    count_all = jnp.sum(small[:, 2 * per_group : 3 * per_group])

    heads_own = wconv.shape[0]
    wide = qkv.shape[2]
    conv_rows_own = wconv.size // width
    low_qkv = qkv.astype(lowp)
    pack_one = jnp.concatenate(
        [
            jnp.swapaxes(low_qkv, 1, 2).reshape(3 * wide, width),
            wout.astype(lowp),
            wconv.astype(lowp).reshape(conv_rows_own, width),
        ]
    )
    own_half, far_half = split(table_rows_all, 0, 2)
    kept = {}

    def beside_lookup(moved):
        moved, kept["far"], kept["own"] = together(
            moved, lookup(far_half, table), lookup(own_half, table)
        )
        return moved

    def beside_memory(moved):
        looked = (kept["own"] + swap(kept["far"], "head", 1)).reshape(2, -1, width)
        mem_normed = state_norm(place, gain_vals[0], memory, 1)[0]
        moved, more, kept["mem"] = together(moved, swap(looked[1], "head", 2), mem_normed)
        looked = (looked[0] + more).reshape(dp_size, half, width)
        kept["looked"] = lax.all_to_all(looked, "dp", 0, 0)
        return moved

    own_one, steps_one = gather_blocks(
        after(pack_one, small_steps[0]), 1, (beside_lookup, beside_memory)
    )
    conv_lanes = jnp.arange(DH, dtype=jnp.int32)
    conv_width = DH // dp_size
    conv_natural = (jnp.asarray(order, jnp.int32)[conv_lanes // conv_width] ^ d) * conv_width
    conv_natural = conv_natural + conv_lanes % conv_width
    conv_shuffle = (conv_natural[:, None] == conv_lanes[None, :]).astype(lowp)
    taps = heads_own * RATE * DH

    def conv_natural_order(rows):
        value = jnp.swapaxes(rows.reshape(conv_rows_own, dp_size, width), 0, 1)
        value = jnp.swapaxes(value.reshape(dp_size, taps, conv_width), 0, 1)
        moved = mm(value.reshape(taps, DH), conv_shuffle).astype(lowp)
        return moved.reshape(heads_own, RATE * DH, DH)

    def conv_block_order(value):
        moved = mm(value.astype(lowp).reshape(taps, DH), conv_shuffle, NT).astype(lowp)
        moved = jnp.swapaxes(moved.reshape(taps, dp_size, conv_width), 0, 1)
        moved = jnp.swapaxes(moved.reshape(dp_size, conv_rows_own, width), 0, 1)
        return moved.reshape(conv_rows_own, D)

    full_conv = conv_natural_order(own_one[4 * wide :])

    hidden_own = wup.shape[1]
    pack_two = jnp.concatenate([wup.astype(lowp).T, wdown.astype(lowp)])

    old_normed = state_norm(place, gain_vals[0], old_states, RATE)

    def beside_old(moved):
        moved, looked, kept["old"] = together(moved, kept["looked"], old_normed)
        kept["embedded"], kept["normed"] = place_embedding(place, looked, gain_vals[0])
        return moved

    def beside_compress(moved):
        moved, *kept["comp"] = together(moved, *compress(kept["old"], own_one, full_conv))
        return moved

    near_two, steps_two = gather_blocks(
        after(pack_two, steps_one[1]), 1, (beside_old, beside_compress), 1
    )
    near_up, near_down = split(near_two, 0, 2)
    far_up, far_down = swap(near_up, "dp", 1), swap(near_down, "dp", 1)
    mem_normed, old_normed = kept["mem"], kept["old"]
    embedded_low = kept["embedded"]
    embedded = embedded_low.astype(single)
    normed = jnp.concatenate(group_both(kept["normed"]))
    comp, old_raw = kept["comp"]

    words = vocab // reach
    z = d // 2
    z_groups = [[2 * i + b for i in range(reach)] for b in range(2)]
    slots = -(-words // 256) * 256


    comp_counts = jnp.where(x == 1, jnp.flip(comp_fill), comp_fill)
    mem_counts = jnp.where(x == 1, jnp.flip(mem_fill), mem_fill)
    info = [comp_counts[0], mem_counts[0], comp_counts[1], mem_counts[1], c * half]
    lane = jnp.arange(8, dtype=jnp.int32)
    info = sum(jnp.where(lane == i, value, 0) for i, value in enumerate(info)).astype(jnp.int32)

    in_weight = own_one[: 3 * wide]
    mem = mm(mem_normed, own_one[wide : 3 * wide], NT).astype(lowp)
    seg = mm(normed, in_weight, NT).astype(lowp).reshape(2, streams, half, 3 * wide)
    low_table = after(table.astype(lowp), seg).reshape(reach, words, width)
    low_table = lax.all_to_all(low_table, "dp", 0, 0, axis_index_groups=z_groups)
    mixed, lse = attend(info, seg, comp, mem)
    mixed = mixed.reshape(-1, wide)
    attn_sum, (far_up,) = core_sum(
        *split(mm(mixed, own_one[3 * wide : 4 * wide]), 0, 2), (far_up,)
    )
    attn_sum, (early, far_down) = stream_sum(attn_sum, (early_sums(mixed), far_down))
    after_attn = embedded + attn_sum
    ffn_in, inv_second = rms(after_attn, gain_vals[1])
    ffn_in, (low_table,) = group_both(ffn_in, (low_table,))
    near_table = [
        lax.dynamic_index_in_dim(low_table, z ^ (m // 2), 0, keepdims=False) for m in order[:reach]
    ]
    near_table = jnp.concatenate(near_table, axis=1)
    near_table = jnp.concatenate([near_table, jnp.zeros((slots - words, D // 2), lowp)], axis=0)
    ffn_in = jnp.concatenate(ffn_in)
    full_up = jnp.concatenate([near_up, far_up], axis=1)
    full_down = jnp.concatenate([near_down, far_down], axis=1)
    far_table = swap(near_table, "dp", 1)
    hidden_pre = mm(ffn_in, full_up, NT)
    hidden_act = jax.nn.gelu(hidden_pre).astype(lowp)
    after_ffn = after_attn + group_sum(mm(hidden_act, full_down))
    final_in, inv_third = rms(after_ffn, gain_vals[2])

    word_start = (h * vocab + z * words).astype(single)
    wanted_all = targets_all - word_start
    wanted_all = jnp.where((wanted_all >= 0) & (wanted_all < words), wanted_all, -1.0)
    info_all = jnp.stack([wanted_all, mask_all] + [jnp.zeros_like(mask_all)] * 6)
    info_all = jnp.transpose(info_all, (1, 0, 2, 3, 4)).reshape(reach, 8, per_group)
    pieces = [final_in]
    chunks = []
    raised = []
    stats = []

    def next_chunk():
        i = len(chunks)
        if i == 0:
            chunks.append(group_both(pieces[i]))
        else:
            chunk, (stats[i - 1],) = group_both(pieces[i], (stats[i - 1],))
            chunks.append(chunk)
        out, stat = logits_part(words, i, info_all, *chunks[i], near_table, far_table)
        raised.append(out)
        stats.append(stat)

    mask = dp_size // 2
    while mask > 1:
        moved = swap(reorder(pieces, mask), "dp", mask)
        if len(pieces) == 1:
            moved, own_codes, own_count = together(
                moved, *own_list(after(token_codes, final_in))
            )
            next_chunk()
        elif len(pieces) == 2:
            moved, stats[0] = together(moved, stats[0])
        pieces += split(moved, 0, len(pieces))
        mask //= 2
    while len(chunks) < reach:
        next_chunk()
    stats = [stat[:3].reshape(3, 1, 2, 2, half) for stat in stats]
    own_stats = jnp.concatenate(stats, axis=1)

    def combine(first, second):
        top = jnp.maximum(first[0], second[0])
        total = first[1] * jnp.exp(first[0] - top) + second[1] * jnp.exp(second[0] - top)
        return jnp.stack([top, total, first[2] + second[2]])

    merged = own_stats
    merged = combine(merged, jnp.flip(swap(merged, "head", 1), 2))
    merged = combine(merged, jnp.flip(swap(merged, "head", 2), 3))
    mask = 2
    while mask < dp_size:
        other = split(swap(merged, "dp", mask), 1, reach)
        other = [other[order.index(j ^ mask)] for j in order[:reach]]
        merged = combine(merged, jnp.concatenate(other, axis=1))
        mask *= 2
    log_total = merged[0] + jnp.log(merged[1])
    loss_local = jnp.sum(mask_all[0, 0, 0] * (log_total[0, 0, 0] - merged[2, 0, 0, 0]))
    factor_all = jnp.exp(own_stats[0] - log_total)

    factor_all = factor_all.reshape(reach, 1, per_group) * info_all[:, 1:2]
    factor_all = jnp.broadcast_to(factor_all, info_all.shape)
    dlogits = [None] * reach
    parts = [None] * reach
    for i in reversed(range(reach)):
        dlogits[i], *core = logits_back(
            i, info_all, factor_all, raised[i], near_table, far_table
        )
        if i + 1 < reach:
            parts[i + 1], (dlogits[i], *core) = stream_sum(parts[i + 1], (dlogits[i], *core))
        parts[i] = core_sum(*core)
    parts[0] = stream_sum(parts[0])
    table_parts = []
    mask = 2
    while len(parts) > 1:
        count = len(parts) // 2
        moved = swap(reorder(parts[count:], mask), "dp", mask)
        if mask == 2:
            moved, dlogits[0] = together(moved, dlogits[0])
        elif mask == 4:
            moved, *table_parts = together(moved, *table_grad_part(dlogits, chunks))
        moved = split(moved.astype(single), 0, count)
        parts = [part + more for part, more in zip(parts, moved)]
        mask *= 2
    final_grad = parts[0]

    grad_after_ffn = rms_back(after_ffn, inv_third, gain_vals[2], final_grad)
    moved_table = swap(table_parts[1], "dp", 1)
    down_in = group_both(grad_after_ffn.astype(lowp))
    down_in = jnp.concatenate(down_in)
    act_grad = mm(down_in, full_down, NT)
    pre_grad = jax.vjp(jax.nn.gelu, hidden_pre)[1](act_grad)[0].astype(lowp)
    two = hidden_grads(pre_grad, hidden_act, ffn_in, down_in)
    ffn_in_grad, (*two, moved_table) = group_sum(mm(pre_grad, full_up), (*two, moved_table))
    keep = table_parts[0] + moved_table.astype(single)
    table_pieces = jnp.stack(split(keep[:words].astype(lowp), 1, reach))
    position = [order.index(2 * i) for i in range(reach)]
    position = jnp.asarray(position, jnp.int32)[jnp.arange(reach) ^ z]
    table_pieces = jnp.concatenate(
        [lax.dynamic_index_in_dim(table_pieces, position[i], 0) for i in range(reach)]
    )
    table_pieces = lax.all_to_all(table_pieces, "dp", 0, 0, axis_index_groups=z_groups)
    grad_after_attn = grad_after_ffn + rms_back(after_attn, inv_second, gain_vals[1], ffn_in_grad)
    attn_in = jnp.concatenate(group_both(grad_after_attn.astype(lowp)))

    mixed_grad = mm(attn_in, own_one[3 * wide : 4 * wide], NT).astype(lowp)
    mixed_grad = mixed_grad.reshape(2, streams, half, wide)
    seg_grad, comp_grad, mem_grad = attend_back(info, seg, comp, mem, lse, mixed_grad)
    seg_grad = seg_grad.reshape(-1, 3 * wide)

    def beside_expand(moved):
        keep, send = split(mm(seg_grad, in_weight), 0, 2)
        more = swap(send.astype(lowp), "head", 1)
        moved, more, kept["table"], *kept["old"] = together(
            moved, more, table_pieces, *expand(comp_grad, old_raw, full_conv)
        )
        kept["seg_in"] = split(keep + more.astype(single), 0, 2)
        return moved

    def beside_sums(moved):
        seg_in, seg_in_far = kept["seg_in"]
        seg_in_far = swap(seg_in_far.astype(lowp), "head", 2)
        old_grad, conv_sum = kept["old"]
        sums = attn_grads(
            seg_grad,
            mixed,
            mem_grad,
            old_grad.reshape(-1, old_grad.shape[-1]),
            normed,
            attn_in,
            mem_normed,
            old_normed.reshape(-1, D),
        )
        conv_sum = split(conv_block_order(conv_sum), 1, 2)
        sums = [jnp.concatenate([part, more.astype(part.dtype)]) for part, more in zip(sums, conv_sum)]
        seg_in_far, *kept["sums"] = together(seg_in_far, *sums)
        rows_grad = embed_back(
            place, embedded_low, gain_vals[0], seg_in, seg_in_far, grad_after_attn
        )
        moved, kept["rows"] = together(moved, lax.all_to_all(rows_grad, "dp", 0, 0))
        return moved

    def beside_rows(moved):
        moved, kept["rows"] = together(moved, kept["rows"])
        return moved

    def beside_streams(moved):
        moved, far = together(moved, swap(kept["rows"], "head", 2))
        kept["rows"] = jnp.stack([kept["rows"], far])
        return moved

    two = reduce_blocks(*two, (beside_expand, beside_sums))
    one = reduce_blocks(*kept["sums"], (beside_rows, beside_streams))
    rows_grad = kept["rows"]
    rows_grad = jnp.stack([rows_grad, swap(rows_grad, "head", 1)]).reshape(-1, width)
    table_base = kept["table"].astype(single).reshape(vocab, width)

    up_grad = two[:hidden_own].T
    down_grad = two[hidden_own:]
    qkv_grad = jnp.swapaxes(one[: 3 * wide].reshape(3, wide, width), 1, 2)
    out_grad = one[3 * wide : 4 * wide]
    conv_grad = one[4 * wide :].reshape(wconv.shape)
    table_grad = scatter(bits, own_count, own_codes, table_base, rows_grad)

    gains_low = gains.astype(lowp).astype(single)
    gain_part = jnp.stack(
        [
            jnp.sum(low_qkv.astype(single) * qkv_grad, axis=(0, 2)),
            jnp.sum(wup.astype(lowp).astype(single) * up_grad, axis=1),
            jnp.sum(table.astype(lowp).astype(single) * table_base, axis=0),
        ]
    )

    grads = (table_grad, qkv_grad, out_grad, conv_grad, up_grad, down_grad)
    def sum_over_dp(joined):
        mask = 1
        while mask < dp_size:
            joined = joined + swap(joined, "dp", mask)
            mask *= 2
        return joined

    row_part = []
    col_part = []
    for grad in grads:
        square = grad * grad
        row_part.append(jnp.sum(square, axis=-1))
        col_part.append(jnp.sum(square, axis=tuple(range(square.ndim - 1))))
    row_q, row_u, col_e, col_o, col_c, col_d, gain_raw, early = lax.psum(
        (
            row_part[1],
            row_part[4],
            col_part[0],
            col_part[2],
            col_part[3],
            col_part[5],
            gain_part,
            early + scalar_row([0.0] * 15 + [loss_local]),
        ),
        "head",
    )
    lanes = [col_e, jnp.sum(row_q, axis=0), col_o]
    lanes += [jnp.concatenate([col_c, jnp.zeros((width - col_c.shape[0],), single)]), row_u, col_d]
    members = [col_part[4], row_part[5], row_part[3], row_part[2], col_part[1], *lanes, row_part[0], early]
    joined = jnp.concatenate([m.reshape(-1) for m in members])
    joined = sum_over_dp(jnp.concatenate([joined, jnp.zeros((-joined.shape[0] % 1024,), single)]))
    sums = []
    start = 0
    for member in members:
        sums.append(joined[start : start + member.size].reshape(member.shape))
        start += member.size
    col_u, row_d, row_c, row_o, col_q, *lanes, row_e, early = sums
    square_total = [jnp.sum(lane) for lane in lanes]
    row_sums = [row_e, row_q, row_o, row_c, row_u, row_d]
    col_sums = [col_e, col_q, col_o, col_c, col_u, col_d]
    weight_total = early[6:15]
    loss_all = early[15]
    inverse = 1.0 / count_all
    decay = 1.0 - STEP ** (-0.8)
    updates = []
    stats_new = []
    scaled = []
    counts = []
    update_sq = []
    for index in range(6):
        rows_total = rows_old[index].size * sizes[row_axes[index]]
        cols_total = cols_old[index].size * sizes[col_axes[index]]
        grad_scaled = grads[index] * inverse
        rows_new = decay * rows_old[index] + (1.0 - decay) * (
            row_sums[index] * inverse * inverse / cols_total + TINY_SQUARE
        )
        cols_new = decay * cols_old[index] + (1.0 - decay) * (
            col_sums[index] * inverse * inverse / rows_total + TINY_SQUARE
        )
        mean_row = decay * early[index] / rows_total + (1.0 - decay) * (
            square_total[index] * inverse * inverse / (rows_total * cols_total) + TINY_SQUARE
        )
        second = rows_new[..., None] * cols_new / mean_row
        direction = grad_scaled * lax.rsqrt(second)
        updates.append(direction)
        stats_new.append((rows_new, cols_new))
        scaled.append(grad_scaled)
        counts.append(rows_total * cols_total)
        update_sq.append(jnp.sum(direction * direction))
    gain_scaled = gain_raw / gains_low * inverse
    second_new = decay * gains_second + (1.0 - decay) * (gain_scaled * gain_scaled + TINY_SQUARE)
    gain_dir = gain_scaled * lax.rsqrt(second_new)
    for which in range(3):
        update_sq.append(jnp.sum(gain_dir[which] * gain_dir[which]) / head_size)
    update_total = after(scalar_row(update_sq, 1024), loss_all)
    for mask in (1, 2):
        update_total = update_total + swap(update_total, "head", mask)
    update_total = sum_over_dp(update_total)[:9]
    results = [loss_all, count_all]
    for index in range(6):
        factor = jnp.maximum(0.001, jnp.sqrt(weight_total[index] / counts[index]))
        denom = jnp.maximum(1.0, jnp.sqrt(update_total[index] / counts[index]) / CLIP_LEVEL)
        new_weight = weights_now[index] - LEARN_RATE * factor * updates[index] / denom
        results += [new_weight, scaled[index], stats_new[index][0], stats_new[index][1]]
    gain_factor = jnp.maximum(0.001, jnp.sqrt(weight_total[6:] / D))[:, None]
    gain_denom = jnp.maximum(1.0, jnp.sqrt(update_total[6:] / D) / CLIP_LEVEL)[:, None]
    results += [gains - LEARN_RATE * gain_factor * gain_dir / gain_denom, gain_scaled, second_new]
    return tuple(results)


def solution(mesh):
    in_specs = (
        P("dp", None),
        P("dp", None),
        P("dp", None),
        P("dp", None, None),
        P("dp", None, None),
        P("dp"),
        P("dp"),
        P("head", "dp"),
        P(None, "dp", "head"),
        P("head", "dp"),
        P("head", None, "dp"),
        P("dp", "head"),
        P("head", "dp"),
        P(None, "dp"),
        P("head"),
        P("dp"),
        P(None, "dp"),
        P("head"),
        P("head"),
        P("dp"),
        P("head", None),
        P("dp"),
        P("dp"),
        P("head"),
        P("head"),
        P("dp"),
        P(None, "dp"),
    )
    out_specs = (
        P(),
        P(),
        P("head", "dp"),
        P("head", "dp"),
        P("head"),
        P("dp"),
        P(None, "dp", "head"),
        P(None, "dp", "head"),
        P(None, "dp"),
        P("head"),
        P("head", "dp"),
        P("head", "dp"),
        P("head"),
        P("dp"),
        P("head", None, "dp"),
        P("head", None, "dp"),
        P("head", None),
        P("dp"),
        P("dp", "head"),
        P("dp", "head"),
        P("dp"),
        P("head"),
        P("head", "dp"),
        P("head", "dp"),
        P("head"),
        P("dp"),
        P(None, "dp"),
        P(None, "dp"),
        P(None, "dp"),
    )
    return jax.shard_map(local, mesh=mesh, in_specs=in_specs, out_specs=out_specs, check_vma=False)
```

```python
import functools

import jax
import jax.numpy as jnp
from jax import lax
from jax.experimental import pallas as pl
from jax.experimental.pallas import tpu as pltpu
from jax.sharding import PartitionSpec as P

D = 1024
H = 8
DH = 128
MEM = 512
CMEM = 512
RATE = 3
STEP = 10


TINY_NORM = 1e-06
TINY_SQUARE = 1e-30
LEARN_RATE = 0.5
CLIP_LEVEL = 1.0

lowp = jnp.bfloat16
single = jnp.float32
NT = (((1,), (1,)), ((), ()))
TN = (((0,), (0,)), ((), ()))
NN = (((1,), (0,)), ((), ()))
MIB = 1024 * 1024


def mm(left, right, dims=NN):
    return lax.dot_general(left, right, dims, preferred_element_type=single)


def swap(value, axis, mask):
    size = lax.axis_size(axis)
    return lax.ppermute(value, axis, [(i, i ^ mask) for i in range(size)])


def after(value, *deps):
    return lax.optimization_barrier((value, *deps))[0]


def together(*values):
    return lax.optimization_barrier(values)


def block_order(size):
    order = [0]
    step = size // 2
    while step:
        order = order + [j + step for j in order]
        step //= 2
    return order


def gather_blocks(piece, axis, beside=(), stop=0):
    steps = []
    mask = lax.axis_size("dp") // 2
    while mask > stop:
        moved = swap(piece, "dp", mask)
        if len(steps) < len(beside):
            moved = beside[len(steps)](moved)
        piece = jnp.concatenate([piece, moved], axis=axis)
        steps.append(piece)
        mask //= 2
    return piece, steps


def split(value, axis, parts):
    width = value.shape[axis] // parts
    return [lax.slice_in_dim(value, i * width, (i + 1) * width, axis=axis) for i in range(parts)]


def reduce_blocks(keep, send, beside=(), mask=1):
    moved = swap(send.astype(lowp), "dp", mask)
    if beside:
        moved = beside[0](moved)
    total = keep + moved.astype(single)
    mask *= 2
    if mask == lax.axis_size("dp"):
        return total
    return reduce_blocks(*split(total, 1, 2), beside[1:], mask)


def reorder_kernel(sources, *refs):
    out_ref = refs[-1]
    width = out_ref.shape[1] // len(sources)
    start = 0
    for in_ref in refs[:-1]:
        rows = slice(start, start + in_ref.shape[0])
        start += in_ref.shape[0]
        for p, q in enumerate(sources):
            block = in_ref[:, q * width : (q + 1) * width]
            out_ref[rows, p * width : (p + 1) * width] = block.astype(out_ref.dtype)


def reorder(values, mask):
    order = block_order(lax.axis_size("dp"))
    sources = [order.index(j ^ mask) for j in order]
    rows = sum(value.shape[0] for value in values)
    if D // len(order) % 128:
        joined = jnp.concatenate([value.astype(lowp) for value in values])
        cols = split(joined, 1, len(order))
        return jnp.concatenate([cols[q] for q in sources], axis=1)
    return pl.pallas_call(
        functools.partial(reorder_kernel, sources),
        name="reorder",
        out_shape=jax.ShapeDtypeStruct((rows, D), lowp),
        in_specs=[vmem()] * len(values),
        out_specs=vmem(),
        compiler_params=params(60),
        cost_estimate=cost(0, 2 * MIB),
    )(*values)


def relative(value, x, c):
    value = jnp.where(x == 1, jnp.flip(value, -3), value)
    value = jnp.where(c == 1, jnp.flip(value, -2), value)
    return jnp.swapaxes(value, -3, -2)


def rms(values, gain):
    inv = lax.rsqrt(jnp.mean(values * values, axis=-1, keepdims=True) + TINY_NORM)
    return (values * inv * gain).astype(lowp), inv


def rms_back(values, inv, gain, upstream):
    scaled = gain * upstream
    inner = jnp.sum(scaled * values, axis=-1, keepdims=True) / D
    return scaled * inv - values * (inner * inv * inv * inv)


def vmem(shape=None, index=None):
    if shape is None:
        return pl.BlockSpec(memory_space=pltpu.VMEM)
    return pl.BlockSpec(shape, index)


def smem():
    return pl.BlockSpec(memory_space=pltpu.SMEM)


def params(mib):
    return pltpu.CompilerParams(vmem_limit_bytes=mib * MIB)


def cost(flops, size, exps=0):
    return pl.CostEstimate(
        flops=int(0.02 * flops), bytes_accessed=int(0.02 * size), transcendentals=exps
    )


def lookup_kernel(row_ref, table_ref, out_ref, tab, held, sem):
    total = row_ref.shape[0]
    vocab = table_ref.shape[0]
    copy = pltpu.make_async_copy(table_ref, tab.at[pl.ds(0, vocab)], sem)
    copy.start()
    tab[pl.ds(vocab, 8), :] = jnp.zeros((8, tab.shape[1]), single)
    copy.wait()

    @pl.loop(0, total // 16)
    def _(g):
        for j in range(16):
            t = g * 16 + j
            held[pl.ds(t, 1), :] = tab[pl.ds(row_ref[t], 1), :]

    @pl.loop(0, total // 512)
    def _(i):
        rows = pl.ds(pl.multiple_of(i * 512, 512), 512)
        out_ref[rows, :] = held[rows, :].astype(lowp)


def lookup(rows, table):
    total = rows.shape[0]
    vocab, width = table.shape
    return pl.pallas_call(
        lookup_kernel,
        name="lookup",
        out_shape=jax.ShapeDtypeStruct((total, width), lowp),
        in_specs=[smem(), pl.BlockSpec(memory_space=pl.ANY)],
        out_specs=vmem(),
        scratch_shapes=[
            pltpu.VMEM((vocab + 8, width), single),
            pltpu.VMEM((total, width), single),
            pltpu.SemaphoreType.DMA(()),
        ],
        compiler_params=params(60),
        cost_estimate=cost(0, 30 * MIB),
    )(rows, table)


def list_kernel(code_ref, out_ref, count_ref):
    total = code_ref.shape[0]

    def group(g, count):
        for j in range(16):
            code = code_ref[g * 16 + j]
            out_ref[count] = code
            count = count + jnp.where(code >= 0, 1, 0)
        return count

    count_ref[0] = lax.fori_loop(0, total // 16, group, jnp.int32(0))


def own_list(codes):
    total = codes.shape[0]
    return pl.pallas_call(
        list_kernel,
        name="own_list",
        out_shape=(
            jax.ShapeDtypeStruct((total + 8,), jnp.int32),
            jax.ShapeDtypeStruct((1,), jnp.int32),
        ),
        in_specs=[smem()],
        out_specs=(smem(), smem()),
        cost_estimate=cost(0, 60 * MIB),
    )(codes)


def place_kernel(order, place_ref, in_ref, gain_ref, out_ref, norm_ref, held):
    width = in_ref.shape[2]
    for p, j in enumerate(order):
        block = in_ref[pl.ds(place_ref[1] ^ j, 1)][0]
        out_ref[:, p * width : (p + 1) * width] = block
        held[:, p * width : (p + 1) * width] = block.astype(single)
    values = held[...]
    inv = lax.rsqrt(jnp.mean(values * values, axis=-1, keepdims=True) + TINY_NORM)
    norm_ref[...] = (values * inv * gain_ref[...]).astype(lowp)


def place_embedding(place, blocks, gain):
    rows = blocks.shape[1]
    return pl.pallas_call(
        functools.partial(place_kernel, block_order(blocks.shape[0])),
        name="place_embedding",
        out_shape=(jax.ShapeDtypeStruct((rows, D), lowp), jax.ShapeDtypeStruct((rows, D), lowp)),
        in_specs=[smem(), vmem(), vmem()],
        out_specs=(vmem(), vmem()),
        scratch_shapes=[pltpu.VMEM((rows, D), single)],
        compiler_params=params(60),
        cost_estimate=cost(0, 3 * MIB),
    )(place, blocks, gain)


def embed_back_kernel(order, place_ref, in_ref, gain_ref, keep_ref, more_ref, grad_ref, out_ref, held):
    values = in_ref[...].astype(single)
    inv = lax.rsqrt(jnp.mean(values * values, axis=-1, keepdims=True) + TINY_NORM)
    upstream = keep_ref[...] + more_ref[...].astype(single)
    held[...] = grad_ref[...] + rms_back(values, inv, gain_ref[...], upstream)
    width = out_ref.shape[2]
    for p, j in enumerate(order):
        block = held[:, p * width : (p + 1) * width].astype(lowp)
        out_ref[pl.ds(place_ref[1] ^ j, 1)] = block[None]


def embed_back(place, values, gain, keep, more, grad):
    rows = values.shape[0]
    size = lax.axis_size("dp")
    return pl.pallas_call(
        functools.partial(embed_back_kernel, block_order(size)),
        name="embed_back",
        out_shape=jax.ShapeDtypeStruct((size, rows, D // size), lowp),
        in_specs=[smem()] + [vmem()] * 5,
        out_specs=vmem(),
        scratch_shapes=[pltpu.VMEM((rows, D), single)],
        compiler_params=params(60),
        cost_estimate=cost(0, 4 * MIB),
    )(place, values, gain, keep, more, grad)


def scatter_kernel(bits, count_ref, code_ref, base_ref, grad_ref, out_ref, rows):
    total = grad_ref.shape[0]
    vocab = base_ref.shape[0]

    @pl.loop(0, total // 512)
    def _(i):
        here = pl.ds(pl.multiple_of(i * 512, 512), 512)
        rows[here, :] = grad_ref[here, :].astype(single)

    rows[pl.ds(total, 8), :] = jnp.zeros((8, rows.shape[1]), single)

    @pl.loop(0, vocab // 400)
    def _(i):
        here = pl.ds(pl.multiple_of(i * 400, 400), 400)
        out_ref[here, :] = base_ref[here, :]

    count = count_ref[0]

    def group(g, carry):
        for j in range(8):
            index = g * 8 + j
            code = jnp.where(index < count, code_ref[index], total << bits)
            token = lax.shift_right_logical(code, bits)
            row = code & ((1 << bits) - 1)
            out_ref[pl.ds(row, 1), :] = out_ref[pl.ds(row, 1), :] + rows[pl.ds(token, 1), :]
        return carry

    lax.fori_loop(0, (count + 7) // 8, group, jnp.int32(0))


def scatter(bits, count, codes, base, grad):
    total, width = grad.shape
    return pl.pallas_call(
        functools.partial(scatter_kernel, bits),
        name="scatter",
        out_shape=jax.ShapeDtypeStruct(base.shape, single),
        in_specs=[smem(), smem(), vmem(), vmem()],
        out_specs=vmem(),
        scratch_shapes=[pltpu.VMEM((total + 8, width), single)],
        compiler_params=params(60),
        cost_estimate=cost(0, 30 * MIB),
    )(count, codes, base, grad)


def state_kernel(order, width, place_ref, gain_ref, in_ref, out_ref, held):
    rows = in_ref.shape[1]
    values = in_ref[0].astype(single)
    inv = lax.rsqrt(jnp.mean(values * values, axis=-1, keepdims=True) + TINY_NORM)
    for p, j in enumerate(order):
        start = pl.multiple_of((place_ref[1] ^ j) * width, width)
        block = in_ref[0, :, pl.ds(start, width)].astype(single)
        held[p] = block * inv * gain_ref[:, p * width : (p + 1) * width]
    groups = out_ref.shape[0]
    for p in range(len(order)):
        cols = slice(p * width, (p + 1) * width)
        if groups == 1:
            out_ref[0, :, cols] = held[p].astype(lowp)
        else:
            for j in range(groups):
                part = held[p, pl.ds(j, rows // groups, stride=groups), :]
                out_ref[j, :, cols] = part.astype(lowp)


def state_norm(place, gain, states, groups):
    size = lax.axis_size("dp")
    order = block_order(size)
    width = D // size
    streams = states.shape[0]
    count = states.shape[1] // groups
    if width % 128:
        values = jnp.where(place[0] == 1, jnp.flip(states, 0), states).astype(single).reshape(-1, D)
        inv = lax.rsqrt(jnp.mean(values * values, axis=-1, keepdims=True) + TINY_NORM)
        lanes = jnp.arange(D, dtype=jnp.int32)
        blocks = jnp.asarray(order, jnp.int32)[lanes // width] ^ place[1]
        source = blocks * width + lanes % width
        shuffle = (lanes[:, None] == source[None, :]).astype(single)
        moved = jnp.dot(values * inv, shuffle, precision=lax.Precision.HIGHEST)
        out = (moved * gain).astype(lowp)
        return jnp.swapaxes(out.reshape(streams * count, groups, D), 0, 1)
    tile = 128
    return pl.pallas_call(
        functools.partial(state_kernel, order, width),
        name="state_norm",
        out_shape=jax.ShapeDtypeStruct((groups, streams * count, D), lowp),
        grid_spec=pltpu.PrefetchScalarGridSpec(
            num_scalar_prefetch=1,
            grid=(streams, count // tile),
            in_specs=[
                pl.BlockSpec((1, D), lambda n, i, s: (0, 0)),
                pl.BlockSpec((1, tile * groups, D), lambda n, i, s: (s[0] ^ n, i, 0)),
            ],
            out_specs=pl.BlockSpec(
                (groups, tile, D), lambda n, i, s: (0, n * (count // tile) + i, 0)
            ),
            scratch_shapes=[pltpu.VMEM((len(order), tile * groups, width), single)],
        ),
        compiler_params=params(60),
        cost_estimate=cost(0, 4 * streams * count * groups * D),
    )(place, gain, states)


def compress_kernel(old_ref, key_ref, value_ref, conv_ref, comp_ref, raw_ref):
    heads = conv_ref.shape[0]
    wide = heads * DH
    for part, weight_ref in enumerate((key_ref, value_ref)):
        sums = [None] * heads
        for j in range(RATE):
            raw = mm(old_ref[j], weight_ref[...], NT).astype(lowp)
            raw_ref[j, :, part * wide : (part + 1) * wide] = raw
            for n in range(heads):
                piece = raw[:, n * DH : (n + 1) * DH]
                term = mm(piece, conv_ref[n, j * DH : (j + 1) * DH, :])
                sums[n] = term if j == 0 else sums[n] + term
        for n in range(heads):
            first = part * wide + n * DH
            comp_ref[:, first : first + DH] = sums[n].astype(lowp)


def compress(old3, weights, conv):
    rows = old3.shape[1]
    wide = conv.shape[0] * DH
    tile = 256
    return pl.pallas_call(
        compress_kernel,
        name="compress",
        grid=(rows // tile,),
        out_shape=(
            jax.ShapeDtypeStruct((rows, 2 * wide), lowp),
            jax.ShapeDtypeStruct((RATE, rows, 2 * wide), lowp),
        ),
        in_specs=[
            pl.BlockSpec((RATE, tile, D), lambda i: (0, i, 0)),
            pl.BlockSpec((wide, D), lambda i: (1, 0)),
            pl.BlockSpec((wide, D), lambda i: (2, 0)),
            pl.BlockSpec(conv.shape, lambda i: (0, 0, 0)),
        ],
        out_specs=(
            pl.BlockSpec((tile, 2 * wide), lambda i: (i, 0)),
            pl.BlockSpec((RATE, tile, 2 * wide), lambda i: (0, i, 0)),
        ),
        compiler_params=params(60),
        cost_estimate=cost(4 * RATE * rows * wide * D, 12 * MIB),
    )(old3, weights, weights, conv)


def expand_kernel(grad_ref, raw_ref, conv_ref, out_ref, conv_out_ref):
    heads = conv_ref.shape[0]
    for h in range(heads):
        for j in range(RATE):
            rows = slice(j * DH, (j + 1) * DH)
            taps = conv_ref[h, rows, :]
            total = None
            for n in (h, heads + h):
                cols = slice(n * DH, (n + 1) * DH)
                grad = grad_ref[:, cols]
                out_ref[j, :, cols] = mm(grad, taps, NT).astype(lowp)
                term = mm(raw_ref[j, :, cols], grad, TN)
                total = term if total is None else total + term
            conv_out_ref[h, rows, :] = total


def expand(grad, raw, conv):
    return pl.pallas_call(
        expand_kernel,
        name="expand",
        out_shape=(
            jax.ShapeDtypeStruct(raw.shape, lowp),
            jax.ShapeDtypeStruct(conv.shape, single),
        ),
        in_specs=[vmem()] * 3,
        out_specs=(vmem(), vmem()),
        compiler_params=params(60),
        cost_estimate=cost(2000 * MIB, 12 * MIB),
    )(grad, raw, conv)


def masked_scores(info_ref, query, keys):
    rows = query.shape[0]
    scale = DH ** (-0.5)
    result = []
    for which, key in enumerate(keys):
        slots = key.shape[0]
        col = lax.broadcasted_iota(jnp.int32, (rows, slots), 1)
        if which < 2:
            seen = col >= slots - info_ref[2 * pl.program_id(0) + which]
        else:
            row = lax.broadcasted_iota(jnp.int32, (rows, slots), 0)
            shift = info_ref[4]
            row = row + shift
            col = col + shift
            row = jnp.where(row >= slots, row - slots, row)
            col = jnp.where(col >= slots, col - slots, col)
            seen = col <= row
        result.append(jnp.where(seen, mm(query, key, NT) * scale, -1e30))
    return result


def rows_of(ref):
    return ref[...].reshape(-1, ref.shape[-1])


def attend_kernel(info_ref, q_ref, ks_ref, vs_ref, kc_ref, vc_ref, km_ref, vm_ref, out_ref, lse_ref):
    query = rows_of(q_ref)
    scores = masked_scores(info_ref, query, [kc_ref[...], km_ref[...], rows_of(ks_ref)])
    top = functools.reduce(jnp.maximum, [jnp.max(s, axis=-1, keepdims=True) for s in scores])
    total = 0.0
    mixed = 0.0
    for score, value in zip(scores, (vc_ref[...], vm_ref[...], rows_of(vs_ref))):
        weight = jnp.exp(score - top)
        total = total + jnp.sum(weight, axis=-1, keepdims=True)
        mixed = mixed + mm(weight.astype(lowp), value)
    out_ref[...] = (mixed / total).astype(lowp).reshape(out_ref.shape)
    lse_ref[0, 0] = top + jnp.log(total)


def attend_back_kernel(
    info_ref, q_ref, ks_ref, vs_ref, kc_ref, vc_ref, km_ref, vm_ref, lse_ref, up_ref,
    seg_ref, comp_ref, mem_ref,
):
    head = pl.program_id(1)
    wide = pl.num_programs(1) * DH
    scale = DH ** (-0.5)
    query = rows_of(q_ref)
    upstream = rows_of(up_ref)
    keys = [kc_ref[...], km_ref[...], rows_of(ks_ref)]
    scores = masked_scores(info_ref, query, keys)
    probs = [jnp.exp(s - lse_ref[0, 0]) for s in scores]
    prob_grads = [
        mm(upstream, v, NT) for v in (vc_ref[...], vm_ref[...], rows_of(vs_ref))
    ]
    inner = 0.0
    for p, g in zip(probs, prob_grads):
        inner = inner + jnp.sum(p * g, axis=-1, keepdims=True)
    here = pl.ds(pl.multiple_of(head * DH, DH), DH)
    second = pl.ds(pl.multiple_of(wide + head * DH, DH), DH)
    third = pl.ds(pl.multiple_of(2 * wide + head * DH, DH), DH)
    query_grad = 0.0
    places = ((comp_ref, here, second), (mem_ref, here, second), (seg_ref, second, third))
    for p, g, key, (ref, key_at, value_at) in zip(probs, prob_grads, keys, places):
        score_grad = (p * (g - inner)).astype(lowp)
        query_grad = query_grad + mm(score_grad, key)
        shape = ref.shape[:-1] + (DH,)
        key_grad = (mm(score_grad, query, TN) * scale).astype(lowp)
        value_grad = mm(p.astype(lowp), upstream, TN).astype(lowp)
        ref[..., key_at] = key_grad.reshape(shape)
        ref[..., value_at] = value_grad.reshape(shape)
    shape = seg_ref.shape[:-1] + (DH,)
    seg_ref[..., here] = (query_grad * scale).astype(lowp).reshape(shape)


def head_specs(seg, comp, mem, heads):
    streams = seg.shape[1]

    def of_seg(first):
        return pl.BlockSpec((2, 1, seg.shape[2], DH), lambda n, h: (0, n, 0, first + h))

    def cols(array, first):
        return pl.BlockSpec((array.shape[0] // streams, DH), lambda n, h: (n, first + h))

    return [
        smem(),
        of_seg(0),
        of_seg(heads),
        of_seg(2 * heads),
        cols(comp, 0),
        cols(comp, heads),
        cols(mem, 0),
        cols(mem, heads),
    ]


def attend(info, seg, comp, mem):
    _, streams, half, _ = seg.shape
    heads = comp.shape[1] // (2 * DH)
    return pl.pallas_call(
        attend_kernel,
        name="attend",
        grid=(streams, heads),
        out_shape=(
            jax.ShapeDtypeStruct((2, streams, half, heads * DH), lowp),
            jax.ShapeDtypeStruct((streams, heads, 2 * half, 1), single),
        ),
        in_specs=head_specs(seg, comp, mem, heads),
        out_specs=(
            pl.BlockSpec((2, 1, half, DH), lambda n, h: (0, n, 0, h)),
            pl.BlockSpec((1, 1, 2 * half, 1), lambda n, h: (n, h, 0, 0)),
        ),
        compiler_params=params(60),
        cost_estimate=cost(7000 * MIB, 6 * MIB),
    )(info, seg, seg, seg, comp, comp, mem, mem)


def attend_back(info, seg, comp, mem, lse, upstream):
    _, streams, half, wide = seg.shape
    heads = comp.shape[1] // (2 * DH)
    slots = comp.shape[0] // streams
    kept = mem.shape[0] // streams
    return pl.pallas_call(
        attend_back_kernel,
        name="attend_back",
        grid=(streams, heads),
        out_shape=(
            jax.ShapeDtypeStruct(seg.shape, lowp),
            jax.ShapeDtypeStruct(comp.shape, lowp),
            jax.ShapeDtypeStruct(mem.shape, lowp),
        ),
        in_specs=head_specs(seg, comp, mem, heads)
        + [
            pl.BlockSpec((1, 1, 2 * half, 1), lambda n, h: (n, h, 0, 0)),
            pl.BlockSpec((2, 1, half, DH), lambda n, h: (0, n, 0, h)),
        ],
        out_specs=(
            pl.BlockSpec((2, 1, half, wide), lambda n, h: (0, n, 0, 0)),
            pl.BlockSpec((slots, comp.shape[1]), lambda n, h: (n, 0)),
            pl.BlockSpec((kept, mem.shape[1]), lambda n, h: (n, 0)),
        ),
        compiler_params=params(60),
        cost_estimate=cost(11000 * MIB, 9 * MIB),
    )(info, seg, seg, seg, comp, comp, mem, mem, lse, upstream)


def columns_of(rows):
    tall = jnp.concatenate([rows, jnp.zeros((120, rows.shape[1]), single)], axis=0)
    return jnp.transpose(tall)


def logits_kernel(words, info_ref, pair_ref, near_ref, left_ref, right_ref, out_ref, stat_ref, held):
    step = pl.program_id(0)

    @pl.when(step == 0)
    def _():
        held[...] = pair_ref[...]

    @pl.when(step == 1)
    def _():
        held[...] = near_ref[...]

    half = left_ref.shape[1]
    slots = left_ref.shape[0]
    logits = mm(held[:, :half], left_ref[...], NT) + mm(held[:, half:], right_ref[...], NT)
    wanted = columns_of(info_ref[0])[:, 0:1].astype(jnp.int32)
    col = lax.broadcasted_iota(jnp.int32, logits.shape, 1)
    hit = jnp.sum(jnp.where(col == wanted, logits, 0.0), axis=-1, keepdims=True)
    edge = slots - 128
    last = jnp.where(col[:, edge:] < words, logits[:, edge:], -1e30)
    top = jnp.max(last, axis=-1, keepdims=True)
    top = jnp.maximum(top, jnp.max(logits[:, :edge], axis=-1, keepdims=True))
    raised = jnp.exp(logits[:, :edge] - top)
    last = jnp.exp(last - top)
    total = jnp.sum(raised, axis=-1, keepdims=True) + jnp.sum(last, axis=-1, keepdims=True)
    out_ref[:, :edge] = raised.astype(lowp)
    out_ref[:, edge:] = last.astype(lowp)
    lane = lax.broadcasted_iota(jnp.int32, (logits.shape[0], 128), 1)
    packed = jnp.where(lane == 0, top, jnp.where(lane == 1, total, jnp.where(lane == 2, hit, 0.0)))
    stat_ref[...] = jnp.transpose(packed)[:8]


def logits_part(words, chunk, info, pair, near, left, right):
    rows = pair.shape[0] + near.shape[0]
    slots = left.shape[0]
    tile = pair.shape[0]
    whole = lambda i: (0, 0)
    return pl.pallas_call(
        functools.partial(logits_kernel, words),
        name="logits_part",
        grid=(2,),
        out_shape=(
            jax.ShapeDtypeStruct((rows, slots), lowp),
            jax.ShapeDtypeStruct((8, rows), single),
        ),
        in_specs=[
            pl.BlockSpec((1, 8, tile), lambda i: (chunk, 0, i)),
            pl.BlockSpec((tile, D), whole),
            pl.BlockSpec((tile, D), whole),
            pl.BlockSpec(left.shape, whole),
            pl.BlockSpec(right.shape, whole),
        ],
        out_specs=(
            pl.BlockSpec((tile, slots), lambda i: (i, 0)),
            pl.BlockSpec((8, tile), lambda i: (0, i)),
        ),
        scratch_shapes=[pltpu.VMEM((tile, D), lowp)],
        compiler_params=params(60),
        cost_estimate=cost(4 * rows * slots * D, 10 * MIB),
    )(info, pair, near, left, right)


def logits_back_kernel(info_ref, factor_ref, in_ref, left_ref, right_ref, out_ref, keep_ref, send_ref):
    step = pl.program_id(0)
    info = columns_of(info_ref[0])
    wanted = info[:, 0:1].astype(jnp.int32)
    counted = info[:, 1:2]
    factor = columns_of(factor_ref[0])[:, 0:1]
    raised = in_ref[...].astype(single)
    col = lax.broadcasted_iota(jnp.int32, raised.shape, 1)
    grads = (raised * factor - jnp.where(col == wanted, counted, 0.0)).astype(lowp)
    out_ref[...] = grads
    half = left_ref.shape[1]
    left = mm(grads, left_ref[...]).astype(lowp)
    right = mm(grads, right_ref[...]).astype(lowp)

    @pl.when(step == 0)
    def _():
        send_ref[:, :half] = left
        send_ref[:, half:] = right

    @pl.when(step == 1)
    def _():
        keep_ref[:, :half] = left
        keep_ref[:, half:] = right


def logits_back(chunk, info, factor, raised, left, right):
    rows, slots = raised.shape
    tile = rows // 2
    whole = lambda i: (0, 0)
    return pl.pallas_call(
        logits_back_kernel,
        name="logits_back",
        grid=(2,),
        out_shape=(
            jax.ShapeDtypeStruct((rows, slots), lowp),
            jax.ShapeDtypeStruct((tile, D), lowp),
            jax.ShapeDtypeStruct((tile, D), lowp),
        ),
        in_specs=[
            pl.BlockSpec((1, 8, tile), lambda i: (chunk, 0, 1 - i)),
            pl.BlockSpec((1, 8, tile), lambda i: (chunk, 0, 1 - i)),
            pl.BlockSpec((tile, slots), lambda i: (1 - i, 0)),
            pl.BlockSpec(left.shape, whole),
            pl.BlockSpec(right.shape, whole),
        ],
        out_specs=(
            pl.BlockSpec((tile, slots), lambda i: (1 - i, 0)),
            pl.BlockSpec((tile, D), whole),
            pl.BlockSpec((tile, D), whole),
        ),
        compiler_params=params(60),
        cost_estimate=cost(4 * rows * slots * D, 12 * MIB),
    )(info, factor, raised, left, right)


def halves(total, keep_ref, send_ref):
    half = keep_ref.shape[1]
    keep_ref[...] = total[:, :half]
    send_ref[...] = total[:, half:].astype(send_ref.dtype)


def table_grad_kernel(count, *refs):
    total = None
    for i in range(count):
        rows = refs[count + 2 * i].shape[0]
        for j in range(2):
            term = mm(refs[i][j * rows : (j + 1) * rows, :], refs[count + 2 * i + j][...], TN)
            total = term if total is None else total + term
    halves(total, *refs[3 * count :])


def table_grad_part(grads, inputs):
    count = len(grads)
    rows = sum(g.shape[0] for g in grads)
    slots = grads[0].shape[1]
    block = 256
    if rows > 4096:
        total = sum(
            mm(g, jnp.concatenate(v), TN) for g, v in zip(grads, inputs)
        )
        keep, send = split(total, 1, 2)
        return keep, send.astype(lowp)
    inputs = [half for pair in inputs for half in pair]
    return pl.pallas_call(
        functools.partial(table_grad_kernel, count),
        name="table_grad_part",
        grid=(slots // block,),
        out_shape=(
            jax.ShapeDtypeStruct((slots, D // 2), single),
            jax.ShapeDtypeStruct((slots, D // 2), lowp),
        ),
        in_specs=[pl.BlockSpec((g.shape[0], block), lambda i: (0, i)) for g in grads]
        + [pl.BlockSpec(v.shape, lambda i: (0, 0)) for v in inputs],
        out_specs=(
            pl.BlockSpec((block, D // 2), lambda i: (i, 0)),
            pl.BlockSpec((block, D // 2), lambda i: (i, 0)),
        ),
        compiler_params=params(60),
        cost_estimate=cost(3 * rows * slots * D, 30 * MIB),
    )(*grads, *inputs)


def hidden_grad_kernel(blocks, pre_ref, act_ref, in_ref, down_ref, keep_ref, send_ref):
    step = pl.program_id(0)

    @pl.when(step < blocks)
    def _():
        halves(mm(pre_ref[...], in_ref[...], TN), keep_ref, send_ref)

    @pl.when(step >= blocks)
    def _():
        halves(mm(act_ref[...], down_ref[...], TN), keep_ref, send_ref)


def hidden_grads(pre_grad, hidden_act, ffn_in, down_in):
    rows, hidden = pre_grad.shape
    block = 256
    blocks = hidden // block
    return pl.pallas_call(
        functools.partial(hidden_grad_kernel, blocks),
        name="hidden_grads",
        grid=(2 * blocks,),
        out_shape=(
            jax.ShapeDtypeStruct((2 * hidden, D // 2), single),
            jax.ShapeDtypeStruct((2 * hidden, D // 2), lowp),
        ),
        in_specs=[
            pl.BlockSpec((rows, block), lambda i: (0, jnp.minimum(i, blocks - 1))),
            pl.BlockSpec((rows, block), lambda i: (0, jnp.maximum(i - blocks, 0))),
            pl.BlockSpec((rows, D), lambda i: (0, 0)),
            pl.BlockSpec((rows, D), lambda i: (0, 0)),
        ],
        out_specs=(
            pl.BlockSpec((block, D // 2), lambda i: (i, 0)),
            pl.BlockSpec((block, D // 2), lambda i: (i, 0)),
        ),
        compiler_params=params(60),
        cost_estimate=cost(6 * rows * hidden * D, 16 * MIB),
    )(pre_grad, hidden_act, ffn_in, down_in)


def attn_grad_kernel(
    seg_ref, mixed_ref, mem_ref, old_ref, normed_ref, up_ref, mem_in_ref, old_in_ref, keep_ref, send_ref
):
    which = pl.program_id(0)

    @pl.when(which == 0)
    def _():
        halves(mm(seg_ref[...], normed_ref[...], TN), keep_ref, send_ref)

    @pl.when(which == 3)
    def _():
        halves(mm(mixed_ref[...], up_ref[...], TN), keep_ref, send_ref)

    @pl.when(jnp.logical_and(which > 0, which < 3))
    def _():
        total = mm(seg_ref[...], normed_ref[...], TN)
        total = total + mm(mem_ref[...], mem_in_ref[...], TN)
        total = total + mm(old_ref[...], old_in_ref[...], TN)
        halves(total, keep_ref, send_ref)


def attn_grads(seg_grad, mixed, mem_grad, old_grad, normed, attn_in, mem_in, old_in):
    block = mixed.shape[1]

    def whole(array):
        return pl.BlockSpec(array.shape, lambda i: (0, 0))

    return pl.pallas_call(
        attn_grad_kernel,
        name="attn_grads",
        grid=(4,),
        out_shape=(
            jax.ShapeDtypeStruct((4 * block, D // 2), single),
            jax.ShapeDtypeStruct((4 * block, D // 2), lowp),
        ),
        in_specs=[
            pl.BlockSpec((seg_grad.shape[0], block), lambda i: (0, jnp.minimum(i, 2))),
            whole(mixed),
            pl.BlockSpec((mem_grad.shape[0], block), lambda i: (0, jnp.clip(i - 1, 0, 1))),
            pl.BlockSpec((old_grad.shape[0], block), lambda i: (0, jnp.clip(i - 1, 0, 1))),
            whole(normed),
            whole(attn_in),
            whole(mem_in),
            whole(old_in),
        ],
        out_specs=(
            pl.BlockSpec((block, D // 2), lambda i: (i, 0)),
            pl.BlockSpec((block, D // 2), lambda i: (i, 0)),
        ),
        compiler_params=params(60),
        cost_estimate=cost(9000 * MIB, 24 * MIB),
    )(seg_grad, mixed, mem_grad, old_grad, normed, attn_in, mem_in, old_in)


def scalar_row(values, length=128):
    lane = jnp.arange(length, dtype=jnp.int32)
    row = jnp.zeros((length,), single)
    for i, value in enumerate(values):
        row = jnp.where(lane == i, value, row)
    return row


def local(
    ids,
    targets,
    target_mask,
    memory,
    old_states,
    mem_fill,
    comp_fill,
    table,
    qkv,
    wout,
    wconv,
    wup,
    wdown,
    gains,
    table_rows,
    table_cols,
    qkv_rows,
    qkv_cols,
    out_rows,
    out_cols,
    conv_rows,
    conv_cols,
    up_rows,
    up_cols,
    down_rows,
    down_cols,
    gains_second,
):
    dp_size, head_size = lax.axis_size("dp"), lax.axis_size("head")
    d, h = lax.axis_index("dp"), lax.axis_index("head")
    x, c = h // 2, h % 2
    order = block_order(dp_size)
    reach = dp_size // 2
    streams, seg_len = ids.shape
    half = seg_len // 2
    per_group = streams * seg_len
    vocab, width = table.shape
    assert head_size == 4 and streams == 2

    weights_now = (table, qkv, wout, wconv, wup, wdown)
    rows_old = (table_rows, qkv_rows, out_rows, conv_rows, up_rows, down_rows)
    cols_old = (table_cols, qkv_cols, out_cols, conv_cols, up_cols, down_cols)
    sizes = {"dp": dp_size, "head": head_size}
    row_axes = ("head", "dp", "head", "head", "dp", "head")
    col_axes = ("dp", "head", "dp", "dp", "head", "dp")

    def early_sums(dep):
        _, *tied = together(dep, *rows_old, *weights_now, gains)
        sums = [jnp.sum(old) / sizes[axis] for old, axis in zip(tied[:6], col_axes)]
        sums += [jnp.sum(weight * weight) for weight in tied[6:12]]
        gain_sums = jnp.sum(tied[12] * tied[12], axis=1) / head_size
        return scalar_row(sums + [gain_sums[0], gain_sums[1], gain_sums[2]])

    def core_sum(keep, send, beside=()):
        more, *beside = together(swap(send.astype(lowp), "head", 1), *beside)
        part = keep.astype(single) + more.astype(single)
        return (part, beside) if beside else part

    def stream_sum(part, beside=()):
        keep, send = split(part, 0, 2)
        more, *beside = together(swap(send.astype(lowp), "head", 2), *beside)
        part = keep + more.astype(single)
        return (part, beside) if beside else part

    def group_sum(part, beside=()):
        return stream_sum(core_sum(*split(part, 0, 2)), beside)

    def group_both(part, beside=()):
        far, *beside = together(swap(part, "head", 2), *beside)
        pair = jnp.concatenate([part, far], axis=0)
        both = (pair, swap(pair, "head", 1))
        return (both, beside) if beside else both

    flat = jnp.concatenate(
        [
            ids.astype(single).reshape(-1),
            targets.astype(single).reshape(-1),
            target_mask.astype(single).reshape(-1),
            gains.astype(lowp).astype(single).reshape(-1),
        ]
    )
    room = -flat.shape[0] % 1024
    flat = jnp.concatenate([flat, jnp.zeros((room,), single)]).reshape(1, -1, 128)
    small, small_steps = gather_blocks(flat, 0)
    small = small.reshape(dp_size, -1)
    place = jnp.stack([x, d])

    def field(raw):
        return relative(raw.reshape(-1, 2, 2, half), x, c)

    ids_all = small[:, :per_group]
    position = [order.index(j) for j in range(dp_size)]
    ids_all = jnp.take(ids_all, jnp.asarray(position, jnp.int32)[jnp.arange(dp_size) ^ d], axis=0)
    ids_all = jnp.transpose(field(ids_all), (1, 2, 0, 3)).reshape(-1).astype(jnp.int32)
    table_rows_all = ids_all - h * vocab
    inside = (table_rows_all >= 0) & (table_rows_all < vocab)
    bits = vocab.bit_length()
    token_codes = (jnp.arange(ids_all.shape[0], dtype=jnp.int32) << bits) | table_rows_all
    token_codes = jnp.where(inside, token_codes, -1)
    table_rows_all = jnp.where(inside, table_rows_all, vocab)
    targets_all = field(small[:reach, per_group : 2 * per_group])
    mask_all = field(small[:reach, 2 * per_group : 3 * per_group])
    gain_blocks = small[:, 3 * per_group : 3 * per_group + 3 * width].reshape(dp_size, 3, width)
    gain_vals = jnp.swapaxes(gain_blocks, 0, 1).reshape(3, 1, D)
    count_all = jnp.sum(small[:, 2 * per_group : 3 * per_group])

    heads_own = wconv.shape[0]
    wide = qkv.shape[2]
    conv_rows_own = wconv.size // width
    low_qkv = qkv.astype(lowp)
    pack_one = jnp.concatenate(
        [
            jnp.swapaxes(low_qkv, 1, 2).reshape(3 * wide, width),
            wout.astype(lowp),
            wconv.astype(lowp).reshape(conv_rows_own, width),
        ]
    )
    own_half, far_half = split(table_rows_all, 0, 2)
    kept = {}

    def beside_lookup(moved):
        moved, kept["far"], kept["own"] = together(
            moved, lookup(far_half, table), lookup(own_half, table)
        )
        return moved

    def beside_memory(moved):
        looked = (kept["own"] + swap(kept["far"], "head", 1)).reshape(2, -1, width)
        mem_normed = state_norm(place, gain_vals[0], memory, 1)[0]
        moved, more, kept["mem"] = together(moved, swap(looked[1], "head", 2), mem_normed)
        looked = (looked[0] + more).reshape(dp_size, half, width)
        kept["looked"] = lax.all_to_all(looked, "dp", 0, 0)
        return moved

    own_one, steps_one = gather_blocks(
        after(pack_one, small_steps[0]), 1, (beside_lookup, beside_memory)
    )
    conv_lanes = jnp.arange(DH, dtype=jnp.int32)
    conv_width = DH // dp_size
    conv_natural = (jnp.asarray(order, jnp.int32)[conv_lanes // conv_width] ^ d) * conv_width
    conv_natural = conv_natural + conv_lanes % conv_width
    conv_shuffle = (conv_natural[:, None] == conv_lanes[None, :]).astype(lowp)
    taps = heads_own * RATE * DH

    def conv_natural_order(rows):
        value = jnp.swapaxes(rows.reshape(conv_rows_own, dp_size, width), 0, 1)
        value = jnp.swapaxes(value.reshape(dp_size, taps, conv_width), 0, 1)
        moved = mm(value.reshape(taps, DH), conv_shuffle).astype(lowp)
        return moved.reshape(heads_own, RATE * DH, DH)

    def conv_block_order(value):
        moved = mm(value.astype(lowp).reshape(taps, DH), conv_shuffle, NT).astype(lowp)
        moved = jnp.swapaxes(moved.reshape(taps, dp_size, conv_width), 0, 1)
        moved = jnp.swapaxes(moved.reshape(dp_size, conv_rows_own, width), 0, 1)
        return moved.reshape(conv_rows_own, D)

    full_conv = conv_natural_order(own_one[4 * wide :])

    hidden_own = wup.shape[1]
    pack_two = jnp.concatenate([wup.astype(lowp).T, wdown.astype(lowp)])

    old_normed = state_norm(place, gain_vals[0], old_states, RATE)

    words = vocab // reach
    z = d // 2
    word_start = (h * vocab + z * words).astype(single)
    wanted_all = targets_all - word_start
    wanted_all = jnp.where((wanted_all >= 0) & (wanted_all < words), wanted_all, -1.0)
    info_all = jnp.stack([wanted_all, mask_all] + [jnp.zeros_like(mask_all)] * 6)
    info_all = jnp.transpose(info_all, (1, 0, 2, 3, 4)).reshape(reach, 8, per_group)

    def beside_old(moved):
        moved, looked, kept["old"], kept["info"] = together(
            moved, kept["looked"], old_normed, info_all
        )
        kept["embedded"], kept["normed"] = place_embedding(place, looked, gain_vals[0])
        return moved

    def beside_compress(moved):
        moved, *kept["comp"] = together(moved, *compress(kept["old"], own_one, full_conv))
        return moved

    near_two, steps_two = gather_blocks(
        after(pack_two, steps_one[1]), 1, (beside_old, beside_compress), 1
    )
    near_up, near_down = split(near_two, 0, 2)
    far_up, far_down = swap(near_up, "dp", 1), swap(near_down, "dp", 1)
    mem_normed, old_normed = kept["mem"], kept["old"]
    embedded_low = kept["embedded"]
    embedded = embedded_low.astype(single)
    normed = jnp.concatenate(group_both(kept["normed"]))
    comp, old_raw = kept["comp"]

    words = vocab // reach
    z = d // 2
    unsigned_z = z.astype(jnp.uint32)
    z_groups = [[2 * i + b for i in range(reach)] for b in range(2)]
    slots = -(-words // 256) * 256


    comp_counts = jnp.where(x == 1, jnp.flip(comp_fill), comp_fill)
    mem_counts = jnp.where(x == 1, jnp.flip(mem_fill), mem_fill)
    info = [comp_counts[0], mem_counts[0], comp_counts[1], mem_counts[1], c * half]
    lane = jnp.arange(8, dtype=jnp.int32)
    info = sum(jnp.where(lane == i, value, 0) for i, value in enumerate(info)).astype(jnp.int32)

    in_weight = own_one[: 3 * wide]
    mem = mm(mem_normed, own_one[wide : 3 * wide], NT).astype(lowp)
    seg = mm(normed, in_weight, NT).astype(lowp).reshape(2, streams, half, 3 * wide)
    low_table = after(table.astype(lowp), seg).reshape(reach, words, width)
    low_table = lax.all_to_all(low_table, "dp", 0, 0, axis_index_groups=z_groups)
    mixed, lse = attend(info, seg, comp, mem)
    mixed = mixed.reshape(-1, wide)
    attn_sum, (far_up,) = core_sum(
        *split(mm(mixed, own_one[3 * wide : 4 * wide]), 0, 2), (far_up,)
    )
    attn_sum, (far_down,) = stream_sum(attn_sum, (far_down,))
    after_attn = embedded + attn_sum
    ffn_in, inv_second = rms(after_attn, gain_vals[1])
    ffn_in, (low_table,) = group_both(ffn_in, (low_table,))
    near_table = [
        lax.dynamic_index_in_dim(low_table, unsigned_z ^ jnp.uint32(m // 2), 0, keepdims=False) for m in order[:reach]
    ]
    near_table = jnp.concatenate(near_table, axis=1)
    near_table = jnp.concatenate([near_table, jnp.zeros((slots - words, D // 2), lowp)], axis=0)
    ffn_in = jnp.concatenate(ffn_in)
    full_up = jnp.concatenate([near_up, far_up], axis=1)
    full_down = jnp.concatenate([near_down, far_down], axis=1)
    far_table = swap(near_table, "dp", 1)
    hidden_pre = mm(ffn_in, full_up, NT)
    hidden_act = jax.nn.gelu(hidden_pre).astype(lowp)
    after_ffn = after_attn + group_sum(mm(hidden_act, full_down))
    final_in, inv_third = rms(after_ffn, gain_vals[2])

    info_all = kept["info"]
    pieces = [final_in]
    chunks = []
    raised = []
    stats = []

    def next_chunk():
        i = len(chunks)
        if i == 0:
            chunks.append(group_both(pieces[i]))
        else:
            chunk, (stats[i - 1],) = group_both(pieces[i], (stats[i - 1],))
            chunks.append(chunk)
        out, stat = logits_part(words, i, info_all, *chunks[i], near_table, far_table)
        raised.append(out)
        stats.append(stat)

    mask = dp_size // 2
    while mask > 1:
        moved = swap(reorder(pieces, mask), "dp", mask)
        if len(pieces) == 1:
            moved, own_codes, own_count = together(
                moved, *own_list(after(token_codes, final_in))
            )
            next_chunk()
        elif len(pieces) == 2:
            moved, stats[0] = together(moved, stats[0])
        pieces += split(moved, 0, len(pieces))
        mask //= 2
    while len(chunks) < reach:
        next_chunk()
    stats = [stat[:3].reshape(3, 1, 2, 2, half) for stat in stats]
    own_stats = jnp.concatenate(stats, axis=1)

    def combine(first, second):
        top = jnp.maximum(first[0], second[0])
        total = first[1] * jnp.exp(first[0] - top) + second[1] * jnp.exp(second[0] - top)
        return jnp.stack([top, total, first[2] + second[2]])

    merged = own_stats
    merged = combine(merged, jnp.flip(swap(merged, "head", 1), 2))
    merged = combine(merged, jnp.flip(swap(merged, "head", 2), 3))
    mask = 2
    while mask < dp_size:
        other = split(swap(merged, "dp", mask), 1, reach)
        other = [other[order.index(j ^ mask)] for j in order[:reach]]
        merged = combine(merged, jnp.concatenate(other, axis=1))
        mask *= 2
    log_total = merged[0] + jnp.log(merged[1])
    loss_local = jnp.sum(mask_all[0, 0, 0] * (log_total[0, 0, 0] - merged[2, 0, 0, 0]))
    factor_all = jnp.exp(own_stats[0] - log_total)

    factor_all = factor_all.reshape(reach, 1, per_group) * info_all[:, 1:2]
    factor_all = jnp.broadcast_to(factor_all, info_all.shape)
    dlogits = [None] * reach
    parts = [None] * reach
    for i in reversed(range(reach)):
        dlogits[i], *core = logits_back(
            i, info_all, factor_all, raised[i], near_table, far_table
        )
        if i + 1 < reach:
            parts[i + 1], (dlogits[i], *core) = stream_sum(parts[i + 1], (dlogits[i], *core))
        parts[i] = core_sum(*core)
    parts[0] = stream_sum(parts[0])
    table_parts = []
    mask = 2
    while len(parts) > 1:
        count = len(parts) // 2
        moved = swap(reorder(parts[count:], mask), "dp", mask)
        if mask == 2:
            moved, dlogits[0], early = together(moved, dlogits[0], early_sums(log_total))
        elif mask == 4:
            moved, *table_parts = together(moved, *table_grad_part(dlogits, chunks))
        moved = split(moved.astype(single), 0, count)
        parts = [part + more for part, more in zip(parts, moved)]
        mask *= 2
    final_grad = parts[0]

    grad_after_ffn = rms_back(after_ffn, inv_third, gain_vals[2], final_grad)
    moved_table = swap(table_parts[1], "dp", 1)
    down_in = group_both(grad_after_ffn.astype(lowp))
    down_in = jnp.concatenate(down_in)
    act_grad = mm(down_in, full_down, NT)
    pre_grad = jax.vjp(jax.nn.gelu, hidden_pre)[1](act_grad)[0].astype(lowp)
    two = hidden_grads(pre_grad, hidden_act, ffn_in, down_in)
    ffn_in_grad, (*two, moved_table) = group_sum(mm(pre_grad, full_up), (*two, moved_table))
    keep = table_parts[0] + moved_table.astype(single)
    table_pieces = jnp.stack(split(keep[:words].astype(lowp), 1, reach))
    turned = sum(
        ((unsigned_z >> bit) & 1) * jnp.uint32(order.index(2 << bit))
        for bit in range(reach.bit_length() - 1)
    )
    table_pieces = jnp.concatenate(
        [
            lax.dynamic_index_in_dim(table_pieces, turned ^ jnp.uint32(order.index(2 * i)), 0)
            for i in range(reach)
        ]
    )
    table_pieces = lax.all_to_all(table_pieces, "dp", 0, 0, axis_index_groups=z_groups)
    grad_after_attn = grad_after_ffn + rms_back(after_attn, inv_second, gain_vals[1], ffn_in_grad)
    attn_in = jnp.concatenate(group_both(grad_after_attn.astype(lowp)))

    mixed_grad = mm(attn_in, own_one[3 * wide : 4 * wide], NT).astype(lowp)
    mixed_grad = mixed_grad.reshape(2, streams, half, wide)
    seg_grad, comp_grad, mem_grad = attend_back(info, seg, comp, mem, lse, mixed_grad)
    seg_grad = seg_grad.reshape(-1, 3 * wide)

    def beside_sums(moved):
        keep, send = split(mm(seg_grad, in_weight), 0, 2)
        more = swap(send.astype(lowp), "head", 1)
        more, *kept["old"] = together(more, *expand(comp_grad, old_raw, full_conv))
        seg_in, seg_in_far = split(keep + more.astype(single), 0, 2)
        seg_in_far = swap(seg_in_far.astype(lowp), "head", 2)
        old_grad, conv_sum = kept["old"]
        sums = attn_grads(
            seg_grad,
            mixed,
            mem_grad,
            old_grad.reshape(-1, old_grad.shape[-1]),
            normed,
            attn_in,
            mem_normed,
            old_normed.reshape(-1, D),
        )
        conv_sum = split(conv_block_order(conv_sum), 1, 2)
        sums = [jnp.concatenate([part, more.astype(part.dtype)]) for part, more in zip(sums, conv_sum)]
        moved, kept["table"], seg_in_far, *kept["sums"] = together(
            moved, table_pieces, seg_in_far, *sums
        )
        rows_grad = embed_back(
            place, embedded_low, gain_vals[0], seg_in, seg_in_far, grad_after_attn
        )
        kept["rows"] = lax.all_to_all(rows_grad, "dp", 0, 0)
        return moved

    def beside_exchange(moved):
        moved, kept["rows"] = together(moved, kept["rows"])
        return moved

    def beside_rows(moved):
        moved, kept["rows"] = together(moved, kept["rows"])
        return moved

    def beside_streams(moved):
        moved, far = together(moved, swap(kept["rows"], "head", 2))
        kept["rows"] = jnp.stack([kept["rows"], far])
        return moved

    two = reduce_blocks(*two, (beside_sums, beside_exchange))
    one = reduce_blocks(*kept["sums"], (beside_rows, beside_streams))
    rows_grad = kept["rows"]
    rows_grad = jnp.stack([rows_grad, swap(rows_grad, "head", 1)]).reshape(-1, width)
    table_base = kept["table"].astype(single).reshape(vocab, width)

    up_grad = two[:hidden_own].T
    down_grad = two[hidden_own:]
    qkv_grad = jnp.swapaxes(one[: 3 * wide].reshape(3, wide, width), 1, 2)
    out_grad = one[3 * wide : 4 * wide]
    conv_grad = one[4 * wide :].reshape(wconv.shape)
    table_grad = scatter(bits, own_count, own_codes, table_base, rows_grad)

    gains_low = gains.astype(lowp).astype(single)
    gain_part = jnp.stack(
        [
            jnp.sum(low_qkv.astype(single) * qkv_grad, axis=(0, 2)),
            jnp.sum(wup.astype(lowp).astype(single) * up_grad, axis=1),
            jnp.sum(table.astype(lowp).astype(single) * table_base, axis=0),
        ]
    )

    grads = (table_grad, qkv_grad, out_grad, conv_grad, up_grad, down_grad)
    def sum_over_dp(joined):
        mask = 1
        while mask < dp_size:
            joined = joined + swap(joined, "dp", mask)
            mask *= 2
        return joined

    row_part = []
    col_part = []
    for grad in grads:
        square = grad * grad
        row_part.append(jnp.sum(square, axis=-1))
        col_part.append(jnp.sum(square, axis=tuple(range(square.ndim - 1))))
    row_q, row_u, col_e, col_o, col_c, col_d, gain_raw, early = lax.psum(
        (
            row_part[1],
            row_part[4],
            col_part[0],
            col_part[2],
            col_part[3],
            col_part[5],
            gain_part,
            early + scalar_row([0.0] * 15 + [loss_local]),
        ),
        "head",
    )
    lanes = [col_e, jnp.sum(row_q, axis=0), col_o]
    lanes += [jnp.concatenate([col_c, jnp.zeros((width - col_c.shape[0],), single)]), row_u, col_d]
    members = [col_part[4], row_part[5], row_part[3], row_part[2], col_part[1], *lanes, row_part[0], early]
    joined = jnp.concatenate([m.reshape(-1) for m in members])
    joined = sum_over_dp(jnp.concatenate([joined, jnp.zeros((-joined.shape[0] % 1024,), single)]))
    sums = []
    start = 0
    for member in members:
        sums.append(joined[start : start + member.size].reshape(member.shape))
        start += member.size
    col_u, row_d, row_c, row_o, col_q, *lanes, row_e, early = sums
    square_total = [jnp.sum(lane) for lane in lanes]
    row_sums = [row_e, row_q, row_o, row_c, row_u, row_d]
    col_sums = [col_e, col_q, col_o, col_c, col_u, col_d]
    weight_total = early[6:15]
    loss_all = early[15]
    inverse = 1.0 / count_all
    decay = 1.0 - STEP ** (-0.8)
    updates = []
    stats_new = []
    scaled = []
    counts = []
    update_sq = []
    for index in range(6):
        rows_total = rows_old[index].size * sizes[row_axes[index]]
        cols_total = cols_old[index].size * sizes[col_axes[index]]
        grad_scaled = grads[index] * inverse
        rows_new = decay * rows_old[index] + (1.0 - decay) * (
            row_sums[index] * inverse * inverse / cols_total + TINY_SQUARE
        )
        cols_new = decay * cols_old[index] + (1.0 - decay) * (
            col_sums[index] * inverse * inverse / rows_total + TINY_SQUARE
        )
        mean_row = decay * early[index] / rows_total + (1.0 - decay) * (
            square_total[index] * inverse * inverse / (rows_total * cols_total) + TINY_SQUARE
        )
        second = rows_new[..., None] * cols_new / mean_row
        direction = grad_scaled * lax.rsqrt(second)
        updates.append(direction)
        stats_new.append((rows_new, cols_new))
        scaled.append(grad_scaled)
        counts.append(rows_total * cols_total)
        update_sq.append(jnp.sum(direction * direction))
    gain_scaled = gain_raw / gains_low * inverse
    second_new = decay * gains_second + (1.0 - decay) * (gain_scaled * gain_scaled + TINY_SQUARE)
    gain_dir = gain_scaled * lax.rsqrt(second_new)
    for which in range(3):
        update_sq.append(jnp.sum(gain_dir[which] * gain_dir[which]) / head_size)
    update_total = after(scalar_row(update_sq, 1024), loss_all)
    for mask in (1, 2):
        update_total = update_total + swap(update_total, "head", mask)
    update_total = sum_over_dp(update_total)[:9]
    results = [loss_all, count_all]
    for index in range(6):
        factor = jnp.maximum(0.001, jnp.sqrt(weight_total[index] / counts[index]))
        denom = jnp.maximum(1.0, jnp.sqrt(update_total[index] / counts[index]) / CLIP_LEVEL)
        new_weight = weights_now[index] - LEARN_RATE * factor * updates[index] / denom
        results += [new_weight, scaled[index], stats_new[index][0], stats_new[index][1]]
    gain_factor = jnp.maximum(0.001, jnp.sqrt(weight_total[6:] / D))[:, None]
    gain_denom = jnp.maximum(1.0, jnp.sqrt(update_total[6:] / D) / CLIP_LEVEL)[:, None]
    results += [gains - LEARN_RATE * gain_factor * gain_dir / gain_denom, gain_scaled, second_new]
    return tuple(results)


def solution(mesh):
    in_specs = (
        P("dp", None),
        P("dp", None),
        P("dp", None),
        P("dp", None, None),
        P("dp", None, None),
        P("dp"),
        P("dp"),
        P("head", "dp"),
        P(None, "dp", "head"),
        P("head", "dp"),
        P("head", None, "dp"),
        P("dp", "head"),
        P("head", "dp"),
        P(None, "dp"),
        P("head"),
        P("dp"),
        P(None, "dp"),
        P("head"),
        P("head"),
        P("dp"),
        P("head", None),
        P("dp"),
        P("dp"),
        P("head"),
        P("head"),
        P("dp"),
        P(None, "dp"),
    )
    out_specs = (
        P(),
        P(),
        P("head", "dp"),
        P("head", "dp"),
        P("head"),
        P("dp"),
        P(None, "dp", "head"),
        P(None, "dp", "head"),
        P(None, "dp"),
        P("head"),
        P("head", "dp"),
        P("head", "dp"),
        P("head"),
        P("dp"),
        P("head", None, "dp"),
        P("head", None, "dp"),
        P("head", None),
        P("dp"),
        P("dp", "head"),
        P("dp", "head"),
        P("dp"),
        P("head"),
        P("head", "dp"),
        P("head", "dp"),
        P("head"),
        P("dp"),
        P(None, "dp"),
        P(None, "dp"),
        P(None, "dp"),
    )
    return jax.shard_map(local, mesh=mesh, in_specs=in_specs, out_specs=out_specs, check_vma=False)
```

```python
import functools

import jax
import jax.numpy as jnp
from jax import lax
from jax.experimental import pallas as pl
from jax.experimental.pallas import tpu as pltpu
from jax.sharding import PartitionSpec as P

D = 1024
H = 8
DH = 128
MEM = 512
CMEM = 512
RATE = 3
STEP = 10


TINY_NORM = 1e-06
TINY_SQUARE = 1e-30
LEARN_RATE = 0.5
CLIP_LEVEL = 1.0

lowp = jnp.bfloat16
single = jnp.float32
NT = (((1,), (1,)), ((), ()))
TN = (((0,), (0,)), ((), ()))
NN = (((1,), (0,)), ((), ()))
MIB = 1024 * 1024


def mm(left, right, dims=NN):
    return lax.dot_general(left, right, dims, preferred_element_type=single)


def swap(value, axis, mask):
    size = lax.axis_size(axis)
    return lax.ppermute(value, axis, [(i, i ^ mask) for i in range(size)])


def after(value, *deps):
    return lax.optimization_barrier((value, *deps))[0]


def together(*values):
    return lax.optimization_barrier(values)


def block_order(size):
    order = [0]
    step = size // 2
    while step:
        order = order + [j + step for j in order]
        step //= 2
    return order


def gather_blocks(piece, axis, beside=(), stop=0):
    steps = []
    mask = lax.axis_size("dp") // 2
    while mask > stop:
        moved = swap(piece, "dp", mask)
        if len(steps) < len(beside):
            moved = beside[len(steps)](moved)
        piece = jnp.concatenate([piece, moved], axis=axis)
        steps.append(piece)
        mask //= 2
    return piece, steps


def split(value, axis, parts):
    width = value.shape[axis] // parts
    return [lax.slice_in_dim(value, i * width, (i + 1) * width, axis=axis) for i in range(parts)]


def reduce_blocks(keep, send, beside=(), mask=1):
    moved = swap(send.astype(lowp), "dp", mask)
    if beside:
        moved = beside[0](moved)
    total = keep + moved.astype(single)
    mask *= 2
    if mask == lax.axis_size("dp"):
        return total
    return reduce_blocks(*split(total, 1, 2), beside[1:], mask)


def reorder_kernel(sources, *refs):
    out_ref = refs[-1]
    width = out_ref.shape[1] // len(sources)
    start = 0
    for in_ref in refs[:-1]:
        rows = slice(start, start + in_ref.shape[0])
        start += in_ref.shape[0]
        for p, q in enumerate(sources):
            block = in_ref[:, q * width : (q + 1) * width]
            out_ref[rows, p * width : (p + 1) * width] = block.astype(out_ref.dtype)


def reorder(values, mask):
    order = block_order(lax.axis_size("dp"))
    sources = [order.index(j ^ mask) for j in order]
    rows = sum(value.shape[0] for value in values)
    if D // len(order) % 128:
        joined = jnp.concatenate([value.astype(lowp) for value in values])
        cols = split(joined, 1, len(order))
        return jnp.concatenate([cols[q] for q in sources], axis=1)
    return pl.pallas_call(
        functools.partial(reorder_kernel, sources),
        name="reorder",
        out_shape=jax.ShapeDtypeStruct((rows, D), lowp),
        in_specs=[vmem()] * len(values),
        out_specs=vmem(),
        compiler_params=params(60),
        cost_estimate=cost(0, 2 * MIB),
    )(*values)


def relative(value, x, c):
    value = jnp.where(x == 1, jnp.flip(value, -3), value)
    value = jnp.where(c == 1, jnp.flip(value, -2), value)
    return jnp.swapaxes(value, -3, -2)


def rms(values, gain):
    inv = lax.rsqrt(jnp.mean(values * values, axis=-1, keepdims=True) + TINY_NORM)
    return (values * inv * gain).astype(lowp), inv


def rms_back(values, inv, gain, upstream):
    scaled = gain * upstream
    inner = jnp.sum(scaled * values, axis=-1, keepdims=True) / D
    return scaled * inv - values * (inner * inv * inv * inv)


def vmem(shape=None, index=None):
    if shape is None:
        return pl.BlockSpec(memory_space=pltpu.VMEM)
    return pl.BlockSpec(shape, index)


def smem():
    return pl.BlockSpec(memory_space=pltpu.SMEM)


def params(mib):
    return pltpu.CompilerParams(vmem_limit_bytes=mib * MIB)


def cost(flops, size, exps=0):
    return pl.CostEstimate(
        flops=int(0.02 * flops), bytes_accessed=int(0.02 * size), transcendentals=exps
    )


def lookup_kernel(row_ref, table_ref, out_ref, tab, held, sem):
    total = row_ref.shape[0]
    vocab = table_ref.shape[0]
    copy = pltpu.make_async_copy(table_ref, tab.at[pl.ds(0, vocab)], sem)
    copy.start()
    tab[pl.ds(vocab, 8), :] = jnp.zeros((8, tab.shape[1]), single)
    copy.wait()

    @pl.loop(0, total // 16)
    def _(g):
        for j in range(16):
            t = g * 16 + j
            held[pl.ds(t, 1), :] = tab[pl.ds(row_ref[t], 1), :]

    @pl.loop(0, total // 512)
    def _(i):
        rows = pl.ds(pl.multiple_of(i * 512, 512), 512)
        out_ref[rows, :] = held[rows, :].astype(lowp)


def lookup(rows, table):
    total = rows.shape[0]
    vocab, width = table.shape
    return pl.pallas_call(
        lookup_kernel,
        name="lookup",
        out_shape=jax.ShapeDtypeStruct((total, width), lowp),
        in_specs=[smem(), pl.BlockSpec(memory_space=pl.ANY)],
        out_specs=vmem(),
        scratch_shapes=[
            pltpu.VMEM((vocab + 8, width), single),
            pltpu.VMEM((total, width), single),
            pltpu.SemaphoreType.DMA(()),
        ],
        compiler_params=params(60),
        cost_estimate=cost(0, 30 * MIB),
    )(rows, table)


def list_kernel(code_ref, out_ref, count_ref):
    total = code_ref.shape[0]

    def group(g, count):
        for j in range(16):
            code = code_ref[g * 16 + j]
            out_ref[count] = code
            count = count + jnp.where(code >= 0, 1, 0)
        return count

    count_ref[0] = lax.fori_loop(0, total // 16, group, jnp.int32(0))


def own_list(codes):
    total = codes.shape[0]
    return pl.pallas_call(
        list_kernel,
        name="own_list",
        out_shape=(
            jax.ShapeDtypeStruct((total + 8,), jnp.int32),
            jax.ShapeDtypeStruct((1,), jnp.int32),
        ),
        in_specs=[smem()],
        out_specs=(smem(), smem()),
        cost_estimate=cost(0, 60 * MIB),
    )(codes)


def place_kernel(order, place_ref, in_ref, gain_ref, out_ref, norm_ref, held):
    width = in_ref.shape[2]
    for p, j in enumerate(order):
        block = in_ref[pl.ds(place_ref[1] ^ j, 1)][0]
        out_ref[:, p * width : (p + 1) * width] = block
        held[:, p * width : (p + 1) * width] = block.astype(single)
    values = held[...]
    inv = lax.rsqrt(jnp.mean(values * values, axis=-1, keepdims=True) + TINY_NORM)
    norm_ref[...] = (values * inv * gain_ref[...]).astype(lowp)


def place_embedding(place, blocks, gain):
    rows = blocks.shape[1]
    return pl.pallas_call(
        functools.partial(place_kernel, block_order(blocks.shape[0])),
        name="place_embedding",
        out_shape=(jax.ShapeDtypeStruct((rows, D), lowp), jax.ShapeDtypeStruct((rows, D), lowp)),
        in_specs=[smem(), vmem(), vmem()],
        out_specs=(vmem(), vmem()),
        scratch_shapes=[pltpu.VMEM((rows, D), single)],
        compiler_params=params(60),
        cost_estimate=cost(0, 3 * MIB),
    )(place, blocks, gain)


def embed_back_kernel(order, place_ref, in_ref, gain_ref, keep_ref, more_ref, grad_ref, out_ref, held):
    values = in_ref[...].astype(single)
    inv = lax.rsqrt(jnp.mean(values * values, axis=-1, keepdims=True) + TINY_NORM)
    upstream = keep_ref[...] + more_ref[...].astype(single)
    held[...] = grad_ref[...] + rms_back(values, inv, gain_ref[...], upstream)
    width = out_ref.shape[2]
    for p, j in enumerate(order):
        block = held[:, p * width : (p + 1) * width].astype(lowp)
        out_ref[pl.ds(place_ref[1] ^ j, 1)] = block[None]


def embed_back(place, values, gain, keep, more, grad):
    rows = values.shape[0]
    size = lax.axis_size("dp")
    return pl.pallas_call(
        functools.partial(embed_back_kernel, block_order(size)),
        name="embed_back",
        out_shape=jax.ShapeDtypeStruct((size, rows, D // size), lowp),
        in_specs=[smem()] + [vmem()] * 5,
        out_specs=vmem(),
        scratch_shapes=[pltpu.VMEM((rows, D), single)],
        compiler_params=params(60),
        cost_estimate=cost(0, 4 * MIB),
    )(place, values, gain, keep, more, grad)


def scatter_kernel(bits, count_ref, code_ref, base_ref, grad_ref, out_ref, rows):
    total = grad_ref.shape[0]
    vocab = base_ref.shape[0]

    @pl.loop(0, total // 512)
    def _(i):
        here = pl.ds(pl.multiple_of(i * 512, 512), 512)
        rows[here, :] = grad_ref[here, :].astype(single)

    rows[pl.ds(total, 8), :] = jnp.zeros((8, rows.shape[1]), single)

    @pl.loop(0, vocab // 400)
    def _(i):
        here = pl.ds(pl.multiple_of(i * 400, 400), 400)
        out_ref[here, :] = base_ref[here, :]

    count = count_ref[0]

    def group(g, carry):
        for j in range(8):
            index = g * 8 + j
            code = jnp.where(index < count, code_ref[index], total << bits)
            token = lax.shift_right_logical(code, bits)
            row = code & ((1 << bits) - 1)
            out_ref[pl.ds(row, 1), :] = out_ref[pl.ds(row, 1), :] + rows[pl.ds(token, 1), :]
        return carry

    lax.fori_loop(0, (count + 7) // 8, group, jnp.int32(0))


def scatter(bits, count, codes, base, grad):
    total, width = grad.shape
    return pl.pallas_call(
        functools.partial(scatter_kernel, bits),
        name="scatter",
        out_shape=jax.ShapeDtypeStruct(base.shape, single),
        in_specs=[smem(), smem(), vmem(), vmem()],
        out_specs=vmem(),
        scratch_shapes=[pltpu.VMEM((total + 8, width), single)],
        compiler_params=params(60),
        cost_estimate=cost(0, 30 * MIB),
    )(count, codes, base, grad)


def state_kernel(order, width, place_ref, gain_ref, in_ref, out_ref, held):
    rows = in_ref.shape[1]
    values = in_ref[0].astype(single)
    inv = lax.rsqrt(jnp.mean(values * values, axis=-1, keepdims=True) + TINY_NORM)
    for p, j in enumerate(order):
        start = pl.multiple_of((place_ref[1] ^ j) * width, width)
        block = in_ref[0, :, pl.ds(start, width)].astype(single)
        held[p] = block * inv * gain_ref[:, p * width : (p + 1) * width]
    groups = out_ref.shape[0]
    for p in range(len(order)):
        cols = slice(p * width, (p + 1) * width)
        if groups == 1:
            out_ref[0, :, cols] = held[p].astype(lowp)
        else:
            for j in range(groups):
                part = held[p, pl.ds(j, rows // groups, stride=groups), :]
                out_ref[j, :, cols] = part.astype(lowp)


def state_norm(place, gain, states, groups):
    size = lax.axis_size("dp")
    order = block_order(size)
    width = D // size
    streams = states.shape[0]
    count = states.shape[1] // groups
    if width % 128:
        values = jnp.where(place[0] == 1, jnp.flip(states, 0), states).astype(single).reshape(-1, D)
        inv = lax.rsqrt(jnp.mean(values * values, axis=-1, keepdims=True) + TINY_NORM)
        lanes = jnp.arange(D, dtype=jnp.int32)
        blocks = jnp.asarray(order, jnp.int32)[lanes // width] ^ place[1]
        source = blocks * width + lanes % width
        shuffle = (lanes[:, None] == source[None, :]).astype(single)
        moved = jnp.dot(values * inv, shuffle, precision=lax.Precision.HIGHEST)
        out = (moved * gain).astype(lowp)
        return jnp.swapaxes(out.reshape(streams * count, groups, D), 0, 1)
    tile = 128
    return pl.pallas_call(
        functools.partial(state_kernel, order, width),
        name="state_norm",
        out_shape=jax.ShapeDtypeStruct((groups, streams * count, D), lowp),
        grid_spec=pltpu.PrefetchScalarGridSpec(
            num_scalar_prefetch=1,
            grid=(streams, count // tile),
            in_specs=[
                pl.BlockSpec((1, D), lambda n, i, s: (0, 0)),
                pl.BlockSpec((1, tile * groups, D), lambda n, i, s: (s[0] ^ n, i, 0)),
            ],
            out_specs=pl.BlockSpec(
                (groups, tile, D), lambda n, i, s: (0, n * (count // tile) + i, 0)
            ),
            scratch_shapes=[pltpu.VMEM((len(order), tile * groups, width), single)],
        ),
        compiler_params=params(60),
        cost_estimate=cost(0, 4 * streams * count * groups * D),
    )(place, gain, states)


def compress_kernel(old_ref, key_ref, value_ref, conv_ref, comp_ref, raw_ref):
    heads = conv_ref.shape[0]
    wide = heads * DH
    for part, weight_ref in enumerate((key_ref, value_ref)):
        sums = [None] * heads
        for j in range(RATE):
            raw = mm(old_ref[j], weight_ref[...], NT).astype(lowp)
            raw_ref[j, :, part * wide : (part + 1) * wide] = raw
            for n in range(heads):
                piece = raw[:, n * DH : (n + 1) * DH]
                term = mm(piece, conv_ref[n, j * DH : (j + 1) * DH, :])
                sums[n] = term if j == 0 else sums[n] + term
        for n in range(heads):
            first = part * wide + n * DH
            comp_ref[:, first : first + DH] = sums[n].astype(lowp)


def compress(old3, weights, conv):
    rows = old3.shape[1]
    wide = conv.shape[0] * DH
    tile = 256
    return pl.pallas_call(
        compress_kernel,
        name="compress",
        grid=(rows // tile,),
        out_shape=(
            jax.ShapeDtypeStruct((rows, 2 * wide), lowp),
            jax.ShapeDtypeStruct((RATE, rows, 2 * wide), lowp),
        ),
        in_specs=[
            pl.BlockSpec((RATE, tile, D), lambda i: (0, i, 0)),
            pl.BlockSpec((wide, D), lambda i: (1, 0)),
            pl.BlockSpec((wide, D), lambda i: (2, 0)),
            pl.BlockSpec(conv.shape, lambda i: (0, 0, 0)),
        ],
        out_specs=(
            pl.BlockSpec((tile, 2 * wide), lambda i: (i, 0)),
            pl.BlockSpec((RATE, tile, 2 * wide), lambda i: (0, i, 0)),
        ),
        compiler_params=params(60),
        cost_estimate=cost(4 * RATE * rows * wide * D, 12 * MIB),
    )(old3, weights, weights, conv)


def expand_kernel(grad_ref, raw_ref, conv_ref, out_ref, conv_out_ref):
    heads = conv_ref.shape[0]
    for h in range(heads):
        for j in range(RATE):
            rows = slice(j * DH, (j + 1) * DH)
            taps = conv_ref[h, rows, :]
            total = None
            for n in (h, heads + h):
                cols = slice(n * DH, (n + 1) * DH)
                grad = grad_ref[:, cols]
                out_ref[j, :, cols] = mm(grad, taps, NT).astype(lowp)
                term = mm(raw_ref[j, :, cols], grad, TN)
                total = term if total is None else total + term
            conv_out_ref[h, rows, :] = total


def expand(grad, raw, conv):
    return pl.pallas_call(
        expand_kernel,
        name="expand",
        out_shape=(
            jax.ShapeDtypeStruct(raw.shape, lowp),
            jax.ShapeDtypeStruct(conv.shape, single),
        ),
        in_specs=[vmem()] * 3,
        out_specs=(vmem(), vmem()),
        compiler_params=params(60),
        cost_estimate=cost(2000 * MIB, 12 * MIB),
    )(grad, raw, conv)


def masked_scores(info_ref, query, keys):
    rows = query.shape[0]
    scale = DH ** (-0.5)
    result = []
    for which, key in enumerate(keys):
        slots = key.shape[0]
        col = lax.broadcasted_iota(jnp.int32, (rows, slots), 1)
        if which < 2:
            seen = col >= slots - info_ref[2 * pl.program_id(0) + which]
        else:
            row = lax.broadcasted_iota(jnp.int32, (rows, slots), 0)
            shift = info_ref[4]
            row = row + shift
            col = col + shift
            row = jnp.where(row >= slots, row - slots, row)
            col = jnp.where(col >= slots, col - slots, col)
            seen = col <= row
        result.append(jnp.where(seen, mm(query, key, NT) * scale, -1e30))
    return result


def rows_of(ref):
    return ref[...].reshape(-1, ref.shape[-1])


def attend_kernel(info_ref, q_ref, ks_ref, vs_ref, kc_ref, vc_ref, km_ref, vm_ref, out_ref, lse_ref):
    query = rows_of(q_ref)
    scores = masked_scores(info_ref, query, [kc_ref[...], km_ref[...], rows_of(ks_ref)])
    top = functools.reduce(jnp.maximum, [jnp.max(s, axis=-1, keepdims=True) for s in scores])
    total = 0.0
    mixed = 0.0
    for score, value in zip(scores, (vc_ref[...], vm_ref[...], rows_of(vs_ref))):
        weight = jnp.exp(score - top)
        total = total + jnp.sum(weight, axis=-1, keepdims=True)
        mixed = mixed + mm(weight.astype(lowp), value)
    out_ref[...] = (mixed / total).astype(lowp).reshape(out_ref.shape)
    lse_ref[0, 0] = top + jnp.log(total)


def attend_back_kernel(
    info_ref, q_ref, ks_ref, vs_ref, kc_ref, vc_ref, km_ref, vm_ref, lse_ref, up_ref,
    seg_ref, comp_ref, mem_ref,
):
    head = pl.program_id(1)
    wide = pl.num_programs(1) * DH
    scale = DH ** (-0.5)
    query = rows_of(q_ref)
    upstream = rows_of(up_ref)
    keys = [kc_ref[...], km_ref[...], rows_of(ks_ref)]
    scores = masked_scores(info_ref, query, keys)
    probs = [jnp.exp(s - lse_ref[0, 0]) for s in scores]
    prob_grads = [
        mm(upstream, v, NT) for v in (vc_ref[...], vm_ref[...], rows_of(vs_ref))
    ]
    inner = 0.0
    for p, g in zip(probs, prob_grads):
        inner = inner + jnp.sum(p * g, axis=-1, keepdims=True)
    here = pl.ds(pl.multiple_of(head * DH, DH), DH)
    second = pl.ds(pl.multiple_of(wide + head * DH, DH), DH)
    third = pl.ds(pl.multiple_of(2 * wide + head * DH, DH), DH)
    query_grad = 0.0
    places = ((comp_ref, here, second), (mem_ref, here, second), (seg_ref, second, third))
    for p, g, key, (ref, key_at, value_at) in zip(probs, prob_grads, keys, places):
        score_grad = (p * (g - inner)).astype(lowp)
        query_grad = query_grad + mm(score_grad, key)
        shape = ref.shape[:-1] + (DH,)
        key_grad = (mm(score_grad, query, TN) * scale).astype(lowp)
        value_grad = mm(p.astype(lowp), upstream, TN).astype(lowp)
        ref[..., key_at] = key_grad.reshape(shape)
        ref[..., value_at] = value_grad.reshape(shape)
    shape = seg_ref.shape[:-1] + (DH,)
    seg_ref[..., here] = (query_grad * scale).astype(lowp).reshape(shape)


def head_specs(seg, comp, mem, heads):
    streams = seg.shape[1]

    def of_seg(first):
        return pl.BlockSpec((2, 1, seg.shape[2], DH), lambda n, h: (0, n, 0, first + h))

    def cols(array, first):
        return pl.BlockSpec((array.shape[0] // streams, DH), lambda n, h: (n, first + h))

    return [
        smem(),
        of_seg(0),
        of_seg(heads),
        of_seg(2 * heads),
        cols(comp, 0),
        cols(comp, heads),
        cols(mem, 0),
        cols(mem, heads),
    ]


def attend(info, seg, comp, mem):
    _, streams, half, _ = seg.shape
    heads = comp.shape[1] // (2 * DH)
    return pl.pallas_call(
        attend_kernel,
        name="attend",
        grid=(streams, heads),
        out_shape=(
            jax.ShapeDtypeStruct((2, streams, half, heads * DH), lowp),
            jax.ShapeDtypeStruct((streams, heads, 2 * half, 1), single),
        ),
        in_specs=head_specs(seg, comp, mem, heads),
        out_specs=(
            pl.BlockSpec((2, 1, half, DH), lambda n, h: (0, n, 0, h)),
            pl.BlockSpec((1, 1, 2 * half, 1), lambda n, h: (n, h, 0, 0)),
        ),
        compiler_params=params(60),
        cost_estimate=cost(7000 * MIB, 6 * MIB),
    )(info, seg, seg, seg, comp, comp, mem, mem)


def attend_back(info, seg, comp, mem, lse, upstream):
    _, streams, half, wide = seg.shape
    heads = comp.shape[1] // (2 * DH)
    slots = comp.shape[0] // streams
    kept = mem.shape[0] // streams
    return pl.pallas_call(
        attend_back_kernel,
        name="attend_back",
        grid=(streams, heads),
        out_shape=(
            jax.ShapeDtypeStruct(seg.shape, lowp),
            jax.ShapeDtypeStruct(comp.shape, lowp),
            jax.ShapeDtypeStruct(mem.shape, lowp),
        ),
        in_specs=head_specs(seg, comp, mem, heads)
        + [
            pl.BlockSpec((1, 1, 2 * half, 1), lambda n, h: (n, h, 0, 0)),
            pl.BlockSpec((2, 1, half, DH), lambda n, h: (0, n, 0, h)),
        ],
        out_specs=(
            pl.BlockSpec((2, 1, half, wide), lambda n, h: (0, n, 0, 0)),
            pl.BlockSpec((slots, comp.shape[1]), lambda n, h: (n, 0)),
            pl.BlockSpec((kept, mem.shape[1]), lambda n, h: (n, 0)),
        ),
        compiler_params=params(60),
        cost_estimate=cost(11000 * MIB, 9 * MIB),
    )(info, seg, seg, seg, comp, comp, mem, mem, lse, upstream)


def columns_of(rows):
    tall = jnp.concatenate([rows, jnp.zeros((120, rows.shape[1]), single)], axis=0)
    return jnp.transpose(tall)


def logits_kernel(
    words, pair_info_ref, near_info_ref, pair_ref, near_ref, left_ref, right_ref,
    pair_out_ref, near_out_ref, stat_ref,
):
    step = pl.program_id(0)
    tile = pair_ref.shape[0]
    half = left_ref.shape[1]
    edge = left_ref.shape[0] - 128
    streams = (
        (pair_info_ref, pair_ref, pair_out_ref),
        (near_info_ref, near_ref, near_out_ref),
    )
    products = [
        mm(ref[:, :half], left_ref[...], NT) + mm(ref[:, half:], right_ref[...], NT)
        for _, ref, _ in streams
    ]
    for n, ((info_ref, _, out_ref), logits) in enumerate(zip(streams, products)):
        wanted = columns_of(info_ref[0])[:, 0:1].astype(jnp.int32)
        col = lax.broadcasted_iota(jnp.int32, logits.shape, 1)
        hit = jnp.sum(jnp.where(col == wanted, logits, 0.0), axis=-1, keepdims=True)
        last = jnp.where(col[:, edge:] < words, logits[:, edge:], -1e30)
        top = jnp.max(last, axis=-1, keepdims=True)
        top = jnp.maximum(top, jnp.max(logits[:, :edge], axis=-1, keepdims=True))
        raised = jnp.exp(logits[:, :edge] - top)
        last = jnp.exp(last - top)
        total = jnp.sum(raised, axis=-1, keepdims=True) + jnp.sum(last, axis=-1, keepdims=True)
        out_ref[:, :edge] = raised.astype(lowp)
        out_ref[:, edge:] = last.astype(lowp)
        lane = lax.broadcasted_iota(jnp.int32, (tile, 128), 1)
        packed = jnp.where(lane == 2, hit, 0.0)
        packed = jnp.where(lane == 0, top, jnp.where(lane == 1, total, packed))
        start = n * (stat_ref.shape[1] // 2) + step * tile
        stat_ref[:, pl.ds(pl.multiple_of(start, tile), tile)] = jnp.transpose(packed)[:8]


def logits_part(words, chunk, info, pair, near, left, right):
    rows, _ = pair.shape
    slots = left.shape[0]
    tile = 256
    tiles = rows // tile
    whole = lambda i: (0, 0)
    return pl.pallas_call(
        functools.partial(logits_kernel, words),
        name="logits_part",
        grid=(tiles,),
        out_shape=(
            jax.ShapeDtypeStruct((rows, slots), lowp),
            jax.ShapeDtypeStruct((rows, slots), lowp),
            jax.ShapeDtypeStruct((8, 2 * rows), single),
        ),
        in_specs=[
            pl.BlockSpec((1, 8, tile), lambda i: (chunk, 0, i)),
            pl.BlockSpec((1, 8, tile), lambda i: (chunk, 0, tiles + i)),
            pl.BlockSpec((tile, D), lambda i: (i, 0)),
            pl.BlockSpec((tile, D), lambda i: (i, 0)),
            pl.BlockSpec(left.shape, whole),
            pl.BlockSpec(right.shape, whole),
        ],
        out_specs=(
            pl.BlockSpec((tile, slots), lambda i: (i, 0)),
            pl.BlockSpec((tile, slots), lambda i: (i, 0)),
            pl.BlockSpec((8, 2 * rows), whole),
        ),
        compiler_params=params(60),
        cost_estimate=cost(8 * rows * slots * D, 10 * MIB),
    )(info, info, pair, near, left, right)


def logits_back_kernel(
    pair_info_ref, near_info_ref, pair_factor_ref, near_factor_ref, pair_ref, near_ref,
    left_ref, right_ref, pair_out_ref, near_out_ref, pair_grad_ref, near_grad_ref,
):
    half = left_ref.shape[1]
    streams = (
        (near_info_ref, near_factor_ref, near_ref, near_out_ref, near_grad_ref),
        (pair_info_ref, pair_factor_ref, pair_ref, pair_out_ref, pair_grad_ref),
    )
    for info_ref, factor_ref, in_ref, out_ref, grad_ref in streams:
        info = columns_of(info_ref[0])
        wanted = info[:, 0:1].astype(jnp.int32)
        counted = info[:, 1:2]
        factor = columns_of(factor_ref[0])[:, 0:1]
        raised = in_ref[...].astype(single)
        col = lax.broadcasted_iota(jnp.int32, raised.shape, 1)
        grads = (raised * factor - jnp.where(col == wanted, counted, 0.0)).astype(lowp)
        out_ref[...] = grads
        grad_ref[:, :half] = mm(grads, left_ref[...]).astype(lowp)
        grad_ref[:, half:] = mm(grads, right_ref[...]).astype(lowp)


def logits_back(chunk, info, factor, raised, left, right):
    rows, slots = raised[0].shape
    tile = 256
    tiles = rows // tile
    whole = lambda i: (0, 0)

    def info_specs():
        return [
            pl.BlockSpec((1, 8, tile), lambda i: (chunk, 0, i)),
            pl.BlockSpec((1, 8, tile), lambda i: (chunk, 0, tiles + i)),
        ]

    return pl.pallas_call(
        logits_back_kernel,
        name="logits_back",
        grid=(tiles,),
        out_shape=(
            jax.ShapeDtypeStruct((rows, slots), lowp),
            jax.ShapeDtypeStruct((rows, slots), lowp),
            jax.ShapeDtypeStruct((rows, D), lowp),
            jax.ShapeDtypeStruct((rows, D), lowp),
        ),
        in_specs=info_specs()
        + info_specs()
        + [pl.BlockSpec((tile, slots), lambda i: (i, 0))] * 2
        + [pl.BlockSpec(left.shape, whole), pl.BlockSpec(right.shape, whole)],
        out_specs=(
            pl.BlockSpec((tile, slots), lambda i: (i, 0)),
            pl.BlockSpec((tile, slots), lambda i: (i, 0)),
            pl.BlockSpec((tile, D), lambda i: (i, 0)),
            pl.BlockSpec((tile, D), lambda i: (i, 0)),
        ),
        compiler_params=params(60),
        cost_estimate=cost(8 * rows * slots * D, 12 * MIB),
    )(info, info, factor, factor, *raised, left, right)


def halves(total, keep_ref, send_ref):
    half = keep_ref.shape[1]
    keep_ref[...] = total[:, :half]
    send_ref[...] = total[:, half:].astype(send_ref.dtype)


def table_grad_kernel(count, *refs):
    total = mm(refs[0][...], refs[count][...], TN)
    for i in range(1, count):
        total = total + mm(refs[i][...], refs[count + i][...], TN)
    halves(total, *refs[2 * count :])


def table_grad_part(grads, inputs):
    grads = [half for pair in grads for half in pair]
    inputs = [half for pair in inputs for half in pair]
    rows = sum(g.shape[0] for g in grads)
    slots = grads[0].shape[1]
    block = 256
    if rows > 4096:
        keep, send = split(sum(mm(g, v, TN) for g, v in zip(grads, inputs)), 1, 2)
        return keep, send.astype(lowp)
    return pl.pallas_call(
        functools.partial(table_grad_kernel, len(grads)),
        name="table_grad_part",
        grid=(slots // block,),
        out_shape=(
            jax.ShapeDtypeStruct((slots, D // 2), single),
            jax.ShapeDtypeStruct((slots, D // 2), lowp),
        ),
        in_specs=[pl.BlockSpec((g.shape[0], block), lambda i: (0, i)) for g in grads]
        + [pl.BlockSpec(v.shape, lambda i: (0, 0)) for v in inputs],
        out_specs=(
            pl.BlockSpec((block, D // 2), lambda i: (i, 0)),
            pl.BlockSpec((block, D // 2), lambda i: (i, 0)),
        ),
        compiler_params=params(60),
        cost_estimate=cost(3 * rows * slots * D, 30 * MIB),
    )(*grads, *inputs)


def hidden_grad_kernel(blocks, pre_ref, act_ref, in_ref, down_ref, keep_ref, send_ref):
    step = pl.program_id(0)

    @pl.when(step < blocks)
    def _():
        halves(mm(pre_ref[...], in_ref[...], TN), keep_ref, send_ref)

    @pl.when(step >= blocks)
    def _():
        halves(mm(act_ref[...], down_ref[...], TN), keep_ref, send_ref)


def hidden_grads(pre_grad, hidden_act, ffn_in, down_in):
    rows, hidden = pre_grad.shape
    block = 256
    blocks = hidden // block
    return pl.pallas_call(
        functools.partial(hidden_grad_kernel, blocks),
        name="hidden_grads",
        grid=(2 * blocks,),
        out_shape=(
            jax.ShapeDtypeStruct((2 * hidden, D // 2), single),
            jax.ShapeDtypeStruct((2 * hidden, D // 2), lowp),
        ),
        in_specs=[
            pl.BlockSpec((rows, block), lambda i: (0, jnp.minimum(i, blocks - 1))),
            pl.BlockSpec((rows, block), lambda i: (0, jnp.maximum(i - blocks, 0))),
            pl.BlockSpec((rows, D), lambda i: (0, 0)),
            pl.BlockSpec((rows, D), lambda i: (0, 0)),
        ],
        out_specs=(
            pl.BlockSpec((block, D // 2), lambda i: (i, 0)),
            pl.BlockSpec((block, D // 2), lambda i: (i, 0)),
        ),
        compiler_params=params(60),
        cost_estimate=cost(6 * rows * hidden * D, 16 * MIB),
    )(pre_grad, hidden_act, ffn_in, down_in)


def attn_grad_kernel(
    seg_ref, mixed_ref, mem_ref, old_ref, normed_ref, up_ref, mem_in_ref, old_in_ref, keep_ref, send_ref
):
    which = pl.program_id(0)

    @pl.when(which == 0)
    def _():
        halves(mm(seg_ref[...], normed_ref[...], TN), keep_ref, send_ref)

    @pl.when(which == 3)
    def _():
        halves(mm(mixed_ref[...], up_ref[...], TN), keep_ref, send_ref)

    @pl.when(jnp.logical_and(which > 0, which < 3))
    def _():
        total = mm(seg_ref[...], normed_ref[...], TN)
        total = total + mm(mem_ref[...], mem_in_ref[...], TN)
        total = total + mm(old_ref[...], old_in_ref[...], TN)
        halves(total, keep_ref, send_ref)


def attn_grads(seg_grad, mixed, mem_grad, old_grad, normed, attn_in, mem_in, old_in):
    block = mixed.shape[1]

    def whole(array):
        return pl.BlockSpec(array.shape, lambda i: (0, 0))

    return pl.pallas_call(
        attn_grad_kernel,
        name="attn_grads",
        grid=(4,),
        out_shape=(
            jax.ShapeDtypeStruct((4 * block, D // 2), single),
            jax.ShapeDtypeStruct((4 * block, D // 2), lowp),
        ),
        in_specs=[
            pl.BlockSpec((seg_grad.shape[0], block), lambda i: (0, jnp.minimum(i, 2))),
            whole(mixed),
            pl.BlockSpec((mem_grad.shape[0], block), lambda i: (0, jnp.clip(i - 1, 0, 1))),
            pl.BlockSpec((old_grad.shape[0], block), lambda i: (0, jnp.clip(i - 1, 0, 1))),
            whole(normed),
            whole(attn_in),
            whole(mem_in),
            whole(old_in),
        ],
        out_specs=(
            pl.BlockSpec((block, D // 2), lambda i: (i, 0)),
            pl.BlockSpec((block, D // 2), lambda i: (i, 0)),
        ),
        compiler_params=params(60),
        cost_estimate=cost(9000 * MIB, 24 * MIB),
    )(seg_grad, mixed, mem_grad, old_grad, normed, attn_in, mem_in, old_in)


def scalar_row(values, length=128):
    lane = jnp.arange(length, dtype=jnp.int32)
    row = jnp.zeros((length,), single)
    for i, value in enumerate(values):
        row = jnp.where(lane == i, value, row)
    return row


def local(
    ids,
    targets,
    target_mask,
    memory,
    old_states,
    mem_fill,
    comp_fill,
    table,
    qkv,
    wout,
    wconv,
    wup,
    wdown,
    gains,
    table_rows,
    table_cols,
    qkv_rows,
    qkv_cols,
    out_rows,
    out_cols,
    conv_rows,
    conv_cols,
    up_rows,
    up_cols,
    down_rows,
    down_cols,
    gains_second,
):
    dp_size, head_size = lax.axis_size("dp"), lax.axis_size("head")
    d, h = lax.axis_index("dp"), lax.axis_index("head")
    x, c = h // 2, h % 2
    order = block_order(dp_size)
    reach = dp_size // 2
    streams, seg_len = ids.shape
    half = seg_len // 2
    per_group = streams * seg_len
    vocab, width = table.shape
    assert head_size == 4 and streams == 2

    weights_now = (table, qkv, wout, wconv, wup, wdown)
    rows_old = (table_rows, qkv_rows, out_rows, conv_rows, up_rows, down_rows)
    cols_old = (table_cols, qkv_cols, out_cols, conv_cols, up_cols, down_cols)
    sizes = {"dp": dp_size, "head": head_size}
    row_axes = ("head", "dp", "head", "head", "dp", "head")
    col_axes = ("dp", "head", "dp", "dp", "head", "dp")

    def early_sums(dep):
        _, *tied = together(dep, *rows_old, *weights_now, gains)
        sums = [jnp.sum(old) / sizes[axis] for old, axis in zip(tied[:6], col_axes)]
        sums += [jnp.sum(weight * weight) for weight in tied[6:12]]
        gain_sums = jnp.sum(tied[12] * tied[12], axis=1) / head_size
        return scalar_row(sums + [gain_sums[0], gain_sums[1], gain_sums[2]])

    def core_sum(keep, send, beside=()):
        more, *beside = together(swap(send.astype(lowp), "head", 1), *beside)
        part = keep.astype(single) + more.astype(single)
        return (part, beside) if beside else part

    def stream_sum(part, beside=()):
        keep, send = split(part, 0, 2)
        more, *beside = together(swap(send.astype(lowp), "head", 2), *beside)
        part = keep + more.astype(single)
        return (part, beside) if beside else part

    def group_sum(part, beside=()):
        return stream_sum(core_sum(*split(part, 0, 2)), beside)

    def group_both(part, beside=()):
        far, *beside = together(swap(part, "head", 2), *beside)
        pair = jnp.concatenate([part, far], axis=0)
        both = (pair, swap(pair, "head", 1))
        return (both, beside) if beside else both

    flat = jnp.concatenate(
        [
            ids.astype(single).reshape(-1),
            targets.astype(single).reshape(-1),
            target_mask.astype(single).reshape(-1),
            gains.astype(lowp).astype(single).reshape(-1),
        ]
    )
    room = -flat.shape[0] % 1024
    flat = jnp.concatenate([flat, jnp.zeros((room,), single)]).reshape(1, -1, 128)
    small, small_steps = gather_blocks(flat, 0)
    small = small.reshape(dp_size, -1)
    place = jnp.stack([x, d])

    def field(raw):
        return relative(raw.reshape(-1, 2, 2, half), x, c)

    ids_all = small[:, :per_group]
    position = [order.index(j) for j in range(dp_size)]
    ids_all = jnp.take(ids_all, jnp.asarray(position, jnp.int32)[jnp.arange(dp_size) ^ d], axis=0)
    ids_all = jnp.transpose(field(ids_all), (1, 2, 0, 3)).reshape(-1).astype(jnp.int32)
    table_rows_all = ids_all - h * vocab
    inside = (table_rows_all >= 0) & (table_rows_all < vocab)
    bits = vocab.bit_length()
    token_codes = (jnp.arange(ids_all.shape[0], dtype=jnp.int32) << bits) | table_rows_all
    token_codes = jnp.where(inside, token_codes, -1)
    table_rows_all = jnp.where(inside, table_rows_all, vocab)
    targets_all = field(small[:reach, per_group : 2 * per_group])
    mask_all = field(small[:reach, 2 * per_group : 3 * per_group])
    gain_blocks = small[:, 3 * per_group : 3 * per_group + 3 * width].reshape(dp_size, 3, width)
    gain_vals = jnp.swapaxes(gain_blocks, 0, 1).reshape(3, 1, D)
    count_all = jnp.sum(small[:, 2 * per_group : 3 * per_group])

    heads_own = wconv.shape[0]
    wide = qkv.shape[2]
    conv_rows_own = wconv.size // width
    low_qkv = qkv.astype(lowp)
    pack_one = jnp.concatenate(
        [
            jnp.swapaxes(low_qkv, 1, 2).reshape(3 * wide, width),
            wout.astype(lowp),
            wconv.astype(lowp).reshape(conv_rows_own, width),
        ]
    )
    own_half, far_half = split(table_rows_all, 0, 2)
    kept = {}

    def beside_lookup(moved):
        moved, kept["far"], kept["own"] = together(
            moved, lookup(far_half, table), lookup(own_half, table)
        )
        return moved

    def beside_memory(moved):
        looked = (kept["own"] + swap(kept["far"], "head", 1)).reshape(2, -1, width)
        mem_normed = state_norm(place, gain_vals[0], memory, 1)[0]
        moved, more, kept["mem"] = together(moved, swap(looked[1], "head", 2), mem_normed)
        looked = (looked[0] + more).reshape(dp_size, half, width)
        kept["looked"] = lax.all_to_all(looked, "dp", 0, 0)
        return moved

    own_one, steps_one = gather_blocks(
        after(pack_one, small_steps[0]), 1, (beside_lookup, beside_memory)
    )
    conv_lanes = jnp.arange(DH, dtype=jnp.int32)
    conv_width = DH // dp_size
    conv_natural = (jnp.asarray(order, jnp.int32)[conv_lanes // conv_width] ^ d) * conv_width
    conv_natural = conv_natural + conv_lanes % conv_width
    conv_shuffle = (conv_natural[:, None] == conv_lanes[None, :]).astype(lowp)
    taps = heads_own * RATE * DH

    def conv_natural_order(rows):
        value = jnp.swapaxes(rows.reshape(conv_rows_own, dp_size, width), 0, 1)
        value = jnp.swapaxes(value.reshape(dp_size, taps, conv_width), 0, 1)
        moved = mm(value.reshape(taps, DH), conv_shuffle).astype(lowp)
        return moved.reshape(heads_own, RATE * DH, DH)

    def conv_block_order(value):
        moved = mm(value.astype(lowp).reshape(taps, DH), conv_shuffle, NT).astype(lowp)
        moved = jnp.swapaxes(moved.reshape(taps, dp_size, conv_width), 0, 1)
        moved = jnp.swapaxes(moved.reshape(dp_size, conv_rows_own, width), 0, 1)
        return moved.reshape(conv_rows_own, D)

    full_conv = conv_natural_order(own_one[4 * wide :])

    hidden_own = wup.shape[1]
    pack_two = jnp.concatenate([wup.astype(lowp).T, wdown.astype(lowp)])

    old_normed = state_norm(place, gain_vals[0], old_states, RATE)

    words = vocab // reach
    z = d // 2
    word_start = (h * vocab + z * words).astype(single)
    wanted_all = targets_all - word_start
    wanted_all = jnp.where((wanted_all >= 0) & (wanted_all < words), wanted_all, -1.0)
    info_all = jnp.stack([wanted_all, mask_all] + [jnp.zeros_like(mask_all)] * 6)
    info_all = jnp.transpose(info_all, (1, 0, 2, 3, 4)).reshape(reach, 8, per_group)

    def beside_old(moved):
        moved, looked, kept["old"], kept["info"] = together(
            moved, kept["looked"], old_normed, info_all
        )
        kept["embedded"], kept["normed"] = place_embedding(place, looked, gain_vals[0])
        return moved

    def beside_compress(moved):
        moved, *kept["comp"] = together(moved, *compress(kept["old"], own_one, full_conv))
        return moved

    near_two, steps_two = gather_blocks(
        after(pack_two, steps_one[1]), 1, (beside_old, beside_compress), 1
    )
    near_up, near_down = split(near_two, 0, 2)
    far_up, far_down = swap(near_up, "dp", 1), swap(near_down, "dp", 1)
    mem_normed, old_normed = kept["mem"], kept["old"]
    embedded_low = kept["embedded"]
    embedded = embedded_low.astype(single)
    normed = jnp.concatenate(group_both(kept["normed"]))
    comp, old_raw = kept["comp"]

    words = vocab // reach
    z = d // 2
    unsigned_z = z.astype(jnp.uint32)
    z_groups = [[2 * i + b for i in range(reach)] for b in range(2)]
    slots = -(-words // 256) * 256


    comp_counts = jnp.where(x == 1, jnp.flip(comp_fill), comp_fill)
    mem_counts = jnp.where(x == 1, jnp.flip(mem_fill), mem_fill)
    info = [comp_counts[0], mem_counts[0], comp_counts[1], mem_counts[1], c * half]
    lane = jnp.arange(8, dtype=jnp.int32)
    info = sum(jnp.where(lane == i, value, 0) for i, value in enumerate(info)).astype(jnp.int32)

    in_weight = own_one[: 3 * wide]
    mem = mm(mem_normed, own_one[wide : 3 * wide], NT).astype(lowp)
    seg = mm(normed, in_weight, NT).astype(lowp).reshape(2, streams, half, 3 * wide)
    low_table = after(table.astype(lowp), seg).reshape(reach, words, width)
    low_table = lax.all_to_all(low_table, "dp", 0, 0, axis_index_groups=z_groups)
    mixed, lse = attend(info, seg, comp, mem)
    mixed = mixed.reshape(-1, wide)
    attn_sum, (far_up,) = core_sum(
        *split(mm(mixed, own_one[3 * wide : 4 * wide]), 0, 2), (far_up,)
    )
    attn_sum, (early, far_down) = stream_sum(attn_sum, (early_sums(mixed), far_down))
    after_attn = embedded + attn_sum
    ffn_in, inv_second = rms(after_attn, gain_vals[1])
    ffn_in, (low_table,) = group_both(ffn_in, (low_table,))
    near_table = [
        lax.dynamic_index_in_dim(low_table, unsigned_z ^ jnp.uint32(m // 2), 0, keepdims=False) for m in order[:reach]
    ]
    near_table = jnp.concatenate(near_table, axis=1)
    near_table = jnp.concatenate([near_table, jnp.zeros((slots - words, D // 2), lowp)], axis=0)
    ffn_in = jnp.concatenate(ffn_in)
    full_up = jnp.concatenate([near_up, far_up], axis=1)
    full_down = jnp.concatenate([near_down, far_down], axis=1)
    far_table = swap(near_table, "dp", 1)
    hidden_pre = mm(ffn_in, full_up, NT)
    hidden_act = jax.nn.gelu(hidden_pre).astype(lowp)
    after_ffn = after_attn + group_sum(mm(hidden_act, full_down))
    final_in, inv_third = rms(after_ffn, gain_vals[2])

    info_all = kept["info"]
    pieces = [final_in]
    chunks = []
    raised = []
    stats = []

    def next_chunk():
        i = len(chunks)
        if i == 0:
            chunk, kept["list"] = group_both(pieces[i], own_list(after(token_codes, final_in)))
            chunks.append(chunk)
        else:
            chunk, (stats[i - 1],) = group_both(pieces[i], (stats[i - 1],))
            chunks.append(chunk)
        *out, stat = logits_part(words, i, info_all, *chunks[i], near_table, far_table)
        raised.append(out)
        stats.append(stat)

    mask = dp_size // 2
    while mask > 1:
        moved = swap(reorder(pieces, mask), "dp", mask)
        if len(pieces) == 1:
            next_chunk()
        elif len(pieces) == 2:
            moved, stats[0] = together(moved, stats[0])
        pieces += split(moved, 0, len(pieces))
        mask //= 2
    while len(chunks) < reach:
        next_chunk()
    own_codes, own_count = kept["list"]
    stats = [stat[:3].reshape(3, 1, 2, 2, half) for stat in stats]
    own_stats = jnp.concatenate(stats, axis=1)

    def combine(first, second):
        top = jnp.maximum(first[0], second[0])
        total = first[1] * jnp.exp(first[0] - top) + second[1] * jnp.exp(second[0] - top)
        return jnp.stack([top, total, first[2] + second[2]])

    merged = own_stats
    merged = combine(merged, jnp.flip(swap(merged, "head", 1), 2))
    merged = combine(merged, jnp.flip(swap(merged, "head", 2), 3))
    mask = 2
    while mask < dp_size:
        other = split(swap(merged, "dp", mask), 1, reach)
        other = [other[order.index(j ^ mask)] for j in order[:reach]]
        merged = combine(merged, jnp.concatenate(other, axis=1))
        mask *= 2
    log_total = merged[0] + jnp.log(merged[1])
    loss_local = jnp.sum(mask_all[0, 0, 0] * (log_total[0, 0, 0] - merged[2, 0, 0, 0]))
    factor_all = jnp.exp(own_stats[0] - log_total)

    factor_all = factor_all.reshape(reach, 1, per_group) * info_all[:, 1:2]
    factor_all = jnp.broadcast_to(factor_all, info_all.shape)
    dlogits = [[] for _ in range(reach)]
    parts = [None] * reach
    for i in reversed(range(reach)):
        *dlogits[i], keep, send = logits_back(
            i, info_all, factor_all, raised[i], near_table, far_table
        )
        if i + 1 < reach:
            parts[i + 1], (*dlogits[i], keep, send) = stream_sum(
                parts[i + 1], (*dlogits[i], keep, send)
            )
        parts[i] = core_sum(keep, send)
    parts[0] = stream_sum(parts[0])
    table_parts = []
    mask = 2
    while len(parts) > 1:
        count = len(parts) // 2
        moved = swap(reorder(parts[count:], mask), "dp", mask)
        if mask == 2:
            moved, *dlogits[0] = together(moved, *dlogits[0])
        elif mask == 4:
            moved, *table_parts = together(moved, *table_grad_part(dlogits, chunks))
        moved = split(moved.astype(single), 0, count)
        parts = [part + more for part, more in zip(parts, moved)]
        mask *= 2
    final_grad = parts[0]

    grad_after_ffn = rms_back(after_ffn, inv_third, gain_vals[2], final_grad)
    moved_table = swap(table_parts[1], "dp", 1)
    down_in = group_both(grad_after_ffn.astype(lowp))
    down_in = jnp.concatenate(down_in)
    act_grad = mm(down_in, full_down, NT)
    pre_grad = jax.vjp(jax.nn.gelu, hidden_pre)[1](act_grad)[0].astype(lowp)
    two = hidden_grads(pre_grad, hidden_act, ffn_in, down_in)
    ffn_in_grad, (*two, moved_table) = group_sum(mm(pre_grad, full_up), (*two, moved_table))
    keep = table_parts[0] + moved_table.astype(single)
    table_pieces = jnp.stack(split(keep[:words].astype(lowp), 1, reach))
    turned = sum(
        ((unsigned_z >> bit) & 1) * jnp.uint32(order.index(2 << bit))
        for bit in range(reach.bit_length() - 1)
    )
    table_pieces = jnp.concatenate(
        [
            lax.dynamic_index_in_dim(table_pieces, turned ^ jnp.uint32(order.index(2 * i)), 0)
            for i in range(reach)
        ]
    )
    table_pieces = lax.all_to_all(table_pieces, "dp", 0, 0, axis_index_groups=z_groups)
    grad_after_attn = grad_after_ffn + rms_back(after_attn, inv_second, gain_vals[1], ffn_in_grad)
    attn_in = jnp.concatenate(group_both(grad_after_attn.astype(lowp)))

    mixed_grad = mm(attn_in, own_one[3 * wide : 4 * wide], NT).astype(lowp)
    mixed_grad = mixed_grad.reshape(2, streams, half, wide)
    seg_grad, comp_grad, mem_grad = attend_back(info, seg, comp, mem, lse, mixed_grad)
    seg_grad = seg_grad.reshape(-1, 3 * wide)

    def beside_expand(moved):
        keep, send = split(mm(seg_grad, in_weight), 0, 2)
        more = swap(send.astype(lowp), "head", 1)
        moved, more, kept["table"], *kept["old"] = together(
            moved, more, table_pieces, *expand(comp_grad, old_raw, full_conv)
        )
        kept["seg_in"] = split(keep + more.astype(single), 0, 2)
        return moved

    def beside_sums(moved):
        seg_in, seg_in_far = kept["seg_in"]
        seg_in_far = swap(seg_in_far.astype(lowp), "head", 2)
        old_grad, conv_sum = kept["old"]
        sums = attn_grads(
            seg_grad,
            mixed,
            mem_grad,
            old_grad.reshape(-1, old_grad.shape[-1]),
            normed,
            attn_in,
            mem_normed,
            old_normed.reshape(-1, D),
        )
        conv_sum = split(conv_block_order(conv_sum), 1, 2)
        sums = [jnp.concatenate([part, more.astype(part.dtype)]) for part, more in zip(sums, conv_sum)]
        seg_in_far, *kept["sums"] = together(seg_in_far, *sums)
        rows_grad = embed_back(
            place, embedded_low, gain_vals[0], seg_in, seg_in_far, grad_after_attn
        )
        moved, kept["rows"] = together(moved, lax.all_to_all(rows_grad, "dp", 0, 0))
        return moved

    def beside_rows(moved):
        moved, kept["rows"] = together(moved, kept["rows"])
        return moved

    def beside_streams(moved):
        moved, far = together(moved, swap(kept["rows"], "head", 2))
        kept["rows"] = jnp.stack([kept["rows"], far])
        return moved

    two = reduce_blocks(*two, (beside_expand, beside_sums))
    one = reduce_blocks(*kept["sums"], (beside_rows, beside_streams))
    rows_grad = kept["rows"]
    rows_grad = jnp.stack([rows_grad, swap(rows_grad, "head", 1)]).reshape(-1, width)
    table_base = kept["table"].astype(single).reshape(vocab, width)

    up_grad = two[:hidden_own].T
    down_grad = two[hidden_own:]
    qkv_grad = jnp.swapaxes(one[: 3 * wide].reshape(3, wide, width), 1, 2)
    out_grad = one[3 * wide : 4 * wide]
    conv_grad = one[4 * wide :].reshape(wconv.shape)
    table_grad = scatter(bits, own_count, own_codes, table_base, rows_grad)

    gains_low = gains.astype(lowp).astype(single)
    gain_part = jnp.stack(
        [
            jnp.sum(low_qkv.astype(single) * qkv_grad, axis=(0, 2)),
            jnp.sum(wup.astype(lowp).astype(single) * up_grad, axis=1),
            jnp.sum(table.astype(lowp).astype(single) * table_base, axis=0),
        ]
    )

    grads = (table_grad, qkv_grad, out_grad, conv_grad, up_grad, down_grad)
    def sum_over_dp(joined):
        mask = 1
        while mask < dp_size:
            joined = joined + swap(joined, "dp", mask)
            mask *= 2
        return joined

    row_part = []
    col_part = []
    for grad in grads:
        square = grad * grad
        row_part.append(jnp.sum(square, axis=-1))
        col_part.append(jnp.sum(square, axis=tuple(range(square.ndim - 1))))
    row_q, row_u, col_e, col_o, col_c, col_d, gain_raw, early = lax.psum(
        (
            row_part[1],
            row_part[4],
            col_part[0],
            col_part[2],
            col_part[3],
            col_part[5],
            gain_part,
            early + scalar_row([0.0] * 15 + [loss_local]),
        ),
        "head",
    )
    lanes = [col_e, jnp.sum(row_q, axis=0), col_o]
    lanes += [jnp.concatenate([col_c, jnp.zeros((width - col_c.shape[0],), single)]), row_u, col_d]
    members = [col_part[4], row_part[5], row_part[3], row_part[2], col_part[1], *lanes, row_part[0], early]
    joined = jnp.concatenate([m.reshape(-1) for m in members])
    joined = sum_over_dp(jnp.concatenate([joined, jnp.zeros((-joined.shape[0] % 1024,), single)]))
    sums = []
    start = 0
    for member in members:
        sums.append(joined[start : start + member.size].reshape(member.shape))
        start += member.size
    col_u, row_d, row_c, row_o, col_q, *lanes, row_e, early = sums
    square_total = [jnp.sum(lane) for lane in lanes]
    row_sums = [row_e, row_q, row_o, row_c, row_u, row_d]
    col_sums = [col_e, col_q, col_o, col_c, col_u, col_d]
    weight_total = early[6:15]
    loss_all = early[15]
    inverse = 1.0 / count_all
    decay = 1.0 - STEP ** (-0.8)
    updates = []
    stats_new = []
    scaled = []
    counts = []
    update_sq = []
    for index in range(6):
        rows_total = rows_old[index].size * sizes[row_axes[index]]
        cols_total = cols_old[index].size * sizes[col_axes[index]]
        grad_scaled = grads[index] * inverse
        rows_new = decay * rows_old[index] + (1.0 - decay) * (
            row_sums[index] * inverse * inverse / cols_total + TINY_SQUARE
        )
        cols_new = decay * cols_old[index] + (1.0 - decay) * (
            col_sums[index] * inverse * inverse / rows_total + TINY_SQUARE
        )
        mean_row = decay * early[index] / rows_total + (1.0 - decay) * (
            square_total[index] * inverse * inverse / (rows_total * cols_total) + TINY_SQUARE
        )
        second = rows_new[..., None] * cols_new / mean_row
        direction = grad_scaled * lax.rsqrt(second)
        updates.append(direction)
        stats_new.append((rows_new, cols_new))
        scaled.append(grad_scaled)
        counts.append(rows_total * cols_total)
        update_sq.append(jnp.sum(direction * direction))
    gain_scaled = gain_raw / gains_low * inverse
    second_new = decay * gains_second + (1.0 - decay) * (gain_scaled * gain_scaled + TINY_SQUARE)
    gain_dir = gain_scaled * lax.rsqrt(second_new)
    for which in range(3):
        update_sq.append(jnp.sum(gain_dir[which] * gain_dir[which]) / head_size)
    update_total = after(scalar_row(update_sq, 1024), loss_all)
    for mask in (1, 2):
        update_total = update_total + swap(update_total, "head", mask)
    update_total = sum_over_dp(update_total)[:9]
    results = [loss_all, count_all]
    for index in range(6):
        factor = jnp.maximum(0.001, jnp.sqrt(weight_total[index] / counts[index]))
        denom = jnp.maximum(1.0, jnp.sqrt(update_total[index] / counts[index]) / CLIP_LEVEL)
        new_weight = weights_now[index] - LEARN_RATE * factor * updates[index] / denom
        results += [new_weight, scaled[index], stats_new[index][0], stats_new[index][1]]
    gain_factor = jnp.maximum(0.001, jnp.sqrt(weight_total[6:] / D))[:, None]
    gain_denom = jnp.maximum(1.0, jnp.sqrt(update_total[6:] / D) / CLIP_LEVEL)[:, None]
    results += [gains - LEARN_RATE * gain_factor * gain_dir / gain_denom, gain_scaled, second_new]
    return tuple(results)


def solution(mesh):
    in_specs = (
        P("dp", None),
        P("dp", None),
        P("dp", None),
        P("dp", None, None),
        P("dp", None, None),
        P("dp"),
        P("dp"),
        P("head", "dp"),
        P(None, "dp", "head"),
        P("head", "dp"),
        P("head", None, "dp"),
        P("dp", "head"),
        P("head", "dp"),
        P(None, "dp"),
        P("head"),
        P("dp"),
        P(None, "dp"),
        P("head"),
        P("head"),
        P("dp"),
        P("head", None),
        P("dp"),
        P("dp"),
        P("head"),
        P("head"),
        P("dp"),
        P(None, "dp"),
    )
    out_specs = (
        P(),
        P(),
        P("head", "dp"),
        P("head", "dp"),
        P("head"),
        P("dp"),
        P(None, "dp", "head"),
        P(None, "dp", "head"),
        P(None, "dp"),
        P("head"),
        P("head", "dp"),
        P("head", "dp"),
        P("head"),
        P("dp"),
        P("head", None, "dp"),
        P("head", None, "dp"),
        P("head", None),
        P("dp"),
        P("dp", "head"),
        P("dp", "head"),
        P("dp"),
        P("head"),
        P("head", "dp"),
        P("head", "dp"),
        P("head"),
        P("dp"),
        P(None, "dp"),
        P(None, "dp"),
        P(None, "dp"),
    )
    return jax.shard_map(local, mesh=mesh, in_specs=in_specs, out_specs=out_specs, check_vma=False)
```

```python
import functools

import jax
import jax.numpy as jnp
from jax import lax
from jax.experimental import pallas as pl
from jax.experimental.pallas import tpu as pltpu
from jax.sharding import PartitionSpec as P

D = 1024
H = 8
DH = 128
MEM = 512
CMEM = 512
RATE = 3
STEP = 10


TINY_NORM = 1e-06
TINY_SQUARE = 1e-30
LEARN_RATE = 0.5
CLIP_LEVEL = 1.0

lowp = jnp.bfloat16
single = jnp.float32
NT = (((1,), (1,)), ((), ()))
TN = (((0,), (0,)), ((), ()))
NN = (((1,), (0,)), ((), ()))
MIB = 1024 * 1024


def mm(left, right, dims=NN):
    return lax.dot_general(left, right, dims, preferred_element_type=single)


def swap(value, axis, mask):
    size = lax.axis_size(axis)
    return lax.ppermute(value, axis, [(i, i ^ mask) for i in range(size)])


def after(value, *deps):
    return lax.optimization_barrier((value, *deps))[0]


def together(*values):
    return lax.optimization_barrier(values)


def block_order(size):
    order = [0]
    step = size // 2
    while step:
        order = order + [j + step for j in order]
        step //= 2
    return order


def gather_blocks(piece, axis, beside=(), stop=0):
    steps = []
    mask = lax.axis_size("dp") // 2
    while mask > stop:
        moved = swap(piece, "dp", mask)
        if len(steps) < len(beside):
            moved = beside[len(steps)](moved)
        piece = jnp.concatenate([piece, moved], axis=axis)
        steps.append(piece)
        mask //= 2
    return piece, steps


def split(value, axis, parts):
    width = value.shape[axis] // parts
    return [lax.slice_in_dim(value, i * width, (i + 1) * width, axis=axis) for i in range(parts)]


def reduce_blocks(keep, send, beside=(), mask=1):
    moved = swap(send.astype(lowp), "dp", mask)
    if beside:
        moved = beside[0](moved)
    total = keep + moved.astype(single)
    mask *= 2
    if mask == lax.axis_size("dp"):
        return total
    return reduce_blocks(*split(total, 1, 2), beside[1:], mask)


def reorder_kernel(sources, *refs):
    out_ref = refs[-1]
    width = out_ref.shape[1] // len(sources)
    start = 0
    for in_ref in refs[:-1]:
        rows = slice(start, start + in_ref.shape[0])
        start += in_ref.shape[0]
        for p, q in enumerate(sources):
            block = in_ref[:, q * width : (q + 1) * width]
            out_ref[rows, p * width : (p + 1) * width] = block.astype(out_ref.dtype)


def reorder(values, mask):
    order = block_order(lax.axis_size("dp"))
    sources = [order.index(j ^ mask) for j in order]
    rows = sum(value.shape[0] for value in values)
    if D // len(order) % 128:
        joined = jnp.concatenate([value.astype(lowp) for value in values])
        cols = split(joined, 1, len(order))
        return jnp.concatenate([cols[q] for q in sources], axis=1)
    return pl.pallas_call(
        functools.partial(reorder_kernel, sources),
        name="reorder",
        out_shape=jax.ShapeDtypeStruct((rows, D), lowp),
        in_specs=[vmem()] * len(values),
        out_specs=vmem(),
        compiler_params=params(60),
        cost_estimate=cost(0, 2 * MIB),
    )(*values)


def relative(value, x, c):
    value = jnp.where(x == 1, jnp.flip(value, -3), value)
    value = jnp.where(c == 1, jnp.flip(value, -2), value)
    return jnp.swapaxes(value, -3, -2)


def rms(values, gain):
    inv = lax.rsqrt(jnp.mean(values * values, axis=-1, keepdims=True) + TINY_NORM)
    return (values * inv * gain).astype(lowp), inv


def rms_back(values, inv, gain, upstream):
    scaled = gain * upstream
    inner = jnp.sum(scaled * values, axis=-1, keepdims=True) / D
    return scaled * inv - values * (inner * inv * inv * inv)


def vmem(shape=None, index=None):
    if shape is None:
        return pl.BlockSpec(memory_space=pltpu.VMEM)
    return pl.BlockSpec(shape, index)


def smem():
    return pl.BlockSpec(memory_space=pltpu.SMEM)


def params(mib):
    return pltpu.CompilerParams(vmem_limit_bytes=mib * MIB)


def cost(flops, size, exps=0):
    return pl.CostEstimate(
        flops=int(0.02 * flops), bytes_accessed=int(0.02 * size), transcendentals=exps
    )


def lookup_kernel(row_ref, table_ref, out_ref, tab, held, sem):
    total = row_ref.shape[0]
    vocab = table_ref.shape[0]
    copy = pltpu.make_async_copy(table_ref, tab.at[pl.ds(0, vocab)], sem)
    copy.start()
    tab[pl.ds(vocab, 8), :] = jnp.zeros((8, tab.shape[1]), single)
    copy.wait()

    @pl.loop(0, total // 16)
    def _(g):
        for j in range(16):
            t = g * 16 + j
            held[pl.ds(t, 1), :] = tab[pl.ds(row_ref[t], 1), :]

    @pl.loop(0, total // 512)
    def _(i):
        rows = pl.ds(pl.multiple_of(i * 512, 512), 512)
        out_ref[rows, :] = held[rows, :].astype(lowp)


def lookup(rows, table):
    total = rows.shape[0]
    vocab, width = table.shape
    return pl.pallas_call(
        lookup_kernel,
        name="lookup",
        out_shape=jax.ShapeDtypeStruct((total, width), lowp),
        in_specs=[smem(), pl.BlockSpec(memory_space=pl.ANY)],
        out_specs=vmem(),
        scratch_shapes=[
            pltpu.VMEM((vocab + 8, width), single),
            pltpu.VMEM((total, width), single),
            pltpu.SemaphoreType.DMA(()),
        ],
        compiler_params=params(60),
        cost_estimate=cost(0, 30 * MIB),
    )(rows, table)


def list_kernel(code_ref, out_ref, count_ref):
    total = code_ref.shape[0]

    def group(g, count):
        for j in range(16):
            code = code_ref[g * 16 + j]
            out_ref[count] = code
            count = count + jnp.where(code >= 0, 1, 0)
        return count

    count_ref[0] = lax.fori_loop(0, total // 16, group, jnp.int32(0))


def own_list(codes):
    total = codes.shape[0]
    return pl.pallas_call(
        list_kernel,
        name="own_list",
        out_shape=(
            jax.ShapeDtypeStruct((total + 8,), jnp.int32),
            jax.ShapeDtypeStruct((1,), jnp.int32),
        ),
        in_specs=[smem()],
        out_specs=(smem(), smem()),
        cost_estimate=cost(0, 60 * MIB),
    )(codes)


def place_kernel(order, place_ref, in_ref, gain_ref, out_ref, norm_ref, held):
    width = in_ref.shape[2]
    for p, j in enumerate(order):
        block = in_ref[pl.ds(place_ref[1] ^ j, 1)][0]
        out_ref[:, p * width : (p + 1) * width] = block
        held[:, p * width : (p + 1) * width] = block.astype(single)
    values = held[...]
    inv = lax.rsqrt(jnp.mean(values * values, axis=-1, keepdims=True) + TINY_NORM)
    norm_ref[...] = (values * inv * gain_ref[...]).astype(lowp)


def place_embedding(place, blocks, gain):
    rows = blocks.shape[1]
    return pl.pallas_call(
        functools.partial(place_kernel, block_order(blocks.shape[0])),
        name="place_embedding",
        out_shape=(jax.ShapeDtypeStruct((rows, D), lowp), jax.ShapeDtypeStruct((rows, D), lowp)),
        in_specs=[smem(), vmem(), vmem()],
        out_specs=(vmem(), vmem()),
        scratch_shapes=[pltpu.VMEM((rows, D), single)],
        compiler_params=params(60),
        cost_estimate=cost(0, 3 * MIB),
    )(place, blocks, gain)


def embed_back_kernel(order, place_ref, in_ref, gain_ref, keep_ref, more_ref, grad_ref, out_ref, held):
    values = in_ref[...].astype(single)
    inv = lax.rsqrt(jnp.mean(values * values, axis=-1, keepdims=True) + TINY_NORM)
    upstream = keep_ref[...] + more_ref[...].astype(single)
    held[...] = grad_ref[...] + rms_back(values, inv, gain_ref[...], upstream)
    width = out_ref.shape[2]
    for p, j in enumerate(order):
        block = held[:, p * width : (p + 1) * width].astype(lowp)
        out_ref[pl.ds(place_ref[1] ^ j, 1)] = block[None]


def embed_back(place, values, gain, keep, more, grad):
    rows = values.shape[0]
    size = lax.axis_size("dp")
    return pl.pallas_call(
        functools.partial(embed_back_kernel, block_order(size)),
        name="embed_back",
        out_shape=jax.ShapeDtypeStruct((size, rows, D // size), lowp),
        in_specs=[smem()] + [vmem()] * 5,
        out_specs=vmem(),
        scratch_shapes=[pltpu.VMEM((rows, D), single)],
        compiler_params=params(60),
        cost_estimate=cost(0, 4 * MIB),
    )(place, values, gain, keep, more, grad)


def scatter_kernel(bits, count_ref, code_ref, base_ref, grad_ref, out_ref, rows):
    total = grad_ref.shape[0]
    vocab = base_ref.shape[0]

    @pl.loop(0, total // 512)
    def _(i):
        here = pl.ds(pl.multiple_of(i * 512, 512), 512)
        rows[here, :] = grad_ref[here, :].astype(single)

    rows[pl.ds(total, 8), :] = jnp.zeros((8, rows.shape[1]), single)

    @pl.loop(0, vocab // 400)
    def _(i):
        here = pl.ds(pl.multiple_of(i * 400, 400), 400)
        out_ref[here, :] = base_ref[here, :]

    count = count_ref[0]

    def group(g, carry):
        for j in range(8):
            index = g * 8 + j
            code = jnp.where(index < count, code_ref[index], total << bits)
            token = lax.shift_right_logical(code, bits)
            row = code & ((1 << bits) - 1)
            out_ref[pl.ds(row, 1), :] = out_ref[pl.ds(row, 1), :] + rows[pl.ds(token, 1), :]
        return carry

    lax.fori_loop(0, (count + 7) // 8, group, jnp.int32(0))


def scatter(bits, count, codes, base, grad):
    total, width = grad.shape
    return pl.pallas_call(
        functools.partial(scatter_kernel, bits),
        name="scatter",
        out_shape=jax.ShapeDtypeStruct(base.shape, single),
        in_specs=[smem(), smem(), vmem(), vmem()],
        out_specs=vmem(),
        scratch_shapes=[pltpu.VMEM((total + 8, width), single)],
        compiler_params=params(60),
        cost_estimate=cost(0, 30 * MIB),
    )(count, codes, base, grad)


def state_kernel(order, width, place_ref, gain_ref, in_ref, out_ref, held):
    rows = in_ref.shape[1]
    values = in_ref[0].astype(single)
    inv = lax.rsqrt(jnp.mean(values * values, axis=-1, keepdims=True) + TINY_NORM)
    for p, j in enumerate(order):
        start = pl.multiple_of((place_ref[1] ^ j) * width, width)
        block = in_ref[0, :, pl.ds(start, width)].astype(single)
        held[p] = block * inv * gain_ref[:, p * width : (p + 1) * width]
    groups = out_ref.shape[0]
    for p in range(len(order)):
        cols = slice(p * width, (p + 1) * width)
        if groups == 1:
            out_ref[0, :, cols] = held[p].astype(lowp)
        else:
            for j in range(groups):
                part = held[p, pl.ds(j, rows // groups, stride=groups), :]
                out_ref[j, :, cols] = part.astype(lowp)


def state_norm(place, gain, states, groups):
    size = lax.axis_size("dp")
    order = block_order(size)
    width = D // size
    streams = states.shape[0]
    count = states.shape[1] // groups
    if width % 128:
        values = jnp.where(place[0] == 1, jnp.flip(states, 0), states).astype(single).reshape(-1, D)
        inv = lax.rsqrt(jnp.mean(values * values, axis=-1, keepdims=True) + TINY_NORM)
        lanes = jnp.arange(D, dtype=jnp.int32)
        blocks = jnp.asarray(order, jnp.int32)[lanes // width] ^ place[1]
        source = blocks * width + lanes % width
        shuffle = (lanes[:, None] == source[None, :]).astype(single)
        moved = jnp.dot(values * inv, shuffle, precision=lax.Precision.HIGHEST)
        out = (moved * gain).astype(lowp)
        return jnp.swapaxes(out.reshape(streams * count, groups, D), 0, 1)
    tile = 128
    return pl.pallas_call(
        functools.partial(state_kernel, order, width),
        name="state_norm",
        out_shape=jax.ShapeDtypeStruct((groups, streams * count, D), lowp),
        grid_spec=pltpu.PrefetchScalarGridSpec(
            num_scalar_prefetch=1,
            grid=(streams, count // tile),
            in_specs=[
                pl.BlockSpec((1, D), lambda n, i, s: (0, 0)),
                pl.BlockSpec((1, tile * groups, D), lambda n, i, s: (s[0] ^ n, i, 0)),
            ],
            out_specs=pl.BlockSpec(
                (groups, tile, D), lambda n, i, s: (0, n * (count // tile) + i, 0)
            ),
            scratch_shapes=[pltpu.VMEM((len(order), tile * groups, width), single)],
        ),
        compiler_params=params(60),
        cost_estimate=cost(0, 4 * streams * count * groups * D),
    )(place, gain, states)


def compress_kernel(old_ref, key_ref, value_ref, conv_ref, comp_ref, raw_ref):
    heads = conv_ref.shape[0]
    wide = heads * DH
    for part, weight_ref in enumerate((key_ref, value_ref)):
        sums = [None] * heads
        for j in range(RATE):
            raw = mm(old_ref[j], weight_ref[...], NT).astype(lowp)
            raw_ref[j, :, part * wide : (part + 1) * wide] = raw
            for n in range(heads):
                piece = raw[:, n * DH : (n + 1) * DH]
                term = mm(piece, conv_ref[n, j * DH : (j + 1) * DH, :])
                sums[n] = term if j == 0 else sums[n] + term
        for n in range(heads):
            first = part * wide + n * DH
            comp_ref[:, first : first + DH] = sums[n].astype(lowp)


def compress(old3, weights, conv):
    rows = old3.shape[1]
    wide = conv.shape[0] * DH
    tile = 256
    return pl.pallas_call(
        compress_kernel,
        name="compress",
        grid=(rows // tile,),
        out_shape=(
            jax.ShapeDtypeStruct((rows, 2 * wide), lowp),
            jax.ShapeDtypeStruct((RATE, rows, 2 * wide), lowp),
        ),
        in_specs=[
            pl.BlockSpec((RATE, tile, D), lambda i: (0, i, 0)),
            pl.BlockSpec((wide, D), lambda i: (1, 0)),
            pl.BlockSpec((wide, D), lambda i: (2, 0)),
            pl.BlockSpec(conv.shape, lambda i: (0, 0, 0)),
        ],
        out_specs=(
            pl.BlockSpec((tile, 2 * wide), lambda i: (i, 0)),
            pl.BlockSpec((RATE, tile, 2 * wide), lambda i: (0, i, 0)),
        ),
        compiler_params=params(60),
        cost_estimate=cost(4 * RATE * rows * wide * D, 12 * MIB),
    )(old3, weights, weights, conv)


def expand_kernel(grad_ref, raw_ref, conv_ref, out_ref, conv_out_ref):
    heads = conv_ref.shape[0]
    for h in range(heads):
        for j in range(RATE):
            rows = slice(j * DH, (j + 1) * DH)
            taps = conv_ref[h, rows, :]
            total = None
            for n in (h, heads + h):
                cols = slice(n * DH, (n + 1) * DH)
                grad = grad_ref[:, cols]
                out_ref[j, :, cols] = mm(grad, taps, NT).astype(lowp)
                term = mm(raw_ref[j, :, cols], grad, TN)
                total = term if total is None else total + term
            conv_out_ref[h, rows, :] = total


def expand(grad, raw, conv):
    return pl.pallas_call(
        expand_kernel,
        name="expand",
        out_shape=(
            jax.ShapeDtypeStruct(raw.shape, lowp),
            jax.ShapeDtypeStruct(conv.shape, single),
        ),
        in_specs=[vmem()] * 3,
        out_specs=(vmem(), vmem()),
        compiler_params=params(60),
        cost_estimate=cost(2000 * MIB, 12 * MIB),
    )(grad, raw, conv)


def masked_scores(info_ref, query, keys):
    rows = query.shape[0]
    scale = DH ** (-0.5)
    result = []
    for which, key in enumerate(keys):
        slots = key.shape[0]
        col = lax.broadcasted_iota(jnp.int32, (rows, slots), 1)
        if which < 2:
            seen = col >= slots - info_ref[2 * pl.program_id(0) + which]
        else:
            row = lax.broadcasted_iota(jnp.int32, (rows, slots), 0)
            shift = info_ref[4]
            row = row + shift
            col = col + shift
            row = jnp.where(row >= slots, row - slots, row)
            col = jnp.where(col >= slots, col - slots, col)
            seen = col <= row
        result.append(jnp.where(seen, mm(query, key, NT) * scale, -1e30))
    return result


def rows_of(ref):
    return ref[...].reshape(-1, ref.shape[-1])


def attend_kernel(info_ref, q_ref, ks_ref, vs_ref, kc_ref, vc_ref, km_ref, vm_ref, out_ref, lse_ref):
    query = rows_of(q_ref)
    scores = masked_scores(info_ref, query, [kc_ref[...], km_ref[...], rows_of(ks_ref)])
    top = functools.reduce(jnp.maximum, [jnp.max(s, axis=-1, keepdims=True) for s in scores])
    total = 0.0
    mixed = 0.0
    for score, value in zip(scores, (vc_ref[...], vm_ref[...], rows_of(vs_ref))):
        weight = jnp.exp(score - top)
        total = total + jnp.sum(weight, axis=-1, keepdims=True)
        mixed = mixed + mm(weight.astype(lowp), value)
    out_ref[...] = (mixed / total).astype(lowp).reshape(out_ref.shape)
    lse_ref[0, 0] = top + jnp.log(total)


def attend_back_kernel(
    info_ref, q_ref, ks_ref, vs_ref, kc_ref, vc_ref, km_ref, vm_ref, lse_ref, up_ref,
    seg_ref, comp_ref, mem_ref,
):
    head = pl.program_id(1)
    wide = pl.num_programs(1) * DH
    scale = DH ** (-0.5)
    query = rows_of(q_ref)
    upstream = rows_of(up_ref)
    keys = [kc_ref[...], km_ref[...], rows_of(ks_ref)]
    scores = masked_scores(info_ref, query, keys)
    probs = [jnp.exp(s - lse_ref[0, 0]) for s in scores]
    prob_grads = [
        mm(upstream, v, NT) for v in (vc_ref[...], vm_ref[...], rows_of(vs_ref))
    ]
    inner = 0.0
    for p, g in zip(probs, prob_grads):
        inner = inner + jnp.sum(p * g, axis=-1, keepdims=True)
    here = pl.ds(pl.multiple_of(head * DH, DH), DH)
    second = pl.ds(pl.multiple_of(wide + head * DH, DH), DH)
    third = pl.ds(pl.multiple_of(2 * wide + head * DH, DH), DH)
    query_grad = 0.0
    places = ((comp_ref, here, second), (mem_ref, here, second), (seg_ref, second, third))
    for p, g, key, (ref, key_at, value_at) in zip(probs, prob_grads, keys, places):
        score_grad = (p * (g - inner)).astype(lowp)
        query_grad = query_grad + mm(score_grad, key)
        shape = ref.shape[:-1] + (DH,)
        key_grad = (mm(score_grad, query, TN) * scale).astype(lowp)
        value_grad = mm(p.astype(lowp), upstream, TN).astype(lowp)
        ref[..., key_at] = key_grad.reshape(shape)
        ref[..., value_at] = value_grad.reshape(shape)
    shape = seg_ref.shape[:-1] + (DH,)
    seg_ref[..., here] = (query_grad * scale).astype(lowp).reshape(shape)


def head_specs(seg, comp, mem, heads):
    streams = seg.shape[1]

    def of_seg(first):
        return pl.BlockSpec((2, 1, seg.shape[2], DH), lambda n, h: (0, n, 0, first + h))

    def cols(array, first):
        return pl.BlockSpec((array.shape[0] // streams, DH), lambda n, h: (n, first + h))

    return [
        smem(),
        of_seg(0),
        of_seg(heads),
        of_seg(2 * heads),
        cols(comp, 0),
        cols(comp, heads),
        cols(mem, 0),
        cols(mem, heads),
    ]


def attend(info, seg, comp, mem):
    _, streams, half, _ = seg.shape
    heads = comp.shape[1] // (2 * DH)
    return pl.pallas_call(
        attend_kernel,
        name="attend",
        grid=(streams, heads),
        out_shape=(
            jax.ShapeDtypeStruct((2, streams, half, heads * DH), lowp),
            jax.ShapeDtypeStruct((streams, heads, 2 * half, 1), single),
        ),
        in_specs=head_specs(seg, comp, mem, heads),
        out_specs=(
            pl.BlockSpec((2, 1, half, DH), lambda n, h: (0, n, 0, h)),
            pl.BlockSpec((1, 1, 2 * half, 1), lambda n, h: (n, h, 0, 0)),
        ),
        compiler_params=params(60),
        cost_estimate=cost(7000 * MIB, 6 * MIB),
    )(info, seg, seg, seg, comp, comp, mem, mem)


def attend_back(info, seg, comp, mem, lse, upstream):
    _, streams, half, wide = seg.shape
    heads = comp.shape[1] // (2 * DH)
    slots = comp.shape[0] // streams
    kept = mem.shape[0] // streams
    return pl.pallas_call(
        attend_back_kernel,
        name="attend_back",
        grid=(streams, heads),
        out_shape=(
            jax.ShapeDtypeStruct(seg.shape, lowp),
            jax.ShapeDtypeStruct(comp.shape, lowp),
            jax.ShapeDtypeStruct(mem.shape, lowp),
        ),
        in_specs=head_specs(seg, comp, mem, heads)
        + [
            pl.BlockSpec((1, 1, 2 * half, 1), lambda n, h: (n, h, 0, 0)),
            pl.BlockSpec((2, 1, half, DH), lambda n, h: (0, n, 0, h)),
        ],
        out_specs=(
            pl.BlockSpec((2, 1, half, wide), lambda n, h: (0, n, 0, 0)),
            pl.BlockSpec((slots, comp.shape[1]), lambda n, h: (n, 0)),
            pl.BlockSpec((kept, mem.shape[1]), lambda n, h: (n, 0)),
        ),
        compiler_params=params(60),
        cost_estimate=cost(11000 * MIB, 9 * MIB),
    )(info, seg, seg, seg, comp, comp, mem, mem, lse, upstream)


def columns_of(rows):
    tall = jnp.concatenate([rows, jnp.zeros((120, rows.shape[1]), single)], axis=0)
    return jnp.transpose(tall)


def logits_kernel(
    words, pair_info_ref, near_info_ref, pair_ref, near_ref, left_ref, right_ref,
    pair_out_ref, near_out_ref, stat_ref,
):
    step = pl.program_id(0)
    tile = pair_ref.shape[0]
    half = left_ref.shape[1]
    edge = left_ref.shape[0] - 128
    streams = (
        (pair_info_ref, pair_ref, pair_out_ref),
        (near_info_ref, near_ref, near_out_ref),
    )
    products = [
        mm(ref[:, :half], left_ref[...], NT) + mm(ref[:, half:], right_ref[...], NT)
        for _, ref, _ in streams
    ]
    for n, ((info_ref, _, out_ref), logits) in enumerate(zip(streams, products)):
        wanted = columns_of(info_ref[0])[:, 0:1].astype(jnp.int32)
        col = lax.broadcasted_iota(jnp.int32, logits.shape, 1)
        hit = jnp.sum(jnp.where(col == wanted, logits, 0.0), axis=-1, keepdims=True)
        last = jnp.where(col[:, edge:] < words, logits[:, edge:], -1e30)
        top = jnp.max(last, axis=-1, keepdims=True)
        top = jnp.maximum(top, jnp.max(logits[:, :edge], axis=-1, keepdims=True))
        raised = jnp.exp(logits[:, :edge] - top)
        last = jnp.exp(last - top)
        total = jnp.sum(raised, axis=-1, keepdims=True) + jnp.sum(last, axis=-1, keepdims=True)
        out_ref[:, :edge] = raised.astype(lowp)
        out_ref[:, edge:] = last.astype(lowp)
        lane = lax.broadcasted_iota(jnp.int32, (tile, 128), 1)
        packed = jnp.where(lane == 2, hit, 0.0)
        packed = jnp.where(lane == 0, top, jnp.where(lane == 1, total, packed))
        start = n * (stat_ref.shape[1] // 2) + step * tile
        stat_ref[:, pl.ds(pl.multiple_of(start, tile), tile)] = jnp.transpose(packed)[:8]


def logits_part(words, chunk, info, pair, near, left, right):
    rows, _ = pair.shape
    slots = left.shape[0]
    tile = 256
    tiles = rows // tile
    whole = lambda i: (0, 0)
    return pl.pallas_call(
        functools.partial(logits_kernel, words),
        name="logits_part",
        grid=(tiles,),
        out_shape=(
            jax.ShapeDtypeStruct((rows, slots), lowp),
            jax.ShapeDtypeStruct((rows, slots), lowp),
            jax.ShapeDtypeStruct((8, 2 * rows), single),
        ),
        in_specs=[
            pl.BlockSpec((1, 8, tile), lambda i: (chunk, 0, i)),
            pl.BlockSpec((1, 8, tile), lambda i: (chunk, 0, tiles + i)),
            pl.BlockSpec((tile, D), lambda i: (i, 0)),
            pl.BlockSpec((tile, D), lambda i: (i, 0)),
            pl.BlockSpec(left.shape, whole),
            pl.BlockSpec(right.shape, whole),
        ],
        out_specs=(
            pl.BlockSpec((tile, slots), lambda i: (i, 0)),
            pl.BlockSpec((tile, slots), lambda i: (i, 0)),
            pl.BlockSpec((8, 2 * rows), whole),
        ),
        compiler_params=params(60),
        cost_estimate=cost(8 * rows * slots * D, 10 * MIB),
    )(info, info, pair, near, left, right)


def logits_back_kernel(
    pair_info_ref, near_info_ref, pair_factor_ref, near_factor_ref, pair_ref, near_ref,
    left_ref, right_ref, pair_out_ref, near_out_ref, pair_grad_ref, near_grad_ref,
):
    half = left_ref.shape[1]
    streams = (
        (near_info_ref, near_factor_ref, near_ref, near_out_ref, near_grad_ref),
        (pair_info_ref, pair_factor_ref, pair_ref, pair_out_ref, pair_grad_ref),
    )
    for info_ref, factor_ref, in_ref, out_ref, grad_ref in streams:
        info = columns_of(info_ref[0])
        wanted = info[:, 0:1].astype(jnp.int32)
        counted = info[:, 1:2]
        factor = columns_of(factor_ref[0])[:, 0:1]
        raised = in_ref[...].astype(single)
        col = lax.broadcasted_iota(jnp.int32, raised.shape, 1)
        grads = (raised * factor - jnp.where(col == wanted, counted, 0.0)).astype(lowp)
        out_ref[...] = grads
        grad_ref[:, :half] = mm(grads, left_ref[...]).astype(lowp)
        grad_ref[:, half:] = mm(grads, right_ref[...]).astype(lowp)


def logits_back(chunk, info, factor, raised, left, right):
    rows, slots = raised[0].shape
    tile = 256
    tiles = rows // tile
    whole = lambda i: (0, 0)

    def info_specs():
        return [
            pl.BlockSpec((1, 8, tile), lambda i: (chunk, 0, i)),
            pl.BlockSpec((1, 8, tile), lambda i: (chunk, 0, tiles + i)),
        ]

    return pl.pallas_call(
        logits_back_kernel,
        name="logits_back",
        grid=(tiles,),
        out_shape=(
            jax.ShapeDtypeStruct((rows, slots), lowp),
            jax.ShapeDtypeStruct((rows, slots), lowp),
            jax.ShapeDtypeStruct((rows, D), lowp),
            jax.ShapeDtypeStruct((rows, D), lowp),
        ),
        in_specs=info_specs()
        + info_specs()
        + [pl.BlockSpec((tile, slots), lambda i: (i, 0))] * 2
        + [pl.BlockSpec(left.shape, whole), pl.BlockSpec(right.shape, whole)],
        out_specs=(
            pl.BlockSpec((tile, slots), lambda i: (i, 0)),
            pl.BlockSpec((tile, slots), lambda i: (i, 0)),
            pl.BlockSpec((tile, D), lambda i: (i, 0)),
            pl.BlockSpec((tile, D), lambda i: (i, 0)),
        ),
        compiler_params=params(60),
        cost_estimate=cost(8 * rows * slots * D, 12 * MIB),
    )(info, info, factor, factor, *raised, left, right)


def halves(total, keep_ref, send_ref):
    half = keep_ref.shape[1]
    keep_ref[...] = total[:, :half]
    send_ref[...] = total[:, half:].astype(send_ref.dtype)


def table_grad_kernel(count, *refs):
    total = mm(refs[0][...], refs[count][...], TN)
    for i in range(1, count):
        total = total + mm(refs[i][...], refs[count + i][...], TN)
    halves(total, *refs[2 * count :])


def table_grad_part(grads, inputs):
    grads = [half for pair in grads for half in pair]
    inputs = [half for pair in inputs for half in pair]
    rows = sum(g.shape[0] for g in grads)
    slots = grads[0].shape[1]
    block = 256
    if rows > 4096:
        keep, send = split(sum(mm(g, v, TN) for g, v in zip(grads, inputs)), 1, 2)
        return keep, send.astype(lowp)
    return pl.pallas_call(
        functools.partial(table_grad_kernel, len(grads)),
        name="table_grad_part",
        grid=(slots // block,),
        out_shape=(
            jax.ShapeDtypeStruct((slots, D // 2), single),
            jax.ShapeDtypeStruct((slots, D // 2), lowp),
        ),
        in_specs=[pl.BlockSpec((g.shape[0], block), lambda i: (0, i)) for g in grads]
        + [pl.BlockSpec(v.shape, lambda i: (0, 0)) for v in inputs],
        out_specs=(
            pl.BlockSpec((block, D // 2), lambda i: (i, 0)),
            pl.BlockSpec((block, D // 2), lambda i: (i, 0)),
        ),
        compiler_params=params(60),
        cost_estimate=cost(3 * rows * slots * D, 30 * MIB),
    )(*grads, *inputs)


def hidden_grad_kernel(blocks, pre_ref, act_ref, in_ref, down_ref, keep_ref, send_ref):
    step = pl.program_id(0)

    @pl.when(step < blocks)
    def _():
        halves(mm(pre_ref[...], in_ref[...], TN), keep_ref, send_ref)

    @pl.when(step >= blocks)
    def _():
        halves(mm(act_ref[...], down_ref[...], TN), keep_ref, send_ref)


def hidden_grads(pre_grad, hidden_act, ffn_in, down_in):
    rows, hidden = pre_grad.shape
    block = 256
    blocks = hidden // block
    return pl.pallas_call(
        functools.partial(hidden_grad_kernel, blocks),
        name="hidden_grads",
        grid=(2 * blocks,),
        out_shape=(
            jax.ShapeDtypeStruct((2 * hidden, D // 2), single),
            jax.ShapeDtypeStruct((2 * hidden, D // 2), lowp),
        ),
        in_specs=[
            pl.BlockSpec((rows, block), lambda i: (0, jnp.minimum(i, blocks - 1))),
            pl.BlockSpec((rows, block), lambda i: (0, jnp.maximum(i - blocks, 0))),
            pl.BlockSpec((rows, D), lambda i: (0, 0)),
            pl.BlockSpec((rows, D), lambda i: (0, 0)),
        ],
        out_specs=(
            pl.BlockSpec((block, D // 2), lambda i: (i, 0)),
            pl.BlockSpec((block, D // 2), lambda i: (i, 0)),
        ),
        compiler_params=params(60),
        cost_estimate=cost(6 * rows * hidden * D, 16 * MIB),
    )(pre_grad, hidden_act, ffn_in, down_in)


def attn_grad_kernel(
    seg_ref, mixed_ref, mem_ref, old_ref, normed_ref, up_ref, mem_in_ref, old_in_ref, keep_ref, send_ref
):
    which = pl.program_id(0)

    @pl.when(which == 0)
    def _():
        halves(mm(seg_ref[...], normed_ref[...], TN), keep_ref, send_ref)

    @pl.when(which == 3)
    def _():
        halves(mm(mixed_ref[...], up_ref[...], TN), keep_ref, send_ref)

    @pl.when(jnp.logical_and(which > 0, which < 3))
    def _():
        total = mm(seg_ref[...], normed_ref[...], TN)
        total = total + mm(mem_ref[...], mem_in_ref[...], TN)
        total = total + mm(old_ref[...], old_in_ref[...], TN)
        halves(total, keep_ref, send_ref)


def attn_grads(seg_grad, mixed, mem_grad, old_grad, normed, attn_in, mem_in, old_in):
    block = mixed.shape[1]

    def whole(array):
        return pl.BlockSpec(array.shape, lambda i: (0, 0))

    return pl.pallas_call(
        attn_grad_kernel,
        name="attn_grads",
        grid=(4,),
        out_shape=(
            jax.ShapeDtypeStruct((4 * block, D // 2), single),
            jax.ShapeDtypeStruct((4 * block, D // 2), lowp),
        ),
        in_specs=[
            pl.BlockSpec((seg_grad.shape[0], block), lambda i: (0, jnp.minimum(i, 2))),
            whole(mixed),
            pl.BlockSpec((mem_grad.shape[0], block), lambda i: (0, jnp.clip(i - 1, 0, 1))),
            pl.BlockSpec((old_grad.shape[0], block), lambda i: (0, jnp.clip(i - 1, 0, 1))),
            whole(normed),
            whole(attn_in),
            whole(mem_in),
            whole(old_in),
        ],
        out_specs=(
            pl.BlockSpec((block, D // 2), lambda i: (i, 0)),
            pl.BlockSpec((block, D // 2), lambda i: (i, 0)),
        ),
        compiler_params=params(60),
        cost_estimate=cost(9000 * MIB, 24 * MIB),
    )(seg_grad, mixed, mem_grad, old_grad, normed, attn_in, mem_in, old_in)


def scalar_row(values, length=128):
    lane = jnp.arange(length, dtype=jnp.int32)
    row = jnp.zeros((length,), single)
    for i, value in enumerate(values):
        row = jnp.where(lane == i, value, row)
    return row


def local(
    ids,
    targets,
    target_mask,
    memory,
    old_states,
    mem_fill,
    comp_fill,
    table,
    qkv,
    wout,
    wconv,
    wup,
    wdown,
    gains,
    table_rows,
    table_cols,
    qkv_rows,
    qkv_cols,
    out_rows,
    out_cols,
    conv_rows,
    conv_cols,
    up_rows,
    up_cols,
    down_rows,
    down_cols,
    gains_second,
):
    dp_size, head_size = lax.axis_size("dp"), lax.axis_size("head")
    d, h = lax.axis_index("dp"), lax.axis_index("head")
    x, c = h // 2, h % 2
    order = block_order(dp_size)
    reach = dp_size // 2
    streams, seg_len = ids.shape
    half = seg_len // 2
    per_group = streams * seg_len
    vocab, width = table.shape
    assert head_size == 4 and streams == 2

    weights_now = (table, qkv, wout, wconv, wup, wdown)
    rows_old = (table_rows, qkv_rows, out_rows, conv_rows, up_rows, down_rows)
    cols_old = (table_cols, qkv_cols, out_cols, conv_cols, up_cols, down_cols)
    sizes = {"dp": dp_size, "head": head_size}
    row_axes = ("head", "dp", "head", "head", "dp", "head")
    col_axes = ("dp", "head", "dp", "dp", "head", "dp")

    def early_sums(dep):
        _, *tied = together(dep, *rows_old, *weights_now, gains)
        sums = [jnp.sum(old) / sizes[axis] for old, axis in zip(tied[:6], col_axes)]
        sums += [jnp.sum(weight * weight) for weight in tied[6:12]]
        gain_sums = jnp.sum(tied[12] * tied[12], axis=1) / head_size
        return scalar_row(sums + [gain_sums[0], gain_sums[1], gain_sums[2]])

    def core_sum(keep, send, beside=()):
        more, *beside = together(swap(send.astype(lowp), "head", 1), *beside)
        part = keep.astype(single) + more.astype(single)
        return (part, beside) if beside else part

    def stream_sum(part, beside=()):
        keep, send = split(part, 0, 2)
        more, *beside = together(swap(send.astype(lowp), "head", 2), *beside)
        part = keep + more.astype(single)
        return (part, beside) if beside else part

    def group_sum(part, beside=()):
        return stream_sum(core_sum(*split(part, 0, 2)), beside)

    def group_both(part, beside=()):
        far, *beside = together(swap(part, "head", 2), *beside)
        pair = jnp.concatenate([part, far], axis=0)
        both = (pair, swap(pair, "head", 1))
        return (both, beside) if beside else both

    flat = jnp.concatenate(
        [
            ids.astype(single).reshape(-1),
            targets.astype(single).reshape(-1),
            target_mask.astype(single).reshape(-1),
            gains.astype(lowp).astype(single).reshape(-1),
        ]
    )
    room = -flat.shape[0] % 1024
    flat = jnp.concatenate([flat, jnp.zeros((room,), single)]).reshape(1, -1, 128)
    small, small_steps = gather_blocks(flat, 0)
    small = small.reshape(dp_size, -1)
    place = jnp.stack([x, d])

    def field(raw):
        return relative(raw.reshape(-1, 2, 2, half), x, c)

    ids_all = small[:, :per_group]
    position = [order.index(j) for j in range(dp_size)]
    ids_all = jnp.take(ids_all, jnp.asarray(position, jnp.int32)[jnp.arange(dp_size) ^ d], axis=0)
    ids_all = jnp.transpose(field(ids_all), (1, 2, 0, 3)).reshape(-1).astype(jnp.int32)
    table_rows_all = ids_all - h * vocab
    inside = (table_rows_all >= 0) & (table_rows_all < vocab)
    bits = vocab.bit_length()
    token_codes = (jnp.arange(ids_all.shape[0], dtype=jnp.int32) << bits) | table_rows_all
    token_codes = jnp.where(inside, token_codes, -1)
    table_rows_all = jnp.where(inside, table_rows_all, vocab)
    targets_all = field(small[:reach, per_group : 2 * per_group])
    mask_all = field(small[:reach, 2 * per_group : 3 * per_group])
    gain_blocks = small[:, 3 * per_group : 3 * per_group + 3 * width].reshape(dp_size, 3, width)
    gain_vals = jnp.swapaxes(gain_blocks, 0, 1).reshape(3, 1, D)
    count_all = jnp.sum(small[:, 2 * per_group : 3 * per_group])

    heads_own = wconv.shape[0]
    wide = qkv.shape[2]
    conv_rows_own = wconv.size // width
    low_qkv = qkv.astype(lowp)
    pack_one = jnp.concatenate(
        [
            jnp.swapaxes(low_qkv, 1, 2).reshape(3 * wide, width),
            wout.astype(lowp),
            wconv.astype(lowp).reshape(conv_rows_own, width),
        ]
    )
    own_half, far_half = split(table_rows_all, 0, 2)
    kept = {}

    def beside_lookup(moved):
        moved, kept["far"], kept["own"] = together(
            moved, lookup(far_half, table), lookup(own_half, table)
        )
        return moved

    def beside_memory(moved):
        looked = (kept["own"] + swap(kept["far"], "head", 1)).reshape(2, -1, width)
        mem_normed = state_norm(place, gain_vals[0], memory, 1)[0]
        moved, more, kept["mem"] = together(moved, swap(looked[1], "head", 2), mem_normed)
        looked = (looked[0] + more).reshape(dp_size, half, width)
        kept["looked"] = lax.all_to_all(looked, "dp", 0, 0)
        return moved

    own_one, steps_one = gather_blocks(
        after(pack_one, small_steps[0]), 1, (beside_lookup, beside_memory)
    )
    conv_lanes = jnp.arange(DH, dtype=jnp.int32)
    conv_width = DH // dp_size
    conv_natural = (jnp.asarray(order, jnp.int32)[conv_lanes // conv_width] ^ d) * conv_width
    conv_natural = conv_natural + conv_lanes % conv_width
    conv_shuffle = (conv_natural[:, None] == conv_lanes[None, :]).astype(lowp)
    taps = heads_own * RATE * DH

    def conv_natural_order(rows):
        value = jnp.swapaxes(rows.reshape(conv_rows_own, dp_size, width), 0, 1)
        value = jnp.swapaxes(value.reshape(dp_size, taps, conv_width), 0, 1)
        moved = mm(value.reshape(taps, DH), conv_shuffle).astype(lowp)
        return moved.reshape(heads_own, RATE * DH, DH)

    def conv_block_order(value):
        moved = mm(value.astype(lowp).reshape(taps, DH), conv_shuffle, NT).astype(lowp)
        moved = jnp.swapaxes(moved.reshape(taps, dp_size, conv_width), 0, 1)
        moved = jnp.swapaxes(moved.reshape(dp_size, conv_rows_own, width), 0, 1)
        return moved.reshape(conv_rows_own, D)

    full_conv = conv_natural_order(own_one[4 * wide :])

    hidden_own = wup.shape[1]
    pack_two = jnp.concatenate([wup.astype(lowp).T, wdown.astype(lowp)])

    old_normed = state_norm(place, gain_vals[0], old_states, RATE)

    words = vocab // reach
    z = d // 2
    word_start = (h * vocab + z * words).astype(single)
    wanted_all = targets_all - word_start
    wanted_all = jnp.where((wanted_all >= 0) & (wanted_all < words), wanted_all, -1.0)
    info_all = jnp.stack([wanted_all, mask_all] + [jnp.zeros_like(mask_all)] * 6)
    info_all = jnp.transpose(info_all, (1, 0, 2, 3, 4)).reshape(reach, 8, per_group)

    def beside_old(moved):
        moved, looked, kept["old"], kept["info"] = together(
            moved, kept["looked"], old_normed, info_all
        )
        kept["embedded"], kept["normed"] = place_embedding(place, looked, gain_vals[0])
        return moved

    def beside_compress(moved):
        moved, *kept["comp"] = together(moved, *compress(kept["old"], own_one, full_conv))
        return moved

    near_two, steps_two = gather_blocks(
        after(pack_two, steps_one[1]), 1, (beside_old, beside_compress), 1
    )
    near_up, near_down = split(near_two, 0, 2)
    far_up, far_down = swap(near_up, "dp", 1), swap(near_down, "dp", 1)
    mem_normed, old_normed = kept["mem"], kept["old"]
    embedded_low = kept["embedded"]
    embedded = embedded_low.astype(single)
    normed = jnp.concatenate(group_both(kept["normed"]))
    comp, old_raw = kept["comp"]

    words = vocab // reach
    z = d // 2
    unsigned_z = z.astype(jnp.uint32)
    z_groups = [[2 * i + b for i in range(reach)] for b in range(2)]
    slots = -(-words // 256) * 256


    comp_fill, mem_fill, _ = together(comp_fill, mem_fill, kept["mem"])
    comp_counts = jnp.where(x == 1, jnp.flip(comp_fill), comp_fill)
    mem_counts = jnp.where(x == 1, jnp.flip(mem_fill), mem_fill)
    info = [comp_counts[0], mem_counts[0], comp_counts[1], mem_counts[1], c * half]
    lane = jnp.arange(8, dtype=jnp.int32)
    info = sum(jnp.where(lane == i, value, 0) for i, value in enumerate(info)).astype(jnp.int32)

    in_weight = own_one[: 3 * wide]
    mem = mm(mem_normed, own_one[wide : 3 * wide], NT).astype(lowp)
    seg = mm(normed, in_weight, NT).astype(lowp).reshape(2, streams, half, 3 * wide)
    low_table = after(table.astype(lowp), seg).reshape(reach, words, width)
    low_table = lax.all_to_all(low_table, "dp", 0, 0, axis_index_groups=z_groups)
    mixed, lse = attend(info, seg, comp, mem)
    mixed = mixed.reshape(-1, wide)
    attn_sum, (far_up,) = core_sum(
        *split(mm(mixed, own_one[3 * wide : 4 * wide]), 0, 2), (far_up,)
    )
    attn_sum, (early, far_down) = stream_sum(attn_sum, (early_sums(mixed), far_down))
    after_attn = embedded + attn_sum
    ffn_in, inv_second = rms(after_attn, gain_vals[1])
    ffn_in, (low_table,) = group_both(ffn_in, (low_table,))
    near_table = [
        lax.dynamic_index_in_dim(low_table, unsigned_z ^ jnp.uint32(m // 2), 0, keepdims=False) for m in order[:reach]
    ]
    near_table = jnp.concatenate(near_table, axis=1)
    near_table = jnp.concatenate([near_table, jnp.zeros((slots - words, D // 2), lowp)], axis=0)
    ffn_in = jnp.concatenate(ffn_in)
    full_up = jnp.concatenate([near_up, far_up], axis=1)
    full_down = jnp.concatenate([near_down, far_down], axis=1)
    far_table = swap(near_table, "dp", 1)
    hidden_pre = mm(ffn_in, full_up, NT)
    hidden_act = jax.nn.gelu(hidden_pre).astype(lowp)
    after_ffn = after_attn + group_sum(mm(hidden_act, full_down))
    final_in, inv_third = rms(after_ffn, gain_vals[2])

    info_all = kept["info"]
    pieces = [final_in]
    chunks = []
    raised = []
    stats = []

    def next_chunk():
        i = len(chunks)
        if i == 0:
            chunk, kept["list"] = group_both(pieces[i], own_list(after(token_codes, final_in)))
            chunks.append(chunk)
        else:
            chunk, (stats[i - 1],) = group_both(pieces[i], (stats[i - 1],))
            chunks.append(chunk)
        *out, stat = logits_part(words, i, info_all, *chunks[i], near_table, far_table)
        raised.append(out)
        stats.append(stat)

    mask = dp_size // 2
    while mask > 1:
        moved = swap(reorder(pieces, mask), "dp", mask)
        if len(pieces) == 1:
            next_chunk()
        elif len(pieces) == 2:
            moved, stats[0] = together(moved, stats[0])
        pieces += split(moved, 0, len(pieces))
        mask //= 2
    while len(chunks) < reach:
        next_chunk()
    own_codes, own_count = kept["list"]
    stats = [stat[:3].reshape(3, 1, 2, 2, half) for stat in stats]
    own_stats = jnp.concatenate(stats, axis=1)

    def combine(first, second):
        top = jnp.maximum(first[0], second[0])
        total = first[1] * jnp.exp(first[0] - top) + second[1] * jnp.exp(second[0] - top)
        return jnp.stack([top, total, first[2] + second[2]])

    merged = own_stats
    merged = combine(merged, jnp.flip(swap(merged, "head", 1), 2))
    merged = combine(merged, jnp.flip(swap(merged, "head", 2), 3))
    mask = 2
    while mask < dp_size:
        other = split(swap(merged, "dp", mask), 1, reach)
        other = [other[order.index(j ^ mask)] for j in order[:reach]]
        merged = combine(merged, jnp.concatenate(other, axis=1))
        mask *= 2
    log_total = merged[0] + jnp.log(merged[1])
    loss_local = jnp.sum(mask_all[0, 0, 0] * (log_total[0, 0, 0] - merged[2, 0, 0, 0]))
    factor_all = jnp.exp(own_stats[0] - log_total)

    factor_all = factor_all.reshape(reach, 1, per_group) * info_all[:, 1:2]
    factor_all = jnp.broadcast_to(factor_all, info_all.shape)
    dlogits = [[] for _ in range(reach)]
    parts = [None] * reach
    for i in reversed(range(reach)):
        *dlogits[i], keep, send = logits_back(
            i, info_all, factor_all, raised[i], near_table, far_table
        )
        if i + 1 < reach:
            parts[i + 1], (*dlogits[i], keep, send) = stream_sum(
                parts[i + 1], (*dlogits[i], keep, send)
            )
        parts[i] = core_sum(keep, send)
    parts[0] = stream_sum(parts[0])
    table_parts = []
    mask = 2
    while len(parts) > 1:
        count = len(parts) // 2
        moved = swap(reorder(parts[count:], mask), "dp", mask)
        if mask == 2:
            moved, *dlogits[0] = together(moved, *dlogits[0])
        elif mask == 4:
            moved, *table_parts = together(moved, *table_grad_part(dlogits, chunks))
        moved = split(moved.astype(single), 0, count)
        parts = [part + more for part, more in zip(parts, moved)]
        mask *= 2
    final_grad = parts[0]

    grad_after_ffn = rms_back(after_ffn, inv_third, gain_vals[2], final_grad)
    moved_table = swap(table_parts[1], "dp", 1)
    down_in = group_both(grad_after_ffn.astype(lowp))
    down_in = jnp.concatenate(down_in)
    act_grad = mm(down_in, full_down, NT)
    pre_grad = jax.vjp(jax.nn.gelu, hidden_pre)[1](act_grad)[0].astype(lowp)
    two = hidden_grads(pre_grad, hidden_act, ffn_in, down_in)
    ffn_in_grad, two = group_sum(mm(pre_grad, full_up), two)
    grad_after_attn = grad_after_ffn + rms_back(after_attn, inv_second, gain_vals[1], ffn_in_grad)
    attn_in, (moved_table,) = group_both(grad_after_attn.astype(lowp), (moved_table,))
    attn_in = jnp.concatenate(attn_in)
    keep = table_parts[0] + moved_table.astype(single)
    table_pieces = jnp.stack(split(keep[:words].astype(lowp), 1, reach))
    turned = sum(
        ((unsigned_z >> bit) & 1) * jnp.uint32(order.index(2 << bit))
        for bit in range(reach.bit_length() - 1)
    )
    table_pieces = jnp.concatenate(
        [
            lax.dynamic_index_in_dim(table_pieces, turned ^ jnp.uint32(order.index(2 * i)), 0)
            for i in range(reach)
        ]
    )
    table_pieces = lax.all_to_all(table_pieces, "dp", 0, 0, axis_index_groups=z_groups)

    mixed_grad = mm(attn_in, own_one[3 * wide : 4 * wide], NT).astype(lowp)
    mixed_grad = mixed_grad.reshape(2, streams, half, wide)
    seg_grad, comp_grad, mem_grad = attend_back(info, seg, comp, mem, lse, mixed_grad)
    seg_grad = seg_grad.reshape(-1, 3 * wide)

    def beside_expand(moved):
        keep, send = split(mm(seg_grad, in_weight), 0, 2)
        more = swap(send.astype(lowp), "head", 1)
        moved, more, kept["table"], *kept["old"] = together(
            moved, more, table_pieces, *expand(comp_grad, old_raw, full_conv)
        )
        kept["seg_in"] = split(keep + more.astype(single), 0, 2)
        return moved

    def beside_sums(moved):
        seg_in, seg_in_far = kept["seg_in"]
        seg_in_far = swap(seg_in_far.astype(lowp), "head", 2)
        old_grad, conv_sum = kept["old"]
        sums = attn_grads(
            seg_grad,
            mixed,
            mem_grad,
            old_grad.reshape(-1, old_grad.shape[-1]),
            normed,
            attn_in,
            mem_normed,
            old_normed.reshape(-1, D),
        )
        conv_sum = split(conv_block_order(conv_sum), 1, 2)
        sums = [jnp.concatenate([part, more.astype(part.dtype)]) for part, more in zip(sums, conv_sum)]
        seg_in_far, *kept["sums"] = together(seg_in_far, *sums)
        rows_grad = embed_back(
            place, embedded_low, gain_vals[0], seg_in, seg_in_far, grad_after_attn
        )
        moved, kept["rows"] = together(moved, lax.all_to_all(rows_grad, "dp", 0, 0))
        return moved

    def beside_streams(moved):
        moved, far = together(moved, swap(kept["rows"], "head", 2))
        rows_grad = jnp.stack([kept["rows"], far])
        kept["rows"] = jnp.stack([rows_grad, swap(rows_grad, "head", 1)]).reshape(-1, width)
        return moved

    def beside_scatter(moved):
        table_base = kept["table"].astype(single).reshape(vocab, width)
        table_grad = scatter(bits, own_count, own_codes, table_base, kept["rows"])
        moved, kept["table"], kept["table_grad"] = together(moved, table_base, table_grad)
        return moved

    two = reduce_blocks(*two, (beside_expand, beside_sums))
    one = reduce_blocks(*kept["sums"], (beside_streams, beside_scatter))
    table_base, table_grad = kept["table"], kept["table_grad"]

    up_grad = two[:hidden_own].T
    down_grad = two[hidden_own:]
    qkv_grad = jnp.swapaxes(one[: 3 * wide].reshape(3, wide, width), 1, 2)
    out_grad = one[3 * wide : 4 * wide]
    conv_grad = one[4 * wide :].reshape(wconv.shape)

    gains_low = gains.astype(lowp).astype(single)
    gain_part = jnp.stack(
        [
            jnp.sum(low_qkv.astype(single) * qkv_grad, axis=(0, 2)),
            jnp.sum(wup.astype(lowp).astype(single) * up_grad, axis=1),
            jnp.sum(table.astype(lowp).astype(single) * table_base, axis=0),
        ]
    )

    grads = (table_grad, qkv_grad, out_grad, conv_grad, up_grad, down_grad)
    def sum_over_dp(joined):
        mask = 1
        while mask < dp_size:
            joined = joined + swap(joined, "dp", mask)
            mask *= 2
        return joined

    row_part = []
    col_part = []
    for grad in grads:
        square = grad * grad
        row_part.append(jnp.sum(square, axis=-1))
        col_part.append(jnp.sum(square, axis=tuple(range(square.ndim - 1))))
    row_q, row_u, col_e, col_o, col_c, col_d, gain_raw, early = lax.psum(
        (
            row_part[1],
            row_part[4],
            col_part[0],
            col_part[2],
            col_part[3],
            col_part[5],
            gain_part,
            early + scalar_row([0.0] * 15 + [loss_local]),
        ),
        "head",
    )
    lanes = [col_e, jnp.sum(row_q, axis=0), col_o]
    lanes += [jnp.concatenate([col_c, jnp.zeros((width - col_c.shape[0],), single)]), row_u, col_d]
    members = [col_part[4], row_part[5], row_part[3], row_part[2], col_part[1], *lanes, row_part[0], early]
    joined = jnp.concatenate([m.reshape(-1) for m in members])
    joined = sum_over_dp(jnp.concatenate([joined, jnp.zeros((-joined.shape[0] % 1024,), single)]))
    sums = []
    start = 0
    for member in members:
        sums.append(joined[start : start + member.size].reshape(member.shape))
        start += member.size
    col_u, row_d, row_c, row_o, col_q, *lanes, row_e, early = sums
    square_total = [jnp.sum(lane) for lane in lanes]
    row_sums = [row_e, row_q, row_o, row_c, row_u, row_d]
    col_sums = [col_e, col_q, col_o, col_c, col_u, col_d]
    weight_total = early[6:15]
    loss_all = early[15]
    inverse = 1.0 / count_all
    decay = 1.0 - STEP ** (-0.8)
    updates = []
    stats_new = []
    scaled = []
    counts = []
    update_sq = []
    for index in range(6):
        rows_total = rows_old[index].size * sizes[row_axes[index]]
        cols_total = cols_old[index].size * sizes[col_axes[index]]
        grad_scaled = grads[index] * inverse
        rows_new = decay * rows_old[index] + (1.0 - decay) * (
            row_sums[index] * inverse * inverse / cols_total + TINY_SQUARE
        )
        cols_new = decay * cols_old[index] + (1.0 - decay) * (
            col_sums[index] * inverse * inverse / rows_total + TINY_SQUARE
        )
        mean_row = decay * early[index] / rows_total + (1.0 - decay) * (
            square_total[index] * inverse * inverse / (rows_total * cols_total) + TINY_SQUARE
        )
        second = rows_new[..., None] * cols_new / mean_row
        direction = grad_scaled * lax.rsqrt(second)
        updates.append(direction)
        stats_new.append((rows_new, cols_new))
        scaled.append(grad_scaled)
        counts.append(rows_total * cols_total)
        update_sq.append(jnp.sum(direction * direction))
    gain_scaled = gain_raw / gains_low * inverse
    second_new = decay * gains_second + (1.0 - decay) * (gain_scaled * gain_scaled + TINY_SQUARE)
    gain_dir = gain_scaled * lax.rsqrt(second_new)
    for which in range(3):
        update_sq.append(jnp.sum(gain_dir[which] * gain_dir[which]) / head_size)
    update_total = after(scalar_row(update_sq, 1024), loss_all)
    for mask in (1, 2):
        update_total = update_total + swap(update_total, "head", mask)
    update_total = sum_over_dp(update_total)[:9]
    results = [loss_all, count_all]
    for index in range(6):
        factor = jnp.maximum(0.001, jnp.sqrt(weight_total[index] / counts[index]))
        denom = jnp.maximum(1.0, jnp.sqrt(update_total[index] / counts[index]) / CLIP_LEVEL)
        new_weight = weights_now[index] - LEARN_RATE * factor * updates[index] / denom
        results += [new_weight, scaled[index], stats_new[index][0], stats_new[index][1]]
    gain_factor = jnp.maximum(0.001, jnp.sqrt(weight_total[6:] / D))[:, None]
    gain_denom = jnp.maximum(1.0, jnp.sqrt(update_total[6:] / D) / CLIP_LEVEL)[:, None]
    results += [gains - LEARN_RATE * gain_factor * gain_dir / gain_denom, gain_scaled, second_new]
    return tuple(results)


def solution(mesh):
    in_specs = (
        P("dp", None),
        P("dp", None),
        P("dp", None),
        P("dp", None, None),
        P("dp", None, None),
        P("dp"),
        P("dp"),
        P("head", "dp"),
        P(None, "dp", "head"),
        P("head", "dp"),
        P("head", None, "dp"),
        P("dp", "head"),
        P("head", "dp"),
        P(None, "dp"),
        P("head"),
        P("dp"),
        P(None, "dp"),
        P("head"),
        P("head"),
        P("dp"),
        P("head", None),
        P("dp"),
        P("dp"),
        P("head"),
        P("head"),
        P("dp"),
        P(None, "dp"),
    )
    out_specs = (
        P(),
        P(),
        P("head", "dp"),
        P("head", "dp"),
        P("head"),
        P("dp"),
        P(None, "dp", "head"),
        P(None, "dp", "head"),
        P(None, "dp"),
        P("head"),
        P("head", "dp"),
        P("head", "dp"),
        P("head"),
        P("dp"),
        P("head", None, "dp"),
        P("head", None, "dp"),
        P("head", None),
        P("dp"),
        P("dp", "head"),
        P("dp", "head"),
        P("dp"),
        P("head"),
        P("head", "dp"),
        P("head", "dp"),
        P("head"),
        P("dp"),
        P(None, "dp"),
        P(None, "dp"),
        P(None, "dp"),
    )
    return jax.shard_map(local, mesh=mesh, in_specs=in_specs, out_specs=out_specs, check_vma=False)
```

```python
import functools

import jax
import jax.numpy as jnp
from jax import lax
from jax.experimental import pallas as pl
from jax.experimental.pallas import tpu as pltpu
from jax.sharding import PartitionSpec as P

D = 1024
H = 8
DH = 128
MEM = 512
CMEM = 512
RATE = 3
STEP = 10


TINY_NORM = 1e-06
TINY_SQUARE = 1e-30
LEARN_RATE = 0.5
CLIP_LEVEL = 1.0

lowp = jnp.bfloat16
single = jnp.float32
NT = (((1,), (1,)), ((), ()))
TN = (((0,), (0,)), ((), ()))
NN = (((1,), (0,)), ((), ()))
MIB = 1024 * 1024


def mm(left, right, dims=NN):
    return lax.dot_general(left, right, dims, preferred_element_type=single)


def swap(value, axis, mask):
    size = lax.axis_size(axis)
    return lax.ppermute(value, axis, [(i, i ^ mask) for i in range(size)])


def after(value, *deps):
    return lax.optimization_barrier((value, *deps))[0]


def together(*values):
    return lax.optimization_barrier(values)


def block_order(size):
    order = [0]
    step = size // 2
    while step:
        order = order + [j + step for j in order]
        step //= 2
    return order


def gather_blocks(piece, axis, beside=(), stop=0, mask=None):
    steps = []
    mask = mask or lax.axis_size("dp") // 2
    while mask > stop:
        moved = swap(piece, "dp", mask)
        if len(steps) < len(beside):
            moved = beside[len(steps)](moved)
        piece = jnp.concatenate([piece, moved], axis=axis)
        steps.append(piece)
        mask //= 2
    return piece, steps


def split(value, axis, parts):
    width = value.shape[axis] // parts
    return [lax.slice_in_dim(value, i * width, (i + 1) * width, axis=axis) for i in range(parts)]


def reduce_blocks(keep, send, beside=(), mask=1):
    moved = swap(send.astype(lowp), "dp", mask)
    if beside:
        moved = beside[0](moved)
    total = keep + moved.astype(single)
    mask *= 2
    if mask == lax.axis_size("dp"):
        return total
    return reduce_blocks(*split(total, 1, 2), beside[1:], mask)


def reorder_kernel(sources, *refs):
    out_ref = refs[-1]
    width = out_ref.shape[1] // len(sources)
    start = 0
    for in_ref in refs[:-1]:
        rows = slice(start, start + in_ref.shape[0])
        start += in_ref.shape[0]
        for p, q in enumerate(sources):
            block = in_ref[:, q * width : (q + 1) * width]
            out_ref[rows, p * width : (p + 1) * width] = block.astype(out_ref.dtype)


def reorder(values, mask):
    order = block_order(lax.axis_size("dp"))
    sources = [order.index(j ^ mask) for j in order]
    rows = sum(value.shape[0] for value in values)
    if D // len(order) % 128:
        joined = jnp.concatenate([value.astype(lowp) for value in values])
        cols = split(joined, 1, len(order))
        return jnp.concatenate([cols[q] for q in sources], axis=1)
    return pl.pallas_call(
        functools.partial(reorder_kernel, sources),
        name="reorder",
        out_shape=jax.ShapeDtypeStruct((rows, D), lowp),
        in_specs=[vmem()] * len(values),
        out_specs=vmem(),
        compiler_params=params(60),
        cost_estimate=cost(0, 2 * MIB),
    )(*values)


def relative(value, x, c):
    value = jnp.where(x == 1, jnp.flip(value, -3), value)
    value = jnp.where(c == 1, jnp.flip(value, -2), value)
    return jnp.swapaxes(value, -3, -2)


def rms(values, gain):
    inv = lax.rsqrt(jnp.mean(values * values, axis=-1, keepdims=True) + TINY_NORM)
    return (values * inv * gain).astype(lowp), inv


def rms_back(values, inv, gain, upstream):
    scaled = gain * upstream
    inner = jnp.sum(scaled * values, axis=-1, keepdims=True) / D
    return scaled * inv - values * (inner * inv * inv * inv)


def vmem(shape=None, index=None):
    if shape is None:
        return pl.BlockSpec(memory_space=pltpu.VMEM)
    return pl.BlockSpec(shape, index)


def smem():
    return pl.BlockSpec(memory_space=pltpu.SMEM)


def params(mib):
    return pltpu.CompilerParams(vmem_limit_bytes=mib * MIB)


def cost(flops, size, exps=0):
    return pl.CostEstimate(
        flops=int(0.02 * flops), bytes_accessed=int(0.02 * size), transcendentals=exps
    )


def lookup_kernel(row_ref, table_ref, out_ref, tab, held, sem):
    total = row_ref.shape[0]
    vocab = table_ref.shape[0]
    copy = pltpu.make_async_copy(table_ref, tab.at[pl.ds(0, vocab)], sem)
    copy.start()
    tab[pl.ds(vocab, 8), :] = jnp.zeros((8, tab.shape[1]), single)
    copy.wait()

    @pl.loop(0, total // 16)
    def _(g):
        for j in range(16):
            t = g * 16 + j
            held[pl.ds(t, 1), :] = tab[pl.ds(row_ref[t], 1), :]

    @pl.loop(0, total // 512)
    def _(i):
        rows = pl.ds(pl.multiple_of(i * 512, 512), 512)
        out_ref[rows, :] = held[rows, :].astype(lowp)


def lookup(rows, table):
    total = rows.shape[0]
    vocab, width = table.shape
    return pl.pallas_call(
        lookup_kernel,
        name="lookup",
        out_shape=jax.ShapeDtypeStruct((total, width), lowp),
        in_specs=[smem(), pl.BlockSpec(memory_space=pl.ANY)],
        out_specs=vmem(),
        scratch_shapes=[
            pltpu.VMEM((vocab + 8, width), single),
            pltpu.VMEM((total, width), single),
            pltpu.SemaphoreType.DMA(()),
        ],
        compiler_params=params(60),
        cost_estimate=cost(0, 30 * MIB),
    )(rows, table)


def list_kernel(code_ref, out_ref, count_ref):
    total = code_ref.shape[0]

    def group(g, count):
        for j in range(16):
            code = code_ref[g * 16 + j]
            out_ref[count] = code
            count = count + jnp.where(code >= 0, 1, 0)
        return count

    count_ref[0] = lax.fori_loop(0, total // 16, group, jnp.int32(0))


def own_list(codes):
    total = codes.shape[0]
    return pl.pallas_call(
        list_kernel,
        name="own_list",
        out_shape=(
            jax.ShapeDtypeStruct((total + 8,), jnp.int32),
            jax.ShapeDtypeStruct((1,), jnp.int32),
        ),
        in_specs=[smem()],
        out_specs=(smem(), smem()),
        cost_estimate=cost(0, 60 * MIB),
    )(codes)


def place_kernel(order, place_ref, in_ref, gain_ref, out_ref, norm_ref, held):
    width = in_ref.shape[2]
    for p, j in enumerate(order):
        block = in_ref[pl.ds(place_ref[1] ^ j, 1)][0]
        out_ref[:, p * width : (p + 1) * width] = block
        held[:, p * width : (p + 1) * width] = block.astype(single)
    values = held[...]
    inv = lax.rsqrt(jnp.mean(values * values, axis=-1, keepdims=True) + TINY_NORM)
    norm_ref[...] = (values * inv * gain_ref[...]).astype(lowp)


def place_embedding(place, blocks, gain):
    rows = blocks.shape[1]
    return pl.pallas_call(
        functools.partial(place_kernel, block_order(blocks.shape[0])),
        name="place_embedding",
        out_shape=(jax.ShapeDtypeStruct((rows, D), lowp), jax.ShapeDtypeStruct((rows, D), lowp)),
        in_specs=[smem(), vmem(), vmem()],
        out_specs=(vmem(), vmem()),
        scratch_shapes=[pltpu.VMEM((rows, D), single)],
        compiler_params=params(60),
        cost_estimate=cost(0, 3 * MIB),
    )(place, blocks, gain)


def embed_back_kernel(order, place_ref, in_ref, gain_ref, keep_ref, more_ref, grad_ref, out_ref, held):
    values = in_ref[...].astype(single)
    inv = lax.rsqrt(jnp.mean(values * values, axis=-1, keepdims=True) + TINY_NORM)
    upstream = keep_ref[...] + more_ref[...].astype(single)
    held[...] = grad_ref[...] + rms_back(values, inv, gain_ref[...], upstream)
    width = out_ref.shape[2]
    for p, j in enumerate(order):
        block = held[:, p * width : (p + 1) * width].astype(lowp)
        out_ref[pl.ds(place_ref[1] ^ j, 1)] = block[None]


def embed_back(place, values, gain, keep, more, grad):
    rows = values.shape[0]
    size = lax.axis_size("dp")
    return pl.pallas_call(
        functools.partial(embed_back_kernel, block_order(size)),
        name="embed_back",
        out_shape=jax.ShapeDtypeStruct((size, rows, D // size), lowp),
        in_specs=[smem()] + [vmem()] * 5,
        out_specs=vmem(),
        scratch_shapes=[pltpu.VMEM((rows, D), single)],
        compiler_params=params(60),
        cost_estimate=cost(0, 4 * MIB),
    )(place, values, gain, keep, more, grad)


def scatter_kernel(bits, count_ref, code_ref, base_ref, grad_ref, out_ref, rows):
    total = grad_ref.shape[0]
    vocab = base_ref.shape[0]

    @pl.loop(0, total // 512)
    def _(i):
        here = pl.ds(pl.multiple_of(i * 512, 512), 512)
        rows[here, :] = grad_ref[here, :].astype(single)

    rows[pl.ds(total, 8), :] = jnp.zeros((8, rows.shape[1]), single)

    @pl.loop(0, vocab // 400)
    def _(i):
        here = pl.ds(pl.multiple_of(i * 400, 400), 400)
        out_ref[here, :] = base_ref[here, :]

    count = count_ref[0]

    def group(g, carry):
        for j in range(8):
            index = g * 8 + j
            code = jnp.where(index < count, code_ref[index], total << bits)
            token = lax.shift_right_logical(code, bits)
            row = code & ((1 << bits) - 1)
            out_ref[pl.ds(row, 1), :] = out_ref[pl.ds(row, 1), :] + rows[pl.ds(token, 1), :]
        return carry

    lax.fori_loop(0, (count + 7) // 8, group, jnp.int32(0))


def scatter(bits, count, codes, base, grad):
    total, width = grad.shape
    return pl.pallas_call(
        functools.partial(scatter_kernel, bits),
        name="scatter",
        out_shape=jax.ShapeDtypeStruct(base.shape, single),
        in_specs=[smem(), smem(), vmem(), vmem()],
        out_specs=vmem(),
        scratch_shapes=[pltpu.VMEM((total + 8, width), single)],
        compiler_params=params(60),
        cost_estimate=cost(0, 30 * MIB),
    )(count, codes, base, grad)


def state_kernel(order, width, place_ref, gain_ref, in_ref, out_ref, held):
    rows = in_ref.shape[1]
    values = in_ref[0].astype(single)
    inv = lax.rsqrt(jnp.mean(values * values, axis=-1, keepdims=True) + TINY_NORM)
    for p, j in enumerate(order):
        start = pl.multiple_of((place_ref[1] ^ j) * width, width)
        block = in_ref[0, :, pl.ds(start, width)].astype(single)
        held[p] = block * inv * gain_ref[:, p * width : (p + 1) * width]
    groups = out_ref.shape[0]
    for p in range(len(order)):
        cols = slice(p * width, (p + 1) * width)
        if groups == 1:
            out_ref[0, :, cols] = held[p].astype(lowp)
        else:
            for j in range(groups):
                part = held[p, pl.ds(j, rows // groups, stride=groups), :]
                out_ref[j, :, cols] = part.astype(lowp)


def state_norm(place, gain, states, groups):
    size = lax.axis_size("dp")
    order = block_order(size)
    width = D // size
    streams = states.shape[0]
    count = states.shape[1] // groups
    if width % 128:
        values = jnp.where(place[0] == 1, jnp.flip(states, 0), states).astype(single).reshape(-1, D)
        inv = lax.rsqrt(jnp.mean(values * values, axis=-1, keepdims=True) + TINY_NORM)
        lanes = jnp.arange(D, dtype=jnp.int32)
        blocks = jnp.asarray(order, jnp.int32)[lanes // width] ^ place[1]
        source = blocks * width + lanes % width
        shuffle = (lanes[:, None] == source[None, :]).astype(single)
        moved = jnp.dot(values * inv, shuffle, precision=lax.Precision.HIGHEST)
        out = (moved * gain).astype(lowp)
        return jnp.swapaxes(out.reshape(streams * count, groups, D), 0, 1)
    tile = 128
    return pl.pallas_call(
        functools.partial(state_kernel, order, width),
        name="state_norm",
        out_shape=jax.ShapeDtypeStruct((groups, streams * count, D), lowp),
        grid_spec=pltpu.PrefetchScalarGridSpec(
            num_scalar_prefetch=1,
            grid=(streams, count // tile),
            in_specs=[
                pl.BlockSpec((1, D), lambda n, i, s: (0, 0)),
                pl.BlockSpec((1, tile * groups, D), lambda n, i, s: (s[0] ^ n, i, 0)),
            ],
            out_specs=pl.BlockSpec(
                (groups, tile, D), lambda n, i, s: (0, n * (count // tile) + i, 0)
            ),
            scratch_shapes=[pltpu.VMEM((len(order), tile * groups, width), single)],
        ),
        compiler_params=params(60),
        cost_estimate=cost(0, 4 * streams * count * groups * D),
    )(place, gain, states)


def compress_kernel(old_ref, key_ref, value_ref, conv_ref, comp_ref, raw_ref):
    heads = conv_ref.shape[0]
    wide = heads * DH
    for part, weight_ref in enumerate((key_ref, value_ref)):
        sums = [None] * heads
        for j in range(RATE):
            raw = mm(old_ref[j], weight_ref[...], NT).astype(lowp)
            raw_ref[j, :, part * wide : (part + 1) * wide] = raw
            for n in range(heads):
                piece = raw[:, n * DH : (n + 1) * DH]
                term = mm(piece, conv_ref[n, j * DH : (j + 1) * DH, :])
                sums[n] = term if j == 0 else sums[n] + term
        for n in range(heads):
            first = part * wide + n * DH
            comp_ref[:, first : first + DH] = sums[n].astype(lowp)


def compress(old3, weights, conv):
    rows = old3.shape[1]
    wide = conv.shape[0] * DH
    tile = 256
    return pl.pallas_call(
        compress_kernel,
        name="compress",
        grid=(rows // tile,),
        out_shape=(
            jax.ShapeDtypeStruct((rows, 2 * wide), lowp),
            jax.ShapeDtypeStruct((RATE, rows, 2 * wide), lowp),
        ),
        in_specs=[
            pl.BlockSpec((RATE, tile, D), lambda i: (0, i, 0)),
            pl.BlockSpec((wide, D), lambda i: (1, 0)),
            pl.BlockSpec((wide, D), lambda i: (2, 0)),
            pl.BlockSpec(conv.shape, lambda i: (0, 0, 0)),
        ],
        out_specs=(
            pl.BlockSpec((tile, 2 * wide), lambda i: (i, 0)),
            pl.BlockSpec((RATE, tile, 2 * wide), lambda i: (0, i, 0)),
        ),
        compiler_params=params(60),
        cost_estimate=cost(4 * RATE * rows * wide * D, 12 * MIB),
    )(old3, weights, weights, conv)


def expand_kernel(grad_ref, raw_ref, conv_ref, out_ref, conv_out_ref):
    heads = conv_ref.shape[0]
    for h in range(heads):
        for j in range(RATE):
            rows = slice(j * DH, (j + 1) * DH)
            taps = conv_ref[h, rows, :]
            total = None
            for n in (h, heads + h):
                cols = slice(n * DH, (n + 1) * DH)
                grad = grad_ref[:, cols]
                out_ref[j, :, cols] = mm(grad, taps, NT).astype(lowp)
                term = mm(raw_ref[j, :, cols], grad, TN)
                total = term if total is None else total + term
            conv_out_ref[h, rows, :] = total


def expand(grad, raw, conv):
    return pl.pallas_call(
        expand_kernel,
        name="expand",
        out_shape=(
            jax.ShapeDtypeStruct(raw.shape, lowp),
            jax.ShapeDtypeStruct(conv.shape, single),
        ),
        in_specs=[vmem()] * 3,
        out_specs=(vmem(), vmem()),
        compiler_params=params(60),
        cost_estimate=cost(2000 * MIB, 12 * MIB),
    )(grad, raw, conv)


def masked_scores(info_ref, query, keys):
    rows = query.shape[0]
    scale = DH ** (-0.5)
    result = []
    for which, key in enumerate(keys):
        slots = key.shape[0]
        col = lax.broadcasted_iota(jnp.int32, (rows, slots), 1)
        if which < 2:
            seen = col >= slots - info_ref[2 * pl.program_id(0) + which]
        else:
            row = lax.broadcasted_iota(jnp.int32, (rows, slots), 0)
            shift = info_ref[4]
            row = row + shift
            col = col + shift
            row = jnp.where(row >= slots, row - slots, row)
            col = jnp.where(col >= slots, col - slots, col)
            seen = col <= row
        result.append(jnp.where(seen, mm(query, key, NT) * scale, -1e30))
    return result


def rows_of(ref):
    return ref[...].reshape(-1, ref.shape[-1])


def attend_kernel(info_ref, q_ref, ks_ref, vs_ref, kc_ref, vc_ref, km_ref, vm_ref, out_ref, lse_ref):
    query = rows_of(q_ref)
    scores = masked_scores(info_ref, query, [kc_ref[...], km_ref[...], rows_of(ks_ref)])
    top = functools.reduce(jnp.maximum, [jnp.max(s, axis=-1, keepdims=True) for s in scores])
    total = 0.0
    mixed = 0.0
    for score, value in zip(scores, (vc_ref[...], vm_ref[...], rows_of(vs_ref))):
        weight = jnp.exp(score - top)
        total = total + jnp.sum(weight, axis=-1, keepdims=True)
        mixed = mixed + mm(weight.astype(lowp), value)
    out_ref[...] = (mixed / total).astype(lowp).reshape(out_ref.shape)
    lse_ref[0, 0] = top + jnp.log(total)


def attend_back_kernel(
    info_ref, q_ref, ks_ref, vs_ref, kc_ref, vc_ref, km_ref, vm_ref, lse_ref, up_ref,
    seg_ref, comp_ref, mem_ref,
):
    head = pl.program_id(1)
    wide = pl.num_programs(1) * DH
    scale = DH ** (-0.5)
    query = rows_of(q_ref)
    upstream = rows_of(up_ref)
    keys = [kc_ref[...], km_ref[...], rows_of(ks_ref)]
    scores = masked_scores(info_ref, query, keys)
    probs = [jnp.exp(s - lse_ref[0, 0]) for s in scores]
    prob_grads = [
        mm(upstream, v, NT) for v in (vc_ref[...], vm_ref[...], rows_of(vs_ref))
    ]
    inner = 0.0
    for p, g in zip(probs, prob_grads):
        inner = inner + jnp.sum(p * g, axis=-1, keepdims=True)
    here = pl.ds(pl.multiple_of(head * DH, DH), DH)
    second = pl.ds(pl.multiple_of(wide + head * DH, DH), DH)
    third = pl.ds(pl.multiple_of(2 * wide + head * DH, DH), DH)
    query_grad = 0.0
    places = ((comp_ref, here, second), (mem_ref, here, second), (seg_ref, second, third))
    for p, g, key, (ref, key_at, value_at) in zip(probs, prob_grads, keys, places):
        score_grad = (p * (g - inner)).astype(lowp)
        query_grad = query_grad + mm(score_grad, key)
        shape = ref.shape[:-1] + (DH,)
        key_grad = (mm(score_grad, query, TN) * scale).astype(lowp)
        value_grad = mm(p.astype(lowp), upstream, TN).astype(lowp)
        ref[..., key_at] = key_grad.reshape(shape)
        ref[..., value_at] = value_grad.reshape(shape)
    shape = seg_ref.shape[:-1] + (DH,)
    seg_ref[..., here] = (query_grad * scale).astype(lowp).reshape(shape)


def head_specs(seg, comp, mem, heads):
    streams = seg.shape[1]

    def of_seg(first):
        return pl.BlockSpec((2, 1, seg.shape[2], DH), lambda n, h: (0, n, 0, first + h))

    def cols(array, first):
        return pl.BlockSpec((array.shape[0] // streams, DH), lambda n, h: (n, first + h))

    return [
        smem(),
        of_seg(0),
        of_seg(heads),
        of_seg(2 * heads),
        cols(comp, 0),
        cols(comp, heads),
        cols(mem, 0),
        cols(mem, heads),
    ]


def attend(info, seg, comp, mem):
    _, streams, half, _ = seg.shape
    heads = comp.shape[1] // (2 * DH)
    return pl.pallas_call(
        attend_kernel,
        name="attend",
        grid=(streams, heads),
        out_shape=(
            jax.ShapeDtypeStruct((2, streams, half, heads * DH), lowp),
            jax.ShapeDtypeStruct((streams, heads, 2 * half, 1), single),
        ),
        in_specs=head_specs(seg, comp, mem, heads),
        out_specs=(
            pl.BlockSpec((2, 1, half, DH), lambda n, h: (0, n, 0, h)),
            pl.BlockSpec((1, 1, 2 * half, 1), lambda n, h: (n, h, 0, 0)),
        ),
        compiler_params=params(60),
        cost_estimate=cost(7000 * MIB, 6 * MIB),
    )(info, seg, seg, seg, comp, comp, mem, mem)


def attend_back(info, seg, comp, mem, lse, upstream):
    _, streams, half, wide = seg.shape
    heads = comp.shape[1] // (2 * DH)
    slots = comp.shape[0] // streams
    kept = mem.shape[0] // streams
    return pl.pallas_call(
        attend_back_kernel,
        name="attend_back",
        grid=(streams, heads),
        out_shape=(
            jax.ShapeDtypeStruct(seg.shape, lowp),
            jax.ShapeDtypeStruct(comp.shape, lowp),
            jax.ShapeDtypeStruct(mem.shape, lowp),
        ),
        in_specs=head_specs(seg, comp, mem, heads)
        + [
            pl.BlockSpec((1, 1, 2 * half, 1), lambda n, h: (n, h, 0, 0)),
            pl.BlockSpec((2, 1, half, DH), lambda n, h: (0, n, 0, h)),
        ],
        out_specs=(
            pl.BlockSpec((2, 1, half, wide), lambda n, h: (0, n, 0, 0)),
            pl.BlockSpec((slots, comp.shape[1]), lambda n, h: (n, 0)),
            pl.BlockSpec((kept, mem.shape[1]), lambda n, h: (n, 0)),
        ),
        compiler_params=params(60),
        cost_estimate=cost(11000 * MIB, 9 * MIB),
    )(info, seg, seg, seg, comp, comp, mem, mem, lse, upstream)


def columns_of(rows):
    tall = jnp.concatenate([rows, jnp.zeros((120, rows.shape[1]), single)], axis=0)
    return jnp.transpose(tall)


def logits_kernel(
    words, pair_info_ref, near_info_ref, pair_ref, near_ref, left_ref, right_ref,
    pair_out_ref, near_out_ref, stat_ref,
):
    step = pl.program_id(0)
    tile = pair_ref.shape[0]
    half = left_ref.shape[1]
    edge = left_ref.shape[0] - 128
    streams = (
        (pair_info_ref, pair_ref, pair_out_ref),
        (near_info_ref, near_ref, near_out_ref),
    )
    products = [
        mm(ref[:, :half], left_ref[...], NT) + mm(ref[:, half:], right_ref[...], NT)
        for _, ref, _ in streams
    ]
    for n, ((info_ref, _, out_ref), logits) in enumerate(zip(streams, products)):
        wanted = columns_of(info_ref[0])[:, 0:1].astype(jnp.int32)
        col = lax.broadcasted_iota(jnp.int32, logits.shape, 1)
        hit = jnp.sum(jnp.where(col == wanted, logits, 0.0), axis=-1, keepdims=True)
        last = jnp.where(col[:, edge:] < words, logits[:, edge:], -1e30)
        top = jnp.max(last, axis=-1, keepdims=True)
        top = jnp.maximum(top, jnp.max(logits[:, :edge], axis=-1, keepdims=True))
        raised = jnp.exp(logits[:, :edge] - top)
        last = jnp.exp(last - top)
        total = jnp.sum(raised, axis=-1, keepdims=True) + jnp.sum(last, axis=-1, keepdims=True)
        out_ref[:, :edge] = raised.astype(lowp)
        out_ref[:, edge:] = last.astype(lowp)
        lane = lax.broadcasted_iota(jnp.int32, (tile, 128), 1)
        packed = jnp.where(lane == 2, hit, 0.0)
        packed = jnp.where(lane == 0, top, jnp.where(lane == 1, total, packed))
        start = n * (stat_ref.shape[1] // 2) + step * tile
        stat_ref[:, pl.ds(pl.multiple_of(start, tile), tile)] = jnp.transpose(packed)[:8]


def logits_part(words, chunk, info, pair, near, left, right):
    rows, _ = pair.shape
    slots = left.shape[0]
    tile = 256
    tiles = rows // tile
    whole = lambda i: (0, 0)
    return pl.pallas_call(
        functools.partial(logits_kernel, words),
        name="logits_part",
        grid=(tiles,),
        out_shape=(
            jax.ShapeDtypeStruct((rows, slots), lowp),
            jax.ShapeDtypeStruct((rows, slots), lowp),
            jax.ShapeDtypeStruct((8, 2 * rows), single),
        ),
        in_specs=[
            pl.BlockSpec((1, 8, tile), lambda i: (chunk, 0, i)),
            pl.BlockSpec((1, 8, tile), lambda i: (chunk, 0, tiles + i)),
            pl.BlockSpec((tile, D), lambda i: (i, 0)),
            pl.BlockSpec((tile, D), lambda i: (i, 0)),
            pl.BlockSpec(left.shape, whole),
            pl.BlockSpec(right.shape, whole),
        ],
        out_specs=(
            pl.BlockSpec((tile, slots), lambda i: (i, 0)),
            pl.BlockSpec((tile, slots), lambda i: (i, 0)),
            pl.BlockSpec((8, 2 * rows), whole),
        ),
        compiler_params=params(60),
        cost_estimate=cost(8 * rows * slots * D, 10 * MIB),
    )(info, info, pair, near, left, right)


def logits_back_kernel(
    pair_info_ref, near_info_ref, pair_factor_ref, near_factor_ref, pair_ref, near_ref,
    left_ref, right_ref, pair_out_ref, near_out_ref, pair_grad_ref, near_grad_ref,
):
    half = left_ref.shape[1]
    streams = (
        (near_info_ref, near_factor_ref, near_ref, near_out_ref, near_grad_ref),
        (pair_info_ref, pair_factor_ref, pair_ref, pair_out_ref, pair_grad_ref),
    )
    for info_ref, factor_ref, in_ref, out_ref, grad_ref in streams:
        info = columns_of(info_ref[0])
        wanted = info[:, 0:1].astype(jnp.int32)
        counted = info[:, 1:2]
        factor = columns_of(factor_ref[0])[:, 0:1]
        raised = in_ref[...].astype(single)
        col = lax.broadcasted_iota(jnp.int32, raised.shape, 1)
        grads = (raised * factor - jnp.where(col == wanted, counted, 0.0)).astype(lowp)
        out_ref[...] = grads
        grad_ref[:, :half] = mm(grads, left_ref[...]).astype(lowp)
        grad_ref[:, half:] = mm(grads, right_ref[...]).astype(lowp)


def logits_back(chunk, info, factor, raised, left, right):
    rows, slots = raised[0].shape
    tile = 256
    tiles = rows // tile
    whole = lambda i: (0, 0)

    def info_specs():
        return [
            pl.BlockSpec((1, 8, tile), lambda i: (chunk, 0, i)),
            pl.BlockSpec((1, 8, tile), lambda i: (chunk, 0, tiles + i)),
        ]

    return pl.pallas_call(
        logits_back_kernel,
        name="logits_back",
        grid=(tiles,),
        out_shape=(
            jax.ShapeDtypeStruct((rows, slots), lowp),
            jax.ShapeDtypeStruct((rows, slots), lowp),
            jax.ShapeDtypeStruct((rows, D), lowp),
            jax.ShapeDtypeStruct((rows, D), lowp),
        ),
        in_specs=info_specs()
        + info_specs()
        + [pl.BlockSpec((tile, slots), lambda i: (i, 0))] * 2
        + [pl.BlockSpec(left.shape, whole), pl.BlockSpec(right.shape, whole)],
        out_specs=(
            pl.BlockSpec((tile, slots), lambda i: (i, 0)),
            pl.BlockSpec((tile, slots), lambda i: (i, 0)),
            pl.BlockSpec((tile, D), lambda i: (i, 0)),
            pl.BlockSpec((tile, D), lambda i: (i, 0)),
        ),
        compiler_params=params(60),
        cost_estimate=cost(8 * rows * slots * D, 12 * MIB),
    )(info, info, factor, factor, *raised, left, right)


def halves(total, keep_ref, send_ref):
    half = keep_ref.shape[1]
    keep_ref[...] = total[:, :half]
    send_ref[...] = total[:, half:].astype(send_ref.dtype)


def table_grad_kernel(count, *refs):
    total = mm(refs[0][...], refs[count][...], TN)
    for i in range(1, count):
        total = total + mm(refs[i][...], refs[count + i][...], TN)
    halves(total, *refs[2 * count :])


def table_grad_part(grads, inputs):
    grads = [half for pair in grads for half in pair]
    inputs = [half for pair in inputs for half in pair]
    rows = sum(g.shape[0] for g in grads)
    slots = grads[0].shape[1]
    block = 256
    if rows > 4096:
        keep, send = split(sum(mm(g, v, TN) for g, v in zip(grads, inputs)), 1, 2)
        return keep, send.astype(lowp)
    return pl.pallas_call(
        functools.partial(table_grad_kernel, len(grads)),
        name="table_grad_part",
        grid=(slots // block,),
        out_shape=(
            jax.ShapeDtypeStruct((slots, D // 2), single),
            jax.ShapeDtypeStruct((slots, D // 2), lowp),
        ),
        in_specs=[pl.BlockSpec((g.shape[0], block), lambda i: (0, i)) for g in grads]
        + [pl.BlockSpec(v.shape, lambda i: (0, 0)) for v in inputs],
        out_specs=(
            pl.BlockSpec((block, D // 2), lambda i: (i, 0)),
            pl.BlockSpec((block, D // 2), lambda i: (i, 0)),
        ),
        compiler_params=params(60),
        cost_estimate=cost(3 * rows * slots * D, 30 * MIB),
    )(*grads, *inputs)


def hidden_grad_kernel(blocks, pre_ref, act_ref, in_ref, down_ref, keep_ref, send_ref):
    step = pl.program_id(0)

    @pl.when(step < blocks)
    def _():
        halves(mm(pre_ref[...], in_ref[...], TN), keep_ref, send_ref)

    @pl.when(step >= blocks)
    def _():
        halves(mm(act_ref[...], down_ref[...], TN), keep_ref, send_ref)


def hidden_grads(pre_grad, hidden_act, ffn_in, down_in):
    rows, hidden = pre_grad.shape
    block = 256
    blocks = hidden // block
    return pl.pallas_call(
        functools.partial(hidden_grad_kernel, blocks),
        name="hidden_grads",
        grid=(2 * blocks,),
        out_shape=(
            jax.ShapeDtypeStruct((2 * hidden, D // 2), single),
            jax.ShapeDtypeStruct((2 * hidden, D // 2), lowp),
        ),
        in_specs=[
            pl.BlockSpec((rows, block), lambda i: (0, jnp.minimum(i, blocks - 1))),
            pl.BlockSpec((rows, block), lambda i: (0, jnp.maximum(i - blocks, 0))),
            pl.BlockSpec((rows, D), lambda i: (0, 0)),
            pl.BlockSpec((rows, D), lambda i: (0, 0)),
        ],
        out_specs=(
            pl.BlockSpec((block, D // 2), lambda i: (i, 0)),
            pl.BlockSpec((block, D // 2), lambda i: (i, 0)),
        ),
        compiler_params=params(60),
        cost_estimate=cost(6 * rows * hidden * D, 16 * MIB),
    )(pre_grad, hidden_act, ffn_in, down_in)


def attn_grad_kernel(
    seg_ref, mixed_ref, mem_ref, old_ref, normed_ref, up_ref, mem_in_ref, old_in_ref, keep_ref, send_ref
):
    which = pl.program_id(0)

    @pl.when(which == 0)
    def _():
        halves(mm(seg_ref[...], normed_ref[...], TN), keep_ref, send_ref)

    @pl.when(which == 3)
    def _():
        halves(mm(mixed_ref[...], up_ref[...], TN), keep_ref, send_ref)

    @pl.when(jnp.logical_and(which > 0, which < 3))
    def _():
        total = mm(seg_ref[...], normed_ref[...], TN)
        total = total + mm(mem_ref[...], mem_in_ref[...], TN)
        total = total + mm(old_ref[...], old_in_ref[...], TN)
        halves(total, keep_ref, send_ref)


def attn_grads(seg_grad, mixed, mem_grad, old_grad, normed, attn_in, mem_in, old_in):
    block = mixed.shape[1]

    def whole(array):
        return pl.BlockSpec(array.shape, lambda i: (0, 0))

    return pl.pallas_call(
        attn_grad_kernel,
        name="attn_grads",
        grid=(4,),
        out_shape=(
            jax.ShapeDtypeStruct((4 * block, D // 2), single),
            jax.ShapeDtypeStruct((4 * block, D // 2), lowp),
        ),
        in_specs=[
            pl.BlockSpec((seg_grad.shape[0], block), lambda i: (0, jnp.minimum(i, 2))),
            whole(mixed),
            pl.BlockSpec((mem_grad.shape[0], block), lambda i: (0, jnp.clip(i - 1, 0, 1))),
            pl.BlockSpec((old_grad.shape[0], block), lambda i: (0, jnp.clip(i - 1, 0, 1))),
            whole(normed),
            whole(attn_in),
            whole(mem_in),
            whole(old_in),
        ],
        out_specs=(
            pl.BlockSpec((block, D // 2), lambda i: (i, 0)),
            pl.BlockSpec((block, D // 2), lambda i: (i, 0)),
        ),
        compiler_params=params(60),
        cost_estimate=cost(9000 * MIB, 24 * MIB),
    )(seg_grad, mixed, mem_grad, old_grad, normed, attn_in, mem_in, old_in)


def scalar_row(values, length=128):
    lane = jnp.arange(length, dtype=jnp.int32)
    row = jnp.zeros((length,), single)
    for i, value in enumerate(values):
        row = jnp.where(lane == i, value, row)
    return row


def local(
    ids,
    targets,
    target_mask,
    memory,
    old_states,
    mem_fill,
    comp_fill,
    table,
    qkv,
    wout,
    wconv,
    wup,
    wdown,
    gains,
    table_rows,
    table_cols,
    qkv_rows,
    qkv_cols,
    out_rows,
    out_cols,
    conv_rows,
    conv_cols,
    up_rows,
    up_cols,
    down_rows,
    down_cols,
    gains_second,
):
    dp_size, head_size = lax.axis_size("dp"), lax.axis_size("head")
    d, h = lax.axis_index("dp"), lax.axis_index("head")
    x, c = h // 2, h % 2
    order = block_order(dp_size)
    reach = dp_size // 2
    streams, seg_len = ids.shape
    half = seg_len // 2
    per_group = streams * seg_len
    vocab, width = table.shape
    assert head_size == 4 and streams == 2

    weights_now = (table, qkv, wout, wconv, wup, wdown)
    rows_old = (table_rows, qkv_rows, out_rows, conv_rows, up_rows, down_rows)
    cols_old = (table_cols, qkv_cols, out_cols, conv_cols, up_cols, down_cols)
    sizes = {"dp": dp_size, "head": head_size}
    row_axes = ("head", "dp", "head", "head", "dp", "head")
    col_axes = ("dp", "head", "dp", "dp", "head", "dp")

    def early_sums(dep):
        _, *tied = together(dep, *rows_old, *weights_now, gains)
        sums = [jnp.sum(old) / sizes[axis] for old, axis in zip(tied[:6], col_axes)]
        sums += [jnp.sum(weight * weight) for weight in tied[6:12]]
        gain_sums = jnp.sum(tied[12] * tied[12], axis=1) / head_size
        return scalar_row(sums + [gain_sums[0], gain_sums[1], gain_sums[2]])

    def core_sum(keep, send, beside=()):
        more, *beside = together(swap(send.astype(lowp), "head", 1), *beside)
        part = keep.astype(single) + more.astype(single)
        return (part, beside) if beside else part

    def stream_sum(part, beside=()):
        keep, send = split(part, 0, 2)
        more, *beside = together(swap(send.astype(lowp), "head", 2), *beside)
        part = keep + more.astype(single)
        return (part, beside) if beside else part

    def group_sum(part, beside=()):
        return stream_sum(core_sum(*split(part, 0, 2)), beside)

    def group_both(part, beside=()):
        far, *beside = together(swap(part, "head", 2), *beside)
        pair = jnp.concatenate([part, far], axis=0)
        both = (pair, swap(pair, "head", 1))
        return (both, beside) if beside else both

    flat = jnp.concatenate(
        [
            ids.astype(single).reshape(-1),
            targets.astype(single).reshape(-1),
            target_mask.astype(single).reshape(-1),
            gains.astype(lowp).astype(single).reshape(-1),
        ]
    )
    room = -flat.shape[0] % 1024
    flat = jnp.concatenate([flat, jnp.zeros((room,), single)]).reshape(1, -1, 128)
    small, small_steps = gather_blocks(flat, 0)
    small = small.reshape(dp_size, -1)
    place = jnp.stack([x, d])

    def field(raw):
        return relative(raw.reshape(-1, 2, 2, half), x, c)

    ids_all = small[:, :per_group]
    position = [order.index(j) for j in range(dp_size)]
    ids_all = jnp.take(ids_all, jnp.asarray(position, jnp.int32)[jnp.arange(dp_size) ^ d], axis=0)
    ids_all = jnp.transpose(field(ids_all), (1, 2, 0, 3)).reshape(-1).astype(jnp.int32)
    table_rows_all = ids_all - h * vocab
    inside = (table_rows_all >= 0) & (table_rows_all < vocab)
    bits = vocab.bit_length()
    token_codes = (jnp.arange(ids_all.shape[0], dtype=jnp.int32) << bits) | table_rows_all
    token_codes = jnp.where(inside, token_codes, -1)
    table_rows_all = jnp.where(inside, table_rows_all, vocab)
    targets_all = field(small[:reach, per_group : 2 * per_group])
    mask_all = field(small[:reach, 2 * per_group : 3 * per_group])
    gain_blocks = small[:, 3 * per_group : 3 * per_group + 3 * width].reshape(dp_size, 3, width)
    gain_vals = jnp.swapaxes(gain_blocks, 0, 1).reshape(3, 1, D)
    count_all = jnp.sum(small[:, 2 * per_group : 3 * per_group])

    heads_own = wconv.shape[0]
    wide = qkv.shape[2]
    conv_rows_own = wconv.size // width
    low_qkv = qkv.astype(lowp)
    pack_one = jnp.concatenate(
        [
            jnp.swapaxes(low_qkv, 1, 2).reshape(3 * wide, width),
            wout.astype(lowp),
            wconv.astype(lowp).reshape(conv_rows_own, width),
        ]
    )
    own_half, far_half = split(table_rows_all, 0, 2)
    kept = {}
    hidden_own = wup.shape[1]
    pack_two = jnp.concatenate([wup.astype(lowp).T, wdown.astype(lowp)])

    def beside_lookup(moved):
        moved, kept["far"], kept["own"] = together(
            moved, lookup(far_half, table), lookup(own_half, table)
        )
        kept["two"] = after(pack_two, moved)
        return moved

    def beside_memory(moved):
        looked = (kept["own"] + swap(kept["far"], "head", 1)).reshape(2, -1, width)
        mem_normed = state_norm(place, gain_vals[0], memory, 1)[0]
        moved, more, kept["mem"], second = together(
            moved, swap(looked[1], "head", 2), mem_normed, swap(kept["two"], "dp", dp_size // 2)
        )
        kept["two"] = jnp.concatenate([kept["two"], second], axis=1)
        looked = (looked[0] + more).reshape(dp_size, half, width)
        kept["looked"] = lax.all_to_all(looked, "dp", 0, 0)
        return moved

    own_one, steps_one = gather_blocks(
        after(pack_one, small_steps[0]), 1, (beside_lookup, beside_memory)
    )
    conv_lanes = jnp.arange(DH, dtype=jnp.int32)
    conv_width = DH // dp_size
    conv_natural = (jnp.asarray(order, jnp.int32)[conv_lanes // conv_width] ^ d) * conv_width
    conv_natural = conv_natural + conv_lanes % conv_width
    conv_shuffle = (conv_natural[:, None] == conv_lanes[None, :]).astype(lowp)
    taps = heads_own * RATE * DH

    def conv_natural_order(rows):
        value = jnp.swapaxes(rows.reshape(conv_rows_own, dp_size, width), 0, 1)
        value = jnp.swapaxes(value.reshape(dp_size, taps, conv_width), 0, 1)
        moved = mm(value.reshape(taps, DH), conv_shuffle).astype(lowp)
        return moved.reshape(heads_own, RATE * DH, DH)

    def conv_block_order(value):
        moved = mm(value.astype(lowp).reshape(taps, DH), conv_shuffle, NT).astype(lowp)
        moved = jnp.swapaxes(moved.reshape(taps, dp_size, conv_width), 0, 1)
        moved = jnp.swapaxes(moved.reshape(dp_size, conv_rows_own, width), 0, 1)
        return moved.reshape(conv_rows_own, D)

    full_conv = conv_natural_order(own_one[4 * wide :])


    old_normed = state_norm(place, gain_vals[0], old_states, RATE)

    words = vocab // reach
    z = d // 2
    word_start = (h * vocab + z * words).astype(single)
    wanted_all = targets_all - word_start
    wanted_all = jnp.where((wanted_all >= 0) & (wanted_all < words), wanted_all, -1.0)
    info_all = jnp.stack([wanted_all, mask_all] + [jnp.zeros_like(mask_all)] * 6)
    info_all = jnp.transpose(info_all, (1, 0, 2, 3, 4)).reshape(reach, 8, per_group)

    looked, old_normed, info_all = together(kept["looked"], old_normed, info_all)
    embedded_low, normed = place_embedding(place, looked, gain_vals[0])
    embedded = embedded_low.astype(single)

    def beside_compress(moved):
        moved, *kept["comp"] = together(moved, *compress(old_normed, own_one, full_conv))
        return moved

    near_two, steps_two = gather_blocks(
        kept["two"], 1, (beside_compress,), 1, dp_size // 4
    )
    near_up, near_down = split(near_two, 0, 2)
    far_up, far_down = swap(near_up, "dp", 1), swap(near_down, "dp", 1)
    mem_normed = kept["mem"]
    normed = jnp.concatenate(group_both(normed))
    comp, old_raw = kept["comp"]

    words = vocab // reach
    z = d // 2
    unsigned_z = z.astype(jnp.uint32)
    z_groups = [[2 * i + b for i in range(reach)] for b in range(2)]
    slots = -(-words // 256) * 256


    comp_fill, mem_fill, _ = together(comp_fill, mem_fill, kept["mem"])
    comp_counts = jnp.where(x == 1, jnp.flip(comp_fill), comp_fill)
    mem_counts = jnp.where(x == 1, jnp.flip(mem_fill), mem_fill)
    info = [comp_counts[0], mem_counts[0], comp_counts[1], mem_counts[1], c * half]
    lane = jnp.arange(8, dtype=jnp.int32)
    info = sum(jnp.where(lane == i, value, 0) for i, value in enumerate(info)).astype(jnp.int32)

    in_weight = own_one[: 3 * wide]
    mem = mm(mem_normed, own_one[wide : 3 * wide], NT).astype(lowp)
    seg = mm(normed, in_weight, NT).astype(lowp).reshape(2, streams, half, 3 * wide)
    low_table = after(table.astype(lowp), seg).reshape(reach, words, width)
    low_table = lax.all_to_all(low_table, "dp", 0, 0, axis_index_groups=z_groups)
    mixed, lse = attend(info, seg, comp, mem)
    mixed = mixed.reshape(-1, wide)
    attn_sum, (far_up,) = core_sum(
        *split(mm(mixed, own_one[3 * wide : 4 * wide]), 0, 2), (far_up,)
    )
    attn_sum, (early, far_down) = stream_sum(attn_sum, (early_sums(mixed), far_down))
    after_attn = embedded + attn_sum
    ffn_in, inv_second = rms(after_attn, gain_vals[1])
    ffn_in, (low_table,) = group_both(ffn_in, (low_table,))
    near_table = [
        lax.dynamic_index_in_dim(low_table, unsigned_z ^ jnp.uint32(m // 2), 0, keepdims=False) for m in order[:reach]
    ]
    near_table = jnp.concatenate(near_table, axis=1)
    near_table = jnp.concatenate([near_table, jnp.zeros((slots - words, D // 2), lowp)], axis=0)
    ffn_in = jnp.concatenate(ffn_in)
    full_up = jnp.concatenate([near_up, far_up], axis=1)
    full_down = jnp.concatenate([near_down, far_down], axis=1)
    far_table = swap(near_table, "dp", 1)
    hidden_pre = mm(ffn_in, full_up, NT)
    hidden_act = jax.nn.gelu(hidden_pre).astype(lowp)
    after_ffn = after_attn + group_sum(mm(hidden_act, full_down))
    final_in, inv_third = rms(after_ffn, gain_vals[2])

    pieces = [final_in]
    chunks = []
    raised = []
    stats = []

    def next_chunk():
        i = len(chunks)
        if i == 0:
            chunk, kept["list"] = group_both(pieces[i], own_list(after(token_codes, final_in)))
            chunks.append(chunk)
        else:
            chunk, (stats[i - 1],) = group_both(pieces[i], (stats[i - 1],))
            chunks.append(chunk)
        *out, stat = logits_part(words, i, info_all, *chunks[i], near_table, far_table)
        raised.append(out)
        stats.append(stat)

    mask = dp_size // 2
    while mask > 1:
        moved = swap(reorder(pieces, mask), "dp", mask)
        if len(pieces) == 1:
            next_chunk()
        elif len(pieces) == 2:
            moved, stats[0] = together(moved, stats[0])
        pieces += split(moved, 0, len(pieces))
        mask //= 2
    while len(chunks) < reach:
        next_chunk()
    own_codes, own_count = kept["list"]
    stats = [stat[:3].reshape(3, 1, 2, 2, half) for stat in stats]
    own_stats = jnp.concatenate(stats, axis=1)

    def combine(first, second):
        top = jnp.maximum(first[0], second[0])
        total = first[1] * jnp.exp(first[0] - top) + second[1] * jnp.exp(second[0] - top)
        return jnp.stack([top, total, first[2] + second[2]])

    merged = own_stats
    merged = combine(merged, jnp.flip(swap(merged, "head", 1), 2))
    merged = combine(merged, jnp.flip(swap(merged, "head", 2), 3))
    mask = 2
    while mask < dp_size:
        other = split(swap(merged, "dp", mask), 1, reach)
        other = [other[order.index(j ^ mask)] for j in order[:reach]]
        merged = combine(merged, jnp.concatenate(other, axis=1))
        mask *= 2
    log_total = merged[0] + jnp.log(merged[1])
    loss_local = jnp.sum(mask_all[0, 0, 0] * (log_total[0, 0, 0] - merged[2, 0, 0, 0]))
    factor_all = jnp.exp(own_stats[0] - log_total)

    factor_all = factor_all.reshape(reach, 1, per_group) * info_all[:, 1:2]
    factor_all = jnp.broadcast_to(factor_all, info_all.shape)
    dlogits = [[] for _ in range(reach)]
    parts = [None] * reach
    for i in reversed(range(reach)):
        *dlogits[i], keep, send = logits_back(
            i, info_all, factor_all, raised[i], near_table, far_table
        )
        if i + 1 < reach:
            parts[i + 1], (*dlogits[i], keep, send) = stream_sum(
                parts[i + 1], (*dlogits[i], keep, send)
            )
        parts[i] = core_sum(keep, send)
    parts[0] = stream_sum(parts[0])
    table_parts = []
    mask = 2
    while len(parts) > 1:
        count = len(parts) // 2
        moved = swap(reorder(parts[count:], mask), "dp", mask)
        if mask == 2:
            moved, *dlogits[0] = together(moved, *dlogits[0])
        elif mask == 4:
            moved, *table_parts = together(moved, *table_grad_part(dlogits, chunks))
        moved = split(moved.astype(single), 0, count)
        parts = [part + more for part, more in zip(parts, moved)]
        mask *= 2
    final_grad = parts[0]

    grad_after_ffn = rms_back(after_ffn, inv_third, gain_vals[2], final_grad)
    moved_table = swap(table_parts[1], "dp", 1)
    down_in = group_both(grad_after_ffn.astype(lowp))
    down_in = jnp.concatenate(down_in)
    act_grad = mm(down_in, full_down, NT)
    pre_grad = jax.vjp(jax.nn.gelu, hidden_pre)[1](act_grad)[0].astype(lowp)
    two = hidden_grads(pre_grad, hidden_act, ffn_in, down_in)
    ffn_in_grad, (*two, moved_table) = group_sum(mm(pre_grad, full_up), (*two, moved_table))
    keep = table_parts[0] + moved_table.astype(single)
    table_pieces = jnp.stack(split(keep[:words].astype(lowp), 1, reach))
    turned = sum(
        ((unsigned_z >> bit) & 1) * jnp.uint32(order.index(2 << bit))
        for bit in range(reach.bit_length() - 1)
    )
    table_pieces = jnp.concatenate(
        [
            lax.dynamic_index_in_dim(table_pieces, turned ^ jnp.uint32(order.index(2 * i)), 0)
            for i in range(reach)
        ]
    )
    table_pieces = lax.all_to_all(table_pieces, "dp", 0, 0, axis_index_groups=z_groups)
    grad_after_attn = grad_after_ffn + rms_back(after_attn, inv_second, gain_vals[1], ffn_in_grad)
    attn_in = jnp.concatenate(group_both(grad_after_attn.astype(lowp)))

    mixed_grad = mm(attn_in, own_one[3 * wide : 4 * wide], NT).astype(lowp)
    mixed_grad = mixed_grad.reshape(2, streams, half, wide)
    seg_grad, comp_grad, mem_grad = attend_back(info, seg, comp, mem, lse, mixed_grad)
    seg_grad = seg_grad.reshape(-1, 3 * wide)

    def beside_expand(moved):
        keep, send = split(mm(seg_grad, in_weight), 0, 2)
        more = swap(send.astype(lowp), "head", 1)
        moved, more, kept["table"], *kept["old"] = together(
            moved, more, table_pieces, *expand(comp_grad, old_raw, full_conv)
        )
        kept["seg_in"] = split(keep + more.astype(single), 0, 2)
        return moved

    def beside_sums(moved):
        seg_in, seg_in_far = kept["seg_in"]
        seg_in_far = swap(seg_in_far.astype(lowp), "head", 2)
        old_grad, conv_sum = kept["old"]
        sums = attn_grads(
            seg_grad,
            mixed,
            mem_grad,
            old_grad.reshape(-1, old_grad.shape[-1]),
            normed,
            attn_in,
            mem_normed,
            old_normed.reshape(-1, D),
        )
        conv_sum = split(conv_block_order(conv_sum), 1, 2)
        sums = [jnp.concatenate([part, more.astype(part.dtype)]) for part, more in zip(sums, conv_sum)]
        seg_in_far, *kept["sums"] = together(seg_in_far, *sums)
        rows_grad = embed_back(
            place, embedded_low, gain_vals[0], seg_in, seg_in_far, grad_after_attn
        )
        moved, kept["rows"] = together(moved, lax.all_to_all(rows_grad, "dp", 0, 0))
        return moved

    def beside_streams(moved):
        moved, far = together(moved, swap(kept["rows"], "head", 2))
        rows_grad = jnp.stack([kept["rows"], far])
        kept["rows"] = jnp.stack([rows_grad, swap(rows_grad, "head", 1)]).reshape(-1, width)
        return moved

    def beside_scatter(moved):
        table_base = kept["table"].astype(single).reshape(vocab, width)
        table_grad = scatter(bits, own_count, own_codes, table_base, kept["rows"])
        moved, kept["table"], kept["table_grad"] = together(moved, table_base, table_grad)
        return moved

    two = reduce_blocks(*two, (beside_expand, beside_sums))
    one = reduce_blocks(*kept["sums"], (beside_streams, beside_scatter))
    table_base, table_grad = kept["table"], kept["table_grad"]

    up_grad = two[:hidden_own].T
    down_grad = two[hidden_own:]
    qkv_grad = jnp.swapaxes(one[: 3 * wide].reshape(3, wide, width), 1, 2)
    out_grad = one[3 * wide : 4 * wide]
    conv_grad = one[4 * wide :].reshape(wconv.shape)

    gains_low = gains.astype(lowp).astype(single)
    gain_part = jnp.stack(
        [
            jnp.sum(low_qkv.astype(single) * qkv_grad, axis=(0, 2)),
            jnp.sum(wup.astype(lowp).astype(single) * up_grad, axis=1),
            jnp.sum(table.astype(lowp).astype(single) * table_base, axis=0),
        ]
    )

    grads = (table_grad, qkv_grad, out_grad, conv_grad, up_grad, down_grad)
    def sum_over_dp(joined):
        mask = 1
        while mask < dp_size:
            joined = joined + swap(joined, "dp", mask)
            mask *= 2
        return joined

    row_part = []
    col_part = []
    for grad in grads:
        square = grad * grad
        row_part.append(jnp.sum(square, axis=-1))
        col_part.append(jnp.sum(square, axis=tuple(range(square.ndim - 1))))
    row_q, row_u, col_e, col_o, col_c, col_d, gain_raw, early = lax.psum(
        (
            row_part[1],
            row_part[4],
            col_part[0],
            col_part[2],
            col_part[3],
            col_part[5],
            gain_part,
            early + scalar_row([0.0] * 15 + [loss_local]),
        ),
        "head",
    )
    lanes = [col_e, jnp.sum(row_q, axis=0), col_o]
    lanes += [jnp.concatenate([col_c, jnp.zeros((width - col_c.shape[0],), single)]), row_u, col_d]
    members = [col_part[4], row_part[5], row_part[3], row_part[2], col_part[1], *lanes, row_part[0], early]
    joined = jnp.concatenate([m.reshape(-1) for m in members])
    joined = sum_over_dp(jnp.concatenate([joined, jnp.zeros((-joined.shape[0] % 1024,), single)]))
    sums = []
    start = 0
    for member in members:
        sums.append(joined[start : start + member.size].reshape(member.shape))
        start += member.size
    col_u, row_d, row_c, row_o, col_q, *lanes, row_e, early = sums
    square_total = [jnp.sum(lane) for lane in lanes]
    row_sums = [row_e, row_q, row_o, row_c, row_u, row_d]
    col_sums = [col_e, col_q, col_o, col_c, col_u, col_d]
    weight_total = early[6:15]
    loss_all = early[15]
    inverse = 1.0 / count_all
    decay = 1.0 - STEP ** (-0.8)
    updates = []
    stats_new = []
    scaled = []
    counts = []
    update_sq = []
    for index in range(6):
        rows_total = rows_old[index].size * sizes[row_axes[index]]
        cols_total = cols_old[index].size * sizes[col_axes[index]]
        grad_scaled = grads[index] * inverse
        rows_new = decay * rows_old[index] + (1.0 - decay) * (
            row_sums[index] * inverse * inverse / cols_total + TINY_SQUARE
        )
        cols_new = decay * cols_old[index] + (1.0 - decay) * (
            col_sums[index] * inverse * inverse / rows_total + TINY_SQUARE
        )
        mean_row = decay * early[index] / rows_total + (1.0 - decay) * (
            square_total[index] * inverse * inverse / (rows_total * cols_total) + TINY_SQUARE
        )
        second = rows_new[..., None] * cols_new / mean_row
        direction = grad_scaled * lax.rsqrt(second)
        updates.append(direction)
        stats_new.append((rows_new, cols_new))
        scaled.append(grad_scaled)
        counts.append(rows_total * cols_total)
        update_sq.append(jnp.sum(direction * direction))
    gain_scaled = gain_raw / gains_low * inverse
    second_new = decay * gains_second + (1.0 - decay) * (gain_scaled * gain_scaled + TINY_SQUARE)
    gain_dir = gain_scaled * lax.rsqrt(second_new)
    for which in range(3):
        update_sq.append(jnp.sum(gain_dir[which] * gain_dir[which]) / head_size)
    update_total = after(scalar_row(update_sq, 1024), loss_all)
    for mask in (1, 2):
        update_total = update_total + swap(update_total, "head", mask)
    update_total = sum_over_dp(update_total)[:9]
    results = [loss_all, count_all]
    for index in range(6):
        factor = jnp.maximum(0.001, jnp.sqrt(weight_total[index] / counts[index]))
        denom = jnp.maximum(1.0, jnp.sqrt(update_total[index] / counts[index]) / CLIP_LEVEL)
        new_weight = weights_now[index] - LEARN_RATE * factor * updates[index] / denom
        results += [new_weight, scaled[index], stats_new[index][0], stats_new[index][1]]
    gain_factor = jnp.maximum(0.001, jnp.sqrt(weight_total[6:] / D))[:, None]
    gain_denom = jnp.maximum(1.0, jnp.sqrt(update_total[6:] / D) / CLIP_LEVEL)[:, None]
    results += [gains - LEARN_RATE * gain_factor * gain_dir / gain_denom, gain_scaled, second_new]
    return tuple(results)


def solution(mesh):
    in_specs = (
        P("dp", None),
        P("dp", None),
        P("dp", None),
        P("dp", None, None),
        P("dp", None, None),
        P("dp"),
        P("dp"),
        P("head", "dp"),
        P(None, "dp", "head"),
        P("head", "dp"),
        P("head", None, "dp"),
        P("dp", "head"),
        P("head", "dp"),
        P(None, "dp"),
        P("head"),
        P("dp"),
        P(None, "dp"),
        P("head"),
        P("head"),
        P("dp"),
        P("head", None),
        P("dp"),
        P("dp"),
        P("head"),
        P("head"),
        P("dp"),
        P(None, "dp"),
    )
    out_specs = (
        P(),
        P(),
        P("head", "dp"),
        P("head", "dp"),
        P("head"),
        P("dp"),
        P(None, "dp", "head"),
        P(None, "dp", "head"),
        P(None, "dp"),
        P("head"),
        P("head", "dp"),
        P("head", "dp"),
        P("head"),
        P("dp"),
        P("head", None, "dp"),
        P("head", None, "dp"),
        P("head", None),
        P("dp"),
        P("dp", "head"),
        P("dp", "head"),
        P("dp"),
        P("head"),
        P("head", "dp"),
        P("head", "dp"),
        P("head"),
        P("dp"),
        P(None, "dp"),
        P(None, "dp"),
        P(None, "dp"),
    )
    return jax.shard_map(local, mesh=mesh, in_specs=in_specs, out_specs=out_specs, check_vma=False)
```

```python
import functools

import jax
import jax.numpy as jnp
from jax import lax
from jax.experimental import pallas as pl
from jax.experimental.pallas import tpu as pltpu
from jax.sharding import PartitionSpec as P

D = 1024
H = 8
DH = 128
MEM = 512
CMEM = 512
RATE = 3
STEP = 10


TINY_NORM = 1e-06
TINY_SQUARE = 1e-30
LEARN_RATE = 0.5
CLIP_LEVEL = 1.0

lowp = jnp.bfloat16
single = jnp.float32
NT = (((1,), (1,)), ((), ()))
TN = (((0,), (0,)), ((), ()))
NN = (((1,), (0,)), ((), ()))
MIB = 1024 * 1024


def mm(left, right, dims=NN):
    return lax.dot_general(left, right, dims, preferred_element_type=single)


def swap(value, axis, mask):
    size = lax.axis_size(axis)
    return lax.ppermute(value, axis, [(i, i ^ mask) for i in range(size)])


def after(value, *deps):
    return lax.optimization_barrier((value, *deps))[0]


def together(*values):
    return lax.optimization_barrier(values)


def block_order(size):
    order = [0]
    step = size // 2
    while step:
        order = order + [j + step for j in order]
        step //= 2
    return order


def gather_blocks(piece, axis, beside=(), stop=0, mask=None):
    steps = []
    mask = mask or lax.axis_size("dp") // 2
    while mask > stop:
        moved = swap(piece, "dp", mask)
        if len(steps) < len(beside):
            moved = beside[len(steps)](moved)
        piece = jnp.concatenate([piece, moved], axis=axis)
        steps.append(piece)
        mask //= 2
    return piece, steps


def split(value, axis, parts):
    width = value.shape[axis] // parts
    return [lax.slice_in_dim(value, i * width, (i + 1) * width, axis=axis) for i in range(parts)]


def reduce_blocks(keep, send, beside=(), mask=1):
    moved = swap(send.astype(lowp), "dp", mask)
    if beside:
        moved = beside[0](moved)
    total = keep + moved.astype(single)
    mask *= 2
    if mask == lax.axis_size("dp"):
        return total
    return reduce_blocks(*split(total, 1, 2), beside[1:], mask)


def reorder_kernel(sources, *refs):
    out_ref = refs[-1]
    width = out_ref.shape[1] // len(sources)
    start = 0
    for in_ref in refs[:-1]:
        rows = slice(start, start + in_ref.shape[0])
        start += in_ref.shape[0]
        for p, q in enumerate(sources):
            block = in_ref[:, q * width : (q + 1) * width]
            out_ref[rows, p * width : (p + 1) * width] = block.astype(out_ref.dtype)


def reorder(values, mask):
    order = block_order(lax.axis_size("dp"))
    sources = [order.index(j ^ mask) for j in order]
    rows = sum(value.shape[0] for value in values)
    if D // len(order) % 128:
        joined = jnp.concatenate([value.astype(lowp) for value in values])
        cols = split(joined, 1, len(order))
        return jnp.concatenate([cols[q] for q in sources], axis=1)
    return pl.pallas_call(
        functools.partial(reorder_kernel, sources),
        name="reorder",
        out_shape=jax.ShapeDtypeStruct((rows, D), lowp),
        in_specs=[vmem()] * len(values),
        out_specs=vmem(),
        compiler_params=params(60),
        cost_estimate=cost(0, 2 * MIB),
    )(*values)


def relative(value, x, c):
    value = jnp.where(x == 1, jnp.flip(value, -3), value)
    value = jnp.where(c == 1, jnp.flip(value, -2), value)
    return jnp.swapaxes(value, -3, -2)


def rms(values, gain):
    inv = lax.rsqrt(jnp.mean(values * values, axis=-1, keepdims=True) + TINY_NORM)
    return (values * inv * gain).astype(lowp), inv


def rms_back(values, inv, gain, upstream):
    scaled = gain * upstream
    inner = jnp.sum(scaled * values, axis=-1, keepdims=True) / D
    return scaled * inv - values * (inner * inv * inv * inv)


def vmem(shape=None, index=None):
    if shape is None:
        return pl.BlockSpec(memory_space=pltpu.VMEM)
    return pl.BlockSpec(shape, index)


def smem():
    return pl.BlockSpec(memory_space=pltpu.SMEM)


def params(mib):
    return pltpu.CompilerParams(vmem_limit_bytes=mib * MIB)


def cost(flops, size, exps=0):
    return pl.CostEstimate(
        flops=int(0.02 * flops), bytes_accessed=int(0.02 * size), transcendentals=exps
    )


def lookup_kernel(row_ref, table_ref, out_ref, tab, held, sem):
    total = row_ref.shape[0]
    vocab = table_ref.shape[0]
    copy = pltpu.make_async_copy(table_ref, tab.at[pl.ds(0, vocab)], sem)
    copy.start()
    tab[pl.ds(vocab, 8), :] = jnp.zeros((8, tab.shape[1]), single)
    copy.wait()

    @pl.loop(0, total // 16)
    def _(g):
        for j in range(16):
            t = g * 16 + j
            held[pl.ds(t, 1), :] = tab[pl.ds(row_ref[t], 1), :]

    @pl.loop(0, total // 512)
    def _(i):
        rows = pl.ds(pl.multiple_of(i * 512, 512), 512)
        out_ref[rows, :] = held[rows, :].astype(lowp)


def lookup(rows, table):
    total = rows.shape[0]
    vocab, width = table.shape
    return pl.pallas_call(
        lookup_kernel,
        name="lookup",
        out_shape=jax.ShapeDtypeStruct((total, width), lowp),
        in_specs=[smem(), pl.BlockSpec(memory_space=pl.ANY)],
        out_specs=vmem(),
        scratch_shapes=[
            pltpu.VMEM((vocab + 8, width), single),
            pltpu.VMEM((total, width), single),
            pltpu.SemaphoreType.DMA(()),
        ],
        compiler_params=params(60),
        cost_estimate=cost(0, 30 * MIB),
    )(rows, table)


def list_kernel(code_ref, out_ref, count_ref):
    total = code_ref.shape[0]

    def group(g, count):
        for j in range(16):
            code = code_ref[g * 16 + j]
            out_ref[count] = code
            count = count + jnp.where(code >= 0, 1, 0)
        return count

    count_ref[0] = lax.fori_loop(0, total // 16, group, jnp.int32(0))


def own_list(codes):
    total = codes.shape[0]
    return pl.pallas_call(
        list_kernel,
        name="own_list",
        out_shape=(
            jax.ShapeDtypeStruct((total + 8,), jnp.int32),
            jax.ShapeDtypeStruct((1,), jnp.int32),
        ),
        in_specs=[smem()],
        out_specs=(smem(), smem()),
        cost_estimate=cost(0, 60 * MIB),
    )(codes)


def place_kernel(order, place_ref, in_ref, gain_ref, out_ref, norm_ref, held):
    width = in_ref.shape[2]
    for p, j in enumerate(order):
        block = in_ref[pl.ds(place_ref[1] ^ j, 1)][0]
        out_ref[:, p * width : (p + 1) * width] = block
        held[:, p * width : (p + 1) * width] = block.astype(single)
    values = held[...]
    inv = lax.rsqrt(jnp.mean(values * values, axis=-1, keepdims=True) + TINY_NORM)
    norm_ref[...] = (values * inv * gain_ref[...]).astype(lowp)


def place_embedding(place, blocks, gain):
    rows = blocks.shape[1]
    return pl.pallas_call(
        functools.partial(place_kernel, block_order(blocks.shape[0])),
        name="place_embedding",
        out_shape=(jax.ShapeDtypeStruct((rows, D), lowp), jax.ShapeDtypeStruct((rows, D), lowp)),
        in_specs=[smem(), vmem(), vmem()],
        out_specs=(vmem(), vmem()),
        scratch_shapes=[pltpu.VMEM((rows, D), single)],
        compiler_params=params(60),
        cost_estimate=cost(0, 3 * MIB),
    )(place, blocks, gain)


def embed_back_kernel(order, place_ref, in_ref, gain_ref, keep_ref, more_ref, grad_ref, out_ref, held):
    values = in_ref[...].astype(single)
    inv = lax.rsqrt(jnp.mean(values * values, axis=-1, keepdims=True) + TINY_NORM)
    upstream = keep_ref[...] + more_ref[...].astype(single)
    held[...] = grad_ref[...] + rms_back(values, inv, gain_ref[...], upstream)
    width = out_ref.shape[2]
    for p, j in enumerate(order):
        block = held[:, p * width : (p + 1) * width].astype(lowp)
        out_ref[pl.ds(place_ref[1] ^ j, 1)] = block[None]


def embed_back(place, values, gain, keep, more, grad):
    rows = values.shape[0]
    size = lax.axis_size("dp")
    return pl.pallas_call(
        functools.partial(embed_back_kernel, block_order(size)),
        name="embed_back",
        out_shape=jax.ShapeDtypeStruct((size, rows, D // size), lowp),
        in_specs=[smem()] + [vmem()] * 5,
        out_specs=vmem(),
        scratch_shapes=[pltpu.VMEM((rows, D), single)],
        compiler_params=params(60),
        cost_estimate=cost(0, 4 * MIB),
    )(place, values, gain, keep, more, grad)


def scatter_kernel(bits, count_ref, code_ref, base_ref, grad_ref, out_ref, rows):
    total = grad_ref.shape[0]
    vocab = base_ref.shape[0]

    @pl.loop(0, total // 512)
    def _(i):
        here = pl.ds(pl.multiple_of(i * 512, 512), 512)
        rows[here, :] = grad_ref[here, :].astype(single)

    rows[pl.ds(total, 8), :] = jnp.zeros((8, rows.shape[1]), single)

    @pl.loop(0, vocab // 400)
    def _(i):
        here = pl.ds(pl.multiple_of(i * 400, 400), 400)
        out_ref[here, :] = base_ref[here, :]

    count = count_ref[0]

    def group(g, carry):
        for j in range(8):
            index = g * 8 + j
            code = jnp.where(index < count, code_ref[index], total << bits)
            token = lax.shift_right_logical(code, bits)
            row = code & ((1 << bits) - 1)
            out_ref[pl.ds(row, 1), :] = out_ref[pl.ds(row, 1), :] + rows[pl.ds(token, 1), :]
        return carry

    lax.fori_loop(0, (count + 7) // 8, group, jnp.int32(0))


def scatter(bits, count, codes, base, grad):
    total, width = grad.shape
    return pl.pallas_call(
        functools.partial(scatter_kernel, bits),
        name="scatter",
        out_shape=jax.ShapeDtypeStruct(base.shape, single),
        in_specs=[smem(), smem(), vmem(), vmem()],
        out_specs=vmem(),
        scratch_shapes=[pltpu.VMEM((total + 8, width), single)],
        compiler_params=params(60),
        cost_estimate=cost(0, 30 * MIB),
    )(count, codes, base, grad)


def state_kernel(order, width, place_ref, gain_ref, in_ref, out_ref, held):
    rows = in_ref.shape[1]
    values = in_ref[0].astype(single)
    inv = lax.rsqrt(jnp.mean(values * values, axis=-1, keepdims=True) + TINY_NORM)
    for p, j in enumerate(order):
        start = pl.multiple_of((place_ref[1] ^ j) * width, width)
        block = in_ref[0, :, pl.ds(start, width)].astype(single)
        held[p] = block * inv * gain_ref[:, p * width : (p + 1) * width]
    groups = out_ref.shape[0]
    for p in range(len(order)):
        cols = slice(p * width, (p + 1) * width)
        if groups == 1:
            out_ref[0, :, cols] = held[p].astype(lowp)
        else:
            for j in range(groups):
                part = held[p, pl.ds(j, rows // groups, stride=groups), :]
                out_ref[j, :, cols] = part.astype(lowp)


def state_norm(place, gain, states, groups):
    size = lax.axis_size("dp")
    order = block_order(size)
    width = D // size
    streams = states.shape[0]
    count = states.shape[1] // groups
    if width % 128:
        values = jnp.where(place[0] == 1, jnp.flip(states, 0), states).astype(single).reshape(-1, D)
        inv = lax.rsqrt(jnp.mean(values * values, axis=-1, keepdims=True) + TINY_NORM)
        lanes = jnp.arange(D, dtype=jnp.int32)
        blocks = jnp.asarray(order, jnp.int32)[lanes // width] ^ place[1]
        source = blocks * width + lanes % width
        shuffle = (lanes[:, None] == source[None, :]).astype(single)
        moved = jnp.dot(values * inv, shuffle, precision=lax.Precision.HIGHEST)
        out = (moved * gain).astype(lowp)
        return jnp.swapaxes(out.reshape(streams * count, groups, D), 0, 1)
    tile = 128
    return pl.pallas_call(
        functools.partial(state_kernel, order, width),
        name="state_norm",
        out_shape=jax.ShapeDtypeStruct((groups, streams * count, D), lowp),
        grid_spec=pltpu.PrefetchScalarGridSpec(
            num_scalar_prefetch=1,
            grid=(streams, count // tile),
            in_specs=[
                pl.BlockSpec((1, D), lambda n, i, s: (0, 0)),
                pl.BlockSpec((1, tile * groups, D), lambda n, i, s: (s[0] ^ n, i, 0)),
            ],
            out_specs=pl.BlockSpec(
                (groups, tile, D), lambda n, i, s: (0, n * (count // tile) + i, 0)
            ),
            scratch_shapes=[pltpu.VMEM((len(order), tile * groups, width), single)],
        ),
        compiler_params=params(60),
        cost_estimate=cost(0, 4 * streams * count * groups * D),
    )(place, gain, states)


def compress_kernel(old_ref, key_ref, value_ref, conv_ref, comp_ref, raw_ref):
    heads = conv_ref.shape[0]
    wide = heads * DH
    for part, weight_ref in enumerate((key_ref, value_ref)):
        sums = [None] * heads
        for j in range(RATE):
            raw = mm(old_ref[j], weight_ref[...], NT).astype(lowp)
            raw_ref[j, :, part * wide : (part + 1) * wide] = raw
            for n in range(heads):
                piece = raw[:, n * DH : (n + 1) * DH]
                term = mm(piece, conv_ref[n, j * DH : (j + 1) * DH, :])
                sums[n] = term if j == 0 else sums[n] + term
        for n in range(heads):
            first = part * wide + n * DH
            comp_ref[:, first : first + DH] = sums[n].astype(lowp)


def compress(old3, weights, conv):
    rows = old3.shape[1]
    wide = conv.shape[0] * DH
    tile = 256
    return pl.pallas_call(
        compress_kernel,
        name="compress",
        grid=(rows // tile,),
        out_shape=(
            jax.ShapeDtypeStruct((rows, 2 * wide), lowp),
            jax.ShapeDtypeStruct((RATE, rows, 2 * wide), lowp),
        ),
        in_specs=[
            pl.BlockSpec((RATE, tile, D), lambda i: (0, i, 0)),
            pl.BlockSpec((wide, D), lambda i: (1, 0)),
            pl.BlockSpec((wide, D), lambda i: (2, 0)),
            pl.BlockSpec(conv.shape, lambda i: (0, 0, 0)),
        ],
        out_specs=(
            pl.BlockSpec((tile, 2 * wide), lambda i: (i, 0)),
            pl.BlockSpec((RATE, tile, 2 * wide), lambda i: (0, i, 0)),
        ),
        compiler_params=params(60),
        cost_estimate=cost(4 * RATE * rows * wide * D, 12 * MIB),
    )(old3, weights, weights, conv)


def expand_kernel(grad_ref, raw_ref, conv_ref, out_ref, conv_out_ref):
    heads = conv_ref.shape[0]
    for h in range(heads):
        for j in range(RATE):
            rows = slice(j * DH, (j + 1) * DH)
            taps = conv_ref[h, rows, :]
            total = None
            for n in (h, heads + h):
                cols = slice(n * DH, (n + 1) * DH)
                grad = grad_ref[:, cols]
                out_ref[j, :, cols] = mm(grad, taps, NT).astype(lowp)
                term = mm(raw_ref[j, :, cols], grad, TN)
                total = term if total is None else total + term
            conv_out_ref[h, rows, :] = total


def expand(grad, raw, conv):
    return pl.pallas_call(
        expand_kernel,
        name="expand",
        out_shape=(
            jax.ShapeDtypeStruct(raw.shape, lowp),
            jax.ShapeDtypeStruct(conv.shape, single),
        ),
        in_specs=[vmem()] * 3,
        out_specs=(vmem(), vmem()),
        compiler_params=params(60),
        cost_estimate=cost(2000 * MIB, 12 * MIB),
    )(grad, raw, conv)


def masked_scores(info_ref, query, keys):
    rows = query.shape[0]
    scale = DH ** (-0.5)
    result = []
    for which, key in enumerate(keys):
        slots = key.shape[0]
        col = lax.broadcasted_iota(jnp.int32, (rows, slots), 1)
        if which < 2:
            seen = col >= slots - info_ref[2 * pl.program_id(0) + which]
        else:
            row = lax.broadcasted_iota(jnp.int32, (rows, slots), 0)
            shift = info_ref[4]
            row = row + shift
            col = col + shift
            row = jnp.where(row >= slots, row - slots, row)
            col = jnp.where(col >= slots, col - slots, col)
            seen = col <= row
        result.append(jnp.where(seen, mm(query, key, NT) * scale, -1e30))
    return result


def rows_of(ref):
    return ref[...].reshape(-1, ref.shape[-1])


def attend_kernel(info_ref, q_ref, ks_ref, vs_ref, kc_ref, vc_ref, km_ref, vm_ref, out_ref, lse_ref):
    query = rows_of(q_ref)
    scores = masked_scores(info_ref, query, [kc_ref[...], km_ref[...], rows_of(ks_ref)])
    top = functools.reduce(jnp.maximum, [jnp.max(s, axis=-1, keepdims=True) for s in scores])
    total = 0.0
    mixed = 0.0
    for score, value in zip(scores, (vc_ref[...], vm_ref[...], rows_of(vs_ref))):
        weight = jnp.exp(score - top)
        total = total + jnp.sum(weight, axis=-1, keepdims=True)
        mixed = mixed + mm(weight.astype(lowp), value)
    out_ref[...] = (mixed / total).astype(lowp).reshape(out_ref.shape)
    lse_ref[0, 0] = top + jnp.log(total)


def attend_back_kernel(
    info_ref, q_ref, ks_ref, vs_ref, kc_ref, vc_ref, km_ref, vm_ref, lse_ref, up_ref,
    seg_ref, comp_ref, mem_ref,
):
    head = pl.program_id(1)
    wide = pl.num_programs(1) * DH
    scale = DH ** (-0.5)
    query = rows_of(q_ref)
    upstream = rows_of(up_ref)
    keys = [kc_ref[...], km_ref[...], rows_of(ks_ref)]
    scores = masked_scores(info_ref, query, keys)
    probs = [jnp.exp(s - lse_ref[0, 0]) for s in scores]
    prob_grads = [
        mm(upstream, v, NT) for v in (vc_ref[...], vm_ref[...], rows_of(vs_ref))
    ]
    inner = 0.0
    for p, g in zip(probs, prob_grads):
        inner = inner + jnp.sum(p * g, axis=-1, keepdims=True)
    here = pl.ds(pl.multiple_of(head * DH, DH), DH)
    second = pl.ds(pl.multiple_of(wide + head * DH, DH), DH)
    third = pl.ds(pl.multiple_of(2 * wide + head * DH, DH), DH)
    query_grad = 0.0
    places = ((comp_ref, here, second), (mem_ref, here, second), (seg_ref, second, third))
    for p, g, key, (ref, key_at, value_at) in zip(probs, prob_grads, keys, places):
        score_grad = (p * (g - inner)).astype(lowp)
        query_grad = query_grad + mm(score_grad, key)
        shape = ref.shape[:-1] + (DH,)
        key_grad = (mm(score_grad, query, TN) * scale).astype(lowp)
        value_grad = mm(p.astype(lowp), upstream, TN).astype(lowp)
        ref[..., key_at] = key_grad.reshape(shape)
        ref[..., value_at] = value_grad.reshape(shape)
    shape = seg_ref.shape[:-1] + (DH,)
    seg_ref[..., here] = (query_grad * scale).astype(lowp).reshape(shape)


def head_specs(seg, comp, mem, heads):
    streams = seg.shape[1]

    def of_seg(first):
        return pl.BlockSpec((2, 1, seg.shape[2], DH), lambda n, h: (0, n, 0, first + h))

    def cols(array, first):
        return pl.BlockSpec((array.shape[0] // streams, DH), lambda n, h: (n, first + h))

    return [
        smem(),
        of_seg(0),
        of_seg(heads),
        of_seg(2 * heads),
        cols(comp, 0),
        cols(comp, heads),
        cols(mem, 0),
        cols(mem, heads),
    ]


def attend(info, seg, comp, mem):
    _, streams, half, _ = seg.shape
    heads = comp.shape[1] // (2 * DH)
    return pl.pallas_call(
        attend_kernel,
        name="attend",
        grid=(streams, heads),
        out_shape=(
            jax.ShapeDtypeStruct((2, streams, half, heads * DH), lowp),
            jax.ShapeDtypeStruct((streams, heads, 2 * half, 1), single),
        ),
        in_specs=head_specs(seg, comp, mem, heads),
        out_specs=(
            pl.BlockSpec((2, 1, half, DH), lambda n, h: (0, n, 0, h)),
            pl.BlockSpec((1, 1, 2 * half, 1), lambda n, h: (n, h, 0, 0)),
        ),
        compiler_params=params(60),
        cost_estimate=cost(7000 * MIB, 6 * MIB),
    )(info, seg, seg, seg, comp, comp, mem, mem)


def attend_back(info, seg, comp, mem, lse, upstream):
    _, streams, half, wide = seg.shape
    heads = comp.shape[1] // (2 * DH)
    slots = comp.shape[0] // streams
    kept = mem.shape[0] // streams
    return pl.pallas_call(
        attend_back_kernel,
        name="attend_back",
        grid=(streams, heads),
        out_shape=(
            jax.ShapeDtypeStruct(seg.shape, lowp),
            jax.ShapeDtypeStruct(comp.shape, lowp),
            jax.ShapeDtypeStruct(mem.shape, lowp),
        ),
        in_specs=head_specs(seg, comp, mem, heads)
        + [
            pl.BlockSpec((1, 1, 2 * half, 1), lambda n, h: (n, h, 0, 0)),
            pl.BlockSpec((2, 1, half, DH), lambda n, h: (0, n, 0, h)),
        ],
        out_specs=(
            pl.BlockSpec((2, 1, half, wide), lambda n, h: (0, n, 0, 0)),
            pl.BlockSpec((slots, comp.shape[1]), lambda n, h: (n, 0)),
            pl.BlockSpec((kept, mem.shape[1]), lambda n, h: (n, 0)),
        ),
        compiler_params=params(60),
        cost_estimate=cost(11000 * MIB, 9 * MIB),
    )(info, seg, seg, seg, comp, comp, mem, mem, lse, upstream)


def columns_of(rows):
    tall = jnp.concatenate([rows, jnp.zeros((120, rows.shape[1]), single)], axis=0)
    return jnp.transpose(tall)


def logits_kernel(
    words, pair_info_ref, near_info_ref, pair_ref, near_ref, left_ref, right_ref,
    pair_out_ref, near_out_ref, stat_ref,
):
    step = pl.program_id(0)
    tile = pair_ref.shape[0]
    half = left_ref.shape[1]
    edge = left_ref.shape[0] - 128
    streams = (
        (pair_info_ref, pair_ref, pair_out_ref),
        (near_info_ref, near_ref, near_out_ref),
    )
    products = [
        mm(ref[:, :half], left_ref[...], NT) + mm(ref[:, half:], right_ref[...], NT)
        for _, ref, _ in streams
    ]
    for n, ((info_ref, _, out_ref), logits) in enumerate(zip(streams, products)):
        wanted = columns_of(info_ref[0])[:, 0:1].astype(jnp.int32)
        col = lax.broadcasted_iota(jnp.int32, logits.shape, 1)
        hit = jnp.sum(jnp.where(col == wanted, logits, 0.0), axis=-1, keepdims=True)
        last = jnp.where(col[:, edge:] < words, logits[:, edge:], -1e30)
        top = jnp.max(last, axis=-1, keepdims=True)
        top = jnp.maximum(top, jnp.max(logits[:, :edge], axis=-1, keepdims=True))
        raised = jnp.exp(logits[:, :edge] - top)
        last = jnp.exp(last - top)
        total = jnp.sum(raised, axis=-1, keepdims=True) + jnp.sum(last, axis=-1, keepdims=True)
        out_ref[:, :edge] = raised.astype(lowp)
        out_ref[:, edge:] = last.astype(lowp)
        lane = lax.broadcasted_iota(jnp.int32, (tile, 128), 1)
        packed = jnp.where(lane == 2, hit, 0.0)
        packed = jnp.where(lane == 0, top, jnp.where(lane == 1, total, packed))
        start = n * (stat_ref.shape[1] // 2) + step * tile
        stat_ref[:, pl.ds(pl.multiple_of(start, tile), tile)] = jnp.transpose(packed)[:8]


def logits_part(words, chunk, info, pair, near, left, right):
    rows, _ = pair.shape
    slots = left.shape[0]
    tile = 256
    tiles = rows // tile
    whole = lambda i: (0, 0)
    return pl.pallas_call(
        functools.partial(logits_kernel, words),
        name="logits_part",
        grid=(tiles,),
        out_shape=(
            jax.ShapeDtypeStruct((rows, slots), lowp),
            jax.ShapeDtypeStruct((rows, slots), lowp),
            jax.ShapeDtypeStruct((8, 2 * rows), single),
        ),
        in_specs=[
            pl.BlockSpec((1, 8, tile), lambda i: (chunk, 0, i)),
            pl.BlockSpec((1, 8, tile), lambda i: (chunk, 0, tiles + i)),
            pl.BlockSpec((tile, D), lambda i: (i, 0)),
            pl.BlockSpec((tile, D), lambda i: (i, 0)),
            pl.BlockSpec(left.shape, whole),
            pl.BlockSpec(right.shape, whole),
        ],
        out_specs=(
            pl.BlockSpec((tile, slots), lambda i: (i, 0)),
            pl.BlockSpec((tile, slots), lambda i: (i, 0)),
            pl.BlockSpec((8, 2 * rows), whole),
        ),
        compiler_params=params(60),
        cost_estimate=cost(8 * rows * slots * D, 10 * MIB),
    )(info, info, pair, near, left, right)


def logits_back_kernel(
    pair_info_ref, near_info_ref, pair_factor_ref, near_factor_ref, pair_ref, near_ref,
    left_ref, right_ref, pair_out_ref, near_out_ref, pair_grad_ref, near_grad_ref,
):
    half = left_ref.shape[1]
    streams = (
        (near_info_ref, near_factor_ref, near_ref, near_out_ref, near_grad_ref),
        (pair_info_ref, pair_factor_ref, pair_ref, pair_out_ref, pair_grad_ref),
    )
    for info_ref, factor_ref, in_ref, out_ref, grad_ref in streams:
        info = columns_of(info_ref[0])
        wanted = info[:, 0:1].astype(jnp.int32)
        counted = info[:, 1:2]
        factor = columns_of(factor_ref[0])[:, 0:1]
        raised = in_ref[...].astype(single)
        col = lax.broadcasted_iota(jnp.int32, raised.shape, 1)
        grads = (raised * factor - jnp.where(col == wanted, counted, 0.0)).astype(lowp)
        out_ref[...] = grads
        grad_ref[:, :half] = mm(grads, left_ref[...]).astype(lowp)
        grad_ref[:, half:] = mm(grads, right_ref[...]).astype(lowp)


def logits_back(chunk, info, factor, raised, left, right):
    rows, slots = raised[0].shape
    tile = 256
    tiles = rows // tile
    whole = lambda i: (0, 0)

    def info_specs():
        return [
            pl.BlockSpec((1, 8, tile), lambda i: (chunk, 0, i)),
            pl.BlockSpec((1, 8, tile), lambda i: (chunk, 0, tiles + i)),
        ]

    return pl.pallas_call(
        logits_back_kernel,
        name="logits_back",
        grid=(tiles,),
        out_shape=(
            jax.ShapeDtypeStruct((rows, slots), lowp),
            jax.ShapeDtypeStruct((rows, slots), lowp),
            jax.ShapeDtypeStruct((rows, D), lowp),
            jax.ShapeDtypeStruct((rows, D), lowp),
        ),
        in_specs=info_specs()
        + info_specs()
        + [pl.BlockSpec((tile, slots), lambda i: (i, 0))] * 2
        + [pl.BlockSpec(left.shape, whole), pl.BlockSpec(right.shape, whole)],
        out_specs=(
            pl.BlockSpec((tile, slots), lambda i: (i, 0)),
            pl.BlockSpec((tile, slots), lambda i: (i, 0)),
            pl.BlockSpec((tile, D), lambda i: (i, 0)),
            pl.BlockSpec((tile, D), lambda i: (i, 0)),
        ),
        compiler_params=params(60),
        cost_estimate=cost(8 * rows * slots * D, 12 * MIB),
    )(info, info, factor, factor, *raised, left, right)


def halves(total, keep_ref, send_ref):
    half = keep_ref.shape[1]
    keep_ref[...] = total[:, :half]
    send_ref[...] = total[:, half:].astype(send_ref.dtype)


def table_grad_kernel(count, *refs):
    total = mm(refs[0][...], refs[count][...], TN)
    for i in range(1, count):
        total = total + mm(refs[i][...], refs[count + i][...], TN)
    halves(total, *refs[2 * count :])


def table_grad_part(grads, inputs):
    grads = [half for pair in grads for half in pair]
    inputs = [half for pair in inputs for half in pair]
    rows = sum(g.shape[0] for g in grads)
    slots = grads[0].shape[1]
    block = 256
    if rows > 4096:
        keep, send = split(sum(mm(g, v, TN) for g, v in zip(grads, inputs)), 1, 2)
        return keep, send.astype(lowp)
    return pl.pallas_call(
        functools.partial(table_grad_kernel, len(grads)),
        name="table_grad_part",
        grid=(slots // block,),
        out_shape=(
            jax.ShapeDtypeStruct((slots, D // 2), single),
            jax.ShapeDtypeStruct((slots, D // 2), lowp),
        ),
        in_specs=[pl.BlockSpec((g.shape[0], block), lambda i: (0, i)) for g in grads]
        + [pl.BlockSpec(v.shape, lambda i: (0, 0)) for v in inputs],
        out_specs=(
            pl.BlockSpec((block, D // 2), lambda i: (i, 0)),
            pl.BlockSpec((block, D // 2), lambda i: (i, 0)),
        ),
        compiler_params=params(60),
        cost_estimate=cost(3 * rows * slots * D, 30 * MIB),
    )(*grads, *inputs)


def hidden_grad_kernel(blocks, pre_ref, act_ref, in_ref, down_ref, keep_ref, send_ref):
    step = pl.program_id(0)

    @pl.when(step < blocks)
    def _():
        halves(mm(pre_ref[...], in_ref[...], TN), keep_ref, send_ref)

    @pl.when(step >= blocks)
    def _():
        halves(mm(act_ref[...], down_ref[...], TN), keep_ref, send_ref)


def hidden_grads(pre_grad, hidden_act, ffn_in, down_in):
    rows, hidden = pre_grad.shape
    block = 256
    blocks = hidden // block
    return pl.pallas_call(
        functools.partial(hidden_grad_kernel, blocks),
        name="hidden_grads",
        grid=(2 * blocks,),
        out_shape=(
            jax.ShapeDtypeStruct((2 * hidden, D // 2), single),
            jax.ShapeDtypeStruct((2 * hidden, D // 2), lowp),
        ),
        in_specs=[
            pl.BlockSpec((rows, block), lambda i: (0, jnp.minimum(i, blocks - 1))),
            pl.BlockSpec((rows, block), lambda i: (0, jnp.maximum(i - blocks, 0))),
            pl.BlockSpec((rows, D), lambda i: (0, 0)),
            pl.BlockSpec((rows, D), lambda i: (0, 0)),
        ],
        out_specs=(
            pl.BlockSpec((block, D // 2), lambda i: (i, 0)),
            pl.BlockSpec((block, D // 2), lambda i: (i, 0)),
        ),
        compiler_params=params(60),
        cost_estimate=cost(6 * rows * hidden * D, 16 * MIB),
    )(pre_grad, hidden_act, ffn_in, down_in)


def attn_grad_kernel(
    seg_ref, mixed_ref, mem_ref, old_ref, normed_ref, up_ref, mem_in_ref, old_in_ref, keep_ref, send_ref
):
    which = pl.program_id(0)

    @pl.when(which == 0)
    def _():
        halves(mm(seg_ref[...], normed_ref[...], TN), keep_ref, send_ref)

    @pl.when(which == 3)
    def _():
        halves(mm(mixed_ref[...], up_ref[...], TN), keep_ref, send_ref)

    @pl.when(jnp.logical_and(which > 0, which < 3))
    def _():
        total = mm(seg_ref[...], normed_ref[...], TN)
        total = total + mm(mem_ref[...], mem_in_ref[...], TN)
        total = total + mm(old_ref[...], old_in_ref[...], TN)
        halves(total, keep_ref, send_ref)


def attn_grads(seg_grad, mixed, mem_grad, old_grad, normed, attn_in, mem_in, old_in):
    block = mixed.shape[1]

    def whole(array):
        return pl.BlockSpec(array.shape, lambda i: (0, 0))

    return pl.pallas_call(
        attn_grad_kernel,
        name="attn_grads",
        grid=(4,),
        out_shape=(
            jax.ShapeDtypeStruct((4 * block, D // 2), single),
            jax.ShapeDtypeStruct((4 * block, D // 2), lowp),
        ),
        in_specs=[
            pl.BlockSpec((seg_grad.shape[0], block), lambda i: (0, jnp.minimum(i, 2))),
            whole(mixed),
            pl.BlockSpec((mem_grad.shape[0], block), lambda i: (0, jnp.clip(i - 1, 0, 1))),
            pl.BlockSpec((old_grad.shape[0], block), lambda i: (0, jnp.clip(i - 1, 0, 1))),
            whole(normed),
            whole(attn_in),
            whole(mem_in),
            whole(old_in),
        ],
        out_specs=(
            pl.BlockSpec((block, D // 2), lambda i: (i, 0)),
            pl.BlockSpec((block, D // 2), lambda i: (i, 0)),
        ),
        compiler_params=params(60),
        cost_estimate=cost(9000 * MIB, 24 * MIB),
    )(seg_grad, mixed, mem_grad, old_grad, normed, attn_in, mem_in, old_in)


def scalar_row(values, length=128):
    lane = jnp.arange(length, dtype=jnp.int32)
    row = jnp.zeros((length,), single)
    for i, value in enumerate(values):
        row = jnp.where(lane == i, value, row)
    return row


def local(
    ids,
    targets,
    target_mask,
    memory,
    old_states,
    mem_fill,
    comp_fill,
    table,
    qkv,
    wout,
    wconv,
    wup,
    wdown,
    gains,
    table_rows,
    table_cols,
    qkv_rows,
    qkv_cols,
    out_rows,
    out_cols,
    conv_rows,
    conv_cols,
    up_rows,
    up_cols,
    down_rows,
    down_cols,
    gains_second,
):
    dp_size, head_size = lax.axis_size("dp"), lax.axis_size("head")
    d, h = lax.axis_index("dp"), lax.axis_index("head")
    x, c = h // 2, h % 2
    order = block_order(dp_size)
    reach = dp_size // 2
    streams, seg_len = ids.shape
    half = seg_len // 2
    per_group = streams * seg_len
    vocab, width = table.shape
    assert head_size == 4 and streams == 2

    weights_now = (table, qkv, wout, wconv, wup, wdown)
    rows_old = (table_rows, qkv_rows, out_rows, conv_rows, up_rows, down_rows)
    cols_old = (table_cols, qkv_cols, out_cols, conv_cols, up_cols, down_cols)
    sizes = {"dp": dp_size, "head": head_size}
    row_axes = ("head", "dp", "head", "head", "dp", "head")
    col_axes = ("dp", "head", "dp", "dp", "head", "dp")

    def early_sums(dep):
        _, *tied = together(dep, *rows_old, *weights_now, gains)
        sums = [jnp.sum(old) / sizes[axis] for old, axis in zip(tied[:6], col_axes)]
        sums += [jnp.sum(weight * weight) for weight in tied[6:12]]
        gain_sums = jnp.sum(tied[12] * tied[12], axis=1) / head_size
        return scalar_row(sums + [gain_sums[0], gain_sums[1], gain_sums[2]])

    def core_sum(keep, send, beside=()):
        more, *beside = together(swap(send.astype(lowp), "head", 1), *beside)
        part = keep.astype(single) + more.astype(single)
        return (part, beside) if beside else part

    def stream_sum(part, beside=()):
        keep, send = split(part, 0, 2)
        more, *beside = together(swap(send.astype(lowp), "head", 2), *beside)
        part = keep + more.astype(single)
        return (part, beside) if beside else part

    def group_sum(part, beside=()):
        return stream_sum(core_sum(*split(part, 0, 2)), beside)

    def group_both(part, beside=()):
        far, *beside = together(swap(part, "head", 2), *beside)
        pair = jnp.concatenate([part, far], axis=0)
        both = (pair, swap(pair, "head", 1))
        return (both, beside) if beside else both

    flat = jnp.concatenate(
        [
            ids.astype(single).reshape(-1),
            targets.astype(single).reshape(-1),
            target_mask.astype(single).reshape(-1),
            gains.astype(lowp).astype(single).reshape(-1),
        ]
    )
    room = -flat.shape[0] % 1024
    flat = jnp.concatenate([flat, jnp.zeros((room,), single)]).reshape(1, -1, 128)
    small, small_steps = gather_blocks(flat, 0)
    small = small.reshape(dp_size, -1)
    place = jnp.stack([x, d])

    def field(raw):
        return relative(raw.reshape(-1, 2, 2, half), x, c)

    ids_all = small[:, :per_group]
    position = [order.index(j) for j in range(dp_size)]
    ids_all = jnp.take(ids_all, jnp.asarray(position, jnp.int32)[jnp.arange(dp_size) ^ d], axis=0)
    ids_all = jnp.transpose(field(ids_all), (1, 2, 0, 3)).reshape(-1).astype(jnp.int32)
    table_rows_all = ids_all - h * vocab
    inside = (table_rows_all >= 0) & (table_rows_all < vocab)
    bits = vocab.bit_length()
    token_codes = (jnp.arange(ids_all.shape[0], dtype=jnp.int32) << bits) | table_rows_all
    token_codes = jnp.where(inside, token_codes, -1)
    table_rows_all = jnp.where(inside, table_rows_all, vocab)
    targets_all = field(small[:reach, per_group : 2 * per_group])
    mask_all = field(small[:reach, 2 * per_group : 3 * per_group])
    gain_blocks = small[:, 3 * per_group : 3 * per_group + 3 * width].reshape(dp_size, 3, width)
    gain_vals = jnp.swapaxes(gain_blocks, 0, 1).reshape(3, 1, D)
    count_all = jnp.sum(small[:, 2 * per_group : 3 * per_group])

    heads_own = wconv.shape[0]
    wide = qkv.shape[2]
    conv_rows_own = wconv.size // width
    low_qkv = qkv.astype(lowp)
    pack_one = jnp.concatenate(
        [
            jnp.swapaxes(low_qkv, 1, 2).reshape(3 * wide, width),
            wout.astype(lowp),
            wconv.astype(lowp).reshape(conv_rows_own, width),
        ]
    )
    own_half, far_half = split(table_rows_all, 0, 2)
    kept = {}
    hidden_own = wup.shape[1]
    pack_two = jnp.concatenate([wup.astype(lowp).T, wdown.astype(lowp)])

    def beside_lookup(moved):
        moved, kept["far"], kept["own"] = together(
            moved, lookup(far_half, table), lookup(own_half, table)
        )
        kept["two"] = after(pack_two, moved)
        return moved

    def beside_memory(moved):
        looked = (kept["own"] + swap(kept["far"], "head", 1)).reshape(2, -1, width)
        mem_normed = state_norm(place, gain_vals[0], memory, 1)[0]
        moved, more, kept["mem"], second = together(
            moved, swap(looked[1], "head", 2), mem_normed, swap(kept["two"], "dp", dp_size // 2)
        )
        kept["two"] = jnp.concatenate([kept["two"], second], axis=1)
        looked = (looked[0] + more).reshape(dp_size, half, width)
        kept["looked"] = lax.all_to_all(looked, "dp", 0, 0)
        return moved

    own_one, steps_one = gather_blocks(
        after(pack_one, small_steps[0]), 1, (beside_lookup, beside_memory)
    )
    conv_lanes = jnp.arange(DH, dtype=jnp.int32)
    conv_width = DH // dp_size
    conv_natural = (jnp.asarray(order, jnp.int32)[conv_lanes // conv_width] ^ d) * conv_width
    conv_natural = conv_natural + conv_lanes % conv_width
    conv_shuffle = (conv_natural[:, None] == conv_lanes[None, :]).astype(lowp)
    taps = heads_own * RATE * DH

    def conv_natural_order(rows):
        value = jnp.swapaxes(rows.reshape(conv_rows_own, dp_size, width), 0, 1)
        value = jnp.swapaxes(value.reshape(dp_size, taps, conv_width), 0, 1)
        moved = mm(value.reshape(taps, DH), conv_shuffle).astype(lowp)
        return moved.reshape(heads_own, RATE * DH, DH)

    def conv_block_order(value):
        moved = mm(value.astype(lowp).reshape(taps, DH), conv_shuffle, NT).astype(lowp)
        moved = jnp.swapaxes(moved.reshape(taps, dp_size, conv_width), 0, 1)
        moved = jnp.swapaxes(moved.reshape(dp_size, conv_rows_own, width), 0, 1)
        return moved.reshape(conv_rows_own, D)

    full_conv = conv_natural_order(own_one[4 * wide :])


    old_normed = state_norm(place, gain_vals[0], old_states, RATE)

    words = vocab // reach
    z = d // 2
    word_start = (h * vocab + z * words).astype(single)
    wanted_all = targets_all - word_start
    wanted_all = jnp.where((wanted_all >= 0) & (wanted_all < words), wanted_all, -1.0)
    info_all = jnp.stack([wanted_all, mask_all] + [jnp.zeros_like(mask_all)] * 6)
    info_all = jnp.transpose(info_all, (1, 0, 2, 3, 4)).reshape(reach, 8, per_group)

    looked, old_normed, info_all = together(kept["looked"], old_normed, info_all)
    embedded_low, normed = place_embedding(place, looked, gain_vals[0])
    embedded = embedded_low.astype(single)

    def beside_compress(moved):
        moved, *kept["comp"] = together(moved, *compress(old_normed, own_one, full_conv))
        return moved

    near_two, steps_two = gather_blocks(
        kept["two"], 1, (beside_compress,), 1, dp_size // 4
    )
    near_up, near_down = split(near_two, 0, 2)
    far_up, far_down = swap(near_up, "dp", 1), swap(near_down, "dp", 1)
    mem_normed = kept["mem"]
    normed = jnp.concatenate(group_both(normed))
    comp, old_raw = kept["comp"]

    words = vocab // reach
    z = d // 2
    unsigned_z = z.astype(jnp.uint32)
    z_groups = [[2 * i + b for i in range(reach)] for b in range(2)]
    slots = -(-words // 256) * 256


    comp_fill, mem_fill, _ = together(comp_fill, mem_fill, kept["mem"])
    comp_counts = jnp.where(x == 1, jnp.flip(comp_fill), comp_fill)
    mem_counts = jnp.where(x == 1, jnp.flip(mem_fill), mem_fill)
    info = [comp_counts[0], mem_counts[0], comp_counts[1], mem_counts[1], c * half]
    lane = jnp.arange(8, dtype=jnp.int32)
    info = sum(jnp.where(lane == i, value, 0) for i, value in enumerate(info)).astype(jnp.int32)

    in_weight = own_one[: 3 * wide]
    mem = mm(mem_normed, own_one[wide : 3 * wide], NT).astype(lowp)
    seg = mm(normed, in_weight, NT).astype(lowp).reshape(2, streams, half, 3 * wide)
    low_table = after(table.astype(lowp), seg).reshape(reach, words, width)
    low_table = lax.all_to_all(low_table, "dp", 0, 0, axis_index_groups=z_groups)
    mixed, lse = attend(info, seg, comp, mem)
    mixed = mixed.reshape(-1, wide)
    attn_sum, (far_up,) = core_sum(
        *split(mm(mixed, own_one[3 * wide : 4 * wide]), 0, 2), (far_up,)
    )
    attn_sum, (far_down,) = stream_sum(attn_sum, (far_down,))
    after_attn = embedded + attn_sum
    ffn_in, inv_second = rms(after_attn, gain_vals[1])
    ffn_in, (low_table,) = group_both(ffn_in, (low_table,))
    near_table = [
        lax.dynamic_index_in_dim(low_table, unsigned_z ^ jnp.uint32(m // 2), 0, keepdims=False) for m in order[:reach]
    ]
    near_table = jnp.concatenate(near_table, axis=1)
    near_table = jnp.concatenate([near_table, jnp.zeros((slots - words, D // 2), lowp)], axis=0)
    ffn_in = jnp.concatenate(ffn_in)
    full_up = jnp.concatenate([near_up, far_up], axis=1)
    full_down = jnp.concatenate([near_down, far_down], axis=1)
    far_table = swap(near_table, "dp", 1)
    hidden_pre = mm(ffn_in, full_up, NT)
    hidden_act = jax.nn.gelu(hidden_pre).astype(lowp)
    after_ffn = after_attn + group_sum(mm(hidden_act, full_down))
    final_in, inv_third = rms(after_ffn, gain_vals[2])

    pieces = [final_in]
    chunks = []
    raised = []
    stats = []

    def next_chunk():
        i = len(chunks)
        if i == 0:
            chunk, kept["list"] = group_both(pieces[i], own_list(after(token_codes, final_in)))
            chunks.append(chunk)
        else:
            chunk, (stats[i - 1],) = group_both(pieces[i], (stats[i - 1],))
            chunks.append(chunk)
        *out, stat = logits_part(words, i, info_all, *chunks[i], near_table, far_table)
        raised.append(out)
        stats.append(stat)

    mask = dp_size // 2
    while mask > 1:
        moved = swap(reorder(pieces, mask), "dp", mask)
        if len(pieces) == 1:
            next_chunk()
        elif len(pieces) == 2:
            moved, stats[0] = together(moved, stats[0])
        pieces += split(moved, 0, len(pieces))
        mask //= 2
    while len(chunks) < reach:
        next_chunk()
    own_codes, own_count = kept["list"]
    stats = [stat[:3].reshape(3, 1, 2, 2, half) for stat in stats]
    own_stats = jnp.concatenate(stats, axis=1)

    def combine(first, second):
        top = jnp.maximum(first[0], second[0])
        total = first[1] * jnp.exp(first[0] - top) + second[1] * jnp.exp(second[0] - top)
        return jnp.stack([top, total, first[2] + second[2]])

    merged = own_stats
    merged = combine(merged, jnp.flip(swap(merged, "head", 1), 2))
    merged = combine(merged, jnp.flip(swap(merged, "head", 2), 3))
    mask = 2
    while mask < dp_size:
        other = split(swap(merged, "dp", mask), 1, reach)
        other = [other[order.index(j ^ mask)] for j in order[:reach]]
        merged = combine(merged, jnp.concatenate(other, axis=1))
        mask *= 2
    log_total = merged[0] + jnp.log(merged[1])
    loss_local = jnp.sum(mask_all[0, 0, 0] * (log_total[0, 0, 0] - merged[2, 0, 0, 0]))
    factor_all = jnp.exp(own_stats[0] - log_total)

    factor_all = factor_all.reshape(reach, 1, per_group) * info_all[:, 1:2]
    factor_all = jnp.broadcast_to(factor_all, info_all.shape)
    dlogits = [[] for _ in range(reach)]
    parts = [None] * reach
    for i in reversed(range(reach)):
        *dlogits[i], keep, send = logits_back(
            i, info_all, factor_all, raised[i], near_table, far_table
        )
        if i + 1 < reach:
            parts[i + 1], (*dlogits[i], keep, send) = stream_sum(
                parts[i + 1], (*dlogits[i], keep, send)
            )
        parts[i] = core_sum(keep, send)
    parts[0] = stream_sum(parts[0])
    table_parts = []
    mask = 2
    while len(parts) > 1:
        count = len(parts) // 2
        moved = swap(reorder(parts[count:], mask), "dp", mask)
        if mask == 2:
            moved, *dlogits[0] = together(moved, *dlogits[0])
        elif mask == 4:
            moved, *table_parts = together(moved, *table_grad_part(dlogits, chunks))
        moved = split(moved.astype(single), 0, count)
        parts = [part + more for part, more in zip(parts, moved)]
        mask *= 2
    final_grad = parts[0]

    grad_after_ffn = rms_back(after_ffn, inv_third, gain_vals[2], final_grad)
    moved_table = swap(table_parts[1], "dp", 1)
    down_in, (early,) = group_both(grad_after_ffn.astype(lowp), (early_sums(final_grad),))
    down_in = jnp.concatenate(down_in)
    act_grad = mm(down_in, full_down, NT)
    pre_grad = jax.vjp(jax.nn.gelu, hidden_pre)[1](act_grad)[0].astype(lowp)
    two = hidden_grads(pre_grad, hidden_act, ffn_in, down_in)
    ffn_in_grad, (*two, moved_table) = group_sum(mm(pre_grad, full_up), (*two, moved_table))
    keep = table_parts[0] + moved_table.astype(single)
    table_pieces = jnp.stack(split(keep[:words].astype(lowp), 1, reach))
    turned = sum(
        ((unsigned_z >> bit) & 1) * jnp.uint32(order.index(2 << bit))
        for bit in range(reach.bit_length() - 1)
    )
    table_pieces = jnp.concatenate(
        [
            lax.dynamic_index_in_dim(table_pieces, turned ^ jnp.uint32(order.index(2 * i)), 0)
            for i in range(reach)
        ]
    )
    table_pieces = lax.all_to_all(table_pieces, "dp", 0, 0, axis_index_groups=z_groups)
    grad_after_attn = grad_after_ffn + rms_back(after_attn, inv_second, gain_vals[1], ffn_in_grad)
    attn_in = jnp.concatenate(group_both(grad_after_attn.astype(lowp)))

    mixed_grad = mm(attn_in, own_one[3 * wide : 4 * wide], NT).astype(lowp)
    mixed_grad = mixed_grad.reshape(2, streams, half, wide)
    seg_grad, comp_grad, mem_grad = attend_back(info, seg, comp, mem, lse, mixed_grad)
    seg_grad = seg_grad.reshape(-1, 3 * wide)

    def beside_expand(moved):
        keep, send = split(mm(seg_grad, in_weight), 0, 2)
        more = swap(send.astype(lowp), "head", 1)
        moved, more, kept["table"], *kept["old"] = together(
            moved, more, table_pieces, *expand(comp_grad, old_raw, full_conv)
        )
        kept["seg_in"] = split(keep + more.astype(single), 0, 2)
        return moved

    def beside_sums(moved):
        seg_in, seg_in_far = kept["seg_in"]
        seg_in_far = swap(seg_in_far.astype(lowp), "head", 2)
        old_grad, conv_sum = kept["old"]
        sums = attn_grads(
            seg_grad,
            mixed,
            mem_grad,
            old_grad.reshape(-1, old_grad.shape[-1]),
            normed,
            attn_in,
            mem_normed,
            old_normed.reshape(-1, D),
        )
        conv_sum = split(conv_block_order(conv_sum), 1, 2)
        sums = [jnp.concatenate([part, more.astype(part.dtype)]) for part, more in zip(sums, conv_sum)]
        seg_in_far, *kept["sums"] = together(seg_in_far, *sums)
        rows_grad = embed_back(
            place, embedded_low, gain_vals[0], seg_in, seg_in_far, grad_after_attn
        )
        moved, kept["rows"] = together(moved, lax.all_to_all(rows_grad, "dp", 0, 0))
        return moved

    def beside_streams(moved):
        moved, far = together(moved, swap(kept["rows"], "head", 2))
        rows_grad = jnp.stack([kept["rows"], far])
        kept["rows"] = jnp.stack([rows_grad, swap(rows_grad, "head", 1)]).reshape(-1, width)
        return moved

    def beside_scatter(moved):
        table_base = kept["table"].astype(single).reshape(vocab, width)
        table_grad = scatter(bits, own_count, own_codes, table_base, kept["rows"])
        moved, kept["table"], kept["table_grad"] = together(moved, table_base, table_grad)
        return moved

    two = reduce_blocks(*two, (beside_expand, beside_sums))
    one = reduce_blocks(*kept["sums"], (beside_streams, beside_scatter))
    table_base, table_grad = kept["table"], kept["table_grad"]

    up_grad = two[:hidden_own].T
    down_grad = two[hidden_own:]
    qkv_grad = jnp.swapaxes(one[: 3 * wide].reshape(3, wide, width), 1, 2)
    out_grad = one[3 * wide : 4 * wide]
    conv_grad = one[4 * wide :].reshape(wconv.shape)

    gains_low = gains.astype(lowp).astype(single)
    gain_part = jnp.stack(
        [
            jnp.sum(low_qkv.astype(single) * qkv_grad, axis=(0, 2)),
            jnp.sum(wup.astype(lowp).astype(single) * up_grad, axis=1),
            jnp.sum(table.astype(lowp).astype(single) * table_base, axis=0),
        ]
    )

    grads = (table_grad, qkv_grad, out_grad, conv_grad, up_grad, down_grad)
    def sum_over_dp(joined):
        mask = 1
        while mask < dp_size:
            joined = joined + swap(joined, "dp", mask)
            mask *= 2
        return joined

    row_part = []
    col_part = []
    for grad in grads:
        square = grad * grad
        row_part.append(jnp.sum(square, axis=-1))
        col_part.append(jnp.sum(square, axis=tuple(range(square.ndim - 1))))
    row_q, row_u, col_e, col_o, col_c, col_d, gain_raw, early = lax.psum(
        (
            row_part[1],
            row_part[4],
            col_part[0],
            col_part[2],
            col_part[3],
            col_part[5],
            gain_part,
            early + scalar_row([0.0] * 15 + [loss_local]),
        ),
        "head",
    )
    lanes = [col_e, jnp.sum(row_q, axis=0), col_o]
    lanes += [jnp.concatenate([col_c, jnp.zeros((width - col_c.shape[0],), single)]), row_u, col_d]
    members = [col_part[4], row_part[5], row_part[3], row_part[2], col_part[1], *lanes, row_part[0], early]
    joined = jnp.concatenate([m.reshape(-1) for m in members])
    joined = sum_over_dp(jnp.concatenate([joined, jnp.zeros((-joined.shape[0] % 1024,), single)]))
    sums = []
    start = 0
    for member in members:
        sums.append(joined[start : start + member.size].reshape(member.shape))
        start += member.size
    col_u, row_d, row_c, row_o, col_q, *lanes, row_e, early = sums
    square_total = [jnp.sum(lane) for lane in lanes]
    row_sums = [row_e, row_q, row_o, row_c, row_u, row_d]
    col_sums = [col_e, col_q, col_o, col_c, col_u, col_d]
    weight_total = early[6:15]
    loss_all = early[15]
    inverse = 1.0 / count_all
    decay = 1.0 - STEP ** (-0.8)
    updates = []
    stats_new = []
    scaled = []
    counts = []
    update_sq = []
    for index in range(6):
        rows_total = rows_old[index].size * sizes[row_axes[index]]
        cols_total = cols_old[index].size * sizes[col_axes[index]]
        grad_scaled = grads[index] * inverse
        rows_new = decay * rows_old[index] + (1.0 - decay) * (
            row_sums[index] * inverse * inverse / cols_total + TINY_SQUARE
        )
        cols_new = decay * cols_old[index] + (1.0 - decay) * (
            col_sums[index] * inverse * inverse / rows_total + TINY_SQUARE
        )
        mean_row = decay * early[index] / rows_total + (1.0 - decay) * (
            square_total[index] * inverse * inverse / (rows_total * cols_total) + TINY_SQUARE
        )
        second = rows_new[..., None] * cols_new / mean_row
        direction = grad_scaled * lax.rsqrt(second)
        updates.append(direction)
        stats_new.append((rows_new, cols_new))
        scaled.append(grad_scaled)
        counts.append(rows_total * cols_total)
        update_sq.append(jnp.sum(direction * direction))
    gain_scaled = gain_raw / gains_low * inverse
    second_new = decay * gains_second + (1.0 - decay) * (gain_scaled * gain_scaled + TINY_SQUARE)
    gain_dir = gain_scaled * lax.rsqrt(second_new)
    for which in range(3):
        update_sq.append(jnp.sum(gain_dir[which] * gain_dir[which]) / head_size)
    update_total = after(scalar_row(update_sq, 1024), loss_all)
    for mask in (1, 2):
        update_total = update_total + swap(update_total, "head", mask)
    update_total = sum_over_dp(update_total)[:9]
    results = [loss_all, count_all]
    for index in range(6):
        factor = jnp.maximum(0.001, jnp.sqrt(weight_total[index] / counts[index]))
        denom = jnp.maximum(1.0, jnp.sqrt(update_total[index] / counts[index]) / CLIP_LEVEL)
        new_weight = weights_now[index] - LEARN_RATE * factor * updates[index] / denom
        results += [new_weight, scaled[index], stats_new[index][0], stats_new[index][1]]
    gain_factor = jnp.maximum(0.001, jnp.sqrt(weight_total[6:] / D))[:, None]
    gain_denom = jnp.maximum(1.0, jnp.sqrt(update_total[6:] / D) / CLIP_LEVEL)[:, None]
    results += [gains - LEARN_RATE * gain_factor * gain_dir / gain_denom, gain_scaled, second_new]
    return tuple(results)


def solution(mesh):
    in_specs = (
        P("dp", None),
        P("dp", None),
        P("dp", None),
        P("dp", None, None),
        P("dp", None, None),
        P("dp"),
        P("dp"),
        P("head", "dp"),
        P(None, "dp", "head"),
        P("head", "dp"),
        P("head", None, "dp"),
        P("dp", "head"),
        P("head", "dp"),
        P(None, "dp"),
        P("head"),
        P("dp"),
        P(None, "dp"),
        P("head"),
        P("head"),
        P("dp"),
        P("head", None),
        P("dp"),
        P("dp"),
        P("head"),
        P("head"),
        P("dp"),
        P(None, "dp"),
    )
    out_specs = (
        P(),
        P(),
        P("head", "dp"),
        P("head", "dp"),
        P("head"),
        P("dp"),
        P(None, "dp", "head"),
        P(None, "dp", "head"),
        P(None, "dp"),
        P("head"),
        P("head", "dp"),
        P("head", "dp"),
        P("head"),
        P("dp"),
        P("head", None, "dp"),
        P("head", None, "dp"),
        P("head", None),
        P("dp"),
        P("dp", "head"),
        P("dp", "head"),
        P("dp"),
        P("head"),
        P("head", "dp"),
        P("head", "dp"),
        P("head"),
        P("dp"),
        P(None, "dp"),
        P(None, "dp"),
        P(None, "dp"),
    )
    return jax.shard_map(local, mesh=mesh, in_specs=in_specs, out_specs=out_specs, check_vma=False)
```
